32 devices in a mesh: grp: 2 (over x), dev: 16 (over z, y, core).
Axes of the slice: x: 2, y: 2, z: 4, core: 2. Of those that a mesh axis runs over, the one named last changes fastest.
Arguments:
- pair_ft: bfloat16 [4096, 2, 1024], P('dev', None, 'grp'), may hold values from -6 to 6
- aux_ft: bfloat16 [4096, 2, 1024], P('dev', None, 'grp'), may hold values from -0.125 to 0.125
- coul_weight: float32 [1024], P('grp'), may hold values from 0.2 to 5
- aux_basis: bfloat16 [128, 4096], replicated, may hold values from -0.5 to 0.5
- aux_decay: float32 [4096], replicated, may hold values from 0.05 to 1
- image_dist: float32 [125], replicated, may hold values from 0 to 3
- image_phase: float32 [125], replicated, may hold values from -3.140625 to 3.140625
- item_pair: bfloat16 [512, 128, 128], P(('grp', 'dev')), may hold values from -4 to 4
- item_image: int32 [512], P(('grp', 'dev')), may hold values from 0 to 124
- item_sub: int32 [512], P(('grp', 'dev')), may hold values from 0 to 1
- item_count: int32 [32], P(('grp', 'dev')), may hold values from 0 to 16, as said below
Outputs:
- j3c: bfloat16 [4096, 2, 4096], P('grp', None, 'dev')
The draws below stay inside these ranges and needn't reach their ends.
Inputs may be any that keep to these rules, and one draw needn't show every extreme that they name: `item_count`: in every index of dev one of the 2 devices holds exactly 16 live slots. The counts of the 2 devices that share an index of dev sum to at most 24, and in every draw some index of dev reaches 24.
All inputs are finite; a program needn't handle non-finite values.
Results may differ from the reference program's by a relative error of at most 0.0047.
Values may be sent and summed in bfloat16 or wider, within the bound.
No kernel may reach another device: no remote copies, remote signals or barrier semaphores. Data moves between devices by JAX's collectives and lax.ppermute only.
A program may use at most 64 MiB of HBM per device.

```python
import math
import jax
import jax.numpy as jnp
from jax import lax

NAUX = 4096
KRANK = 128
SUB_ROWS = 128
NIMG = 125
CAP = 16
ROW_DEV = 256
GROUPS = 2
BLOCKS = 16
NPAIR = 4096
NG = 1024
SUBS = 2
DEVICES = 32


def draw_item_count(key, part):
    subkeys = jax.random.split(jax.random.fold_in(key, 17), 3)
    others = jax.random.randint(subkeys[0], (GROUPS, BLOCKS), 0, 9)
    busiest = jax.random.randint(subkeys[1], (BLOCKS,), 0, GROUPS)
    fullest = jax.random.randint(subkeys[2], (), 0, BLOCKS)
    group_ids = jnp.arange(GROUPS, dtype=jnp.int32)[:, None]
    column_ids = jnp.arange(BLOCKS, dtype=jnp.int32)[None, :]
    others = jnp.where(column_ids == fullest, 8, others)
    counts = jnp.where(group_ids == busiest[None, :], CAP, others)
    return counts.reshape(GROUPS * BLOCKS).astype(jnp.int32)


def with_ends(drawn, stream_key, low, largest):
    place = [jax.random.randint(jax.random.fold_in(stream_key, axis), (), 0, length) for axis, length in enumerate(drawn.shape)]
    widest = drawn.shape.index(max(drawn.shape))
    next_to = place[:widest] + [(place[widest] + 1) % drawn.shape[widest]] + place[widest + 1:]
    return drawn.at[tuple(place)].set(low).at[tuple(next_to)].set(largest)


def level_of(stream_key, extent, cuts, least, largest):
    loudness = 1.0
    for dim, parts in cuts:
        steps = jax.random.uniform(jax.random.fold_in(jax.random.fold_in(stream_key, 6), dim), (parts,), jnp.float32, least / len(cuts), largest / len(cuts))
        loudness = loudness * jnp.repeat(jnp.exp(steps), extent[dim] // parts).reshape((-1,) + (1,) * (len(extent) - 1 - dim))
    return loudness


def scatter_about(rng, dims, scale, reach, shards=(), held_as=jnp.bfloat16):
    loudness = level_of(rng, dims, shards, -0.22, 0.18) if shards else 1.0
    entries = jax.random.normal(rng, dims, jnp.float32) * scale * loudness
    return jnp.minimum(jnp.maximum(entries, -reach), reach).astype(held_as)


def setup_inputs(seed: int = 0) -> dict:
    streams_of = jax.random.split(jax.random.key(seed), 12)
    pair_ft = scatter_about(streams_of[0], (NPAIR, 2, NG), 1.0, 6.0, ((0, 16), (2, 2)))
    aux_ft = scatter_about(streams_of[1], (NAUX, 2, NG), (2 * NG) ** -0.5, 0.125, ((0, 16), (2, 2)))
    coul_weight = jnp.clip(jnp.exp(math.log(5.0) - 3.218876 * jax.random.uniform(streams_of[2], (NG,), jnp.float32) ** level_of(streams_of[2], (NG,), ((0, 2),), -0.2, 0.2)), 0.2, 5.0)
    aux_basis = scatter_about(streams_of[3], (KRANK, NAUX), KRANK ** -0.5, 0.5)
    aux_decay = jnp.clip(jnp.exp(jax.random.uniform(streams_of[4], (NAUX,), jnp.float32, math.log(0.05), math.log(1.0))), 0.05, 1.0)
    image_dist = jnp.clip(jax.random.uniform(streams_of[5], (NIMG,), jnp.float32, 0.0, 3.0), 0.0, 3.0)
    image_phase = jnp.clip(jax.random.uniform(streams_of[6], (NIMG,), jnp.float32, -3.140625, 3.140625), -3.140625, 3.140625)
    item_pair = scatter_about(streams_of[7], (DEVICES * CAP, KRANK, SUB_ROWS), 0.3, 4.0, ((0, 32),))
    item_image = with_ends(jax.random.randint(streams_of[8], (DEVICES * CAP,), 0, NIMG), jax.random.fold_in(streams_of[8], 1), 0, NIMG - 1).astype(jnp.int32)
    item_sub = with_ends(jax.random.randint(streams_of[9], (DEVICES * CAP,), 0, SUBS), jax.random.fold_in(streams_of[9], 1), 0, SUBS - 1).astype(jnp.int32)
    item_count = draw_item_count(jax.random.fold_in(streams_of[11], 71), 0)
    return {"pair_ft": pair_ft, "aux_ft": aux_ft, "coul_weight": coul_weight, "aux_basis": aux_basis, "aux_decay": aux_decay, "image_dist": image_dist, "image_phase": image_phase, "item_pair": item_pair, "item_image": item_image, "item_sub": item_sub, "item_count": item_count}


def reference(pair_ft, aux_ft, coul_weight, aux_basis, aux_decay, image_dist, image_phase, item_pair, item_image, item_sub, item_count):
    weighted = (pair_ft.astype(jnp.float32) * coul_weight[None, None, :]).astype(jnp.bfloat16)
    weighted = lax.optimization_barrier(weighted).astype(jnp.float32)
    real_part = weighted[:, 0, :].T
    imag_part = weighted[:, 1, :].T
    real_cols = jnp.concatenate([real_part, imag_part], axis=0)
    imag_cols = jnp.concatenate([imag_part, -real_part], axis=0)
    pair_matrix = jnp.concatenate([real_cols, imag_cols], axis=1)
    aux_rows = aux_ft.astype(jnp.float32).reshape(NAUX, 2 * NG)
    long_range = jnp.dot(aux_rows, pair_matrix, precision=lax.Precision.HIGHEST).reshape(NAUX, 2, NPAIR)
    basis_full = aux_basis.astype(jnp.float32)

    def add_item(running, slot_index):
        device = slot_index // CAP
        slot_pos = slot_index % CAP
        column = device % BLOCKS
        usable = slot_pos < item_count[device]

        def compute(current_sum):
            pair_block = item_pair[slot_index].astype(jnp.float32)
            product = jnp.dot(basis_full.T, pair_block, precision=lax.Precision.HIGHEST)
            image_now = item_image[slot_index]
            damping = jnp.exp(-aux_decay * image_dist[image_now])
            phase_value = image_phase[image_now]
            contribution = jnp.stack([jnp.cos(phase_value) * damping[:, None] * product, jnp.sin(phase_value) * damping[:, None] * product], axis=1)
            first_row = (column * ROW_DEV + item_sub[slot_index] * SUB_ROWS).astype(jnp.int32)
            anchor = (jnp.int32(0), jnp.int32(0), first_row)
            current = lax.dynamic_slice(current_sum, anchor, (NAUX, 2, SUB_ROWS))
            return lax.dynamic_update_slice(current_sum, current + contribution, anchor)

        def unchanged(current_sum):
            return current_sum

        return lax.cond(usable, compute, unchanged, running), None

    short_range, _ = lax.scan(add_item, jnp.zeros((NAUX, 2, NPAIR), jnp.float32), jnp.arange(DEVICES * CAP, dtype=jnp.int32))
    return (long_range + short_range).astype(jnp.bfloat16)
```

```python
import functools

import jax
import jax.numpy as jnp
from jax import lax
from jax.experimental import pallas as pl
from jax.experimental.pallas import tpu as pltpu
from jax.sharding import PartitionSpec as P

AXES = ("grp", "dev")
CORES = 2
GROUP_ITEMS = 4
VMEM_BYTES = 48 * 1024 * 1024


def short_kernel(
    half_ref, live_ref, sub_ref, meta_ref, basis_ref, decay_ref, items_ref, out_ref,
    basis_f32, left, acc, dists, group_sub, cursor, *, slots, subs, depth, width,
):
    step = pl.program_id(0)

    @pl.when(step == 0)
    def _():
        left[...] = jnp.zeros_like(left)
        for s in range(subs):
            cursor[s] = 0

        def count(i, carry):
            cursor[sub_ref[i]] = cursor[sub_ref[i]] + live_ref[i]
            return carry

        lax.fori_loop(0, slots, count, 0)
        first = jnp.int32(0)
        for s in range(subs):
            groups = (cursor[s] + GROUP_ITEMS - 1) // GROUP_ITEMS

            def mark(i, carry, s=s):
                group_sub[i] = s
                return carry

            lax.fori_loop(first, first + groups, mark, 0)
            cursor[s] = first * GROUP_ITEMS
            first = first + groups
        cursor[subs] = first

        def clear(i, carry):
            dists[i] = 0.0
            return carry

        lax.fori_loop(0, first * GROUP_ITEMS, clear, 0)

        def place(i, carry):
            @pl.when(live_ref[i] > 0)
            def _():
                s = sub_ref[i]
                at = cursor[s]
                cursor[s] = at + 1
                dists[at] = meta_ref[0, i]
                turned = items_ref[i].astype(jnp.float32).T
                lanes = pl.ds(pl.multiple_of((at % GROUP_ITEMS) * depth, depth), depth)
                left[at // GROUP_ITEMS, 0:width, lanes] = (turned * meta_ref[1, i]).astype(left.dtype)
                left[at // GROUP_ITEMS, width:, lanes] = (turned * meta_ref[2, i]).astype(left.dtype)

            return carry

        lax.fori_loop(0, slots, place, 0)

    basis_f32[...] = basis_ref[...].astype(jnp.float32)
    acc[...] = jnp.zeros_like(acc)
    decay = decay_ref[...]

    def one_group(group, carry):
        parts = []
        for k in range(GROUP_ITEMS):
            damping = jnp.exp(decay * -dists[group * GROUP_ITEMS + k])
            parts.append((basis_f32[...] * damping).astype(jnp.bfloat16))
        right = jnp.concatenate(parts, axis=0)
        s = group_sub[group]
        acc[s] += jnp.dot(left[group], right, preferred_element_type=jnp.float32)
        return carry

    lax.fori_loop(0, cursor[subs], one_group, 0)
    for s in range(subs):
        for c in range(2):
            column = (c * subs + s) * width
            out_ref[:, column : column + width] = acc[s, c * width : (c + 1) * width, :].T


def short_range(half, live, sub_ids, meta, aux_basis, aux_decay, items, row_count, subs):
    slots, depth, width = items.shape
    tile = min(row_count, 512)
    steps = row_count // tile
    groups = slots // GROUP_ITEMS + subs
    kernel = functools.partial(short_kernel, slots=slots, subs=subs, depth=depth, width=width)
    return pl.pallas_call(
        kernel,
        out_shape=jax.ShapeDtypeStruct((row_count, 2 * subs * width), jnp.float32),
        grid_spec=pltpu.PrefetchScalarGridSpec(
            num_scalar_prefetch=4,
            grid=(steps,),
            in_specs=[
                pl.BlockSpec((depth, tile), lambda t, half, *_: (0, half[0] * steps + t)),
                pl.BlockSpec((1, tile), lambda t, half, *_: (0, half[0] * steps + t)),
                pl.BlockSpec((slots, depth, width), lambda t, *_: (0, 0, 0)),
            ],
            out_specs=pl.BlockSpec((tile, 2 * subs * width), lambda t, *_: (t, 0)),
            scratch_shapes=[
                pltpu.VMEM((depth, tile), jnp.float32),
                pltpu.VMEM((groups, 2 * width, GROUP_ITEMS * depth), jnp.bfloat16),
                pltpu.VMEM((subs, 2 * width, tile), jnp.float32),
                pltpu.SMEM((groups * GROUP_ITEMS,), jnp.float32),
                pltpu.SMEM((groups,), jnp.int32),
                pltpu.SMEM((subs + 1,), jnp.int32),
            ],
        ),
        compiler_params=pltpu.CompilerParams(vmem_limit_bytes=VMEM_BYTES),
        cost_estimate=pl.CostEstimate(
            flops=2 * row_count * slots * depth * width * 2,
            bytes_accessed=row_count * 2 * subs * width * 4 + slots * depth * width * 2,
            transcendentals=0,
        ),
        name="short_range",
    )(half, live, sub_ids, meta, aux_basis, aux_decay.reshape(1, -1), items)


def long_kernel(place_ref, *refs, chains, pieces, rows, depth):
    names = []
    at = 0
    for count in chains:
        names.append(refs[at : at + count])
        at += count
    factors = refs[at : at + pieces * len(chains)]
    at += pieces * len(chains)
    outs = refs[at : at + pieces]
    at += pieces
    block, left, right, block_sem, right_sem = refs[at:]
    for chain, candidates in enumerate(names):
        for k, ref in enumerate(candidates):

            @pl.when(place_ref[0] == k)
            def _(ref=ref, chain=chain):
                pltpu.make_async_copy(ref, block.at[chain], block_sem.at[chain]).start()

    for n, ref in enumerate(factors):
        pltpu.make_async_copy(ref, right.at[n], right_sem.at[n]).start()
    half = depth // 2
    for chain, candidates in enumerate(names):
        pltpu.make_async_copy(candidates[0], block.at[chain], block_sem.at[chain]).wait()
        left[chain, 0:rows, :] = block[chain]
        left[chain, rows:, 0:half] = -block[chain, :, half:]
        left[chain, rows:, half:] = block[chain, :, 0:half]
    for piece in range(pieces):
        total = None
        for chain in range(len(chains)):
            n = piece * len(chains) + chain
            pltpu.make_async_copy(factors[n], right.at[n], right_sem.at[n]).wait()
            part = jnp.dot(left[chain], right[n], preferred_element_type=jnp.float32)
            total = part if total is None else total + part
        width = total.shape[1]
        outs[piece][:, 0:width] = total[0:rows].astype(outs[piece].dtype)
        outs[piece][:, width:] = total[rows:].astype(outs[piece].dtype)


def long_range(place, chains, factors, out_dtypes):
    rows, depth = chains[0][0].shape
    width = factors[0][0].shape[1]
    pieces = len(factors)
    count = pieces * len(chains)
    blocks = [block for candidates in chains for block in candidates]
    flat = [factor for per_piece in factors for factor in per_piece]
    kernel = functools.partial(
        long_kernel, chains=[len(c) for c in chains], pieces=pieces, rows=rows, depth=depth
    )
    return pl.pallas_call(
        kernel,
        out_shape=[jax.ShapeDtypeStruct((rows, 2 * width), dtype) for dtype in out_dtypes],
        in_specs=[pl.BlockSpec(memory_space=pltpu.SMEM)]
        + [pl.BlockSpec(memory_space=pl.ANY)] * (len(blocks) + len(flat)),
        out_specs=[pl.BlockSpec(memory_space=pltpu.VMEM)] * pieces,
        scratch_shapes=[
            pltpu.VMEM((len(chains), rows, depth), jnp.bfloat16),
            pltpu.VMEM((len(chains), 2 * rows, depth), jnp.bfloat16),
            pltpu.VMEM((count, depth, width), jnp.bfloat16),
            pltpu.SemaphoreType.DMA((len(chains),)),
            pltpu.SemaphoreType.DMA((count,)),
        ],
        compiler_params=pltpu.CompilerParams(vmem_limit_bytes=VMEM_BYTES),
        cost_estimate=pl.CostEstimate(
            flops=2 * 2 * rows * depth * width * count,
            bytes_accessed=2 * (count * depth * width + len(chains) * rows * depth + pieces * rows * 2 * width),
            transcendentals=0,
        ),
        name="long_range",
    )(place, *blocks, *flat)


def final_kernel(offset_ref, *refs, pieces, rows):
    short_ref = refs[pieces]
    out_ref = refs[pieces + 1]
    for n in range(pieces):
        window = pl.ds(pl.multiple_of(offset_ref[n], rows), rows)
        total = (refs[n][...].astype(jnp.float32) + short_ref[window, :]).astype(out_ref.dtype)
        width = total.shape[1] // 2
        out_ref[window, 0, :] = total[:, 0:width]
        out_ref[window, 1, :] = total[:, width:]


def final_sum(offsets, pieces, short):
    rows, columns = pieces[0].shape
    row_count = short.shape[0]
    return pl.pallas_call(
        functools.partial(final_kernel, pieces=len(pieces), rows=rows),
        out_shape=jax.ShapeDtypeStruct((row_count, 2, columns // 2), jnp.bfloat16),
        in_specs=[pl.BlockSpec(memory_space=pltpu.SMEM)]
        + [pl.BlockSpec(memory_space=pltpu.VMEM)] * (len(pieces) + 1),
        out_specs=pl.BlockSpec(memory_space=pltpu.VMEM),
        compiler_params=pltpu.CompilerParams(vmem_limit_bytes=VMEM_BYTES),
        cost_estimate=pl.CostEstimate(
            flops=row_count * columns, bytes_accessed=row_count * columns * 8, transcendentals=0
        ),
        name="final_sum",
    )(offsets, *pieces, short)


def slot_table(image_dist, image_phase, item_image, item_sub, item_count):
    chosen = item_image[None, :] == jnp.arange(image_dist.shape[0], dtype=jnp.int32)[:, None]
    distance = jnp.sum(jnp.where(chosen, image_dist[:, None], 0.0), axis=0)
    cosine = jnp.sum(jnp.where(chosen, jnp.cos(image_phase)[:, None], 0.0), axis=0)
    sine = jnp.sum(jnp.where(chosen, jnp.sin(image_phase)[:, None], 0.0), axis=0)
    live = jnp.arange(item_image.shape[0], dtype=jnp.int32) < item_count[0]
    return jnp.stack(
        [distance, cosine, sine, item_sub.astype(jnp.float32), live.astype(jnp.float32)]
    )


def split_table(table):
    return table[4].astype(jnp.int32), table[3].astype(jnp.int32), table[0:3]


def body(
    pair_ft,
    aux_ft,
    coul_weight,
    aux_basis,
    aux_decay,
    image_dist,
    image_phase,
    item_pair,
    item_image,
    item_sub,
    item_count,
):
    group_count = lax.axis_size("grp")
    member_count = lax.axis_size("dev")
    group = lax.axis_index("grp")
    member = lax.axis_index("dev")
    local_rows, _, local_g = pair_ft.shape
    subs = local_rows // item_pair.shape[2]
    rows = aux_ft.shape[0]
    row_count = rows * member_count // group_count
    half = jnp.reshape(group, (1,)).astype(jnp.int32)

    chips = member_count // CORES
    breadth = max(n for n in range(1, chips + 1) if chips % n == 0 and n * n <= chips)
    length = chips // breadth

    aux_flat = aux_ft.reshape(rows, 2 * local_g)
    weighted = (pair_ft.astype(jnp.float32) * coul_weight[None, None, :]).astype(jnp.bfloat16)
    turned = weighted.reshape(local_rows, 2 * local_g).T
    table = slot_table(image_dist, image_phase, item_image, item_sub, item_count)

    if group_count != 2 or length % 2:
        everything = lax.all_gather(aux_flat, "dev", axis=0, tiled=True)
        mine = lax.all_to_all(everything, "grp", split_axis=0, concat_axis=1, tiled=True)
        factor = lax.all_gather(turned, "grp", axis=0, tiled=True)
        parts = factor.reshape(group_count, 2, local_g, local_rows)
        other = jnp.stack([parts[:, 1], -parts[:, 0]], axis=1).reshape(factor.shape)
        long_part = jnp.concatenate(
            [
                jnp.dot(mine, factor, preferred_element_type=jnp.float32),
                jnp.dot(mine, other, preferred_element_type=jnp.float32),
            ],
            axis=1,
        )
        items = lax.all_gather(item_pair, "grp", axis=0, tiled=True)
        live, sub_ids, meta = split_table(lax.all_gather(table, "grp", axis=1, tiled=True))
        short = short_range(
            half, live, sub_ids, meta, aux_basis, aux_decay, items, row_count, subs
        )
        return (long_part + short).astype(jnp.bfloat16).reshape(row_count, 2, local_rows)

    home = length // 2
    up = member // (breadth * CORES)
    across = member // CORES % breadth
    core = member % CORES
    logical = jnp.where(group == 0, up, length - 1 - up)

    def send(value, route):
        def index(g, u, y, c):
            z = u if g == 0 else length - 1 - u
            return g * member_count + (z * breadth + y) * CORES + c

        pairs = []
        for g in range(group_count):
            for u in range(length):
                for y in range(breadth):
                    for c in range(CORES):
                        target = route(g, u, y, c)
                        if target is not None:
                            pairs.append((index(g, u, y, c), index(*target)))
        return lax.ppermute(value, AXES, pairs)

    def mirrored(g, u, y, c):
        return 1 - g, length - 1 - u, y, c

    crossed = send(aux_flat, lambda g, u, y, c: mirrored(g, u, y, c) if u >= home else None)

    def chain_of(head):
        rising = {0: head}
        for s in range(1, length):
            rising[s] = send(
                rising[s - 1],
                lambda g, u, y, c, s=s: (g, u + 1, y, c)
                if u + 1 < length and 0 <= u - (s - 1) < home
                else None,
            )
        falling = {0: head}
        for s in range(1, home):
            falling[s] = send(
                falling[s - 1],
                lambda g, u, y, c, s=s: (g, u - 1, y, c)
                if u >= 1 and u + s - 1 < home
                else None,
            )
        return [
            [rising[u - j] if u >= j else falling[j - u] for u in range(length)]
            for j in range(home)
        ]

    turned_x = send(turned, mirrored)
    items_x = send(item_pair, mirrored)
    table_x = send(table, mirrored)
    chains = [chain_of(aux_flat), chain_of(crossed)]

    factors = []
    partners = [(s, t) for s in range(breadth) for t in range(CORES)]
    over_y = {0: [turned, turned_x]}
    for s in range(1, breadth):
        over_y[s] = [
            send(v, lambda g, u, y, c, s=s: (g, u, (y - s) % breadth, c)) for v in over_y[0]
        ]
    for s, t in partners:
        if t == 0:
            factors.append(over_y[s])
        else:
            factors.append(
                [send(v, lambda g, u, y, c, t=t: (g, u, y, (c - t) % CORES)) for v in over_y[s]]
            )

    live, sub_ids, meta = split_table(jnp.concatenate([table, table_x], axis=1))
    items = jnp.concatenate([item_pair, items_x], axis=0)
    short = short_range(half, live, sub_ids, meta, aux_basis, aux_decay, items, row_count, subs)

    place = jnp.reshape(logical, (1,)).astype(jnp.int32)
    results = []
    offsets = []
    for j in reversed(range(home)):
        made = long_range(
            place,
            [chain[j] for chain in chains],
            factors,
            [jnp.float32 if n == 0 else jnp.bfloat16 for n in range(len(partners))],
        )
        slab = jnp.where(group == 0, j, home - 1 - j)
        for (s, t), piece in zip(partners, made):
            if (s, t) != (0, 0):
                piece = send(
                    piece,
                    lambda g, u, y, c, s=s, t=t: (g, u, (y + s) % breadth, (c + t) % CORES),
                )
            results.append(piece)
            offsets.append(
                ((slab * breadth + (across - s) % breadth) * CORES + (core - t) % CORES) * rows
            )
    return final_sum(jnp.stack(offsets).astype(jnp.int32), results, short)


def solution(mesh):
    return jax.shard_map(
        body,
        mesh=mesh,
        in_specs=(
            P("dev", None, "grp"),
            P("dev", None, "grp"),
            P("grp"),
            P(),
            P(),
            P(),
            P(),
            P(("grp", "dev"), None, None),
            P(("grp", "dev")),
            P(("grp", "dev")),
            P(("grp", "dev")),
        ),
        out_specs=P("grp", None, "dev"),
        check_vma=False,
    )
```

```python
import functools

import jax
import jax.numpy as jnp
from jax import lax
from jax.experimental import pallas as pl
from jax.experimental.pallas import tpu as pltpu
from jax.sharding import PartitionSpec as P

AXES = ("grp", "dev")
CORES = 2
GROUP_ITEMS = 4
VMEM_BYTES = 32 * 1024 * 1024


def short_kernel(
    half_ref, live_ref, sub_ref, meta_ref, basis_ref, decay_ref, *refs, share, subs, depth, width
):
    items, (out_ref, basis_f32, left, acc, dists, group_sub, cursor) = refs[:-7], refs[-7:]
    slots = share * len(items)
    step = pl.program_id(0)

    @pl.when(step == 0)
    def _():
        left[...] = jnp.zeros_like(left)
        for s in range(subs):
            cursor[s] = 0

        def count(i, carry):
            cursor[sub_ref[i]] = cursor[sub_ref[i]] + live_ref[i]
            return carry

        lax.fori_loop(0, slots, count, 0)
        first = jnp.int32(0)
        for s in range(subs):
            groups = (cursor[s] + GROUP_ITEMS - 1) // GROUP_ITEMS

            def mark(i, carry, s=s):
                group_sub[i] = s
                return carry

            lax.fori_loop(first, first + groups, mark, 0)
            cursor[s] = first * GROUP_ITEMS
            first = first + groups
        cursor[subs] = first

        def clear(i, carry):
            dists[i] = 0.0
            return carry

        lax.fori_loop(0, first * GROUP_ITEMS, clear, 0)

        for n, items_ref in enumerate(items):

            def place(k, carry, first=n * share, items_ref=items_ref):
                i = first + k

                @pl.when(live_ref[i] > 0)
                def _():
                    s = sub_ref[i]
                    at = cursor[s]
                    cursor[s] = at + 1
                    dists[at] = meta_ref[0, i]
                    turned = items_ref[k].astype(jnp.float32)
                    lanes = pl.ds(pl.multiple_of((at % GROUP_ITEMS) * depth, depth), depth)
                    group = at // GROUP_ITEMS
                    left[group, 0:width, lanes] = (turned * meta_ref[1, i]).astype(left.dtype)
                    left[group, width:, lanes] = (turned * meta_ref[2, i]).astype(left.dtype)

                return carry

            lax.fori_loop(0, share, place, 0)

    basis_f32[...] = basis_ref[...].astype(jnp.float32)
    acc[...] = jnp.zeros_like(acc)
    decay = decay_ref[...]

    def one_group(group, carry):
        parts = []
        for k in range(GROUP_ITEMS):
            damping = jnp.exp(decay * -dists[group * GROUP_ITEMS + k])
            parts.append((basis_f32[...] * damping).astype(jnp.bfloat16))
        right = jnp.concatenate(parts, axis=0)
        s = group_sub[group]
        acc[s] += jnp.dot(left[group], right, preferred_element_type=jnp.float32)
        return carry

    lax.fori_loop(0, cursor[subs], one_group, 0)
    for s in range(subs):
        for c in range(2):
            column = (c * subs + s) * width
            out_ref[:, column : column + width] = acc[s, c * width : (c + 1) * width, :].T


def short_range(half, live, sub_ids, meta, aux_basis, aux_decay, items, row_count, subs):
    _, width, depth = items[0].shape
    slots = live.shape[0]
    share = slots // len(items)
    tile = min(row_count, 512)
    steps = row_count // tile
    groups = slots // GROUP_ITEMS + subs
    kernel = functools.partial(short_kernel, share=share, subs=subs, depth=depth, width=width)
    return pl.pallas_call(
        kernel,
        out_shape=jax.ShapeDtypeStruct((row_count, 2 * subs * width), jnp.float32),
        grid_spec=pltpu.PrefetchScalarGridSpec(
            num_scalar_prefetch=4,
            grid=(steps,),
            in_specs=[
                pl.BlockSpec((depth, tile), lambda t, half, *_: (0, half[0] * steps + t)),
                pl.BlockSpec((1, tile), lambda t, half, *_: (0, half[0] * steps + t)),
            ]
            + [pl.BlockSpec((share, width, depth), lambda t, *_: (0, 0, 0))] * len(items),
            out_specs=pl.BlockSpec((tile, 2 * subs * width), lambda t, *_: (t, 0)),
            scratch_shapes=[
                pltpu.VMEM((depth, tile), jnp.float32),
                pltpu.VMEM((groups, 2 * width, GROUP_ITEMS * depth), jnp.bfloat16),
                pltpu.VMEM((subs, 2 * width, tile), jnp.float32),
                pltpu.SMEM((groups * GROUP_ITEMS,), jnp.float32),
                pltpu.SMEM((groups,), jnp.int32),
                pltpu.SMEM((subs + 1,), jnp.int32),
            ],
        ),
        compiler_params=pltpu.CompilerParams(vmem_limit_bytes=VMEM_BYTES),
        cost_estimate=pl.CostEstimate(
            flops=2 * row_count * slots * depth * width * 2,
            bytes_accessed=row_count * 2 * subs * width * 4 + slots * depth * width * 2,
            transcendentals=0,
        ),
        name="short_range",
    )(half, live, sub_ids, meta, aux_basis, aux_decay.reshape(1, -1), *items)


def long_kernel(place_ref, *refs, chains, pieces, rows, depth):
    names = []
    at = 0
    for count in chains:
        names.append(refs[at : at + count])
        at += count
    factors = refs[at : at + pieces * len(chains)]
    at += pieces * len(chains)
    outs = refs[at : at + pieces]
    block, left, right, block_sem, right_sem = refs[at + pieces :]
    for chain, candidates in enumerate(names):
        for k, ref in enumerate(candidates):

            @pl.when(place_ref[0] == k)
            def _(ref=ref, chain=chain):
                pltpu.make_async_copy(ref, block.at[chain], block_sem.at[chain]).start()

    copies = {}
    for piece in reversed(range(pieces)):
        for chain in range(len(chains)):
            copies[piece, chain] = pltpu.make_async_copy(
                factors[piece * len(chains) + chain],
                right.at[piece, pl.ds(chain * depth, depth), :],
                right_sem.at[piece, chain],
            )
            copies[piece, chain].start()
    half = depth // 2
    for chain, candidates in enumerate(names):
        pltpu.make_async_copy(candidates[0], block.at[chain], block_sem.at[chain]).wait()
        at = chain * depth
        left[0:rows, at : at + depth] = block[chain]
        left[rows:, at : at + half] = -block[chain, :, half:]
        left[rows:, at + half : at + depth] = block[chain, :, 0:half]
    for piece in reversed(range(pieces)):
        for chain in range(len(chains)):
            copies[piece, chain].wait()
        total = jnp.dot(left[...], right[piece], preferred_element_type=jnp.float32)
        width = total.shape[1]
        outs[piece][:, 0:width] = total[0:rows].astype(outs[piece].dtype)
        outs[piece][:, width:] = total[rows:].astype(outs[piece].dtype)


def long_range(place, chains, factors, out_dtypes):
    rows, depth = chains[0][0].shape
    width = factors[0][0].shape[1]
    pieces = len(factors)
    count = pieces * len(chains)
    blocks = [block for candidates in chains for block in candidates]
    flat = [factor for per_piece in factors for factor in per_piece]
    kernel = functools.partial(
        long_kernel, chains=[len(c) for c in chains], pieces=pieces, rows=rows, depth=depth
    )
    return pl.pallas_call(
        kernel,
        out_shape=[jax.ShapeDtypeStruct((rows, 2 * width), dtype) for dtype in out_dtypes],
        in_specs=[pl.BlockSpec(memory_space=pltpu.SMEM)]
        + [pl.BlockSpec(memory_space=pl.ANY)] * (len(blocks) + len(flat)),
        out_specs=[pl.BlockSpec(memory_space=pltpu.VMEM)] * pieces,
        scratch_shapes=[
            pltpu.VMEM((len(chains), rows, depth), jnp.bfloat16),
            pltpu.VMEM((2 * rows, len(chains) * depth), jnp.bfloat16),
            pltpu.VMEM((pieces, len(chains) * depth, width), jnp.bfloat16),
            pltpu.SemaphoreType.DMA((len(chains),)),
            pltpu.SemaphoreType.DMA((pieces, len(chains))),
        ],
        compiler_params=pltpu.CompilerParams(vmem_limit_bytes=VMEM_BYTES),
        cost_estimate=pl.CostEstimate(
            flops=2 * 2 * rows * depth * width * count,
            bytes_accessed=2 * (count * depth * width + len(chains) * rows * depth + pieces * rows * 2 * width),
            transcendentals=0,
        ),
        name="long_range",
    )(place, *blocks, *flat)


def final_kernel(order_ref, *refs, pieces):
    short_ref, out_ref = refs[pieces], refs[-1]
    width = out_ref.shape[2]
    for n in range(pieces):

        @pl.when(pl.program_id(0) == n)
        def _(n=n):
            total = (refs[n][...].astype(jnp.float32) + short_ref[...]).astype(out_ref.dtype)
            out_ref[:, 0, :] = total[:, 0:width]
            out_ref[:, 1, :] = total[:, width:]


def final_sum(order, pieces, short, earlier):
    rows, columns = pieces[0].shape
    row_count = short.shape[0]
    count = len(pieces)
    return pl.pallas_call(
        functools.partial(final_kernel, pieces=count),
        out_shape=jax.ShapeDtypeStruct((row_count, 2, columns // 2), jnp.bfloat16),
        grid_spec=pltpu.PrefetchScalarGridSpec(
            num_scalar_prefetch=1,
            grid=(count,),
            in_specs=[pl.BlockSpec((rows, columns), lambda n, order: (0, 0))] * count
            + [pl.BlockSpec((rows, columns), lambda n, order: (order[n], 0))]
            + [pl.BlockSpec(memory_space=pl.ANY)] * (earlier is not None),
            out_specs=pl.BlockSpec((rows, 2, columns // 2), lambda n, order: (order[n], 0, 0)),
        ),
        input_output_aliases={count + 2: 0} if earlier is not None else {},
        compiler_params=pltpu.CompilerParams(vmem_limit_bytes=VMEM_BYTES),
        cost_estimate=pl.CostEstimate(
            flops=count * rows * columns, bytes_accessed=count * rows * columns * 8, transcendentals=0
        ),
        name="final_sum",
    )(order, *pieces, short, *([earlier] if earlier is not None else []))


def slot_table(image_dist, image_phase, images):
    chosen = images[None, :] == jnp.arange(image_dist.shape[0], dtype=jnp.int32)[:, None]
    distance = jnp.sum(jnp.where(chosen, image_dist[:, None], 0.0), axis=0)
    phase = jnp.sum(jnp.where(chosen, image_phase[:, None], 0.0), axis=0)
    return jnp.stack([distance, jnp.cos(phase), jnp.sin(phase)])


def slot_block(slots, items):
    digits = jnp.concatenate([slots // 128, slots % 128], axis=0).astype(items.dtype)
    fill = [(0, full - used) for full, used in zip(items.shape[1:], digits.shape)]
    return jnp.pad(digits, fill)[None]


def read_slots(packed, slots):
    count, share = slots.shape
    digits = packed[-1, 0 : 2 * count, 0:share].astype(jnp.int32)
    return digits[0:count] * 128 + digits[count:]


def after(value, *earlier):
    return lax.optimization_barrier((value, *earlier))[0] if earlier else value


def body(
    pair_ft,
    aux_ft,
    coul_weight,
    aux_basis,
    aux_decay,
    image_dist,
    image_phase,
    item_pair,
    item_image,
    item_sub,
    item_count,
):
    group_count = lax.axis_size("grp")
    member_count = lax.axis_size("dev")
    group = lax.axis_index("grp")
    member = lax.axis_index("dev")
    local_rows, _, local_g = pair_ft.shape
    subs = local_rows // item_pair.shape[2]
    rows = aux_ft.shape[0]
    row_count = rows * member_count // group_count
    half = jnp.reshape(group, (1,)).astype(jnp.int32)

    chips = member_count // CORES
    breadth = max(n for n in range(1, chips + 1) if chips % n == 0 and n * n <= chips)
    length = chips // breadth

    aux_flat = aux_ft.reshape(rows, 2 * local_g)
    weighted = (pair_ft.astype(jnp.float32) * coul_weight[None, None, :]).astype(jnp.bfloat16)
    turned = weighted.reshape(local_rows, 2 * local_g).T
    item_rows = jnp.swapaxes(item_pair, 1, 2)
    live = (jnp.arange(item_image.shape[0], dtype=jnp.int32) < item_count[0]).astype(jnp.int32)
    slots = jnp.stack([item_image, item_sub, live])

    if group_count != 2 or length % 2:
        everything = lax.all_gather(aux_flat, "dev", axis=0, tiled=True)
        mine = lax.all_to_all(everything, "grp", split_axis=0, concat_axis=1, tiled=True)
        factor = lax.all_gather(turned, "grp", axis=0, tiled=True)
        parts = factor.reshape(group_count, 2, local_g, local_rows)
        other = jnp.stack([parts[:, 1], -parts[:, 0]], axis=1).reshape(factor.shape)
        long_part = jnp.concatenate(
            [
                jnp.dot(mine, factor, preferred_element_type=jnp.float32),
                jnp.dot(mine, other, preferred_element_type=jnp.float32),
            ],
            axis=1,
        )
        items = lax.all_gather(item_rows, "grp", axis=0, tiled=True)
        images, sub_ids, live = lax.all_gather(slots, "grp", axis=1, tiled=True)
        table = slot_table(image_dist, image_phase, images)
        short = short_range(
            half, live, sub_ids, table, aux_basis, aux_decay, [items], row_count, subs
        )
        return (long_part + short).astype(jnp.bfloat16).reshape(row_count, 2, local_rows)

    home = length // 2
    up = member // (breadth * CORES)
    across = member // CORES % breadth
    core = member % CORES
    logical = jnp.where(group == 0, up, length - 1 - up)

    def send(value, route):
        def index(g, u, y, c):
            z = u if g == 0 else length - 1 - u
            return g * member_count + (z * breadth + y) * CORES + c

        pairs = []
        for g in range(group_count):
            for u in range(length):
                for y in range(breadth):
                    for c in range(CORES):
                        target = route(g, u, y, c)
                        if target is not None:
                            pairs.append((index(g, u, y, c), index(*target)))
        return lax.ppermute(value, AXES, pairs)

    def mirrored(g, u, y, c):
        return 1 - g, length - 1 - u, y, c

    outward = {0: aux_flat}
    inward = {0: aux_flat}
    across_x = {}

    def hop(s):
        outward[s] = send(
            outward[s - 1],
            lambda g, u, y, c: (g, u + 1, y, c) if u + 1 < length and u - (s - 1) >= 0 else None,
        )
        inward[s] = send(
            inward[s - 1],
            lambda g, u, y, c: (g, u - 1, y, c) if u >= 1 and u + (s - 1) < length else None,
        )

    def cross(s, *earlier):
        block = after(outward[s] if s >= 0 else inward[-s], *earlier)
        across_x[s] = send(
            block, lambda g, u, y, c: mirrored(g, u, y, c) if home <= u - s < length else None
        )

    def over_y(value, s):
        return send(value, lambda g, u, y, c: (g, u, (y - s) % breadth, c))

    def over_core(value, t):
        return send(value, lambda g, u, y, c: (g, u, y, (c - t) % CORES))

    hop(1)
    turned_x = send(turned, mirrored)
    packed = jnp.concatenate([item_rows, slot_block(slots, item_rows)], axis=0)
    items_x = send(after(packed, turned_x, outward[1], inward[1]), mirrored)
    for s in range(2, length):
        hop(s)

    shifts = [s for s in range(1 - length, home)]
    early = [s for s in shifts if s % 2 == 0]
    late = [s for s in shifts if s % 2]
    for s in early:
        cross(s, items_x)

    images, sub_ids, live = jnp.concatenate([slots, read_slots(items_x, slots)], axis=1)
    table = slot_table(image_dist, image_phase, images)
    short = short_range(
        half, live, sub_ids, table, aux_basis, aux_decay, [packed, items_x], row_count, subs
    )
    for s in late:
        cross(s, items_x, inward[length - 1], short)

    partners = [(s, t) for s in range(breadth) for t in range(CORES)]
    factors = []
    for s, t in partners:
        pair = [turned, turned_x]
        if s:
            pair = [over_y(v, s) for v in pair]
        if t:
            pair = [over_core(v, t) for v in pair]
        factors.append(pair)

    place = jnp.reshape(logical, (1,)).astype(jnp.int32)
    out = None
    for k in range(home):
        mine = [sorted(range(home), key=lambda j: ((j - u) % 2, abs(u - j)))[k] for u in range(length)]
        own = [outward[u - j] if u >= j else inward[j - u] for u, j in enumerate(mine)]
        other = [across_x[j - u] for u, j in enumerate(mine)]
        made = long_range(
            place,
            [own, other],
            factors,
            [jnp.float32 if n == 0 else jnp.bfloat16 for n in range(len(partners))],
        )
        block = sum(jnp.where(logical == u, j, 0) for u, j in enumerate(mine))
        slab = jnp.where(group == 0, block, home - 1 - block)
        results = []
        order = []
        for (s, t), piece in zip(partners, made):
            if (s, t) != (0, 0):
                piece = send(
                    piece,
                    lambda g, u, y, c, s=s, t=t: (g, u, (y + s) % breadth, (c + t) % CORES),
                )
            results.append(piece)
            order.append((slab * breadth + (across - s) % breadth) * CORES + (core - t) % CORES)
        out = final_sum(jnp.stack(order).astype(jnp.int32), results, short, out)
    return out


def solution(mesh):
    return jax.shard_map(
        body,
        mesh=mesh,
        in_specs=(
            P("dev", None, "grp"),
            P("dev", None, "grp"),
            P("grp"),
            P(),
            P(),
            P(),
            P(),
            P(("grp", "dev"), None, None),
            P(("grp", "dev")),
            P(("grp", "dev")),
            P(("grp", "dev")),
        ),
        out_specs=P("grp", None, "dev"),
        check_vma=False,
    )
```

```python
import functools

import jax
import jax.numpy as jnp
from jax import lax
from jax.experimental import pallas as pl
from jax.experimental.pallas import tpu as pltpu
from jax.sharding import PartitionSpec as P

AXES = ("grp", "dev")
CORES = 2
GROUP_ITEMS = 4
VMEM_BYTES = 20 * 1024 * 1024


def short_kernel(
    half_ref, live_ref, sub_ref, meta_ref, basis_ref, decay_ref, *refs, share, subs, depth, width
):
    items, (out_ref, basis_f32, left, acc, dists, group_sub, cursor) = refs[:-7], refs[-7:]
    slots = share * len(items)
    row_count = out_ref.shape[0]
    left[...] = jnp.zeros_like(left)
    acc[...] = jnp.zeros_like(acc)
    mine = pl.ds(pl.multiple_of(half_ref[0] * row_count, row_count), row_count)
    basis_f32[...] = basis_ref[:, mine].astype(jnp.float32)

    for s in range(subs):
        cursor[s] = 0

    def count(i, carry):
        cursor[sub_ref[i]] = cursor[sub_ref[i]] + live_ref[i]
        return carry

    lax.fori_loop(0, slots, count, 0)
    first = jnp.int32(0)
    for s in range(subs):
        groups = (cursor[s] + GROUP_ITEMS - 1) // GROUP_ITEMS

        def mark(i, carry, s=s):
            group_sub[i] = s
            return carry

        lax.fori_loop(first, first + groups, mark, 0)
        cursor[s] = first * GROUP_ITEMS
        first = first + groups

    def clear(i, carry):
        dists[i] = 0.0
        return carry

    lax.fori_loop(0, first * GROUP_ITEMS, clear, 0)

    for n, items_ref in enumerate(items):

        def place(k, carry, first=n * share, items_ref=items_ref):
            i = first + k

            @pl.when(live_ref[i] > 0)
            def _():
                s = sub_ref[i]
                at = cursor[s]
                cursor[s] = at + 1
                dists[at] = meta_ref[0, i]
                turned = items_ref[k].astype(jnp.float32)
                lanes = pl.ds(pl.multiple_of((at % GROUP_ITEMS) * depth, depth), depth)
                group = at // GROUP_ITEMS
                left[group, 0:width, lanes] = (turned * meta_ref[1, i]).astype(left.dtype)
                left[group, width:, lanes] = (turned * meta_ref[2, i]).astype(left.dtype)

            return carry

        lax.fori_loop(0, share, place, 0)

    tile = min(row_count, 512)
    decay = decay_ref[:, mine]

    def one_group(group, carry):
        s = group_sub[group]
        damping = [jnp.exp(decay * -dists[group * GROUP_ITEMS + k]) for k in range(GROUP_ITEMS)]
        for t in range(0, row_count, tile):
            right = jnp.concatenate(
                [
                    (basis_f32[:, t : t + tile] * damping[k][:, t : t + tile]).astype(jnp.bfloat16)
                    for k in range(GROUP_ITEMS)
                ],
                axis=0,
            )
            acc[s, :, t : t + tile] += jnp.dot(
                left[group], right, preferred_element_type=jnp.float32
            )
        return carry

    lax.fori_loop(0, first, one_group, 0)
    for s in range(subs):
        for c in range(2):
            column = (c * subs + s) * width
            for t in range(0, row_count, tile):
                out_ref[t : t + tile, column : column + width] = acc[
                    s, c * width : (c + 1) * width, t : t + tile
                ].T


def short_range(half, live, sub_ids, meta, aux_basis, aux_decay, items, row_count, subs):
    _, width, depth = items[0].shape
    slots = live.shape[0]
    share = slots // len(items)
    groups = slots // GROUP_ITEMS + subs
    kernel = functools.partial(short_kernel, share=share, subs=subs, depth=depth, width=width)
    return pl.pallas_call(
        kernel,
        out_shape=jax.ShapeDtypeStruct((row_count, 2 * subs * width), jnp.float32),
        in_specs=[pl.BlockSpec(memory_space=pltpu.SMEM)] * 4
        + [pl.BlockSpec(memory_space=pltpu.VMEM)] * (2 + len(items)),
        out_specs=pl.BlockSpec(memory_space=pltpu.VMEM),
        scratch_shapes=[
            pltpu.VMEM((depth, row_count), jnp.float32),
            pltpu.VMEM((groups, 2 * width, GROUP_ITEMS * depth), jnp.bfloat16),
            pltpu.VMEM((subs, 2 * width, row_count), jnp.float32),
            pltpu.SMEM((groups * GROUP_ITEMS,), jnp.float32),
            pltpu.SMEM((groups,), jnp.int32),
            pltpu.SMEM((subs,), jnp.int32),
        ],
        compiler_params=pltpu.CompilerParams(vmem_limit_bytes=VMEM_BYTES),
        cost_estimate=pl.CostEstimate(
            flops=2 * row_count * slots * depth * width * 2,
            bytes_accessed=row_count * 2 * subs * width * 4 + slots * depth * width * 2,
            transcendentals=0,
        ),
        name="short_range",
    )(half, live, sub_ids, meta, aux_basis, aux_decay.reshape(1, -1), *items)


def long_kernel(*refs, blocks, chains, pieces):
    parts = refs[: blocks * chains]
    factors = refs[blocks * chains : (blocks + pieces) * chains]
    outs = refs[(blocks + pieces) * chains : -1]
    left = refs[-1]
    rows, depth = parts[0].shape
    half = depth // 2
    for block in range(blocks):
        top = block * rows
        low = (blocks + block) * rows
        for chain in range(chains):
            part = parts[block * chains + chain]
            at = chain * depth
            left[top : top + rows, at : at + depth] = part[...]
            left[low : low + rows, at : at + half] = -part[:, half:]
            left[low : low + rows, at + half : at + depth] = part[:, 0:half]
    for piece in reversed(range(pieces)):
        total = None
        for chain in range(chains):
            term = jnp.dot(
                left[:, chain * depth : (chain + 1) * depth],
                factors[piece * chains + chain][...],
                preferred_element_type=jnp.float32,
            )
            total = term if total is None else total + term
        width = total.shape[1]
        outs[piece][:, 0:width] = total[0 : blocks * rows].astype(outs[piece].dtype)
        outs[piece][:, width:] = total[blocks * rows :].astype(outs[piece].dtype)


def long_range(blocks, factors, out_dtypes):
    rows, depth = blocks[0][0].shape
    width = factors[0][0].shape[1]
    chains = len(blocks[0])
    pieces = len(factors)
    all_rows = len(blocks) * rows
    flat = [v for group in blocks + factors for v in group]
    return pl.pallas_call(
        functools.partial(long_kernel, blocks=len(blocks), chains=chains, pieces=pieces),
        out_shape=[jax.ShapeDtypeStruct((all_rows, 2 * width), dtype) for dtype in out_dtypes],
        in_specs=[pl.BlockSpec(memory_space=pltpu.VMEM)] * len(flat),
        out_specs=[pl.BlockSpec(memory_space=pltpu.VMEM)] * pieces,
        scratch_shapes=[pltpu.VMEM((2 * all_rows, chains * depth), jnp.bfloat16)],
        compiler_params=pltpu.CompilerParams(vmem_limit_bytes=VMEM_BYTES),
        cost_estimate=pl.CostEstimate(
            flops=2 * 2 * all_rows * depth * chains * width * pieces,
            bytes_accessed=2 * len(flat) * rows * depth + 6 * all_rows * 2 * width,
            transcendentals=0,
        ),
        name="long_range",
    )(*flat)


def final_kernel(order_ref, *refs, pieces, blocks):
    short_ref, out_ref = refs[pieces], refs[-1]
    rows, _, width = out_ref.shape
    for n in range(pieces * blocks):

        @pl.when(pl.program_id(0) == n)
        def _(n=n):
            top = n % blocks * rows
            window = pl.ds(pl.multiple_of(order_ref[n] * rows, rows), rows)
            piece = refs[n // blocks][top : top + rows, :].astype(jnp.float32)
            total = (piece + short_ref[window, :]).astype(out_ref.dtype)
            out_ref[:, 0, :] = total[:, 0:width]
            out_ref[:, 1, :] = total[:, width:]


def final_sum(order, pieces, short, earlier, rows):
    columns = pieces[0].shape[1]
    row_count = short.shape[0]
    count = len(pieces)
    blocks = pieces[0].shape[0] // rows
    steps = count * blocks
    whole = pl.BlockSpec(memory_space=pltpu.VMEM)
    return pl.pallas_call(
        functools.partial(final_kernel, pieces=count, blocks=blocks),
        out_shape=jax.ShapeDtypeStruct((row_count, 2, columns // 2), jnp.bfloat16),
        grid_spec=pltpu.PrefetchScalarGridSpec(
            num_scalar_prefetch=1,
            grid=(steps,),
            in_specs=[whole] * (count + 1)
            + [pl.BlockSpec(memory_space=pl.ANY)] * (earlier is not None),
            out_specs=pl.BlockSpec((rows, 2, columns // 2), lambda n, order: (order[n], 0, 0)),
        ),
        input_output_aliases={count + 2: 0} if earlier is not None else {},
        compiler_params=pltpu.CompilerParams(vmem_limit_bytes=VMEM_BYTES),
        cost_estimate=pl.CostEstimate(
            flops=steps * rows * columns, bytes_accessed=steps * rows * columns * 8, transcendentals=0
        ),
        name="final_sum",
    )(order, *pieces, short, *([earlier] if earlier is not None else []))


def slot_table(image_dist, image_phase, images):
    chosen = images[None, :] == jnp.arange(image_dist.shape[0], dtype=jnp.int32)[:, None]
    distance = jnp.sum(jnp.where(chosen, image_dist[:, None], 0.0), axis=0)
    phase = jnp.sum(jnp.where(chosen, image_phase[:, None], 0.0), axis=0)
    return jnp.stack([distance, jnp.cos(phase), jnp.sin(phase)])


def slot_block(slots, items):
    digits = jnp.concatenate([slots // 128, slots % 128], axis=0).astype(items.dtype)
    fill = [(0, full - used) for full, used in zip(items.shape[1:], digits.shape)]
    return jnp.pad(digits, fill)[None]


def read_slots(packed, slots):
    count, share = slots.shape
    digits = packed[-1, 0 : 2 * count, 0:share].astype(jnp.int32)
    return digits[0:count] * 128 + digits[count:]


def after(value, *earlier):
    return lax.optimization_barrier((value, *earlier))[0] if earlier else value


def body(
    pair_ft,
    aux_ft,
    coul_weight,
    aux_basis,
    aux_decay,
    image_dist,
    image_phase,
    item_pair,
    item_image,
    item_sub,
    item_count,
):
    group_count = lax.axis_size("grp")
    member_count = lax.axis_size("dev")
    group = lax.axis_index("grp")
    member = lax.axis_index("dev")
    local_rows, _, local_g = pair_ft.shape
    subs = local_rows // item_pair.shape[2]
    rows = aux_ft.shape[0]
    row_count = rows * member_count // group_count
    half = jnp.reshape(group, (1,)).astype(jnp.int32)

    chips = member_count // CORES
    breadth = max(n for n in range(1, chips + 1) if chips % n == 0 and n * n <= chips)
    length = chips // breadth

    aux_flat = aux_ft.reshape(rows, 2 * local_g)
    weighted = (pair_ft.astype(jnp.float32) * coul_weight[None, None, :]).astype(jnp.bfloat16)
    turned = weighted.reshape(local_rows, 2 * local_g).T
    item_rows = jnp.swapaxes(item_pair, 1, 2)
    live = (jnp.arange(item_image.shape[0], dtype=jnp.int32) < item_count[0]).astype(jnp.int32)
    slots = jnp.stack([item_image, item_sub, live])

    if group_count != 2 or length % 2:
        everything = lax.all_gather(aux_flat, "dev", axis=0, tiled=True)
        mine = lax.all_to_all(everything, "grp", split_axis=0, concat_axis=1, tiled=True)
        factor = lax.all_gather(turned, "grp", axis=0, tiled=True)
        parts = factor.reshape(group_count, 2, local_g, local_rows)
        other = jnp.stack([parts[:, 1], -parts[:, 0]], axis=1).reshape(factor.shape)
        long_part = jnp.concatenate(
            [
                jnp.dot(mine, factor, preferred_element_type=jnp.float32),
                jnp.dot(mine, other, preferred_element_type=jnp.float32),
            ],
            axis=1,
        )
        items = lax.all_gather(item_rows, "grp", axis=0, tiled=True)
        images, sub_ids, live = lax.all_gather(slots, "grp", axis=1, tiled=True)
        table = slot_table(image_dist, image_phase, images)
        short = short_range(
            half, live, sub_ids, table, aux_basis, aux_decay, [items], row_count, subs
        )
        return (long_part + short).astype(jnp.bfloat16).reshape(row_count, 2, local_rows)

    home = length // 2
    place = member // (breadth * CORES)
    across = member // CORES % breadth
    core = member % CORES

    def send(value, route):
        def index(g, z, y, c):
            return g * member_count + (z * breadth + y) * CORES + c

        pairs = []
        for g in range(group_count):
            for z in range(length):
                for y in range(breadth):
                    for c in range(CORES):
                        pairs.append((index(g, z, y, c), index(*route(g, z, y, c))))
        return lax.ppermute(value, AXES, pairs)

    def to_plane(value):
        return send(value, lambda g, z, y, c: (1 - g, z, y, c))

    def along(value):
        return send(value, lambda g, z, y, c: (g, (z + 1) % length, y, c))

    def over_y(value, s):
        return send(value, lambda g, z, y, c: (g, z, (y + s) % breadth, c))

    def over_core(value, t):
        return send(value, lambda g, z, y, c: (g, z, y, (c + t) % CORES))

    def hops_of(g, z):
        return sorted((z - j) % length for j in range(g * home, (g + 1) * home))

    def pick(held, g_of, n):
        wanted = sum(
            jnp.where((group == g) & (place == z), hops_of(g_of(g), z)[n], 0)
            for g in range(group_count)
            for z in range(length)
        )
        possible = sorted({hops_of(g, z)[n] for g in range(group_count) for z in range(length)})
        value = held[possible[-1]]
        for k in reversed(possible[:-1]):
            value = jnp.where(wanted == k, held[k], value)
        return value, wanted

    held = [aux_flat]
    held.append(along(held[0]))
    turned_x = to_plane(turned)
    factors = [[turned, turned_x]] + [[over_y(turned, s)] for s in range(1, breadth)]
    packed = jnp.concatenate([item_rows, slot_block(slots, item_rows)], axis=0)
    items_x = to_plane(after(packed, turned_x, held[1], *(pair[0] for pair in factors[1:])))
    for s in range(1, breadth):
        factors[s].append(over_y(turned_x, s))
    for k in range(2, length):
        held.append(along(held[-1]))

    images, sub_ids, live = jnp.concatenate([slots, read_slots(items_x, slots)], axis=1)
    table = slot_table(image_dist, image_phase, images)
    short = short_range(
        half, live, sub_ids, table, aux_basis, aux_decay, [packed, items_x], row_count, subs
    )

    ready = []
    order = []
    out = None
    latest = [items_x] + [pair[1] for pair in factors[1:]]
    for n in range(home):
        if n:
            held = lax.optimization_barrier((*held, *latest, short))[:length]
        mine, hops = pick(held, lambda g: g, n)
        theirs, _ = pick(held, lambda g: 1 - g, n)
        crossed = to_plane(after(theirs, *latest))
        latest = [crossed]
        blocks = [[after(mine, short), crossed]]
        for t in range(1, CORES):
            blocks.append([over_core(v, t) for v in blocks[0]])
        made = long_range(
            blocks, factors, [jnp.float32 if s == 0 else jnp.bfloat16 for s in range(breadth)]
        )
        slab = (place - hops) % length - group * home
        for s in range(breadth):
            piece = over_y(made[s], s) if s else made[s]
            numbers = [
                (slab * breadth + (across - s) % breadth) * CORES + (core - t) % CORES
                for t in range(CORES)
            ]
            ready.append(piece)
            order.append(numbers)
    last = breadth - 1
    for chosen in (slice(0, len(ready) - last), slice(len(ready) - last, None)):
        numbers = jnp.stack([v for group_of in order[chosen] for v in group_of]).astype(jnp.int32)
        out = final_sum(numbers, ready[chosen], short, out, rows)
    return out


def solution(mesh):
    return jax.shard_map(
        body,
        mesh=mesh,
        in_specs=(
            P("dev", None, "grp"),
            P("dev", None, "grp"),
            P("grp"),
            P(),
            P(),
            P(),
            P(),
            P(("grp", "dev"), None, None),
            P(("grp", "dev")),
            P(("grp", "dev")),
            P(("grp", "dev")),
        ),
        out_specs=P("grp", None, "dev"),
        check_vma=False,
    )
```

```python
import functools

import jax
import jax.numpy as jnp
from jax import lax
from jax.experimental import pallas as pl
from jax.experimental.pallas import tpu as pltpu
from jax.sharding import PartitionSpec as P

AXES = ("grp", "dev")
CORES = 2
GROUP_ITEMS = 4
SHORT_VMEM_BYTES = 28 * 1024 * 1024
VMEM_BYTES = 16 * 1024 * 1024


def short_kernel(
    half_ref, live_ref, sub_ref, meta_ref, basis_ref, decay_ref, *refs, share, subs, depth, width
):
    items, scratch = refs[:-11], refs[-11:]
    out_ref, basis, basis_f32, left, acc, made, dists, group_sub, cursor, basis_sem, out_sem = scratch
    slots = share * len(items)
    row_count = out_ref.shape[0]
    mine = pl.ds(pl.multiple_of(half_ref[0] * row_count, row_count), row_count)
    basis_copy = pltpu.make_async_copy(basis_ref.at[:, mine], basis, basis_sem)
    basis_copy.start()
    left[...] = jnp.zeros_like(left)
    acc[...] = jnp.zeros_like(acc)

    for s in range(subs):
        cursor[s] = 0

    def count(i, carry):
        cursor[sub_ref[i]] = cursor[sub_ref[i]] + live_ref[i]
        return carry

    lax.fori_loop(0, slots, count, 0)
    first = jnp.int32(0)
    for s in range(subs):
        groups = (cursor[s] + GROUP_ITEMS - 1) // GROUP_ITEMS

        def mark(i, carry, s=s):
            group_sub[i] = s
            return carry

        lax.fori_loop(first, first + groups, mark, 0)
        cursor[s] = first * GROUP_ITEMS
        first = first + groups

    def clear(i, carry):
        dists[i] = 0.0
        return carry

    lax.fori_loop(0, first * GROUP_ITEMS, clear, 0)

    for n, items_ref in enumerate(items):

        def place(k, carry, first=n * share, items_ref=items_ref):
            i = first + k

            @pl.when(live_ref[i] > 0)
            def _():
                s = sub_ref[i]
                at = cursor[s]
                cursor[s] = at + 1
                dists[at] = meta_ref[0, i]
                turned = items_ref[k].astype(jnp.float32)
                lanes = pl.ds(pl.multiple_of((at % GROUP_ITEMS) * depth, depth), depth)
                group = at // GROUP_ITEMS
                left[group, 0:width, lanes] = (turned * meta_ref[1, i]).astype(left.dtype)
                left[group, width:, lanes] = (turned * meta_ref[2, i]).astype(left.dtype)

            return carry

        lax.fori_loop(0, share, place, 0)

    tile = min(row_count, made.shape[1])
    decay = decay_ref[:, mine]
    basis_copy.wait()
    basis_f32[...] = basis[...].astype(jnp.float32)

    def one_group(group, carry):
        s = group_sub[group]
        damping = [jnp.exp(decay * -dists[group * GROUP_ITEMS + k]) for k in range(GROUP_ITEMS)]
        for t in range(0, row_count, tile):
            right = jnp.concatenate(
                [
                    (basis_f32[:, t : t + tile] * damping[k][:, t : t + tile]).astype(jnp.bfloat16)
                    for k in range(GROUP_ITEMS)
                ],
                axis=0,
            )
            acc[s, :, t : t + tile] += jnp.dot(
                left[group], right, preferred_element_type=jnp.float32
            )
        return carry

    lax.fori_loop(0, first, one_group, 0)
    copies = []
    for n, t in enumerate(range(0, row_count, tile)):
        for s in range(subs):
            for c in range(2):
                column = (c * subs + s) * width
                made[n, :, column : column + width] = acc[
                    s, c * width : (c + 1) * width, t : t + tile
                ].T
        copies.append(pltpu.make_async_copy(made.at[n], out_ref.at[pl.ds(t, tile), :], out_sem.at[n]))
        copies[-1].start()
    for copy in copies:
        copy.wait()


def short_range(half, live, sub_ids, meta, aux_basis, aux_decay, items, row_count, subs):
    _, width, depth = items[0].shape
    slots = live.shape[0]
    share = slots // len(items)
    groups = slots // GROUP_ITEMS + subs
    tile = min(row_count, 512)
    kernel = functools.partial(short_kernel, share=share, subs=subs, depth=depth, width=width)
    return pl.pallas_call(
        kernel,
        out_shape=jax.ShapeDtypeStruct((row_count, 2 * subs * width), jnp.float32),
        in_specs=[pl.BlockSpec(memory_space=pltpu.SMEM)] * 4
        + [pl.BlockSpec(memory_space=pltpu.HBM)]
        + [pl.BlockSpec(memory_space=pltpu.VMEM)] * (1 + len(items)),
        out_specs=pl.BlockSpec(memory_space=pltpu.HBM),
        scratch_shapes=[
            pltpu.VMEM((depth, row_count), jnp.bfloat16),
            pltpu.VMEM((depth, row_count), jnp.float32),
            pltpu.VMEM((groups, 2 * width, GROUP_ITEMS * depth), jnp.bfloat16),
            pltpu.VMEM((subs, 2 * width, row_count), jnp.float32),
            pltpu.VMEM((row_count // tile, tile, 2 * subs * width), jnp.float32),
            pltpu.SMEM((groups * GROUP_ITEMS,), jnp.float32),
            pltpu.SMEM((groups,), jnp.int32),
            pltpu.SMEM((subs,), jnp.int32),
            pltpu.SemaphoreType.DMA,
            pltpu.SemaphoreType.DMA((row_count // tile,)),
        ],
        compiler_params=pltpu.CompilerParams(vmem_limit_bytes=SHORT_VMEM_BYTES),
        cost_estimate=pl.CostEstimate(
            flops=2 * row_count * slots * depth * width * 2,
            bytes_accessed=row_count * 2 * subs * width * 4 + slots * depth * width * 2,
            transcendentals=0,
        ),
        name="short_range",
    )(half, live, sub_ids, meta, aux_basis, aux_decay.reshape(1, -1), *items)


def long_kernel(*refs, blocks, chains, window):
    parts = refs[: blocks * chains]
    factors = refs[blocks * chains : (blocks + 1) * chains]
    out_ref, right = refs[-2:]
    depth, width = factors[0].shape
    half = depth // 2
    for chain, factor in enumerate(factors):
        top = chain * depth
        right[top : top + depth, 0:width] = factor[...]
        right[top : top + half, width:] = factor[half:, :]
        right[top + half : top + depth, width:] = -factor[0:half, :]
    left = jnp.concatenate(
        [
            jnp.concatenate(
                [
                    parts[block * chains + chain][pl.ds(window[chain], window[-1]), :]
                    for block in range(blocks)
                ],
                axis=0,
            )
            for chain in range(chains)
        ],
        axis=1,
    )
    out_ref[...] = jnp.dot(left, right[...], preferred_element_type=jnp.float32).astype(out_ref.dtype)


def long_range(blocks, factors, window, dtype):
    depth, width = factors[0].shape
    chains = len(factors)
    all_rows = len(blocks) * window[-1]
    flat = [v for group in blocks for v in group] + list(factors)
    return pl.pallas_call(
        functools.partial(long_kernel, blocks=len(blocks), chains=chains, window=window),
        out_shape=jax.ShapeDtypeStruct((all_rows, 2 * width), dtype),
        in_specs=[pl.BlockSpec(memory_space=pltpu.VMEM)] * len(flat),
        out_specs=pl.BlockSpec(memory_space=pltpu.VMEM),
        scratch_shapes=[pltpu.VMEM((chains * depth, 2 * width), jnp.bfloat16)],
        compiler_params=pltpu.CompilerParams(vmem_limit_bytes=VMEM_BYTES),
        cost_estimate=pl.CostEstimate(
            flops=2 * all_rows * depth * chains * 2 * width,
            bytes_accessed=2 * chains * depth * (all_rows + width) + 4 * all_rows * width,
            transcendentals=0,
        ),
        name="long_range",
    )(*flat)


def final_kernel(order_ref, *refs, pieces, blocks, rows, aliased):
    short_ref = refs[pieces]
    out_ref, terms, made, term_sem, out_sem = refs[pieces + 1 + aliased :]
    steps = pieces * blocks
    windows = [pl.ds(pl.multiple_of(order_ref[n] * rows, rows), rows) for n in range(steps)]
    arriving = []
    for n, window in enumerate(windows):
        arriving.append(
            pltpu.make_async_copy(short_ref.at[window, :], terms.at[n], term_sem.at[n])
        )
        arriving[-1].start()
    leaving = []
    for n, window in enumerate(windows):
        arriving[n].wait()
        top = n % blocks * rows
        total = refs[n // blocks][top : top + rows, :].astype(jnp.float32) + terms[n]
        made[n] = total.astype(made.dtype).reshape(made.shape[1:])
        leaving.append(pltpu.make_async_copy(made.at[n], out_ref.at[window], out_sem.at[n]))
        leaving[-1].start()
    for copy in leaving:
        copy.wait()


def final_sum(order, pieces, short, earlier, rows):
    columns = pieces[0].shape[1]
    row_count = short.shape[0]
    count = len(pieces)
    blocks = pieces[0].shape[0] // rows
    steps = count * blocks
    aliased = earlier is not None
    return pl.pallas_call(
        functools.partial(final_kernel, pieces=count, blocks=blocks, rows=rows, aliased=aliased),
        out_shape=jax.ShapeDtypeStruct((row_count, 2, columns // 2), jnp.bfloat16),
        in_specs=[pl.BlockSpec(memory_space=pltpu.SMEM)]
        + [pl.BlockSpec(memory_space=pltpu.VMEM)] * count
        + [pl.BlockSpec(memory_space=pltpu.HBM)] * (1 + aliased),
        out_specs=pl.BlockSpec(memory_space=pltpu.HBM),
        scratch_shapes=[
            pltpu.VMEM((steps, rows, columns), jnp.float32),
            pltpu.VMEM((steps, rows, 2, columns // 2), jnp.bfloat16),
            pltpu.SemaphoreType.DMA((steps,)),
            pltpu.SemaphoreType.DMA((steps,)),
        ],
        input_output_aliases={count + 2: 0} if aliased else {},
        compiler_params=pltpu.CompilerParams(vmem_limit_bytes=VMEM_BYTES),
        cost_estimate=pl.CostEstimate(
            flops=steps * rows * columns, bytes_accessed=steps * rows * columns * 8, transcendentals=0
        ),
        name="final_sum",
    )(order, *pieces, short, *([earlier] if aliased else []))


def slot_table(image_dist, image_phase, images):
    chosen = images[None, :] == jnp.arange(image_dist.shape[0], dtype=jnp.int32)[:, None]
    distance = jnp.sum(jnp.where(chosen, image_dist[:, None], 0.0), axis=0)
    phase = jnp.sum(jnp.where(chosen, image_phase[:, None], 0.0), axis=0)
    return jnp.stack([distance, jnp.cos(phase), jnp.sin(phase)])


def slot_block(slots, items):
    digits = jnp.concatenate([slots // 128, slots % 128], axis=0).astype(items.dtype)
    fill = [(0, full - used) for full, used in zip(items.shape[1:], digits.shape)]
    return jnp.pad(digits, fill)[None]


def read_slots(packed, slots):
    count, share = slots.shape
    digits = packed[-1, 0 : 2 * count, 0:share].astype(jnp.int32)
    return digits[0:count] * 128 + digits[count:]


def after(value, *earlier):
    return lax.optimization_barrier((value, *earlier))[0] if earlier else value


def body(
    pair_ft,
    aux_ft,
    coul_weight,
    aux_basis,
    aux_decay,
    image_dist,
    image_phase,
    item_pair,
    item_image,
    item_sub,
    item_count,
):
    group_count = lax.axis_size("grp")
    member_count = lax.axis_size("dev")
    group = lax.axis_index("grp")
    member = lax.axis_index("dev")
    local_rows, _, local_g = pair_ft.shape
    subs = local_rows // item_pair.shape[2]
    rows = aux_ft.shape[0]
    row_count = rows * member_count // group_count
    half = jnp.reshape(group, (1,)).astype(jnp.int32)

    chips = member_count // CORES
    breadth = max(n for n in range(1, chips + 1) if chips % n == 0 and n * n <= chips)
    length = chips // breadth

    aux_flat = aux_ft.reshape(rows, 2 * local_g)
    weighted = (pair_ft.astype(jnp.float32) * coul_weight[None, None, :]).astype(jnp.bfloat16)
    turned = weighted.reshape(local_rows, 2 * local_g).T
    item_rows = jnp.swapaxes(item_pair, 1, 2)
    live = (jnp.arange(item_image.shape[0], dtype=jnp.int32) < item_count[0]).astype(jnp.int32)
    slots = jnp.stack([item_image, item_sub, live])

    if group_count != 2 or length % 2:
        everything = lax.all_gather(aux_flat, "dev", axis=0, tiled=True)
        mine = lax.all_to_all(everything, "grp", split_axis=0, concat_axis=1, tiled=True)
        factor = lax.all_gather(turned, "grp", axis=0, tiled=True)
        parts = factor.reshape(group_count, 2, local_g, local_rows)
        other = jnp.stack([parts[:, 1], -parts[:, 0]], axis=1).reshape(factor.shape)
        long_part = jnp.concatenate(
            [
                jnp.dot(mine, factor, preferred_element_type=jnp.float32),
                jnp.dot(mine, other, preferred_element_type=jnp.float32),
            ],
            axis=1,
        )
        items = lax.all_gather(item_rows, "grp", axis=0, tiled=True)
        images, sub_ids, live = lax.all_gather(slots, "grp", axis=1, tiled=True)
        table = slot_table(image_dist, image_phase, images)
        short = short_range(
            half, live, sub_ids, table, aux_basis, aux_decay, [items], row_count, subs
        )
        return (long_part + short).astype(jnp.bfloat16).reshape(row_count, 2, local_rows)

    home = length // 2
    place = member // (breadth * CORES)
    across = member // CORES % breadth
    core = member % CORES

    def send(value, route):
        def index(g, z, y, c):
            return g * member_count + (z * breadth + y) * CORES + c

        pairs = []
        for g in range(group_count):
            for z in range(length):
                for y in range(breadth):
                    for c in range(CORES):
                        pairs.append((index(g, z, y, c), index(*route(g, z, y, c))))
        return lax.ppermute(value, AXES, pairs)

    def to_plane(value):
        return send(value, lambda g, z, y, c: (1 - g, z, y, c))

    ring = [*range(0, length, 2), *reversed(range(1, length, 2))]
    turn = {z: n for n, z in enumerate(ring)}

    def along(value):
        return send(value, lambda g, z, y, c: (g, ring[(turn[z] + 1) % length], y, c))

    def over_y(value, s):
        return send(value, lambda g, z, y, c: (g, z, (y + s) % breadth, c))

    def over_core(value, t):
        return send(value, lambda g, z, y, c: (g, z, y, (c + t) % CORES))

    def hops_of(g, z):
        return sorted((turn[z] - turn[j]) % length for j in range(g * home, (g + 1) * home))

    def here(number):
        return sum(
            jnp.where((group == g) & (place == z), number(g, z), 0)
            for g in range(group_count)
            for z in range(length)
        )

    def pick(other, n, window, *earlier):
        wanted = here(lambda g, z: hops_of(g ^ other, z)[n])
        possible = sorted({hops_of(g, z)[n] for g in range(group_count) for z in range(length)})
        blocks = lax.optimization_barrier((*(held[k] for k in possible), *earlier))
        value = blocks[len(possible) - 1][window]
        for k, block in reversed(list(zip(possible[:-1], blocks))):
            value = jnp.where(wanted == k, block[window], value)
        return value

    def numbers_of(n, s):
        slab = here(lambda g, z: ring[(turn[z] - hops_of(g, z)[n]) % length] - g * home)
        return [
            (slab * breadth + (across - s) % breadth) * CORES + (core - t) % CORES
            for t in range(CORES)
        ]

    def with_cores(value):
        return [value] + [over_core(value, t) for t in range(1, CORES)]

    held = [aux_flat]
    held.append(along(held[0]))
    turned_x = to_plane(turned)
    factors = [[turned, turned_x]] + [[over_y(turned, s)] for s in range(1, breadth)]
    packed = jnp.concatenate([item_rows, slot_block(slots, item_rows)], axis=0)
    items_x = to_plane(after(packed, turned_x, held[1], *(pair[0] for pair in factors[1:])))
    for s in range(1, breadth):
        factors[s].append(over_y(turned_x, s))
    for k in range(2, length):
        held.append(along(held[-1]))

    images, sub_ids, live = jnp.concatenate([slots, read_slots(items_x, slots)], axis=1)
    table = slot_table(image_dist, image_phase, images)
    short = short_range(
        half, live, sub_ids, table, aux_basis, aux_decay, [packed, items_x], row_count, subs
    )

    parts = 2 if rows % 32 == 0 else 1
    units = [(n, 0, rows) for n in range(home - 1)]
    units += [(home - 1, k * (rows // parts), rows // parts) for k in range(parts)]
    mine = {}
    theirs = []
    crossed = []
    away = []
    arriving = []
    own = []

    def product(i, s, *earlier):
        n, first, count = units[i]
        blocks = list(zip(mine[n], [after(crossed[i][0], *earlier), *crossed[i][1:]]))
        return long_range(blocks, factors[s], (first, 0, count), jnp.bfloat16 if s else jnp.float32)

    def multiply(i, *earlier):
        away.append([product(i, s, *earlier) for s in range(1, breadth)])
        arriving.append([over_y(v, s) for s, v in enumerate(away[i], 1)])

    for i, (n, first, count) in enumerate(units):
        if i == 0:
            gate = [items_x, *(pair[1] for pair in factors[1:])]
        elif i == 1:
            gate = [crossed[0][0], short]
        else:
            gate = away[i - 2]
        theirs.append(pick(True, n, slice(first, first + count), *gate))
        moved = to_plane(theirs[i])
        if first + count == rows:
            mine[n] = with_cores(pick(False, n, slice(None), theirs[i]))
        if i:
            multiply(i - 1)
        crossed.append(with_cores(after(moved, *away[i - 1] if i else [short])))
        if i > 1:
            own.append(product(i - 2, 0, theirs[i]))
    last = len(units) - 1
    multiply(last, *(arriving[0] if last > 1 else []))
    if last:
        own.append(product(last - 1, 0, crossed[last][0]))
    own.append(product(last, 0))

    def place_of(piece, i, s):
        n, first, count = units[i]
        return piece, [v * (rows // count) + first // count for v in numbers_of(n, s)]

    calls = []
    for i, (_, _, count) in enumerate(units):
        here_now = [place_of(own[i], i, 0)]
        arrived = [place_of(v, i, s) for s, v in enumerate(arriving[i], 1)]
        for entries in [here_now + arrived] if i < last else [here_now, arrived]:
            if calls and calls[-1][0] == count and entries is not arrived:
                calls[-1][1].extend(entries)
            elif entries:
                calls.append((count, entries))
    out = None
    for count, entries in calls:
        numbers = jnp.stack([v for _, each in entries for v in each]).astype(jnp.int32)
        out = final_sum(numbers, [piece for piece, _ in entries], short, out, count)
    return out


def solution(mesh):
    return jax.shard_map(
        body,
        mesh=mesh,
        in_specs=(
            P("dev", None, "grp"),
            P("dev", None, "grp"),
            P("grp"),
            P(),
            P(),
            P(),
            P(),
            P(("grp", "dev"), None, None),
            P(("grp", "dev")),
            P(("grp", "dev")),
            P(("grp", "dev")),
        ),
        out_specs=P("grp", None, "dev"),
        check_vma=False,
    )
```

```python
import functools

import jax
import jax.numpy as jnp
from jax import lax
from jax.experimental import pallas as pl
from jax.experimental.pallas import tpu as pltpu
from jax.sharding import PartitionSpec as P

AXES = ("grp", "dev")
CORES = 2
SMALL_COST = pl.CostEstimate(flops=1, bytes_accessed=1, transcendentals=0)
GROUP_ITEMS = 4
SHORT_VMEM_BYTES = 20 * 1024 * 1024
VMEM_BYTES = 10 * 1024 * 1024


def short_kernel(
    half_ref, live_ref, sub_ref, meta_ref, basis_ref, decay_ref, *refs, share, subs, depth, width
):
    items, scratch = refs[:-11], refs[-11:]
    out_ref, basis, basis_f32, left, acc, made, dists, group_sub, cursor, basis_sem, out_sem = scratch
    slots = share * len(items)
    row_count = out_ref.shape[0]
    mine = pl.ds(pl.multiple_of(half_ref[0] * row_count, row_count), row_count)
    basis_copy = pltpu.make_async_copy(basis_ref.at[:, mine], basis, basis_sem)
    basis_copy.start()
    left[...] = jnp.zeros_like(left)
    acc[...] = jnp.zeros_like(acc)

    for s in range(subs):
        cursor[s] = 0

    def count(i, carry):
        cursor[sub_ref[i]] = cursor[sub_ref[i]] + live_ref[i]
        return carry

    lax.fori_loop(0, slots, count, 0)
    first = jnp.int32(0)
    for s in range(subs):
        groups = (cursor[s] + GROUP_ITEMS - 1) // GROUP_ITEMS

        def mark(i, carry, s=s):
            group_sub[i] = s
            return carry

        lax.fori_loop(first, first + groups, mark, 0)
        cursor[s] = first * GROUP_ITEMS
        first = first + groups

    def clear(i, carry):
        dists[i] = 0.0
        return carry

    lax.fori_loop(0, first * GROUP_ITEMS, clear, 0)

    for n, items_ref in enumerate(items):

        def place(k, carry, first=n * share, items_ref=items_ref):
            i = first + k

            @pl.when(live_ref[i] > 0)
            def _():
                s = sub_ref[i]
                at = cursor[s]
                cursor[s] = at + 1
                dists[at] = meta_ref[0, i]
                turned = items_ref[k].astype(jnp.float32)
                lanes = pl.ds(pl.multiple_of((at % GROUP_ITEMS) * depth, depth), depth)
                group = at // GROUP_ITEMS
                left[group, 0:width, lanes] = (turned * meta_ref[1, i]).astype(left.dtype)
                left[group, width:, lanes] = (turned * meta_ref[2, i]).astype(left.dtype)

            return carry

        lax.fori_loop(0, share, place, 0)

    tile = min(row_count, made.shape[1])
    decay = decay_ref[:, mine]
    basis_copy.wait()
    basis_f32[...] = basis[...].astype(jnp.float32)

    def one_group(group, carry):
        s = group_sub[group]
        damping = [jnp.exp(decay * -dists[group * GROUP_ITEMS + k]) for k in range(GROUP_ITEMS)]
        for t in range(0, row_count, tile):
            right = jnp.concatenate(
                [
                    (basis_f32[:, t : t + tile] * damping[k][:, t : t + tile]).astype(jnp.bfloat16)
                    for k in range(GROUP_ITEMS)
                ],
                axis=0,
            )
            acc[s, :, t : t + tile] += jnp.dot(
                left[group], right, preferred_element_type=jnp.float32
            )
        return carry

    lax.fori_loop(0, first, one_group, 0)
    copies = []
    for n, t in enumerate(range(0, row_count, tile)):
        for s in range(subs):
            for c in range(2):
                column = (c * subs + s) * width
                made[n, :, column : column + width] = acc[
                    s, c * width : (c + 1) * width, t : t + tile
                ].T
        copies.append(pltpu.make_async_copy(made.at[n], out_ref.at[pl.ds(t, tile), :], out_sem.at[n]))
        copies[-1].start()
    for copy in copies:
        copy.wait()


def short_range(half, live, sub_ids, meta, aux_basis, aux_decay, items, row_count, subs):
    _, width, depth = items[0].shape
    slots = live.shape[0]
    share = slots // len(items)
    groups = slots // GROUP_ITEMS + subs
    tile = min(row_count, 512)
    kernel = functools.partial(short_kernel, share=share, subs=subs, depth=depth, width=width)
    return pl.pallas_call(
        kernel,
        out_shape=jax.ShapeDtypeStruct((row_count, 2 * subs * width), jnp.float32),
        in_specs=[pl.BlockSpec(memory_space=pltpu.SMEM)] * 4
        + [pl.BlockSpec(memory_space=pltpu.HBM)]
        + [pl.BlockSpec(memory_space=pltpu.VMEM)] * (1 + len(items)),
        out_specs=pl.BlockSpec(memory_space=pltpu.HBM),
        scratch_shapes=[
            pltpu.VMEM((depth, row_count), jnp.bfloat16),
            pltpu.VMEM((depth, row_count), jnp.float32),
            pltpu.VMEM((groups, 2 * width, GROUP_ITEMS * depth), jnp.bfloat16),
            pltpu.VMEM((subs, 2 * width, row_count), jnp.float32),
            pltpu.VMEM((row_count // tile, tile, 2 * subs * width), jnp.float32),
            pltpu.SMEM((groups * GROUP_ITEMS,), jnp.float32),
            pltpu.SMEM((groups,), jnp.int32),
            pltpu.SMEM((subs,), jnp.int32),
            pltpu.SemaphoreType.DMA,
            pltpu.SemaphoreType.DMA((row_count // tile,)),
        ],
        compiler_params=pltpu.CompilerParams(vmem_limit_bytes=SHORT_VMEM_BYTES),
        cost_estimate=pl.CostEstimate(
            flops=4 * row_count * slots * depth * width, bytes_accessed=1, transcendentals=0
        ),
        name="short_range",
    )(half, live, sub_ids, meta, aux_basis, aux_decay.reshape(1, -1), *items)


def long_kernel(*refs, blocks, chains, window):
    parts = refs[: blocks * chains]
    factors = refs[blocks * chains : (blocks + 1) * chains]
    out_ref, right = refs[-2:]
    depth, width = factors[0].shape
    half = depth // 2
    for chain, factor in enumerate(factors):
        top = chain * depth
        right[top : top + depth, 0:width] = factor[...]
        right[top : top + half, width:] = factor[half:, :]
        right[top + half : top + depth, width:] = -factor[0:half, :]
    count = window[-1]
    for block in range(blocks):
        left = jnp.concatenate(
            [
                parts[block * chains + chain][pl.ds(window[chain], count), :]
                for chain in range(chains)
            ],
            axis=1,
        )
        made = jnp.dot(left, right[...], preferred_element_type=jnp.float32)
        out_ref[block * count : (block + 1) * count, :] = made.astype(out_ref.dtype)


def long_range(blocks, factors, window, dtype):
    depth, width = factors[0].shape
    chains = len(factors)
    all_rows = len(blocks) * window[-1]
    flat = [v for group in blocks for v in group] + list(factors)
    return pl.pallas_call(
        functools.partial(long_kernel, blocks=len(blocks), chains=chains, window=window),
        out_shape=jax.ShapeDtypeStruct((all_rows, 2 * width), dtype),
        in_specs=[pl.BlockSpec(memory_space=pltpu.VMEM)] * len(flat),
        out_specs=pl.BlockSpec(memory_space=pltpu.VMEM),
        scratch_shapes=[pltpu.VMEM((chains * depth, 2 * width), jnp.bfloat16)],
        compiler_params=pltpu.CompilerParams(vmem_limit_bytes=VMEM_BYTES),
        cost_estimate=SMALL_COST,
        name="long_range",
    )(*flat)


def final_kernel(order_ref, *refs, pieces, blocks, rows, aliased):
    short_ref = refs[pieces]
    out_ref, terms, made, term_sem, out_sem = refs[pieces + 1 + aliased :]
    steps = pieces * blocks
    windows = [pl.ds(pl.multiple_of(order_ref[n] * rows, rows), rows) for n in range(steps)]
    arriving = []
    for n, window in enumerate(windows):
        arriving.append(
            pltpu.make_async_copy(short_ref.at[window, :], terms.at[n], term_sem.at[n])
        )
        arriving[-1].start()
    leaving = []
    for n, window in enumerate(windows):
        arriving[n].wait()
        top = n % blocks * rows
        total = refs[n // blocks][top : top + rows, :].astype(jnp.float32) + terms[n]
        made[n] = total.astype(made.dtype).reshape(made.shape[1:])
        leaving.append(pltpu.make_async_copy(made.at[n], out_ref.at[window], out_sem.at[n]))
        leaving[-1].start()
    for copy in leaving:
        copy.wait()


def final_sum(order, pieces, short, earlier, rows):
    columns = pieces[0].shape[1]
    row_count = short.shape[0]
    count = len(pieces)
    blocks = pieces[0].shape[0] // rows
    steps = count * blocks
    aliased = earlier is not None
    return pl.pallas_call(
        functools.partial(final_kernel, pieces=count, blocks=blocks, rows=rows, aliased=aliased),
        out_shape=jax.ShapeDtypeStruct((row_count, 2, columns // 2), jnp.bfloat16),
        in_specs=[pl.BlockSpec(memory_space=pltpu.SMEM)]
        + [pl.BlockSpec(memory_space=pltpu.VMEM)] * count
        + [pl.BlockSpec(memory_space=pltpu.HBM)] * (1 + aliased),
        out_specs=pl.BlockSpec(memory_space=pltpu.HBM),
        scratch_shapes=[
            pltpu.VMEM((steps, rows, columns), jnp.float32),
            pltpu.VMEM((steps, rows, 2, columns // 2), jnp.bfloat16),
            pltpu.SemaphoreType.DMA((steps,)),
            pltpu.SemaphoreType.DMA((steps,)),
        ],
        input_output_aliases={count + 2: 0} if aliased else {},
        compiler_params=pltpu.CompilerParams(vmem_limit_bytes=VMEM_BYTES),
        cost_estimate=SMALL_COST,
        name="final_sum",
    )(order, *pieces, short, *([earlier] if aliased else []))


def slot_table(image_dist, image_phase, images):
    chosen = images[None, :] == jnp.arange(image_dist.shape[0], dtype=jnp.int32)[:, None]
    distance = jnp.sum(jnp.where(chosen, image_dist[:, None], 0.0), axis=0)
    phase = jnp.sum(jnp.where(chosen, image_phase[:, None], 0.0), axis=0)
    return jnp.stack([distance, jnp.cos(phase), jnp.sin(phase)])


def slot_block(slots, items):
    digits = jnp.concatenate([slots // 128, slots % 128], axis=0).astype(items.dtype)
    fill = [(0, full - used) for full, used in zip(items.shape[1:], digits.shape)]
    return jnp.pad(digits, fill)[None]


def read_slots(packed, slots):
    count, share = slots.shape
    digits = packed[-1, 0 : 2 * count, 0:share].astype(jnp.int32)
    return digits[0:count] * 128 + digits[count:]


def after(value, *earlier):
    return lax.optimization_barrier((value, *earlier))[0] if earlier else value


def body(
    pair_ft,
    aux_ft,
    coul_weight,
    aux_basis,
    aux_decay,
    image_dist,
    image_phase,
    item_pair,
    item_image,
    item_sub,
    item_count,
):
    group_count = lax.axis_size("grp")
    member_count = lax.axis_size("dev")
    group = lax.axis_index("grp")
    member = lax.axis_index("dev")
    local_rows, _, local_g = pair_ft.shape
    subs = local_rows // item_pair.shape[2]
    rows = aux_ft.shape[0]
    row_count = rows * member_count // group_count
    half = jnp.reshape(group, (1,)).astype(jnp.int32)

    chips = member_count // CORES
    breadth = max(n for n in range(1, chips + 1) if chips % n == 0 and n * n <= chips)
    length = chips // breadth

    aux_flat = aux_ft.reshape(rows, 2 * local_g)
    pairs = after(pair_ft, aux_flat).astype(jnp.float32)
    weighted = (pairs * coul_weight[None, None, :]).astype(jnp.bfloat16)
    turned = weighted.reshape(local_rows, 2 * local_g).T
    item_rows = jnp.swapaxes(item_pair, 1, 2)
    live = (jnp.arange(item_image.shape[0], dtype=jnp.int32) < item_count[0]).astype(jnp.int32)
    slots = jnp.stack([item_image, item_sub, live])

    if group_count != 2 or length % 2:
        everything = lax.all_gather(aux_flat, "dev", axis=0, tiled=True)
        mine = lax.all_to_all(everything, "grp", split_axis=0, concat_axis=1, tiled=True)
        factor = lax.all_gather(turned, "grp", axis=0, tiled=True)
        parts = factor.reshape(group_count, 2, local_g, local_rows)
        other = jnp.stack([parts[:, 1], -parts[:, 0]], axis=1).reshape(factor.shape)
        long_part = jnp.concatenate(
            [
                jnp.dot(mine, factor, preferred_element_type=jnp.float32),
                jnp.dot(mine, other, preferred_element_type=jnp.float32),
            ],
            axis=1,
        )
        items = lax.all_gather(item_rows, "grp", axis=0, tiled=True)
        images, sub_ids, live = lax.all_gather(slots, "grp", axis=1, tiled=True)
        table = slot_table(image_dist, image_phase, images)
        short = short_range(
            half, live, sub_ids, table, aux_basis, aux_decay, [items], row_count, subs
        )
        return (long_part + short).astype(jnp.bfloat16).reshape(row_count, 2, local_rows)

    home = length // 2
    place = member // (breadth * CORES)
    across = member // CORES % breadth
    core = member % CORES

    def send(value, route):
        def index(g, z, y, c):
            return g * member_count + (z * breadth + y) * CORES + c

        pairs = []
        for g in range(group_count):
            for z in range(length):
                for y in range(breadth):
                    for c in range(CORES):
                        pairs.append((index(g, z, y, c), index(*route(g, z, y, c))))
        return lax.ppermute(value, AXES, pairs)

    def to_plane(value):
        return send(value, lambda g, z, y, c: (1 - g, z, y, c))

    ring = [*range(0, length, 2), *reversed(range(1, length, 2))]
    turn = {z: n for n, z in enumerate(ring)}

    def along(value):
        return send(value, lambda g, z, y, c: (g, ring[(turn[z] + 1) % length], y, c))

    def over_y(value, s):
        return send(value, lambda g, z, y, c: (g, z, (y + s) % breadth, c))

    def over_core(value, t):
        return send(value, lambda g, z, y, c: (g, z, y, (c + t) % CORES))

    def hops_of(g, z):
        return sorted((turn[z] - turn[j]) % length for j in range(g * home, (g + 1) * home))

    def here(number):
        return sum(
            jnp.where((group == g) & (place == z), number(g, z), 0)
            for g in range(group_count)
            for z in range(length)
        )

    def pick(other, n, window, *earlier):
        wanted = here(lambda g, z: hops_of(g ^ other, z)[n])
        possible = sorted({hops_of(g, z)[n] for g in range(group_count) for z in range(length)})
        blocks = lax.optimization_barrier((*(held[k] for k in possible), *earlier))
        value = blocks[len(possible) - 1][window]
        for k, block in reversed(list(zip(possible[:-1], blocks))):
            value = jnp.where(wanted == k, block[window], value)
        return value

    def numbers_of(n, s):
        slab = here(lambda g, z: ring[(turn[z] - hops_of(g, z)[n]) % length] - g * home)
        return [
            (slab * breadth + (across - s) % breadth) * CORES + (core - t) % CORES
            for t in range(CORES)
        ]

    def with_cores(value):
        return [value] + [over_core(value, t) for t in range(1, CORES)]

    held = [aux_flat]
    held.append(along(after(aux_flat, turned)))
    turned_x = to_plane(turned)
    factors = [[turned, turned_x]] + [[over_y(turned, s)] for s in range(1, breadth)]
    packed = jnp.concatenate([item_rows, slot_block(slots, item_rows)], axis=0)
    items_x = to_plane(after(packed, held[1], turned_x, *(pair[0] for pair in factors[1:])))
    for s in range(1, breadth):
        factors[s].append(over_y(turned_x, s))
    for k in range(2, length):
        held.append(along(after(held[-1], turned_x)))

    images, sub_ids, live = jnp.concatenate([slots, read_slots(items_x, slots)], axis=1)
    table = slot_table(image_dist, image_phase, images)
    short = short_range(
        half, live, sub_ids, table, aux_basis, aux_decay, [packed, items_x], row_count, subs
    )

    parts = 2 if rows % 32 == 0 else 1
    units = [(n, 0, rows) for n in range(home - 1)]
    units += [(home - 1, k * (rows // parts), rows // parts) for k in range(parts)]
    mine = {}
    theirs = []
    crossed = []
    away = []
    arriving = []
    own = []

    def product(i, s, *earlier):
        n, first, count = units[i]
        blocks = list(zip(mine[n], [after(crossed[i][0], *earlier), *crossed[i][1:]]))
        return long_range(blocks, factors[s], (first, 0, count), jnp.bfloat16 if s else jnp.float32)

    def multiply(i, *earlier):
        away.append([product(i, s, *earlier) for s in range(1, breadth)])
        arriving.append([over_y(v, s) for s, v in enumerate(away[i], 1)])

    for i, (n, first, count) in enumerate(units):
        if i == 0:
            gate = [items_x, *(pair[1] for pair in factors[1:])]
        elif i == 1:
            gate = [crossed[0][0], short]
        else:
            gate = away[i - 2]
        theirs.append(pick(True, n, slice(first, first + count), *gate))
        moved = to_plane(theirs[i])
        if first + count == rows:
            mine[n] = with_cores(pick(False, n, slice(None), theirs[i]))
        if i:
            multiply(i - 1)
        earlier = [short] if i == 0 else away[i - 1] + (arriving[i - 2] if i > 1 else [])
        crossed.append(with_cores(after(moved, *earlier)))
        if i > 1:
            own.append(product(i - 2, 0, theirs[i]))
    last = len(units) - 1
    if last:
        own.append(product(last - 1, 0))
    multiply(last, *own)
    own.append(product(last, 0))

    def place_of(piece, i, s):
        n, first, count = units[i]
        return piece, [v * (rows // count) + first // count for v in numbers_of(n, s)]

    calls = []
    for i, (_, _, count) in enumerate(units):
        here_now = [place_of(own[i], i, 0)]
        arrived = [place_of(v, i, s) for s, v in enumerate(arriving[i], 1)]
        for entries in [here_now + arrived] if i < last else [here_now, arrived]:
            if calls and calls[-1][0] == count and entries is not arrived:
                calls[-1][1].extend(entries)
            elif entries:
                calls.append((count, entries))
    out = None
    for count, entries in calls:
        numbers = jnp.stack([v for _, each in entries for v in each]).astype(jnp.int32)
        out = final_sum(numbers, [piece for piece, _ in entries], short, out, count)
    return out


def solution(mesh):
    return jax.shard_map(
        body,
        mesh=mesh,
        in_specs=(
            P("dev", None, "grp"),
            P("dev", None, "grp"),
            P("grp"),
            P(),
            P(),
            P(),
            P(),
            P(("grp", "dev"), None, None),
            P(("grp", "dev")),
            P(("grp", "dev")),
            P(("grp", "dev")),
        ),
        out_specs=P("grp", None, "dev"),
        check_vma=False,
    )
```

```python
import functools

import jax
import jax.numpy as jnp
from jax import lax
from jax.experimental import pallas as pl
from jax.experimental.pallas import tpu as pltpu
from jax.sharding import PartitionSpec as P

AXES = ("grp", "dev")
CORES = 2
SMALL_COST = pl.CostEstimate(flops=1, bytes_accessed=1, transcendentals=0)
GROUP_ITEMS = 4
SHORT_VMEM_BYTES = 20 * 1024 * 1024
VMEM_BYTES = 10 * 1024 * 1024


def in_hbm(value):
    return pltpu.with_memory_space_constraint(value, pltpu.HBM)


def short_kernel(
    half_ref, live_ref, sub_ref, meta_ref, basis_ref, decay_ref, *refs, share, subs, depth, width
):
    items, scratch = refs[:-11], refs[-11:]
    out_ref, basis, basis_f32, left, acc, made, dists, group_sub, cursor, basis_sem, out_sem = scratch
    slots = share * len(items)
    row_count = out_ref.shape[0]
    mine = pl.ds(pl.multiple_of(half_ref[0] * row_count, row_count), row_count)
    basis_copy = pltpu.make_async_copy(basis_ref.at[:, mine], basis, basis_sem)
    basis_copy.start()
    left[...] = jnp.zeros_like(left)
    acc[...] = jnp.zeros_like(acc)

    for s in range(subs):
        cursor[s] = 0

    def count(i, carry):
        cursor[sub_ref[i]] = cursor[sub_ref[i]] + live_ref[i]
        return carry

    lax.fori_loop(0, slots, count, 0)
    first = jnp.int32(0)
    for s in range(subs):
        groups = (cursor[s] + GROUP_ITEMS - 1) // GROUP_ITEMS

        def mark(i, carry, s=s):
            group_sub[i] = s
            return carry

        lax.fori_loop(first, first + groups, mark, 0)
        cursor[s] = first * GROUP_ITEMS
        first = first + groups

    def clear(i, carry):
        dists[i] = 0.0
        return carry

    lax.fori_loop(0, first * GROUP_ITEMS, clear, 0)

    for n, items_ref in enumerate(items):

        def place(k, carry, first=n * share, items_ref=items_ref):
            i = first + k

            @pl.when(live_ref[i] > 0)
            def _():
                s = sub_ref[i]
                at = cursor[s]
                cursor[s] = at + 1
                dists[at] = meta_ref[0, i]
                turned = items_ref[k].astype(jnp.float32)
                lanes = pl.ds(pl.multiple_of((at % GROUP_ITEMS) * depth, depth), depth)
                group = at // GROUP_ITEMS
                left[group, 0:width, lanes] = (turned * meta_ref[1, i]).astype(left.dtype)
                left[group, width:, lanes] = (turned * meta_ref[2, i]).astype(left.dtype)

            return carry

        lax.fori_loop(0, share, place, 0)

    tile = min(row_count, made.shape[1])
    decay = decay_ref[:, mine]
    basis_copy.wait()
    basis_f32[...] = basis[...].astype(jnp.float32)

    def one_group(group, carry):
        s = group_sub[group]
        damping = [jnp.exp(decay * -dists[group * GROUP_ITEMS + k]) for k in range(GROUP_ITEMS)]
        for t in range(0, row_count, tile):
            right = jnp.concatenate(
                [
                    (basis_f32[:, t : t + tile] * damping[k][:, t : t + tile]).astype(jnp.bfloat16)
                    for k in range(GROUP_ITEMS)
                ],
                axis=0,
            )
            acc[s, :, t : t + tile] += jnp.dot(
                left[group], right, preferred_element_type=jnp.float32
            )
        return carry

    lax.fori_loop(0, first, one_group, 0)
    copies = []
    for n, t in enumerate(range(0, row_count, tile)):
        for s in range(subs):
            for c in range(2):
                column = (c * subs + s) * width
                made[n, :, column : column + width] = acc[
                    s, c * width : (c + 1) * width, t : t + tile
                ].T
        copies.append(pltpu.make_async_copy(made.at[n], out_ref.at[pl.ds(t, tile), :], out_sem.at[n]))
        copies[-1].start()
    for copy in copies:
        copy.wait()


def short_range(half, live, sub_ids, meta, aux_basis, aux_decay, items, row_count, subs):
    _, width, depth = items[0].shape
    slots = live.shape[0]
    share = slots // len(items)
    groups = slots // GROUP_ITEMS + subs
    tile = min(row_count, 512)
    kernel = functools.partial(short_kernel, share=share, subs=subs, depth=depth, width=width)
    return pl.pallas_call(
        kernel,
        out_shape=pltpu.HBM((row_count, 2 * subs * width), jnp.float32),
        in_specs=[pl.BlockSpec(memory_space=pltpu.SMEM)] * 4
        + [pl.BlockSpec(memory_space=pltpu.HBM)]
        + [pl.BlockSpec(memory_space=pltpu.VMEM)] * (1 + len(items)),
        out_specs=pl.BlockSpec(memory_space=pltpu.HBM),
        scratch_shapes=[
            pltpu.VMEM((depth, row_count), jnp.bfloat16),
            pltpu.VMEM((depth, row_count), jnp.float32),
            pltpu.VMEM((groups, 2 * width, GROUP_ITEMS * depth), jnp.bfloat16),
            pltpu.VMEM((subs, 2 * width, row_count), jnp.float32),
            pltpu.VMEM((row_count // tile, tile, 2 * subs * width), jnp.float32),
            pltpu.SMEM((groups * GROUP_ITEMS,), jnp.float32),
            pltpu.SMEM((groups,), jnp.int32),
            pltpu.SMEM((subs,), jnp.int32),
            pltpu.SemaphoreType.DMA,
            pltpu.SemaphoreType.DMA((row_count // tile,)),
        ],
        compiler_params=pltpu.CompilerParams(vmem_limit_bytes=SHORT_VMEM_BYTES),
        cost_estimate=pl.CostEstimate(
            flops=4 * row_count * slots * depth * width, bytes_accessed=1, transcendentals=0
        ),
        name="short_range",
    )(half, live, sub_ids, meta, in_hbm(aux_basis), aux_decay.reshape(1, -1), *items)


def long_kernel(*refs, blocks, chains, window):
    parts = refs[: blocks * chains]
    factors = refs[blocks * chains : (blocks + 1) * chains]
    out_ref, right = refs[-2:]
    depth, width = factors[0].shape
    half = depth // 2
    for chain, factor in enumerate(factors):
        top = chain * depth
        right[top : top + depth, 0:width] = factor[...]
        right[top : top + half, width:] = factor[half:, :]
        right[top + half : top + depth, width:] = -factor[0:half, :]
    count = window[-1]
    for block in range(blocks):
        left = jnp.concatenate(
            [
                parts[block * chains + chain][pl.ds(window[chain], count), :]
                for chain in range(chains)
            ],
            axis=1,
        )
        made = jnp.dot(left, right[...], preferred_element_type=jnp.float32)
        out_ref[block * count : (block + 1) * count, :] = made.astype(out_ref.dtype)


def long_range(blocks, factors, window, dtype):
    depth, width = factors[0].shape
    chains = len(factors)
    all_rows = len(blocks) * window[-1]
    flat = [v for group in blocks for v in group] + list(factors)
    return pl.pallas_call(
        functools.partial(long_kernel, blocks=len(blocks), chains=chains, window=window),
        out_shape=jax.ShapeDtypeStruct((all_rows, 2 * width), dtype),
        in_specs=[pl.BlockSpec(memory_space=pltpu.VMEM)] * len(flat),
        out_specs=pl.BlockSpec(memory_space=pltpu.VMEM),
        scratch_shapes=[pltpu.VMEM((chains * depth, 2 * width), jnp.bfloat16)],
        compiler_params=pltpu.CompilerParams(vmem_limit_bytes=VMEM_BYTES),
        cost_estimate=SMALL_COST,
        name="long_range",
    )(*flat)


def final_kernel(order_ref, *refs, pieces, blocks, rows, aliased):
    short_ref = refs[pieces]
    out_ref, terms, made, term_sem, out_sem = refs[pieces + 1 + aliased :]
    steps = pieces * blocks
    windows = [pl.ds(pl.multiple_of(order_ref[n] * rows, rows), rows) for n in range(steps)]
    arriving = []
    for n, window in enumerate(windows):
        arriving.append(
            pltpu.make_async_copy(short_ref.at[window, :], terms.at[n], term_sem.at[n])
        )
        arriving[-1].start()
    leaving = []
    for n, window in enumerate(windows):
        arriving[n].wait()
        top = n % blocks * rows
        total = refs[n // blocks][top : top + rows, :].astype(jnp.float32) + terms[n]
        made[n] = total.astype(made.dtype).reshape(made.shape[1:])
        leaving.append(pltpu.make_async_copy(made.at[n], out_ref.at[window], out_sem.at[n]))
        leaving[-1].start()
    for copy in leaving:
        copy.wait()


def final_sum(order, pieces, short, earlier, rows):
    columns = pieces[0].shape[1]
    row_count = short.shape[0]
    count = len(pieces)
    blocks = pieces[0].shape[0] // rows
    steps = count * blocks
    aliased = earlier is not None
    return pl.pallas_call(
        functools.partial(final_kernel, pieces=count, blocks=blocks, rows=rows, aliased=aliased),
        out_shape=jax.ShapeDtypeStruct((row_count, 2, columns // 2), jnp.bfloat16),
        in_specs=[pl.BlockSpec(memory_space=pltpu.SMEM)]
        + [pl.BlockSpec(memory_space=pltpu.VMEM)] * count
        + [pl.BlockSpec(memory_space=pltpu.HBM)] * (1 + aliased),
        out_specs=pl.BlockSpec(memory_space=pltpu.HBM),
        scratch_shapes=[
            pltpu.VMEM((steps, rows, columns), jnp.float32),
            pltpu.VMEM((steps, rows, 2, columns // 2), jnp.bfloat16),
            pltpu.SemaphoreType.DMA((steps,)),
            pltpu.SemaphoreType.DMA((steps,)),
        ],
        input_output_aliases={count + 2: 0} if aliased else {},
        compiler_params=pltpu.CompilerParams(vmem_limit_bytes=VMEM_BYTES),
        cost_estimate=SMALL_COST,
        name="final_sum",
    )(order, *pieces, in_hbm(short), *([earlier] if aliased else []))


def slot_table(image_dist, image_phase, images):
    chosen = images[None, :] == jnp.arange(image_dist.shape[0], dtype=jnp.int32)[:, None]
    distance = jnp.sum(jnp.where(chosen, image_dist[:, None], 0.0), axis=0)
    phase = jnp.sum(jnp.where(chosen, image_phase[:, None], 0.0), axis=0)
    return jnp.stack([distance, jnp.cos(phase), jnp.sin(phase)])


def slot_block(slots, items):
    digits = jnp.concatenate([slots // 128, slots % 128], axis=0).astype(items.dtype)
    fill = [(0, full - used) for full, used in zip(items.shape[1:], digits.shape)]
    return jnp.pad(digits, fill)[None]


def read_slots(packed, slots):
    count, share = slots.shape
    digits = packed[-1, 0 : 2 * count, 0:share].astype(jnp.int32)
    return digits[0:count] * 128 + digits[count:]


def after(value, *earlier):
    return lax.optimization_barrier((value, *earlier))[0] if earlier else value


def body(
    pair_ft,
    aux_ft,
    coul_weight,
    aux_basis,
    aux_decay,
    image_dist,
    image_phase,
    item_pair,
    item_image,
    item_sub,
    item_count,
):
    group_count = lax.axis_size("grp")
    member_count = lax.axis_size("dev")
    group = lax.axis_index("grp")
    member = lax.axis_index("dev")
    local_rows, _, local_g = pair_ft.shape
    subs = local_rows // item_pair.shape[2]
    rows = aux_ft.shape[0]
    row_count = rows * member_count // group_count
    half = jnp.reshape(group, (1,)).astype(jnp.int32)

    chips = member_count // CORES
    breadth = max(n for n in range(1, chips + 1) if chips % n == 0 and n * n <= chips)
    length = chips // breadth

    aux_flat = aux_ft.reshape(rows, 2 * local_g)
    pairs = after(pair_ft, aux_flat).astype(jnp.float32)
    weighted = (pairs * coul_weight[None, None, :]).astype(jnp.bfloat16)
    turned = weighted.reshape(local_rows, 2 * local_g).T
    item_rows = jnp.swapaxes(item_pair, 1, 2)
    live = (jnp.arange(item_image.shape[0], dtype=jnp.int32) < item_count[0]).astype(jnp.int32)
    slots = jnp.stack([item_image, item_sub, live])

    if group_count != 2 or length % 2:
        everything = lax.all_gather(aux_flat, "dev", axis=0, tiled=True)
        mine = lax.all_to_all(everything, "grp", split_axis=0, concat_axis=1, tiled=True)
        factor = lax.all_gather(turned, "grp", axis=0, tiled=True)
        parts = factor.reshape(group_count, 2, local_g, local_rows)
        other = jnp.stack([parts[:, 1], -parts[:, 0]], axis=1).reshape(factor.shape)
        long_part = jnp.concatenate(
            [
                jnp.dot(mine, factor, preferred_element_type=jnp.float32),
                jnp.dot(mine, other, preferred_element_type=jnp.float32),
            ],
            axis=1,
        )
        items = lax.all_gather(item_rows, "grp", axis=0, tiled=True)
        images, sub_ids, live = lax.all_gather(slots, "grp", axis=1, tiled=True)
        table = slot_table(image_dist, image_phase, images)
        short = short_range(
            half, live, sub_ids, table, aux_basis, aux_decay, [items], row_count, subs
        )
        return (long_part + short).astype(jnp.bfloat16).reshape(row_count, 2, local_rows)

    home = length // 2
    place = member // (breadth * CORES)
    across = member // CORES % breadth
    core = member % CORES

    def send(value, route):
        def index(g, z, y, c):
            return g * member_count + (z * breadth + y) * CORES + c

        pairs = []
        for g in range(group_count):
            for z in range(length):
                for y in range(breadth):
                    for c in range(CORES):
                        pairs.append((index(g, z, y, c), index(*route(g, z, y, c))))
        return lax.ppermute(value, AXES, pairs)

    def to_plane(value):
        return send(value, lambda g, z, y, c: (1 - g, z, y, c))

    ring = [*range(0, length, 2), *reversed(range(1, length, 2))]
    turn = {z: n for n, z in enumerate(ring)}

    def along(value, step):
        return send(value, lambda g, z, y, c: (g, ring[(turn[z] + step) % length], y, c))

    def over_y(value, s):
        return send(value, lambda g, z, y, c: (g, z, (y + s) % breadth, c))

    def over_core(value, t):
        return send(value, lambda g, z, y, c: (g, z, y, (c + t) % CORES))

    def hops_of(g, z):
        hops = [(turn[z] - turn[j]) % length for j in range(g * home, (g + 1) * home)]
        return sorted(hops, key=lambda k: (min(k, length - k), k))

    def here(number):
        return sum(
            jnp.where((group == g) & (place == z), number(g, z), 0)
            for g in range(group_count)
            for z in range(length)
        )

    def pick(other, n, window, *earlier):
        wanted = here(lambda g, z: hops_of(g ^ other, z)[n])
        possible = sorted({hops_of(g, z)[n] for g in range(group_count) for z in range(length)})
        blocks = lax.optimization_barrier((*(held[k] for k in possible), *earlier))
        value = blocks[len(possible) - 1][window]
        for k, block in reversed(list(zip(possible[:-1], blocks))):
            value = jnp.where(wanted == k, block[window], value)
        return value

    def numbers_of(n, s):
        slab = here(lambda g, z: ring[(turn[z] - hops_of(g, z)[n]) % length] - g * home)
        return [
            (slab * breadth + (across - s) % breadth) * CORES + (core - t) % CORES
            for t in range(CORES)
        ]

    def with_cores(value):
        return [value] + [over_core(value, t) for t in range(1, CORES)]

    held = {0: aux_flat, 1: along(aux_flat, 1), length - 1: along(aux_flat, -1)}
    turned_x = to_plane(turned)
    factors = [[turned, turned_x]] + [[over_y(turned, s)] for s in range(1, breadth)]
    packed = jnp.concatenate([item_rows, slot_block(slots, item_rows)], axis=0)
    items_x = to_plane(after(packed, turned_x, held[1], *(pair[0] for pair in factors[1:])))
    for s in range(1, breadth):
        factors[s].append(over_y(turned_x, s))
    for k in range(2, length // 2 + 1):
        held[k] = along(after(held[k - 1], turned_x), 1)
    for k in range(2, (length + 1) // 2):
        held[length - k] = along(after(held[length - k + 1], turned_x), -1)

    images, sub_ids, live = jnp.concatenate([slots, read_slots(items_x, slots)], axis=1)
    table = slot_table(image_dist, image_phase, images)
    short = short_range(
        half, live, sub_ids, table, aux_basis, aux_decay, [packed, items_x], row_count, subs
    )

    parts = 2 if rows % 32 == 0 else 1
    units = [(n, 0, rows) for n in range(home - 1)]
    units += [(home - 1, k * (rows // parts), rows // parts) for k in range(parts)]
    mine = {}
    theirs = []
    crossed = []
    away = []
    arriving = []
    own = []

    def product(i, s, *earlier):
        n, first, count = units[i]
        blocks = list(zip(mine[n], [after(crossed[i][0], *earlier), *crossed[i][1:]]))
        return long_range(blocks, factors[s], (first, 0, count), jnp.bfloat16 if s else jnp.float32)

    def multiply(i, *earlier):
        away.append([product(i, s, *earlier) for s in range(1, breadth)])
        arriving.append([over_y(v, s) for s, v in enumerate(away[i], 1)])

    for i, (n, first, count) in enumerate(units):
        if i == 0:
            gate = [items_x, *(pair[1] for pair in factors[1:])]
        elif i == 1:
            gate = [crossed[0][0], short]
        else:
            gate = away[i - 2]
        theirs.append(pick(True, n, slice(first, first + count), *gate))
        moved = to_plane(theirs[i])
        if first + count == rows:
            mine[n] = with_cores(pick(False, n, slice(None), theirs[i]))
        if i > 1:
            own.append(product(i - 2, 0, theirs[i]))
        if i:
            multiply(i - 1, *own[-1:])
        crossed.append(with_cores(after(moved, *away[i - 1] if i else [short])))
    last = len(units) - 1
    if last:
        own.append(product(last - 1, 0))

    def place_of(piece, i, s):
        n, first, count = units[i]
        return piece, [v * (rows // count) + first // count for v in numbers_of(n, s)]

    calls = []
    for i, (_, _, count) in enumerate(units[:-1]):
        entries = [place_of(v, i, s) for s, v in enumerate([own[i], *arriving[i]])]
        if calls and calls[-1][0] == count:
            calls[-1][1].extend(entries)
        else:
            calls.append((count, entries))

    def add_up(out, count, entries):
        numbers = jnp.stack([v for _, each in entries for v in each]).astype(jnp.int32)
        return final_sum(numbers, [piece for piece, _ in entries], short, out, count)

    out = add_up(None, *calls.pop(0)) if calls else None
    multiply(last, *own, *([] if out is None else [out]))
    own.append(product(last, 0))
    count = units[last][2]
    calls.append((count, [place_of(own[last], last, 0)]))
    if len(calls) > 1 and calls[-2][0] == count:
        entries = calls.pop()[1]
        calls[-1][1].extend(entries)
    if breadth > 1:
        calls.append((count, [place_of(v, last, s) for s, v in enumerate(arriving[last], 1)]))
    for call in calls:
        out = add_up(out, *call)
    return out


def solution(mesh):
    return jax.shard_map(
        body,
        mesh=mesh,
        in_specs=(
            P("dev", None, "grp"),
            P("dev", None, "grp"),
            P("grp"),
            P(),
            P(),
            P(),
            P(),
            P(("grp", "dev"), None, None),
            P(("grp", "dev")),
            P(("grp", "dev")),
            P(("grp", "dev")),
        ),
        out_specs=P("grp", None, "dev"),
        check_vma=False,
    )
```

```python
import functools

import jax
import jax.numpy as jnp
from jax import lax
from jax.experimental import pallas as pl
from jax.experimental.pallas import tpu as pltpu
from jax.sharding import PartitionSpec as P

AXES = ("grp", "dev")
CORES = 2
SMALL_COST = pl.CostEstimate(flops=1, bytes_accessed=1, transcendentals=0)
GROUP_ITEMS = 4
SHORT_VMEM_BYTES = 20 * 1024 * 1024
VMEM_BYTES = 10 * 1024 * 1024


def in_hbm(value):
    return pltpu.with_memory_space_constraint(value, pltpu.HBM)


def short_kernel(
    half_ref, live_ref, sub_ref, meta_ref, basis_ref, decay_ref, *refs, share, subs, depth, width
):
    items, scratch = refs[:-11], refs[-11:]
    out_ref, basis, basis_f32, left, acc, made, dists, group_sub, cursor, basis_sem, out_sem = scratch
    slots = share * len(items)
    row_count = out_ref.shape[0]
    mine = pl.ds(pl.multiple_of(half_ref[0] * row_count, row_count), row_count)
    basis_copy = pltpu.make_async_copy(basis_ref.at[:, mine], basis, basis_sem)
    basis_copy.start()
    left[...] = jnp.zeros_like(left)
    acc[...] = jnp.zeros_like(acc)

    for s in range(subs):
        cursor[s] = 0

    def count(i, carry):
        cursor[sub_ref[i]] = cursor[sub_ref[i]] + live_ref[i]
        return carry

    lax.fori_loop(0, slots, count, 0)
    first = jnp.int32(0)
    for s in range(subs):
        groups = (cursor[s] + GROUP_ITEMS - 1) // GROUP_ITEMS

        def mark(i, carry, s=s):
            group_sub[i] = s
            return carry

        lax.fori_loop(first, first + groups, mark, 0)
        cursor[s] = first * GROUP_ITEMS
        first = first + groups

    def clear(i, carry):
        dists[i] = 0.0
        return carry

    lax.fori_loop(0, first * GROUP_ITEMS, clear, 0)

    for n, items_ref in enumerate(items):

        def place(k, carry, first=n * share, items_ref=items_ref):
            i = first + k

            @pl.when(live_ref[i] > 0)
            def _():
                s = sub_ref[i]
                at = cursor[s]
                cursor[s] = at + 1
                dists[at] = meta_ref[0, i]
                turned = items_ref[k].astype(jnp.float32)
                lanes = pl.ds(pl.multiple_of((at % GROUP_ITEMS) * depth, depth), depth)
                group = at // GROUP_ITEMS
                left[group, 0:width, lanes] = (turned * meta_ref[1, i]).astype(left.dtype)
                left[group, width:, lanes] = (turned * meta_ref[2, i]).astype(left.dtype)

            return carry

        lax.fori_loop(0, share, place, 0)

    tile = min(row_count, made.shape[1])
    decay = decay_ref[:, mine]
    basis_copy.wait()
    basis_f32[...] = basis[...].astype(jnp.float32)

    def one_group(group, carry):
        s = group_sub[group]
        damping = [jnp.exp(decay * -dists[group * GROUP_ITEMS + k]) for k in range(GROUP_ITEMS)]
        for t in range(0, row_count, tile):
            right = jnp.concatenate(
                [
                    (basis_f32[:, t : t + tile] * damping[k][:, t : t + tile]).astype(jnp.bfloat16)
                    for k in range(GROUP_ITEMS)
                ],
                axis=0,
            )
            acc[s, :, t : t + tile] += jnp.dot(
                left[group], right, preferred_element_type=jnp.float32
            )
        return carry

    lax.fori_loop(0, first, one_group, 0)
    copies = []
    for n, t in enumerate(range(0, row_count, tile)):
        for s in range(subs):
            for c in range(2):
                column = (c * subs + s) * width
                made[n, :, column : column + width] = acc[
                    s, c * width : (c + 1) * width, t : t + tile
                ].T
        copies.append(pltpu.make_async_copy(made.at[n], out_ref.at[pl.ds(t, tile), :], out_sem.at[n]))
        copies[-1].start()
    for copy in copies:
        copy.wait()


def short_range(half, live, sub_ids, meta, aux_basis, aux_decay, items, row_count, subs):
    _, width, depth = items[0].shape
    slots = live.shape[0]
    share = slots // len(items)
    groups = slots // GROUP_ITEMS + subs
    tile = min(row_count, 512)
    kernel = functools.partial(short_kernel, share=share, subs=subs, depth=depth, width=width)
    return pl.pallas_call(
        kernel,
        out_shape=pltpu.HBM((row_count, 2 * subs * width), jnp.float32),
        in_specs=[pl.BlockSpec(memory_space=pltpu.SMEM)] * 4
        + [pl.BlockSpec(memory_space=pltpu.HBM)]
        + [pl.BlockSpec(memory_space=pltpu.VMEM)] * (1 + len(items)),
        out_specs=pl.BlockSpec(memory_space=pltpu.HBM),
        scratch_shapes=[
            pltpu.VMEM((depth, row_count), jnp.bfloat16),
            pltpu.VMEM((depth, row_count), jnp.float32),
            pltpu.VMEM((groups, 2 * width, GROUP_ITEMS * depth), jnp.bfloat16),
            pltpu.VMEM((subs, 2 * width, row_count), jnp.float32),
            pltpu.VMEM((row_count // tile, tile, 2 * subs * width), jnp.float32),
            pltpu.SMEM((groups * GROUP_ITEMS,), jnp.float32),
            pltpu.SMEM((groups,), jnp.int32),
            pltpu.SMEM((subs,), jnp.int32),
            pltpu.SemaphoreType.DMA,
            pltpu.SemaphoreType.DMA((row_count // tile,)),
        ],
        compiler_params=pltpu.CompilerParams(vmem_limit_bytes=SHORT_VMEM_BYTES),
        cost_estimate=pl.CostEstimate(
            flops=4 * row_count * slots * depth * width, bytes_accessed=1, transcendentals=0
        ),
        name="short_range",
    )(half, live, sub_ids, meta, in_hbm(aux_basis), aux_decay.reshape(1, -1), *items)


def long_kernel(*refs, blocks, chains, pieces, window):
    parts = refs[: blocks * chains]
    factors = refs[blocks * chains : (blocks + pieces) * chains]
    outs = refs[(blocks + pieces) * chains : -3]
    right, own, own_sem = refs[-3:]
    depth, width = factors[0].shape
    half = depth // 2
    count = window[-1]
    copies = []
    for piece in reversed(range(pieces)):
        for chain in range(chains):
            factor = factors[piece * chains + chain]
            top = chain * depth
            right[top : top + depth, 0:width] = factor[...]
            right[top : top + half, width:] = factor[half:, :]
            right[top + half : top + depth, width:] = -factor[0:half, :]
        for block in range(blocks):
            left = jnp.concatenate(
                [
                    parts[block * chains + chain][pl.ds(window[chain], count), :]
                    for chain in range(chains)
                ],
                axis=1,
            )
            total = jnp.dot(left, right[...], preferred_element_type=jnp.float32)
            if piece:
                outs[piece][block * count : (block + 1) * count, :] = total.astype(outs[piece].dtype)
                continue
            own[block] = total
            target = outs[0].at[pl.ds(block * count, count), :]
            copies.append(pltpu.make_async_copy(own.at[block], target, own_sem.at[block]))
            copies[-1].start()
    for copy in copies:
        copy.wait()


def long_range(blocks, factors, window):
    depth, width = factors[0][0].shape
    chains = len(factors[0])
    pieces = len(factors)
    count = window[-1]
    shape = (len(blocks) * count, 2 * width)
    flat = [v for group in [*blocks, *factors] for v in group]
    return pl.pallas_call(
        functools.partial(
            long_kernel, blocks=len(blocks), chains=chains, pieces=pieces, window=window
        ),
        out_shape=[pltpu.HBM(shape, jnp.float32)]
        + [jax.ShapeDtypeStruct(shape, jnp.bfloat16)] * (pieces - 1),
        in_specs=[pl.BlockSpec(memory_space=pltpu.VMEM)] * len(flat),
        out_specs=[pl.BlockSpec(memory_space=pltpu.HBM)]
        + [pl.BlockSpec(memory_space=pltpu.VMEM)] * (pieces - 1),
        scratch_shapes=[
            pltpu.VMEM((chains * depth, 2 * width), jnp.bfloat16),
            pltpu.VMEM((len(blocks), count, 2 * width), jnp.float32),
            pltpu.SemaphoreType.DMA((len(blocks),)),
        ],
        compiler_params=pltpu.CompilerParams(vmem_limit_bytes=VMEM_BYTES),
        cost_estimate=SMALL_COST,
        name="long_range",
    )(*flat)


def final_kernel(order_ref, *refs, pieces, blocks, rows, aliased, stay):
    short_ref = refs[pieces]
    out_ref, *scratch = refs[pieces + 1 + aliased :]
    parts, (terms, made, part_sem, term_sem, out_sem) = scratch[:-5], scratch[-5:]
    parts = [parts.pop(0) if held else ref for held, ref in zip(stay, refs)]
    steps = pieces * blocks
    windows = [pl.ds(pl.multiple_of(order_ref[n] * rows, rows), rows) for n in range(steps)]
    arriving = []
    for n, window in enumerate(windows):
        arriving.append(
            pltpu.make_async_copy(short_ref.at[window, :], terms.at[n], term_sem.at[n])
        )
        arriving[-1].start()
        piece = n // blocks
        if n % blocks == 0 and stay[piece]:
            part = pltpu.make_async_copy(refs[piece], parts[piece], part_sem.at[piece])
            part.start()
            arriving[-1] = (part, arriving[-1])
        else:
            arriving[-1] = (arriving[-1],)
    leaving = []
    for n, window in enumerate(windows):
        for copy in arriving[n]:
            copy.wait()
        top = n % blocks * rows
        total = parts[n // blocks][top : top + rows, :].astype(jnp.float32) + terms[n]
        made[n] = total.astype(made.dtype).reshape(made.shape[1:])
        leaving.append(pltpu.make_async_copy(made.at[n], out_ref.at[window], out_sem.at[n]))
        leaving[-1].start()
    for copy in leaving:
        copy.wait()


def final_sum(order, pieces, short, earlier, rows):
    columns = pieces[0].shape[1]
    row_count = short.shape[0]
    count = len(pieces)
    blocks = pieces[0].shape[0] // rows
    steps = count * blocks
    aliased = earlier is not None
    stay = [piece.dtype == jnp.float32 for piece in pieces]
    return pl.pallas_call(
        functools.partial(
            final_kernel, pieces=count, blocks=blocks, rows=rows, aliased=aliased, stay=stay
        ),
        out_shape=pltpu.HBM((row_count, 2, columns // 2), jnp.bfloat16),
        in_specs=[pl.BlockSpec(memory_space=pltpu.SMEM)]
        + [pl.BlockSpec(memory_space=pltpu.HBM if held else pltpu.VMEM) for held in stay]
        + [pl.BlockSpec(memory_space=pltpu.HBM)] * (1 + aliased),
        out_specs=pl.BlockSpec(memory_space=pltpu.HBM),
        scratch_shapes=[pltpu.VMEM(piece.shape, piece.dtype) for piece, held in zip(pieces, stay) if held]
        + [
            pltpu.VMEM((steps, rows, columns), jnp.float32),
            pltpu.VMEM((steps, rows, 2, columns // 2), jnp.bfloat16),
            pltpu.SemaphoreType.DMA((count,)),
            pltpu.SemaphoreType.DMA((steps,)),
            pltpu.SemaphoreType.DMA((steps,)),
        ],
        input_output_aliases={count + 2: 0} if aliased else {},
        compiler_params=pltpu.CompilerParams(vmem_limit_bytes=VMEM_BYTES),
        cost_estimate=SMALL_COST,
        name="final_sum",
    )(
        order,
        *(in_hbm(piece) if held else piece for piece, held in zip(pieces, stay)),
        in_hbm(short),
        *([earlier] if aliased else []),
    )


def slot_table(image_dist, image_phase, images):
    chosen = images[None, :] == jnp.arange(image_dist.shape[0], dtype=jnp.int32)[:, None]
    distance = jnp.sum(jnp.where(chosen, image_dist[:, None], 0.0), axis=0)
    phase = jnp.sum(jnp.where(chosen, image_phase[:, None], 0.0), axis=0)
    return jnp.stack([distance, jnp.cos(phase), jnp.sin(phase)])


def slot_block(slots, items):
    digits = jnp.concatenate([slots // 128, slots % 128], axis=0).astype(items.dtype)
    fill = [(0, full - used) for full, used in zip(items.shape[1:], digits.shape)]
    return jnp.pad(digits, fill)[None]


def read_slots(packed, slots):
    count, share = slots.shape
    digits = packed[-1, 0 : 2 * count, 0:share].astype(jnp.int32)
    return digits[0:count] * 128 + digits[count:]


def after(value, *earlier):
    return lax.optimization_barrier((value, *earlier))[0] if earlier else value


def body(
    pair_ft,
    aux_ft,
    coul_weight,
    aux_basis,
    aux_decay,
    image_dist,
    image_phase,
    item_pair,
    item_image,
    item_sub,
    item_count,
):
    group_count = lax.axis_size("grp")
    member_count = lax.axis_size("dev")
    group = lax.axis_index("grp")
    member = lax.axis_index("dev")
    local_rows, _, local_g = pair_ft.shape
    subs = local_rows // item_pair.shape[2]
    rows = aux_ft.shape[0]
    row_count = rows * member_count // group_count
    half = jnp.reshape(group, (1,)).astype(jnp.int32)

    chips = member_count // CORES
    breadth = max(n for n in range(1, chips + 1) if chips % n == 0 and n * n <= chips)
    length = chips // breadth

    aux_flat = aux_ft.reshape(rows, 2 * local_g)
    pairs = after(pair_ft, aux_flat).astype(jnp.float32)
    weighted = (pairs * coul_weight[None, None, :]).astype(jnp.bfloat16)
    turned = weighted.reshape(local_rows, 2 * local_g).T
    item_rows = jnp.swapaxes(item_pair, 1, 2)
    live = (jnp.arange(item_image.shape[0], dtype=jnp.int32) < item_count[0]).astype(jnp.int32)
    slots = jnp.stack([item_image, item_sub, live])

    if group_count != 2 or length % 2:
        everything = lax.all_gather(aux_flat, "dev", axis=0, tiled=True)
        mine = lax.all_to_all(everything, "grp", split_axis=0, concat_axis=1, tiled=True)
        factor = lax.all_gather(turned, "grp", axis=0, tiled=True)
        parts = factor.reshape(group_count, 2, local_g, local_rows)
        other = jnp.stack([parts[:, 1], -parts[:, 0]], axis=1).reshape(factor.shape)
        long_part = jnp.concatenate(
            [
                jnp.dot(mine, factor, preferred_element_type=jnp.float32),
                jnp.dot(mine, other, preferred_element_type=jnp.float32),
            ],
            axis=1,
        )
        items = lax.all_gather(item_rows, "grp", axis=0, tiled=True)
        images, sub_ids, live = lax.all_gather(slots, "grp", axis=1, tiled=True)
        table = slot_table(image_dist, image_phase, images)
        short = short_range(
            half, live, sub_ids, table, aux_basis, aux_decay, [items], row_count, subs
        )
        return (long_part + short).astype(jnp.bfloat16).reshape(row_count, 2, local_rows)

    home = length // 2
    place = member // (breadth * CORES)
    across = member // CORES % breadth
    core = member % CORES

    def send(value, route):
        def index(g, z, y, c):
            return g * member_count + (z * breadth + y) * CORES + c

        pairs = []
        for g in range(group_count):
            for z in range(length):
                for y in range(breadth):
                    for c in range(CORES):
                        pairs.append((index(g, z, y, c), index(*route(g, z, y, c))))
        return lax.ppermute(value, AXES, pairs)

    def to_plane(value):
        return send(value, lambda g, z, y, c: (1 - g, z, y, c))

    ring = [*range(0, length, 2), *reversed(range(1, length, 2))]
    turn = {z: n for n, z in enumerate(ring)}

    def along(value, step):
        return send(value, lambda g, z, y, c: (g, ring[(turn[z] + step) % length], y, c))

    def over_y(value, s):
        return send(value, lambda g, z, y, c: (g, z, (y + s) % breadth, c))

    def over_core(value, t):
        return send(value, lambda g, z, y, c: (g, z, y, (c + t) % CORES))

    def hops_of(g, z):
        hops = [(turn[z] - turn[j]) % length for j in range(g * home, (g + 1) * home)]
        return sorted(hops, key=lambda k: (min(k, length - k), k))

    def here(number):
        return sum(
            jnp.where((group == g) & (place == z), number(g, z), 0)
            for g in range(group_count)
            for z in range(length)
        )

    def pick(other, n, window, *earlier):
        wanted = here(lambda g, z: hops_of(g ^ other, z)[n])
        possible = sorted({hops_of(g, z)[n] for g in range(group_count) for z in range(length)})
        blocks = lax.optimization_barrier((*(held[k] for k in possible), *earlier))
        value = blocks[len(possible) - 1][window]
        for k, block in reversed(list(zip(possible[:-1], blocks))):
            value = jnp.where(wanted == k, block[window], value)
        return value

    def numbers_of(n, s):
        slab = here(lambda g, z: ring[(turn[z] - hops_of(g, z)[n]) % length] - g * home)
        return [
            (slab * breadth + (across - s) % breadth) * CORES + (core - t) % CORES
            for t in range(CORES)
        ]

    def with_cores(value):
        return [value] + [over_core(value, t) for t in range(1, CORES)]

    held = {0: aux_flat, 1: along(aux_flat, 1), length - 1: along(aux_flat, -1)}
    turned_x = to_plane(turned)
    factors = [[turned, turned_x]] + [[over_y(turned, s)] for s in range(1, breadth)]
    packed = jnp.concatenate([item_rows, slot_block(slots, item_rows)], axis=0)
    items_x = to_plane(packed)
    begun = [items_x, turned_x, *(pair[0] for pair in factors[1:]), held[1], held[length - 1]]
    for s in range(1, breadth):
        factors[s].append(over_y(after(turned_x, *begun), s))
    for k in range(2, length // 2 + 1):
        held[k] = along(after(held[k - 1], *begun), 1)
    for k in range(2, (length + 1) // 2):
        held[length - k] = along(after(held[length - k + 1], *begun), -1)

    images, sub_ids, live = jnp.concatenate([slots, read_slots(items_x, slots)], axis=1)
    table = slot_table(image_dist, image_phase, images)
    short = short_range(
        half, live, sub_ids, table, aux_basis, aux_decay, [packed, items_x], row_count, subs
    )

    parts = 2 if rows % 32 == 0 else 1
    units = [(n, 0, rows) for n in range(home - 1)]
    units += [(home - 1, k * (rows // parts), rows // parts) for k in range(parts)]
    mine = {}
    theirs = []
    crossed = []
    away = []
    arriving = []
    own = []

    def multiply(i, *earlier):
        n, first, count = units[i]
        blocks = list(zip(mine[n], [after(crossed[i][0], *earlier), *crossed[i][1:]]))
        made = long_range(blocks, factors, (first, 0, count))
        own.append(made[0])
        away.append(made[1:])
        arriving.append([over_y(v, s) for s, v in enumerate(made[1:], 1)])

    for i, (n, first, count) in enumerate(units):
        gate = begun if i == 0 else [crossed[0][0], short] if i == 1 else away[i - 2]
        theirs.append(pick(True, n, slice(first, first + count), *gate))
        moved = to_plane(theirs[i])
        if first + count == rows:
            mine[n] = with_cores(pick(False, n, slice(None), theirs[i]))
        if i:
            multiply(i - 1)
        crossed.append(with_cores(after(moved, *away[i - 1] if i else [short])))
    last = len(units) - 1

    def place_of(piece, i, s):
        n, first, count = units[i]
        return piece, [v * (rows // count) + first // count for v in numbers_of(n, s)]

    calls = []
    for i, (_, _, count) in enumerate(units[:-1]):
        entries = [place_of(v, i, s) for s, v in enumerate([own[i], *arriving[i]])]
        if calls and calls[-1][0] == count:
            calls[-1][1].extend(entries)
        else:
            calls.append((count, entries))

    def add_up(out, count, entries):
        numbers = jnp.stack([v for _, each in entries for v in each]).astype(jnp.int32)
        return final_sum(numbers, [piece for piece, _ in entries], short, out, count)

    out = add_up(None, *calls.pop(0)) if calls else None
    multiply(last, *([] if out is None else [out]))
    count = units[last][2]
    calls.append((count, [place_of(own[last], last, 0)]))
    if len(calls) > 1 and calls[-2][0] == count:
        entries = calls.pop()[1]
        calls[-1][1].extend(entries)
    if breadth > 1:
        calls.append((count, [place_of(v, last, s) for s, v in enumerate(arriving[last], 1)]))
    for call in calls:
        out = add_up(out, *call)
    return out


def solution(mesh):
    return jax.shard_map(
        body,
        mesh=mesh,
        in_specs=(
            P("dev", None, "grp"),
            P("dev", None, "grp"),
            P("grp"),
            P(),
            P(),
            P(),
            P(),
            P(("grp", "dev"), None, None),
            P(("grp", "dev")),
            P(("grp", "dev")),
            P(("grp", "dev")),
        ),
        out_specs=P("grp", None, "dev"),
        check_vma=False,
    )
```

```python
import functools

import jax
import jax.numpy as jnp
from jax import lax
from jax.experimental import pallas as pl
from jax.experimental.pallas import tpu as pltpu
from jax.sharding import PartitionSpec as P

AXES = ("grp", "dev")
CORES = 2
SMALL_COST = pl.CostEstimate(flops=1, bytes_accessed=1, transcendentals=0)
GROUP_ITEMS = 4
SHORT_VMEM_BYTES = 20 * 1024 * 1024
VMEM_BYTES = 10 * 1024 * 1024


def in_hbm(value):
    return pltpu.with_memory_space_constraint(value, pltpu.HBM)


def short_kernel(
    half_ref, live_ref, sub_ref, meta_ref, basis_ref, decay_ref, *refs, share, subs, depth, width
):
    items, scratch = refs[:-11], refs[-11:]
    out_ref, basis, basis_f32, left, acc, made, dists, group_sub, cursor, basis_sem, out_sem = scratch
    slots = share * len(items)
    row_count = out_ref.shape[0]
    mine = pl.ds(pl.multiple_of(half_ref[0] * row_count, row_count), row_count)
    basis_copy = pltpu.make_async_copy(basis_ref.at[:, mine], basis, basis_sem)
    basis_copy.start()
    left[...] = jnp.zeros_like(left)
    acc[...] = jnp.zeros_like(acc)

    for s in range(subs):
        cursor[s] = 0

    def count(i, carry):
        cursor[sub_ref[i]] = cursor[sub_ref[i]] + live_ref[i]
        return carry

    lax.fori_loop(0, slots, count, 0)
    first = jnp.int32(0)
    for s in range(subs):
        groups = (cursor[s] + GROUP_ITEMS - 1) // GROUP_ITEMS

        def mark(i, carry, s=s):
            group_sub[i] = s
            return carry

        lax.fori_loop(first, first + groups, mark, 0)
        cursor[s] = first * GROUP_ITEMS
        first = first + groups

    def clear(i, carry):
        dists[i] = 0.0
        return carry

    lax.fori_loop(0, first * GROUP_ITEMS, clear, 0)

    for n, items_ref in enumerate(items):

        def place(k, carry, first=n * share, items_ref=items_ref):
            i = first + k

            @pl.when(live_ref[i] > 0)
            def _():
                s = sub_ref[i]
                at = cursor[s]
                cursor[s] = at + 1
                dists[at] = meta_ref[0, i]
                turned = items_ref[k].astype(jnp.float32)
                lanes = pl.ds(pl.multiple_of((at % GROUP_ITEMS) * depth, depth), depth)
                group = at // GROUP_ITEMS
                left[group, 0:width, lanes] = (turned * meta_ref[1, i]).astype(left.dtype)
                left[group, width:, lanes] = (turned * meta_ref[2, i]).astype(left.dtype)

            return carry

        lax.fori_loop(0, share, place, 0)

    tile = min(row_count, made.shape[1])
    decay = decay_ref[:, mine]
    basis_copy.wait()
    basis_f32[...] = basis[...].astype(jnp.float32)

    def one_group(group, carry):
        s = group_sub[group]
        damping = [jnp.exp(decay * -dists[group * GROUP_ITEMS + k]) for k in range(GROUP_ITEMS)]
        for t in range(0, row_count, tile):
            right = jnp.concatenate(
                [
                    (basis_f32[:, t : t + tile] * damping[k][:, t : t + tile]).astype(jnp.bfloat16)
                    for k in range(GROUP_ITEMS)
                ],
                axis=0,
            )
            acc[s, :, t : t + tile] += jnp.dot(
                left[group], right, preferred_element_type=jnp.float32
            )
        return carry

    lax.fori_loop(0, first, one_group, 0)
    copies = []
    for n, t in enumerate(range(0, row_count, tile)):
        for s in range(subs):
            for c in range(2):
                column = (c * subs + s) * width
                made[n, :, column : column + width] = acc[
                    s, c * width : (c + 1) * width, t : t + tile
                ].T
        copies.append(pltpu.make_async_copy(made.at[n], out_ref.at[pl.ds(t, tile), :], out_sem.at[n]))
        copies[-1].start()
    for copy in copies:
        copy.wait()


def short_range(half, live, sub_ids, meta, aux_basis, aux_decay, items, row_count, subs):
    _, width, depth = items[0].shape
    slots = live.shape[0]
    share = slots // len(items)
    groups = slots // GROUP_ITEMS + subs
    tile = min(row_count, 512)
    kernel = functools.partial(short_kernel, share=share, subs=subs, depth=depth, width=width)
    return pl.pallas_call(
        kernel,
        out_shape=pltpu.HBM((row_count, 2 * subs * width), jnp.float32),
        in_specs=[pl.BlockSpec(memory_space=pltpu.SMEM)] * 4
        + [pl.BlockSpec(memory_space=pltpu.HBM)]
        + [pl.BlockSpec(memory_space=pltpu.VMEM)] * (1 + len(items)),
        out_specs=pl.BlockSpec(memory_space=pltpu.HBM),
        scratch_shapes=[
            pltpu.VMEM((depth, row_count), jnp.bfloat16),
            pltpu.VMEM((depth, row_count), jnp.float32),
            pltpu.VMEM((groups, 2 * width, GROUP_ITEMS * depth), jnp.bfloat16),
            pltpu.VMEM((subs, 2 * width, row_count), jnp.float32),
            pltpu.VMEM((row_count // tile, tile, 2 * subs * width), jnp.float32),
            pltpu.SMEM((groups * GROUP_ITEMS,), jnp.float32),
            pltpu.SMEM((groups,), jnp.int32),
            pltpu.SMEM((subs,), jnp.int32),
            pltpu.SemaphoreType.DMA,
            pltpu.SemaphoreType.DMA((row_count // tile,)),
        ],
        compiler_params=pltpu.CompilerParams(vmem_limit_bytes=SHORT_VMEM_BYTES),
        cost_estimate=pl.CostEstimate(
            flops=4 * row_count * slots * depth * width, bytes_accessed=1, transcendentals=0
        ),
        name="short_range",
    )(half, live, sub_ids, meta, in_hbm(aux_basis), aux_decay.reshape(1, -1), *items)


def long_kernel(*refs, blocks, chains, pieces, window):
    parts = refs[: blocks * chains]
    factors = refs[blocks * chains : (blocks + pieces) * chains]
    outs, scratch = refs[(blocks + pieces) * chains :][:pieces], refs[-pieces - 2 :]
    right, made, out_sem = scratch[0], scratch[1:-1], scratch[-1]
    depth, width = factors[0].shape
    half = depth // 2
    count = window[-1]
    copies = []
    for piece in reversed(range(pieces)):
        for chain in range(chains):
            factor = factors[piece * chains + chain]
            top = chain * depth
            right[top : top + depth, 0:width] = factor[...]
            right[top : top + half, width:] = factor[half:, :]
            right[top + half : top + depth, width:] = -factor[0:half, :]
        for block in range(blocks):
            left = jnp.concatenate(
                [
                    parts[block * chains + chain][pl.ds(window[chain], count), :]
                    for chain in range(chains)
                ],
                axis=1,
            )
            total = jnp.dot(left, right[...], preferred_element_type=jnp.float32)
            made[piece][block] = total.astype(outs[piece].dtype)
            target = outs[piece].at[pl.ds(block * count, count), :]
            copies.append(
                pltpu.make_async_copy(made[piece].at[block], target, out_sem.at[piece, block])
            )
            copies[-1].start()
    for copy in copies:
        copy.wait()


def long_range(blocks, factors, window):
    depth, width = factors[0][0].shape
    chains = len(factors[0])
    pieces = len(factors)
    count = window[-1]
    shape = (len(blocks) * count, 2 * width)
    dtypes = [jnp.bfloat16 if piece else jnp.float32 for piece in range(pieces)]
    flat = [v for group in [*blocks, *factors] for v in group]
    return pl.pallas_call(
        functools.partial(
            long_kernel, blocks=len(blocks), chains=chains, pieces=pieces, window=window
        ),
        out_shape=[pltpu.HBM(shape, dtype) for dtype in dtypes],
        in_specs=[pl.BlockSpec(memory_space=pltpu.VMEM)] * len(flat),
        out_specs=[pl.BlockSpec(memory_space=pltpu.HBM)] * pieces,
        scratch_shapes=[pltpu.VMEM((chains * depth, 2 * width), jnp.bfloat16)]
        + [pltpu.VMEM((len(blocks), count, 2 * width), dtype) for dtype in dtypes]
        + [pltpu.SemaphoreType.DMA((pieces, len(blocks)))],
        compiler_params=pltpu.CompilerParams(vmem_limit_bytes=VMEM_BYTES),
        cost_estimate=SMALL_COST,
        name="long_range",
    )(*flat)


def final_kernel(order_ref, *refs, pieces, blocks, rows, aliased, stay):
    short_ref = refs[pieces]
    out_ref, *scratch = refs[pieces + 1 + aliased :]
    parts, (terms, made, part_sem, term_sem, out_sem) = scratch[:-5], scratch[-5:]
    parts = [parts.pop(0) if held else ref for held, ref in zip(stay, refs)]
    steps = pieces * blocks
    windows = [pl.ds(pl.multiple_of(order_ref[n] * rows, rows), rows) for n in range(steps)]
    arriving = []
    for n, window in enumerate(windows):
        arriving.append(
            pltpu.make_async_copy(short_ref.at[window, :], terms.at[n], term_sem.at[n])
        )
        arriving[-1].start()
        piece = n // blocks
        if n % blocks == 0 and stay[piece]:
            part = pltpu.make_async_copy(refs[piece], parts[piece], part_sem.at[piece])
            part.start()
            arriving[-1] = (part, arriving[-1])
        else:
            arriving[-1] = (arriving[-1],)
    leaving = []
    for n, window in enumerate(windows):
        for copy in arriving[n]:
            copy.wait()
        top = n % blocks * rows
        total = parts[n // blocks][top : top + rows, :].astype(jnp.float32) + terms[n]
        made[n] = total.astype(made.dtype).reshape(made.shape[1:])
        leaving.append(pltpu.make_async_copy(made.at[n], out_ref.at[window], out_sem.at[n]))
        leaving[-1].start()
    for copy in leaving:
        copy.wait()


def final_sum(order, pieces, short, earlier, rows):
    columns = pieces[0].shape[1]
    row_count = short.shape[0]
    count = len(pieces)
    blocks = pieces[0].shape[0] // rows
    steps = count * blocks
    aliased = earlier is not None
    stay = [piece.dtype == jnp.float32 for piece in pieces]
    return pl.pallas_call(
        functools.partial(
            final_kernel, pieces=count, blocks=blocks, rows=rows, aliased=aliased, stay=stay
        ),
        out_shape=pltpu.HBM((row_count, 2, columns // 2), jnp.bfloat16),
        in_specs=[pl.BlockSpec(memory_space=pltpu.SMEM)]
        + [pl.BlockSpec(memory_space=pltpu.HBM if held else pltpu.VMEM) for held in stay]
        + [pl.BlockSpec(memory_space=pltpu.HBM)] * (1 + aliased),
        out_specs=pl.BlockSpec(memory_space=pltpu.HBM),
        scratch_shapes=[pltpu.VMEM(piece.shape, piece.dtype) for piece, held in zip(pieces, stay) if held]
        + [
            pltpu.VMEM((steps, rows, columns), jnp.float32),
            pltpu.VMEM((steps, rows, 2, columns // 2), jnp.bfloat16),
            pltpu.SemaphoreType.DMA((count,)),
            pltpu.SemaphoreType.DMA((steps,)),
            pltpu.SemaphoreType.DMA((steps,)),
        ],
        input_output_aliases={count + 2: 0} if aliased else {},
        compiler_params=pltpu.CompilerParams(vmem_limit_bytes=VMEM_BYTES),
        cost_estimate=SMALL_COST,
        name="final_sum",
    )(
        order,
        *(in_hbm(piece) if held else piece for piece, held in zip(pieces, stay)),
        in_hbm(short),
        *([earlier] if aliased else []),
    )


def slot_table(image_dist, image_phase, images):
    chosen = images[None, :] == jnp.arange(image_dist.shape[0], dtype=jnp.int32)[:, None]
    distance = jnp.sum(jnp.where(chosen, image_dist[:, None], 0.0), axis=0)
    phase = jnp.sum(jnp.where(chosen, image_phase[:, None], 0.0), axis=0)
    return jnp.stack([distance, jnp.cos(phase), jnp.sin(phase)])


def slot_block(slots, items):
    digits = jnp.concatenate([slots // 128, slots % 128], axis=0).astype(items.dtype)
    fill = [(0, full - used) for full, used in zip(items.shape[1:], digits.shape)]
    return jnp.pad(digits, fill)[None]


def read_slots(packed, slots):
    count, share = slots.shape
    digits = packed[-1, 0 : 2 * count, 0:share].astype(jnp.int32)
    return digits[0:count] * 128 + digits[count:]


def after(value, *earlier):
    return lax.optimization_barrier((value, *earlier))[0] if earlier else value


def body(
    pair_ft,
    aux_ft,
    coul_weight,
    aux_basis,
    aux_decay,
    image_dist,
    image_phase,
    item_pair,
    item_image,
    item_sub,
    item_count,
):
    group_count = lax.axis_size("grp")
    member_count = lax.axis_size("dev")
    group = lax.axis_index("grp")
    member = lax.axis_index("dev")
    local_rows, _, local_g = pair_ft.shape
    subs = local_rows // item_pair.shape[2]
    rows = aux_ft.shape[0]
    row_count = rows * member_count // group_count
    half = jnp.reshape(group, (1,)).astype(jnp.int32)

    chips = member_count // CORES
    breadth = max(n for n in range(1, chips + 1) if chips % n == 0 and n * n <= chips)
    length = chips // breadth

    aux_flat = aux_ft.reshape(rows, 2 * local_g)
    pairs = after(pair_ft, aux_flat).astype(jnp.float32)
    weighted = (pairs * coul_weight[None, None, :]).astype(jnp.bfloat16)
    turned = weighted.reshape(local_rows, 2 * local_g).T
    item_rows = jnp.swapaxes(item_pair, 1, 2)
    live = (jnp.arange(item_image.shape[0], dtype=jnp.int32) < item_count[0]).astype(jnp.int32)
    slots = jnp.stack([item_image, item_sub, live])

    if group_count != 2 or length % 2:
        everything = lax.all_gather(aux_flat, "dev", axis=0, tiled=True)
        mine = lax.all_to_all(everything, "grp", split_axis=0, concat_axis=1, tiled=True)
        factor = lax.all_gather(turned, "grp", axis=0, tiled=True)
        parts = factor.reshape(group_count, 2, local_g, local_rows)
        other = jnp.stack([parts[:, 1], -parts[:, 0]], axis=1).reshape(factor.shape)
        long_part = jnp.concatenate(
            [
                jnp.dot(mine, factor, preferred_element_type=jnp.float32),
                jnp.dot(mine, other, preferred_element_type=jnp.float32),
            ],
            axis=1,
        )
        items = lax.all_gather(item_rows, "grp", axis=0, tiled=True)
        images, sub_ids, live = lax.all_gather(slots, "grp", axis=1, tiled=True)
        table = slot_table(image_dist, image_phase, images)
        short = short_range(
            half, live, sub_ids, table, aux_basis, aux_decay, [items], row_count, subs
        )
        return (long_part + short).astype(jnp.bfloat16).reshape(row_count, 2, local_rows)

    home = length // 2
    place = member // (breadth * CORES)
    across = member // CORES % breadth
    core = member % CORES

    def send(value, route):
        def index(g, z, y, c):
            return g * member_count + (z * breadth + y) * CORES + c

        pairs = []
        for g in range(group_count):
            for z in range(length):
                for y in range(breadth):
                    for c in range(CORES):
                        pairs.append((index(g, z, y, c), index(*route(g, z, y, c))))
        return lax.ppermute(value, AXES, pairs)

    def to_plane(value):
        return send(value, lambda g, z, y, c: (1 - g, z, y, c))

    ring = [*range(0, length, 2), *reversed(range(1, length, 2))]
    turn = {z: n for n, z in enumerate(ring)}

    def along(value, step):
        return send(value, lambda g, z, y, c: (g, ring[(turn[z] + step) % length], y, c))

    def over_y(value, s):
        return send(value, lambda g, z, y, c: (g, z, (y + s) % breadth, c))

    def over_core(value, t):
        return send(value, lambda g, z, y, c: (g, z, y, (c + t) % CORES))

    def hops_of(g, z):
        hops = [(turn[z] - turn[j]) % length for j in range(g * home, (g + 1) * home)]
        return sorted(hops, key=lambda k: (min(k, length - k), k))

    def here(number):
        return sum(
            jnp.where((group == g) & (place == z), number(g, z), 0)
            for g in range(group_count)
            for z in range(length)
        )

    def pick(other, n, window, *earlier):
        wanted = here(lambda g, z: hops_of(g ^ other, z)[n])
        possible = sorted({hops_of(g, z)[n] for g in range(group_count) for z in range(length)})
        blocks = lax.optimization_barrier((*(held[k] for k in possible), *earlier))
        value = blocks[len(possible) - 1][window]
        for k, block in reversed(list(zip(possible[:-1], blocks))):
            value = jnp.where(wanted == k, block[window], value)
        return value

    def numbers_of(n, s):
        slab = here(lambda g, z: ring[(turn[z] - hops_of(g, z)[n]) % length] - g * home)
        return [
            (slab * breadth + (across - s) % breadth) * CORES + (core - t) % CORES
            for t in range(CORES)
        ]

    def with_cores(value):
        return [value] + [over_core(value, t) for t in range(1, CORES)]

    held = {0: aux_flat, 1: along(aux_flat, 1), length - 1: along(aux_flat, -1)}
    packed = jnp.concatenate([item_rows, slot_block(slots, item_rows)], axis=0)
    items_x = to_plane(packed)
    turned_x = to_plane(after(turned, items_x))
    factors = [[turned, turned_x]] + [[over_y(turned, s)] for s in range(1, breadth)]
    begun = [turned_x, *(pair[0] for pair in factors[1:]), held[1], held[length - 1]]
    for s in range(1, breadth):
        factors[s].append(over_y(after(turned_x, *begun), s))
    for k in range(2, length // 2 + 1):
        held[k] = along(after(held[k - 1], *begun), 1)
    for k in range(2, (length + 1) // 2):
        held[length - k] = along(after(held[length - k + 1], *begun), -1)

    images, sub_ids, live = jnp.concatenate([slots, read_slots(items_x, slots)], axis=1)
    table = slot_table(image_dist, image_phase, images)
    short = short_range(
        half, live, sub_ids, table, aux_basis, aux_decay, [packed, items_x], row_count, subs
    )

    parts = 2 if rows % 32 == 0 else 1
    units = [(n, 0, rows) for n in range(home - 1)]
    units += [(home - 1, k * (rows // parts), rows // parts) for k in range(parts)]
    mine = {}
    theirs = []
    crossed = []
    away = []
    arriving = []
    own = []

    def multiply(i, *earlier):
        n, first, count = units[i]
        blocks = list(zip(mine[n], [after(crossed[i][0], *earlier), *crossed[i][1:]]))
        made = long_range(blocks, factors, (first, 0, count))
        own.append(made[0])
        away.append(made[1:])
        arriving.append([over_y(v, s) for s, v in enumerate(made[1:], 1)])

    for i, (n, first, count) in enumerate(units):
        gate = [*begun, short] if i == 0 else [moved, *(away[i - 2] if i > 1 else [])]
        theirs.append(pick(True, n, slice(first, first + count), *gate))
        moved = to_plane(theirs[i])
        if n not in mine:
            mine[n] = with_cores(pick(False, n, slice(None), theirs[i]))
        if i:
            multiply(i - 1)
        crossed.append(with_cores(after(moved, *away[i - 1] if i else [])))
    last = len(units) - 1

    def place_of(piece, i, s):
        n, first, count = units[i]
        return piece, [v * (rows // count) + first // count for v in numbers_of(n, s)]

    calls = []
    for i, (_, _, count) in enumerate(units[:-1]):
        entries = [place_of(v, i, s) for s, v in enumerate([own[i], *arriving[i]])]
        if calls and calls[-1][0] == count:
            calls[-1][1].extend(entries)
        else:
            calls.append((count, entries))

    def add_up(out, count, entries):
        numbers = jnp.stack([v for _, each in entries for v in each]).astype(jnp.int32)
        return final_sum(numbers, [piece for piece, _ in entries], short, out, count)

    out = add_up(None, *calls.pop(0)) if calls else None
    multiply(last)
    count = units[last][2]
    calls.append((count, [place_of(own[last], last, 0)]))
    if len(calls) > 1 and calls[-2][0] == count:
        entries = calls.pop()[1]
        calls[-1][1].extend(entries)
    if breadth > 1:
        calls.append((count, [place_of(v, last, s) for s, v in enumerate(arriving[last], 1)]))
    for call in calls:
        out = add_up(out, *call)
    return out


def solution(mesh):
    return jax.shard_map(
        body,
        mesh=mesh,
        in_specs=(
            P("dev", None, "grp"),
            P("dev", None, "grp"),
            P("grp"),
            P(),
            P(),
            P(),
            P(),
            P(("grp", "dev"), None, None),
            P(("grp", "dev")),
            P(("grp", "dev")),
            P(("grp", "dev")),
        ),
        out_specs=P("grp", None, "dev"),
        check_vma=False,
    )
```

```python
import functools

import jax
import jax.numpy as jnp
from jax import lax
from jax.experimental import pallas as pl
from jax.experimental.pallas import tpu as pltpu
from jax.sharding import PartitionSpec as P

AXES = ("grp", "dev")
CORES = 2
SMALL_COST = pl.CostEstimate(flops=1, bytes_accessed=1, transcendentals=0)
GROUP_ITEMS = 4
SHORT_VMEM_BYTES = 20 * 1024 * 1024
VMEM_BYTES = 10 * 1024 * 1024


def in_hbm(value):
    return pltpu.with_memory_space_constraint(value, pltpu.HBM)


def short_kernel(
    half_ref, live_ref, sub_ref, meta_ref, basis_ref, decay_ref, *refs, share, subs, depth, width
):
    items, scratch = refs[:-11], refs[-11:]
    out_ref, basis, basis_f32, left, acc, made, dists, group_sub, cursor, basis_sem, out_sem = scratch
    slots = share * len(items)
    row_count = out_ref.shape[0]
    mine = pl.ds(pl.multiple_of(half_ref[0] * row_count, row_count), row_count)
    basis_copy = pltpu.make_async_copy(basis_ref.at[:, mine], basis, basis_sem)
    basis_copy.start()
    left[...] = jnp.zeros_like(left)
    acc[...] = jnp.zeros_like(acc)

    for s in range(subs):
        cursor[s] = 0

    def count(i, carry):
        cursor[sub_ref[i]] = cursor[sub_ref[i]] + live_ref[i]
        return carry

    lax.fori_loop(0, slots, count, 0)
    first = jnp.int32(0)
    for s in range(subs):
        groups = (cursor[s] + GROUP_ITEMS - 1) // GROUP_ITEMS

        def mark(i, carry, s=s):
            group_sub[i] = s
            return carry

        lax.fori_loop(first, first + groups, mark, 0)
        cursor[s] = first * GROUP_ITEMS
        first = first + groups

    def clear(i, carry):
        dists[i] = 0.0
        return carry

    lax.fori_loop(0, first * GROUP_ITEMS, clear, 0)

    for n, items_ref in enumerate(items):

        def place(k, carry, first=n * share, items_ref=items_ref):
            i = first + k

            @pl.when(live_ref[i] > 0)
            def _():
                s = sub_ref[i]
                at = cursor[s]
                cursor[s] = at + 1
                dists[at] = meta_ref[0, i]
                turned = items_ref[k].astype(jnp.float32)
                lanes = pl.ds(pl.multiple_of((at % GROUP_ITEMS) * depth, depth), depth)
                group = at // GROUP_ITEMS
                left[group, 0:width, lanes] = (turned * meta_ref[1, i]).astype(left.dtype)
                left[group, width:, lanes] = (turned * meta_ref[2, i]).astype(left.dtype)

            return carry

        lax.fori_loop(0, share, place, 0)

    tile = min(row_count, made.shape[1])
    decay = decay_ref[:, mine]
    basis_copy.wait()
    basis_f32[...] = basis[...].astype(jnp.float32)

    def one_group(group, carry):
        s = group_sub[group]
        damping = [jnp.exp(decay * -dists[group * GROUP_ITEMS + k]) for k in range(GROUP_ITEMS)]
        for t in range(0, row_count, tile):
            right = jnp.concatenate(
                [
                    (basis_f32[:, t : t + tile] * damping[k][:, t : t + tile]).astype(jnp.bfloat16)
                    for k in range(GROUP_ITEMS)
                ],
                axis=0,
            )
            acc[s, :, t : t + tile] += jnp.dot(
                left[group], right, preferred_element_type=jnp.float32
            )
        return carry

    lax.fori_loop(0, first, one_group, 0)
    copies = []
    for n, t in enumerate(range(0, row_count, tile)):
        for s in range(subs):
            for c in range(2):
                column = (c * subs + s) * width
                made[n, :, column : column + width] = acc[
                    s, c * width : (c + 1) * width, t : t + tile
                ].T
        copies.append(pltpu.make_async_copy(made.at[n], out_ref.at[pl.ds(t, tile), :], out_sem.at[n]))
        copies[-1].start()
    for copy in copies:
        copy.wait()


def short_range(half, live, sub_ids, meta, aux_basis, aux_decay, items, row_count, subs):
    _, width, depth = items[0].shape
    slots = live.shape[0]
    share = slots // len(items)
    groups = slots // GROUP_ITEMS + subs
    tile = min(row_count, 512)
    kernel = functools.partial(short_kernel, share=share, subs=subs, depth=depth, width=width)
    return pl.pallas_call(
        kernel,
        out_shape=pltpu.HBM((row_count, 2 * subs * width), jnp.float32),
        in_specs=[pl.BlockSpec(memory_space=pltpu.SMEM)] * 4
        + [pl.BlockSpec(memory_space=pltpu.HBM)]
        + [pl.BlockSpec(memory_space=pltpu.VMEM)] * (1 + len(items)),
        out_specs=pl.BlockSpec(memory_space=pltpu.HBM),
        scratch_shapes=[
            pltpu.VMEM((depth, row_count), jnp.bfloat16),
            pltpu.VMEM((depth, row_count), jnp.float32),
            pltpu.VMEM((groups, 2 * width, GROUP_ITEMS * depth), jnp.bfloat16),
            pltpu.VMEM((subs, 2 * width, row_count), jnp.float32),
            pltpu.VMEM((row_count // tile, tile, 2 * subs * width), jnp.float32),
            pltpu.SMEM((groups * GROUP_ITEMS,), jnp.float32),
            pltpu.SMEM((groups,), jnp.int32),
            pltpu.SMEM((subs,), jnp.int32),
            pltpu.SemaphoreType.DMA,
            pltpu.SemaphoreType.DMA((row_count // tile,)),
        ],
        compiler_params=pltpu.CompilerParams(vmem_limit_bytes=SHORT_VMEM_BYTES),
        cost_estimate=pl.CostEstimate(
            flops=4 * row_count * slots * depth * width, bytes_accessed=1, transcendentals=0
        ),
        name="short_range",
    )(half, live, sub_ids, meta, in_hbm(aux_basis), aux_decay.reshape(1, -1), *items)


def long_kernel(*refs, blocks, chains, pieces, window):
    parts = refs[: blocks * chains]
    factors = refs[blocks * chains : (blocks + pieces) * chains]
    outs, scratch = refs[(blocks + pieces) * chains :][:pieces], refs[-pieces - 2 :]
    right, made, out_sem = scratch[0], scratch[1:-1], scratch[-1]
    depth, width = factors[0].shape
    half = depth // 2
    count = window[-1]
    copies = []
    for piece in reversed(range(pieces)):
        for chain in range(chains):
            factor = factors[piece * chains + chain]
            top = chain * depth
            right[top : top + depth, 0:width] = factor[...]
            right[top : top + half, width:] = factor[half:, :]
            right[top + half : top + depth, width:] = -factor[0:half, :]
        for block in range(blocks):
            left = jnp.concatenate(
                [
                    parts[block * chains + chain][pl.ds(window[chain], count), :]
                    for chain in range(chains)
                ],
                axis=1,
            )
            total = jnp.dot(left, right[...], preferred_element_type=jnp.float32)
            made[piece][block] = total.astype(outs[piece].dtype)
            target = outs[piece].at[pl.ds(block * count, count), :]
            copies.append(
                pltpu.make_async_copy(made[piece].at[block], target, out_sem.at[piece, block])
            )
            copies[-1].start()
    for copy in copies:
        copy.wait()


def long_range(blocks, factors, window):
    depth, width = factors[0][0].shape
    chains = len(factors[0])
    pieces = len(factors)
    count = window[-1]
    shape = (len(blocks) * count, 2 * width)
    dtypes = [jnp.bfloat16 if piece else jnp.float32 for piece in range(pieces)]
    flat = [v for group in [*blocks, *factors] for v in group]
    return pl.pallas_call(
        functools.partial(
            long_kernel, blocks=len(blocks), chains=chains, pieces=pieces, window=window
        ),
        out_shape=[pltpu.HBM(shape, dtype) for dtype in dtypes],
        in_specs=[pl.BlockSpec(memory_space=pltpu.VMEM)] * len(flat),
        out_specs=[pl.BlockSpec(memory_space=pltpu.HBM)] * pieces,
        scratch_shapes=[pltpu.VMEM((chains * depth, 2 * width), jnp.bfloat16)]
        + [pltpu.VMEM((len(blocks), count, 2 * width), dtype) for dtype in dtypes]
        + [pltpu.SemaphoreType.DMA((pieces, len(blocks)))],
        compiler_params=pltpu.CompilerParams(vmem_limit_bytes=VMEM_BYTES),
        cost_estimate=SMALL_COST,
        name="long_range",
    )(*flat)


def final_kernel(order_ref, *refs, pieces, blocks, rows, aliased, stay):
    short_ref = refs[pieces]
    out_ref, *scratch = refs[pieces + 1 + aliased :]
    parts, (terms, made, part_sem, term_sem, out_sem) = scratch[:-5], scratch[-5:]
    parts = [parts.pop(0) if held else ref for held, ref in zip(stay, refs)]
    steps = pieces * blocks
    windows = [pl.ds(pl.multiple_of(order_ref[n] * rows, rows), rows) for n in range(steps)]
    arriving = []
    for n, window in enumerate(windows):
        arriving.append(
            pltpu.make_async_copy(short_ref.at[window, :], terms.at[n], term_sem.at[n])
        )
        arriving[-1].start()
        piece = n // blocks
        if n % blocks == 0 and stay[piece]:
            part = pltpu.make_async_copy(refs[piece], parts[piece], part_sem.at[piece])
            part.start()
            arriving[-1] = (part, arriving[-1])
        else:
            arriving[-1] = (arriving[-1],)
    leaving = []
    for n, window in enumerate(windows):
        for copy in arriving[n]:
            copy.wait()
        top = n % blocks * rows
        total = parts[n // blocks][top : top + rows, :].astype(jnp.float32) + terms[n]
        made[n] = total.astype(made.dtype).reshape(made.shape[1:])
        leaving.append(pltpu.make_async_copy(made.at[n], out_ref.at[window], out_sem.at[n]))
        leaving[-1].start()
    for copy in leaving:
        copy.wait()


def final_sum(order, pieces, short, earlier, rows):
    columns = pieces[0].shape[1]
    row_count = short.shape[0]
    count = len(pieces)
    blocks = pieces[0].shape[0] // rows
    steps = count * blocks
    aliased = earlier is not None
    stay = [piece.dtype == jnp.float32 for piece in pieces]
    return pl.pallas_call(
        functools.partial(
            final_kernel, pieces=count, blocks=blocks, rows=rows, aliased=aliased, stay=stay
        ),
        out_shape=pltpu.HBM((row_count, 2, columns // 2), jnp.bfloat16),
        in_specs=[pl.BlockSpec(memory_space=pltpu.SMEM)]
        + [pl.BlockSpec(memory_space=pltpu.HBM if held else pltpu.VMEM) for held in stay]
        + [pl.BlockSpec(memory_space=pltpu.HBM)] * (1 + aliased),
        out_specs=pl.BlockSpec(memory_space=pltpu.HBM),
        scratch_shapes=[pltpu.VMEM(piece.shape, piece.dtype) for piece, held in zip(pieces, stay) if held]
        + [
            pltpu.VMEM((steps, rows, columns), jnp.float32),
            pltpu.VMEM((steps, rows, 2, columns // 2), jnp.bfloat16),
            pltpu.SemaphoreType.DMA((count,)),
            pltpu.SemaphoreType.DMA((steps,)),
            pltpu.SemaphoreType.DMA((steps,)),
        ],
        input_output_aliases={count + 2: 0} if aliased else {},
        compiler_params=pltpu.CompilerParams(vmem_limit_bytes=VMEM_BYTES),
        cost_estimate=SMALL_COST,
        name="final_sum",
    )(
        order,
        *(in_hbm(piece) if held else piece for piece, held in zip(pieces, stay)),
        in_hbm(short),
        *([earlier] if aliased else []),
    )


def slot_table(image_dist, image_phase, images):
    chosen = images[None, :] == jnp.arange(image_dist.shape[0], dtype=jnp.int32)[:, None]
    distance = jnp.sum(jnp.where(chosen, image_dist[:, None], 0.0), axis=0)
    phase = jnp.sum(jnp.where(chosen, image_phase[:, None], 0.0), axis=0)
    return jnp.stack([distance, jnp.cos(phase), jnp.sin(phase)])


def slot_block(slots, items):
    digits = jnp.concatenate([slots // 128, slots % 128], axis=0).astype(items.dtype)
    fill = [(0, full - used) for full, used in zip(items.shape[1:], digits.shape)]
    return jnp.pad(digits, fill)[None]


def read_slots(packed, slots):
    count, share = slots.shape
    digits = packed[-1, 0 : 2 * count, 0:share].astype(jnp.int32)
    return digits[0:count] * 128 + digits[count:]


def after(value, *earlier):
    return lax.optimization_barrier((value, *earlier))[0] if earlier else value


def body(
    pair_ft,
    aux_ft,
    coul_weight,
    aux_basis,
    aux_decay,
    image_dist,
    image_phase,
    item_pair,
    item_image,
    item_sub,
    item_count,
):
    group_count = lax.axis_size("grp")
    member_count = lax.axis_size("dev")
    group = lax.axis_index("grp")
    member = lax.axis_index("dev")
    local_rows, _, local_g = pair_ft.shape
    subs = local_rows // item_pair.shape[2]
    rows = aux_ft.shape[0]
    row_count = rows * member_count // group_count
    half = jnp.reshape(group, (1,)).astype(jnp.int32)

    chips = member_count // CORES
    breadth = max(n for n in range(1, chips + 1) if chips % n == 0 and n * n <= chips)
    length = chips // breadth

    aux_flat = aux_ft.reshape(rows, 2 * local_g)
    pairs = after(pair_ft, aux_flat).astype(jnp.float32)
    weighted = (pairs * coul_weight[None, None, :]).astype(jnp.bfloat16)
    turned = weighted.reshape(local_rows, 2 * local_g).T
    item_rows = jnp.swapaxes(item_pair, 1, 2)
    live = (jnp.arange(item_image.shape[0], dtype=jnp.int32) < item_count[0]).astype(jnp.int32)
    slots = jnp.stack([item_image, item_sub, live])

    if group_count != 2 or length % 2:
        everything = lax.all_gather(aux_flat, "dev", axis=0, tiled=True)
        mine = lax.all_to_all(everything, "grp", split_axis=0, concat_axis=1, tiled=True)
        factor = lax.all_gather(turned, "grp", axis=0, tiled=True)
        parts = factor.reshape(group_count, 2, local_g, local_rows)
        other = jnp.stack([parts[:, 1], -parts[:, 0]], axis=1).reshape(factor.shape)
        long_part = jnp.concatenate(
            [
                jnp.dot(mine, factor, preferred_element_type=jnp.float32),
                jnp.dot(mine, other, preferred_element_type=jnp.float32),
            ],
            axis=1,
        )
        items = lax.all_gather(item_rows, "grp", axis=0, tiled=True)
        images, sub_ids, live = lax.all_gather(slots, "grp", axis=1, tiled=True)
        table = slot_table(image_dist, image_phase, images)
        short = short_range(
            half, live, sub_ids, table, aux_basis, aux_decay, [items], row_count, subs
        )
        return (long_part + short).astype(jnp.bfloat16).reshape(row_count, 2, local_rows)

    home = length // 2
    place = member // (breadth * CORES)
    across = member // CORES % breadth
    core = member % CORES

    def send(value, route):
        def index(g, z, y, c):
            return g * member_count + (z * breadth + y) * CORES + c

        pairs = []
        for g in range(group_count):
            for z in range(length):
                for y in range(breadth):
                    for c in range(CORES):
                        pairs.append((index(g, z, y, c), index(*route(g, z, y, c))))
        return lax.ppermute(value, AXES, pairs)

    def to_plane(value):
        return send(value, lambda g, z, y, c: (1 - g, z, y, c))

    ring = [*range(0, length, 2), *reversed(range(1, length, 2))]
    turn = {z: n for n, z in enumerate(ring)}

    def along(value, step):
        return send(value, lambda g, z, y, c: (g, ring[(turn[z] + step) % length], y, c))

    def over_y(value, s):
        return send(value, lambda g, z, y, c: (g, z, (y + s) % breadth, c))

    def over_core(value, t):
        return send(value, lambda g, z, y, c: (g, z, y, (c + t) % CORES))

    def hops_of(g, z):
        hops = [(turn[z] - turn[j]) % length for j in range(g * home, (g + 1) * home)]
        return sorted(hops, key=lambda k: (min(k, length - k), k))

    def here(number):
        return sum(
            jnp.where((group == g) & (place == z), number(g, z), 0)
            for g in range(group_count)
            for z in range(length)
        )

    def pick(other, n, window, *earlier):
        wanted = here(lambda g, z: hops_of(g ^ other, z)[n])
        possible = sorted({hops_of(g, z)[n] for g in range(group_count) for z in range(length)})
        blocks = lax.optimization_barrier((*(held[k] for k in possible), *earlier))
        value = blocks[len(possible) - 1][window]
        for k, block in reversed(list(zip(possible[:-1], blocks))):
            value = jnp.where(wanted == k, block[window], value)
        return value

    def numbers_of(n, s):
        slab = here(lambda g, z: ring[(turn[z] - hops_of(g, z)[n]) % length] - g * home)
        return [
            (slab * breadth + (across - s) % breadth) * CORES + (core - t) % CORES
            for t in range(CORES)
        ]

    def with_cores(value):
        return [value] + [over_core(value, t) for t in range(1, CORES)]

    held = {0: aux_flat, 1: along(aux_flat, 1), length - 1: along(aux_flat, -1)}
    packed = jnp.concatenate([item_rows, slot_block(slots, item_rows)], axis=0)
    items_x = to_plane(packed)
    turned_x = to_plane(turned)
    factors = [[turned, turned_x]] + [[over_y(turned, s)] for s in range(1, breadth)]
    parts = 2 if rows % 32 == 0 else 1
    units = [(n, 0, rows) for n in range(home - 1)]
    units += [(home - 1, k * (rows // parts), rows // parts) for k in range(parts)]
    mine = {}
    theirs = []
    crossed = []
    away = []
    arriving = []
    own = []

    def multiply(i, *earlier):
        n, first, count = units[i]
        blocks = list(zip(mine[n], [after(crossed[i][0], *earlier), *crossed[i][1:]]))
        made = long_range(blocks, factors, (first, 0, count))
        own.append(made[0])
        away.append(made[1:])
        arriving.append([over_y(v, s) for s, v in enumerate(made[1:], 1)])

    def foreign(i, *earlier):
        n, first, count = units[i]
        theirs.append(pick(True, n, slice(first, first + count), *earlier))
        return to_plane(theirs[i])

    moved = foreign(0)
    begun = [items_x, turned_x, *(pair[0] for pair in factors[1:]), held[1], held[length - 1]]
    begun = [theirs[0], *begun]
    for k in range(2, length // 2 + 1):
        held[k] = along(after(held[k - 1], *begun), 1)
    for k in range(2, (length + 1) // 2):
        held[length - k] = along(after(held[length - k + 1], *begun), -1)
    for s in range(1, breadth):
        factors[s].append(over_y(after(turned_x, *begun), s))
    seen, sub_ids, live = jnp.concatenate([slots, read_slots(after(items_x, *begun), slots)], axis=1)
    table = slot_table(image_dist, image_phase, seen)
    short = short_range(
        half, live, sub_ids, table, aux_basis, aux_decay, [packed, items_x], row_count, subs
    )
    for i, (n, first, count) in enumerate(units):
        if i:
            moved = foreign(i, theirs[i - 1], *(away[i - 2] if i > 1 else [short]))
        if n not in mine:
            mine[n] = with_cores(pick(False, n, slice(None), theirs[i]))
        if i:
            multiply(i - 1)
        crossed.append(with_cores(after(moved, *away[i - 1] if i else [short])))
    last = len(units) - 1

    def place_of(piece, i, s):
        n, first, count = units[i]
        return piece, [v * (rows // count) + first // count for v in numbers_of(n, s)]

    calls = []
    for i, (_, _, count) in enumerate(units[:-1]):
        entries = [place_of(v, i, s) for s, v in enumerate([own[i], *arriving[i]])]
        if calls and calls[-1][0] == count:
            calls[-1][1].extend(entries)
        else:
            calls.append((count, entries))

    def add_up(out, count, entries):
        numbers = jnp.stack([v for _, each in entries for v in each]).astype(jnp.int32)
        return final_sum(numbers, [piece for piece, _ in entries], short, out, count)

    out = add_up(None, *calls.pop(0)) if calls else None
    multiply(last)
    count = units[last][2]
    calls.append((count, [place_of(own[last], last, 0)]))
    if len(calls) > 1 and calls[-2][0] == count:
        entries = calls.pop()[1]
        calls[-1][1].extend(entries)
    if breadth > 1:
        calls.append((count, [place_of(v, last, s) for s, v in enumerate(arriving[last], 1)]))
    for call in calls:
        out = add_up(out, *call)
    return out


def solution(mesh):
    return jax.shard_map(
        body,
        mesh=mesh,
        in_specs=(
            P("dev", None, "grp"),
            P("dev", None, "grp"),
            P("grp"),
            P(),
            P(),
            P(),
            P(),
            P(("grp", "dev"), None, None),
            P(("grp", "dev")),
            P(("grp", "dev")),
            P(("grp", "dev")),
        ),
        out_specs=P("grp", None, "dev"),
        check_vma=False,
    )
```

```python
import functools

import jax
import jax.numpy as jnp
from jax import lax
from jax.experimental import pallas as pl
from jax.experimental.pallas import tpu as pltpu
from jax.sharding import PartitionSpec as P

AXES = ("grp", "dev")
CORES = 2
SMALL_COST = pl.CostEstimate(flops=1, bytes_accessed=1, transcendentals=0)
GROUP_ITEMS = 4
SHORT_VMEM_BYTES = 20 * 1024 * 1024
VMEM_BYTES = 10 * 1024 * 1024


def in_hbm(value):
    return pltpu.with_memory_space_constraint(value, pltpu.HBM)


def short_kernel(
    half_ref, live_ref, sub_ref, meta_ref, basis_ref, decay_ref, *refs, share, subs, depth, width
):
    items, scratch = refs[:-11], refs[-11:]
    out_ref, basis, basis_f32, left, acc, made, dists, group_sub, cursor, basis_sem, out_sem = scratch
    slots = share * len(items)
    row_count = out_ref.shape[0]
    mine = pl.ds(pl.multiple_of(half_ref[0] * row_count, row_count), row_count)
    basis_copy = pltpu.make_async_copy(basis_ref.at[:, mine], basis, basis_sem)
    basis_copy.start()
    left[...] = jnp.zeros_like(left)
    acc[...] = jnp.zeros_like(acc)

    for s in range(subs):
        cursor[s] = 0

    def count(i, carry):
        cursor[sub_ref[i]] = cursor[sub_ref[i]] + live_ref[i]
        return carry

    lax.fori_loop(0, slots, count, 0)
    first = jnp.int32(0)
    for s in range(subs):
        groups = (cursor[s] + GROUP_ITEMS - 1) // GROUP_ITEMS

        def mark(i, carry, s=s):
            group_sub[i] = s
            return carry

        lax.fori_loop(first, first + groups, mark, 0)
        cursor[s] = first * GROUP_ITEMS
        first = first + groups

    def clear(i, carry):
        dists[i] = 0.0
        return carry

    lax.fori_loop(0, first * GROUP_ITEMS, clear, 0)

    for n, items_ref in enumerate(items):

        def place(k, carry, first=n * share, items_ref=items_ref):
            i = first + k

            @pl.when(live_ref[i] > 0)
            def _():
                s = sub_ref[i]
                at = cursor[s]
                cursor[s] = at + 1
                dists[at] = meta_ref[0, i]
                turned = items_ref[k].astype(jnp.float32)
                lanes = pl.ds(pl.multiple_of((at % GROUP_ITEMS) * depth, depth), depth)
                group = at // GROUP_ITEMS
                left[group, 0:width, lanes] = (turned * meta_ref[1, i]).astype(left.dtype)
                left[group, width:, lanes] = (turned * meta_ref[2, i]).astype(left.dtype)

            return carry

        lax.fori_loop(0, share, place, 0)

    tile = min(row_count, made.shape[1])
    decay = decay_ref[:, mine]
    basis_copy.wait()
    basis_f32[...] = basis[...].astype(jnp.float32)

    def one_group(group, carry):
        s = group_sub[group]
        damping = [jnp.exp(decay * -dists[group * GROUP_ITEMS + k]) for k in range(GROUP_ITEMS)]
        for t in range(0, row_count, tile):
            right = jnp.concatenate(
                [
                    (basis_f32[:, t : t + tile] * damping[k][:, t : t + tile]).astype(jnp.bfloat16)
                    for k in range(GROUP_ITEMS)
                ],
                axis=0,
            )
            acc[s, :, t : t + tile] += jnp.dot(
                left[group], right, preferred_element_type=jnp.float32
            )
        return carry

    lax.fori_loop(0, first, one_group, 0)
    copies = []
    for n, t in enumerate(range(0, row_count, tile)):
        for s in range(subs):
            for c in range(2):
                column = (c * subs + s) * width
                made[n, :, column : column + width] = acc[
                    s, c * width : (c + 1) * width, t : t + tile
                ].T
        copies.append(pltpu.make_async_copy(made.at[n], out_ref.at[pl.ds(t, tile), :], out_sem.at[n]))
        copies[-1].start()
    for copy in copies:
        copy.wait()


def short_range(half, live, sub_ids, meta, aux_basis, aux_decay, items, row_count, subs):
    _, width, depth = items[0].shape
    slots = live.shape[0]
    share = slots // len(items)
    groups = slots // GROUP_ITEMS + subs
    tile = min(row_count, 512)
    kernel = functools.partial(short_kernel, share=share, subs=subs, depth=depth, width=width)
    return pl.pallas_call(
        kernel,
        out_shape=pltpu.HBM((row_count, 2 * subs * width), jnp.float32),
        in_specs=[pl.BlockSpec(memory_space=pltpu.SMEM)] * 4
        + [pl.BlockSpec(memory_space=pltpu.HBM)]
        + [pl.BlockSpec(memory_space=pltpu.VMEM)] * (1 + len(items)),
        out_specs=pl.BlockSpec(memory_space=pltpu.HBM),
        scratch_shapes=[
            pltpu.VMEM((depth, row_count), jnp.bfloat16),
            pltpu.VMEM((depth, row_count), jnp.float32),
            pltpu.VMEM((groups, 2 * width, GROUP_ITEMS * depth), jnp.bfloat16),
            pltpu.VMEM((subs, 2 * width, row_count), jnp.float32),
            pltpu.VMEM((row_count // tile, tile, 2 * subs * width), jnp.float32),
            pltpu.SMEM((groups * GROUP_ITEMS,), jnp.float32),
            pltpu.SMEM((groups,), jnp.int32),
            pltpu.SMEM((subs,), jnp.int32),
            pltpu.SemaphoreType.DMA,
            pltpu.SemaphoreType.DMA((row_count // tile,)),
        ],
        compiler_params=pltpu.CompilerParams(vmem_limit_bytes=SHORT_VMEM_BYTES),
        cost_estimate=pl.CostEstimate(
            flops=4 * row_count * slots * depth * width, bytes_accessed=1, transcendentals=0
        ),
        name="short_range",
    )(half, live, sub_ids, meta, in_hbm(aux_basis), aux_decay.reshape(1, -1), *items)


def long_kernel(*refs, blocks, chains, pieces, window):
    parts = refs[: blocks * chains]
    factors = refs[blocks * chains : (blocks + pieces) * chains]
    outs, scratch = refs[(blocks + pieces) * chains :][:pieces], refs[-pieces - 2 :]
    right, made, out_sem = scratch[0], scratch[1:-1], scratch[-1]
    depth, width = factors[0].shape
    half = depth // 2
    count = window[-1]
    copies = []
    for piece in reversed(range(pieces)):
        for chain in range(chains):
            factor = factors[piece * chains + chain]
            top = chain * depth
            right[top : top + depth, 0:width] = factor[...]
            right[top : top + half, width:] = factor[half:, :]
            right[top + half : top + depth, width:] = -factor[0:half, :]
        for block in range(blocks):
            left = jnp.concatenate(
                [
                    parts[block * chains + chain][pl.ds(window[chain], count), :]
                    for chain in range(chains)
                ],
                axis=1,
            )
            total = jnp.dot(left, right[...], preferred_element_type=jnp.float32)
            made[piece][block] = total.astype(outs[piece].dtype)
            target = outs[piece].at[pl.ds(block * count, count), :]
            copies.append(
                pltpu.make_async_copy(made[piece].at[block], target, out_sem.at[piece, block])
            )
            copies[-1].start()
    for copy in copies:
        copy.wait()


def long_range(blocks, factors, window):
    depth, width = factors[0][0].shape
    chains = len(factors[0])
    pieces = len(factors)
    count = window[-1]
    shape = (len(blocks) * count, 2 * width)
    dtypes = [jnp.bfloat16 if piece else jnp.float32 for piece in range(pieces)]
    flat = [v for group in [*blocks, *factors] for v in group]
    return pl.pallas_call(
        functools.partial(
            long_kernel, blocks=len(blocks), chains=chains, pieces=pieces, window=window
        ),
        out_shape=[pltpu.HBM(shape, dtype) for dtype in dtypes],
        in_specs=[pl.BlockSpec(memory_space=pltpu.VMEM)] * len(flat),
        out_specs=[pl.BlockSpec(memory_space=pltpu.HBM)] * pieces,
        scratch_shapes=[pltpu.VMEM((chains * depth, 2 * width), jnp.bfloat16)]
        + [pltpu.VMEM((len(blocks), count, 2 * width), dtype) for dtype in dtypes]
        + [pltpu.SemaphoreType.DMA((pieces, len(blocks)))],
        compiler_params=pltpu.CompilerParams(vmem_limit_bytes=VMEM_BYTES),
        cost_estimate=SMALL_COST,
        name="long_range",
    )(*flat)


def final_kernel(order_ref, *refs, pieces, blocks, rows, aliased, stay):
    short_ref = refs[pieces]
    out_ref, *scratch = refs[pieces + 1 + aliased :]
    parts, (terms, made, part_sem, term_sem, out_sem) = scratch[:-5], scratch[-5:]
    parts = [parts.pop(0) if held else ref for held, ref in zip(stay, refs)]
    steps = pieces * blocks
    windows = [pl.ds(pl.multiple_of(order_ref[n] * rows, rows), rows) for n in range(steps)]
    arriving = []
    for n, window in enumerate(windows):
        arriving.append(
            pltpu.make_async_copy(short_ref.at[window, :], terms.at[n], term_sem.at[n])
        )
        arriving[-1].start()
        piece = n // blocks
        if n % blocks == 0 and stay[piece]:
            part = pltpu.make_async_copy(refs[piece], parts[piece], part_sem.at[piece])
            part.start()
            arriving[-1] = (part, arriving[-1])
        else:
            arriving[-1] = (arriving[-1],)
    leaving = []
    for n, window in enumerate(windows):
        for copy in arriving[n]:
            copy.wait()
        top = n % blocks * rows
        total = parts[n // blocks][top : top + rows, :].astype(jnp.float32) + terms[n]
        made[n] = total.astype(made.dtype).reshape(made.shape[1:])
        leaving.append(pltpu.make_async_copy(made.at[n], out_ref.at[window], out_sem.at[n]))
        leaving[-1].start()
    for copy in leaving:
        copy.wait()


def final_sum(order, pieces, short, earlier, rows):
    columns = pieces[0].shape[1]
    row_count = short.shape[0]
    count = len(pieces)
    blocks = pieces[0].shape[0] // rows
    steps = count * blocks
    aliased = earlier is not None
    stay = [piece.dtype == jnp.float32 for piece in pieces]
    return pl.pallas_call(
        functools.partial(
            final_kernel, pieces=count, blocks=blocks, rows=rows, aliased=aliased, stay=stay
        ),
        out_shape=pltpu.HBM((row_count, 2, columns // 2), jnp.bfloat16),
        in_specs=[pl.BlockSpec(memory_space=pltpu.SMEM)]
        + [pl.BlockSpec(memory_space=pltpu.HBM if held else pltpu.VMEM) for held in stay]
        + [pl.BlockSpec(memory_space=pltpu.HBM)] * (1 + aliased),
        out_specs=pl.BlockSpec(memory_space=pltpu.HBM),
        scratch_shapes=[pltpu.VMEM(piece.shape, piece.dtype) for piece, held in zip(pieces, stay) if held]
        + [
            pltpu.VMEM((steps, rows, columns), jnp.float32),
            pltpu.VMEM((steps, rows, 2, columns // 2), jnp.bfloat16),
            pltpu.SemaphoreType.DMA((count,)),
            pltpu.SemaphoreType.DMA((steps,)),
            pltpu.SemaphoreType.DMA((steps,)),
        ],
        input_output_aliases={count + 2: 0} if aliased else {},
        compiler_params=pltpu.CompilerParams(vmem_limit_bytes=VMEM_BYTES),
        cost_estimate=SMALL_COST,
        name="final_sum",
    )(
        order,
        *(in_hbm(piece) if held else piece for piece, held in zip(pieces, stay)),
        in_hbm(short),
        *([earlier] if aliased else []),
    )


def slot_table(image_dist, image_phase, images):
    chosen = images[None, :] == jnp.arange(image_dist.shape[0], dtype=jnp.int32)[:, None]
    distance = jnp.sum(jnp.where(chosen, image_dist[:, None], 0.0), axis=0)
    phase = jnp.sum(jnp.where(chosen, image_phase[:, None], 0.0), axis=0)
    return jnp.stack([distance, jnp.cos(phase), jnp.sin(phase)])


def slot_block(slots, items):
    digits = jnp.concatenate([slots // 128, slots % 128], axis=0).astype(items.dtype)
    fill = [(0, full - used) for full, used in zip(items.shape[1:], digits.shape)]
    return jnp.pad(digits, fill)[None]


def read_slots(packed, slots):
    count, share = slots.shape
    digits = packed[-1, 0 : 2 * count, 0:share].astype(jnp.int32)
    return digits[0:count] * 128 + digits[count:]


def after(value, *earlier):
    return lax.optimization_barrier((value, *earlier))[0] if earlier else value


def body(
    pair_ft,
    aux_ft,
    coul_weight,
    aux_basis,
    aux_decay,
    image_dist,
    image_phase,
    item_pair,
    item_image,
    item_sub,
    item_count,
):
    group_count = lax.axis_size("grp")
    member_count = lax.axis_size("dev")
    group = lax.axis_index("grp")
    member = lax.axis_index("dev")
    local_rows, _, local_g = pair_ft.shape
    subs = local_rows // item_pair.shape[2]
    rows = aux_ft.shape[0]
    row_count = rows * member_count // group_count
    half = jnp.reshape(group, (1,)).astype(jnp.int32)

    chips = member_count // CORES
    breadth = max(n for n in range(1, chips + 1) if chips % n == 0 and n * n <= chips)
    length = chips // breadth

    aux_flat = aux_ft.reshape(rows, 2 * local_g)
    pairs = after(pair_ft, aux_flat).astype(jnp.float32)
    weighted = (pairs * coul_weight[None, None, :]).astype(jnp.bfloat16)
    turned = weighted.reshape(local_rows, 2 * local_g).T
    item_rows = jnp.swapaxes(item_pair, 1, 2)
    live = (jnp.arange(item_image.shape[0], dtype=jnp.int32) < item_count[0]).astype(jnp.int32)
    slots = jnp.stack([item_image, item_sub, live])

    if group_count != 2 or length % 2:
        everything = lax.all_gather(aux_flat, "dev", axis=0, tiled=True)
        mine = lax.all_to_all(everything, "grp", split_axis=0, concat_axis=1, tiled=True)
        factor = lax.all_gather(turned, "grp", axis=0, tiled=True)
        parts = factor.reshape(group_count, 2, local_g, local_rows)
        other = jnp.stack([parts[:, 1], -parts[:, 0]], axis=1).reshape(factor.shape)
        long_part = jnp.concatenate(
            [
                jnp.dot(mine, factor, preferred_element_type=jnp.float32),
                jnp.dot(mine, other, preferred_element_type=jnp.float32),
            ],
            axis=1,
        )
        items = lax.all_gather(item_rows, "grp", axis=0, tiled=True)
        images, sub_ids, live = lax.all_gather(slots, "grp", axis=1, tiled=True)
        table = slot_table(image_dist, image_phase, images)
        short = short_range(
            half, live, sub_ids, table, aux_basis, aux_decay, [items], row_count, subs
        )
        return (long_part + short).astype(jnp.bfloat16).reshape(row_count, 2, local_rows)

    home = length // 2
    place = member // (breadth * CORES)
    across = member // CORES % breadth
    core = member % CORES

    def send(value, route):
        def index(g, z, y, c):
            return g * member_count + (z * breadth + y) * CORES + c

        pairs = []
        for g in range(group_count):
            for z in range(length):
                for y in range(breadth):
                    for c in range(CORES):
                        pairs.append((index(g, z, y, c), index(*route(g, z, y, c))))
        return lax.ppermute(value, AXES, pairs)

    def to_plane(value):
        return send(value, lambda g, z, y, c: (1 - g, z, y, c))

    ring = [*range(0, length, 2), *reversed(range(1, length, 2))]
    turn = {z: n for n, z in enumerate(ring)}

    def along(value, step):
        return send(value, lambda g, z, y, c: (g, ring[(turn[z] + step) % length], y, c))

    def over_y(value, s):
        return send(value, lambda g, z, y, c: (g, z, (y + s) % breadth, c))

    def over_core(value, t):
        return send(value, lambda g, z, y, c: (g, z, y, (c + t) % CORES))

    def hops_of(g, z):
        hops = [(turn[z] - turn[j]) % length for j in range(g * home, (g + 1) * home)]
        return sorted(hops, key=lambda k: (min(k, length - k), k))

    def here(number):
        return sum(
            jnp.where((group == g) & (place == z), number(g, z), 0)
            for g in range(group_count)
            for z in range(length)
        )

    def pick(other, n, window, *earlier):
        wanted = here(lambda g, z: hops_of(g ^ other, z)[n])
        possible = sorted({hops_of(g, z)[n] for g in range(group_count) for z in range(length)})
        blocks = lax.optimization_barrier((*(held[k] for k in possible), *earlier))
        value = blocks[len(possible) - 1][window]
        for k, block in reversed(list(zip(possible[:-1], blocks))):
            value = jnp.where(wanted == k, block[window], value)
        return value

    def numbers_of(n, s):
        slab = here(lambda g, z: ring[(turn[z] - hops_of(g, z)[n]) % length] - g * home)
        return [
            (slab * breadth + (across - s) % breadth) * CORES + (core - t) % CORES
            for t in range(CORES)
        ]

    def with_cores(value):
        return [value] + [over_core(value, t) for t in range(1, CORES)]

    held = {0: aux_flat, 1: along(aux_flat, 1), length - 1: along(aux_flat, -1)}
    packed = jnp.concatenate([item_rows, slot_block(slots, item_rows)], axis=0)
    turned_x = to_plane(turned)
    factors = [[turned, turned_x]] + [[over_y(turned, s)] for s in range(1, breadth)]
    items_x = to_plane(after(packed, *(pair[0] for pair in factors[1:]), turned_x, held[1]))
    for s in range(1, breadth):
        factors[s].append(over_y(turned_x, s))
    units = [(n, 0, rows) for n in range(home)]
    mine = {}
    theirs = []
    crossed = []
    away = []
    arriving = []
    own = []

    def multiply(i, *earlier):
        n, first, count = units[i]
        blocks = list(zip(mine[n], [after(crossed[i][0], *earlier), *crossed[i][1:]]))
        made = long_range(blocks, factors, (first, 0, count))
        own.append(made[0])
        away.append(made[1:])
        arriving.append([over_y(v, s) for s, v in enumerate(made[1:], 1)])

    def foreign(i, *earlier):
        n, first, count = units[i]
        theirs.append(pick(True, n, slice(first, first + count), *earlier))
        return to_plane(theirs[i])

    moved = foreign(0, items_x, *(pair[1] for pair in factors[1:]))
    begun = [theirs[0], held[1], held[length - 1]]
    for k in range(2, length // 2 + 1):
        held[k] = along(after(held[k - 1], *begun), 1)
    for k in range(2, (length + 1) // 2):
        held[length - k] = along(after(held[length - k + 1], *begun), -1)
    for i, (n, _, _) in enumerate(units):
        if i:
            moved = foreign(i, theirs[i - 1], *(away[i - 2] if i > 1 else []))
        mine[n] = with_cores(pick(False, n, slice(None), theirs[i]))
        if i:
            multiply(i - 1)
        crossed.append(with_cores(after(moved, *away[i - 1] if i else [])))
    slots_x = read_slots(after(items_x, *(away[0] if away else [])), slots)
    seen, sub_ids, live = jnp.concatenate([slots, slots_x], axis=1)
    table = slot_table(image_dist, image_phase, seen)
    short = short_range(
        half, live, sub_ids, table, aux_basis, aux_decay, [packed, items_x], row_count, subs
    )
    last = len(units) - 1

    def place_of(piece, i, s):
        n, first, count = units[i]
        return piece, [v * (rows // count) + first // count for v in numbers_of(n, s)]

    calls = []
    for i, (_, _, count) in enumerate(units[:-1]):
        entries = [place_of(v, i, s) for s, v in enumerate([own[i], *arriving[i]])]
        if calls and calls[-1][0] == count:
            calls[-1][1].extend(entries)
        else:
            calls.append((count, entries))

    def add_up(out, count, entries):
        numbers = jnp.stack([v for _, each in entries for v in each]).astype(jnp.int32)
        return final_sum(numbers, [piece for piece, _ in entries], short, out, count)

    out = add_up(None, *calls.pop(0)) if calls else None
    multiply(last)
    count = units[last][2]
    calls.append((count, [place_of(own[last], last, 0)]))
    if len(calls) > 1 and calls[-2][0] == count:
        entries = calls.pop()[1]
        calls[-1][1].extend(entries)
    if breadth > 1:
        calls.append((count, [place_of(v, last, s) for s, v in enumerate(arriving[last], 1)]))
    for call in calls:
        out = add_up(out, *call)
    return out


def solution(mesh):
    return jax.shard_map(
        body,
        mesh=mesh,
        in_specs=(
            P("dev", None, "grp"),
            P("dev", None, "grp"),
            P("grp"),
            P(),
            P(),
            P(),
            P(),
            P(("grp", "dev"), None, None),
            P(("grp", "dev")),
            P(("grp", "dev")),
            P(("grp", "dev")),
        ),
        out_specs=P("grp", None, "dev"),
        check_vma=False,
    )
```

```python
import functools

import jax
import jax.numpy as jnp
from jax import lax
from jax.experimental import pallas as pl
from jax.experimental.pallas import tpu as pltpu
from jax.sharding import PartitionSpec as P

AXES = ("grp", "dev")
CORES = 2
SMALL_COST = pl.CostEstimate(flops=1, bytes_accessed=1, transcendentals=0)
GROUP_ITEMS = 4
SHORT_VMEM_BYTES = 20 * 1024 * 1024
VMEM_BYTES = 10 * 1024 * 1024


def in_hbm(value):
    return pltpu.with_memory_space_constraint(value, pltpu.HBM)


def short_kernel(
    half_ref, live_ref, sub_ref, meta_ref, basis_ref, decay_ref, *refs, share, subs, depth, width
):
    items, scratch = refs[:-11], refs[-11:]
    out_ref, basis, basis_f32, left, acc, made, dists, group_sub, cursor, basis_sem, out_sem = scratch
    slots = share * len(items)
    row_count = out_ref.shape[0]
    mine = pl.ds(pl.multiple_of(half_ref[0] * row_count, row_count), row_count)
    basis_copy = pltpu.make_async_copy(basis_ref.at[:, mine], basis, basis_sem)
    basis_copy.start()
    left[...] = jnp.zeros_like(left)
    acc[...] = jnp.zeros_like(acc)

    for s in range(subs):
        cursor[s] = 0

    def count(i, carry):
        cursor[sub_ref[i]] = cursor[sub_ref[i]] + live_ref[i]
        return carry

    lax.fori_loop(0, slots, count, 0)
    first = jnp.int32(0)
    for s in range(subs):
        groups = (cursor[s] + GROUP_ITEMS - 1) // GROUP_ITEMS

        def mark(i, carry, s=s):
            group_sub[i] = s
            return carry

        lax.fori_loop(first, first + groups, mark, 0)
        cursor[s] = first * GROUP_ITEMS
        first = first + groups

    def clear(i, carry):
        dists[i] = 0.0
        return carry

    lax.fori_loop(0, first * GROUP_ITEMS, clear, 0)

    for n, items_ref in enumerate(items):

        def place(k, carry, first=n * share, items_ref=items_ref):
            i = first + k

            @pl.when(live_ref[i] > 0)
            def _():
                s = sub_ref[i]
                at = cursor[s]
                cursor[s] = at + 1
                dists[at] = meta_ref[0, i]
                turned = items_ref[k].astype(jnp.float32)
                lanes = pl.ds(pl.multiple_of((at % GROUP_ITEMS) * depth, depth), depth)
                group = at // GROUP_ITEMS
                left[group, 0:width, lanes] = (turned * meta_ref[1, i]).astype(left.dtype)
                left[group, width:, lanes] = (turned * meta_ref[2, i]).astype(left.dtype)

            return carry

        lax.fori_loop(0, share, place, 0)

    tile = min(row_count, made.shape[1])
    decay = decay_ref[:, mine]
    basis_copy.wait()
    basis_f32[...] = basis[...].astype(jnp.float32)

    def one_group(group, carry):
        s = group_sub[group]
        damping = [jnp.exp(decay * -dists[group * GROUP_ITEMS + k]) for k in range(GROUP_ITEMS)]
        for t in range(0, row_count, tile):
            right = jnp.concatenate(
                [
                    (basis_f32[:, t : t + tile] * damping[k][:, t : t + tile]).astype(jnp.bfloat16)
                    for k in range(GROUP_ITEMS)
                ],
                axis=0,
            )
            acc[s, :, t : t + tile] += jnp.dot(
                left[group], right, preferred_element_type=jnp.float32
            )
        return carry

    lax.fori_loop(0, first, one_group, 0)
    copies = []
    for n, t in enumerate(range(0, row_count, tile)):
        for s in range(subs):
            for c in range(2):
                column = (c * subs + s) * width
                made[n, :, column : column + width] = acc[
                    s, c * width : (c + 1) * width, t : t + tile
                ].T
        copies.append(pltpu.make_async_copy(made.at[n], out_ref.at[pl.ds(t, tile), :], out_sem.at[n]))
        copies[-1].start()
    for copy in copies:
        copy.wait()


def short_range(half, live, sub_ids, meta, aux_basis, aux_decay, items, row_count, subs):
    _, width, depth = items[0].shape
    slots = live.shape[0]
    share = slots // len(items)
    groups = slots // GROUP_ITEMS + subs
    tile = min(row_count, 512)
    kernel = functools.partial(short_kernel, share=share, subs=subs, depth=depth, width=width)
    return pl.pallas_call(
        kernel,
        out_shape=pltpu.HBM((row_count, 2 * subs * width), jnp.float32),
        in_specs=[pl.BlockSpec(memory_space=pltpu.SMEM)] * 4
        + [pl.BlockSpec(memory_space=pltpu.HBM)]
        + [pl.BlockSpec(memory_space=pltpu.VMEM)] * (1 + len(items)),
        out_specs=pl.BlockSpec(memory_space=pltpu.HBM),
        scratch_shapes=[
            pltpu.VMEM((depth, row_count), jnp.bfloat16),
            pltpu.VMEM((depth, row_count), jnp.float32),
            pltpu.VMEM((groups, 2 * width, GROUP_ITEMS * depth), jnp.bfloat16),
            pltpu.VMEM((subs, 2 * width, row_count), jnp.float32),
            pltpu.VMEM((row_count // tile, tile, 2 * subs * width), jnp.float32),
            pltpu.SMEM((groups * GROUP_ITEMS,), jnp.float32),
            pltpu.SMEM((groups,), jnp.int32),
            pltpu.SMEM((subs,), jnp.int32),
            pltpu.SemaphoreType.DMA,
            pltpu.SemaphoreType.DMA((row_count // tile,)),
        ],
        compiler_params=pltpu.CompilerParams(vmem_limit_bytes=SHORT_VMEM_BYTES),
        cost_estimate=pl.CostEstimate(
            flops=4 * row_count * slots * depth * width, bytes_accessed=1, transcendentals=0
        ),
        name="short_range",
    )(half, live, sub_ids, meta, in_hbm(aux_basis), aux_decay.reshape(1, -1), *items)


def long_kernel(*refs, blocks, chains, pieces):
    parts = refs[: blocks * chains]
    factors = refs[blocks * chains : (blocks + pieces) * chains]
    outs, scratch = refs[(blocks + pieces) * chains :][:pieces], refs[-pieces - 2 :]
    right, made, out_sem = scratch[0], scratch[1:-1], scratch[-1]
    depth, width = factors[0].shape
    half = depth // 2
    count = parts[0].shape[0]
    copies = []
    for piece in reversed(range(pieces)):
        for chain in range(chains):
            factor = factors[piece * chains + chain]
            top = chain * depth
            right[top : top + depth, 0:width] = factor[...]
            right[top : top + half, width:] = factor[half:, :]
            right[top + half : top + depth, width:] = -factor[0:half, :]
        for block in range(blocks):
            left = jnp.concatenate(
                [parts[block * chains + chain][...] for chain in range(chains)], axis=1
            )
            total = jnp.dot(left, right[...], preferred_element_type=jnp.float32)
            made[piece][block] = total.astype(outs[piece].dtype)
            target = outs[piece].at[pl.ds(block * count, count), :]
            copies.append(
                pltpu.make_async_copy(made[piece].at[block], target, out_sem.at[piece, block])
            )
            copies[-1].start()
    for copy in copies:
        copy.wait()


def long_range(blocks, factors):
    depth, width = factors[0][0].shape
    chains = len(factors[0])
    pieces = len(factors)
    count = blocks[0][0].shape[0]
    shape = (len(blocks) * count, 2 * width)
    dtypes = [jnp.bfloat16] * pieces
    flat = [v for group in [*blocks, *factors] for v in group]
    return pl.pallas_call(
        functools.partial(long_kernel, blocks=len(blocks), chains=chains, pieces=pieces),
        out_shape=[pltpu.HBM(shape, dtype) for dtype in dtypes],
        in_specs=[pl.BlockSpec(memory_space=pltpu.VMEM)] * len(flat),
        out_specs=[pl.BlockSpec(memory_space=pltpu.HBM)] * pieces,
        scratch_shapes=[pltpu.VMEM((chains * depth, 2 * width), jnp.bfloat16)]
        + [pltpu.VMEM((len(blocks), count, 2 * width), dtype) for dtype in dtypes]
        + [pltpu.SemaphoreType.DMA((pieces, len(blocks)))],
        compiler_params=pltpu.CompilerParams(vmem_limit_bytes=VMEM_BYTES),
        cost_estimate=SMALL_COST,
        name="long_range",
    )(*flat)


def own_kernel(order_ref, *refs, blocks, chains, aliased):
    parts = refs[: blocks * chains]
    factors = refs[blocks * chains : (blocks + 1) * chains]
    short_ref = refs[(blocks + 1) * chains]
    out_ref, right, terms, made, term_sem, out_sem = refs[(blocks + 1) * chains + 1 + aliased :]
    rows = terms.shape[1]
    depth, width = factors[0].shape
    half = depth // 2
    windows = [pl.ds(pl.multiple_of(order_ref[n] * rows, rows), rows) for n in range(blocks)]
    arriving = []
    for n, window in enumerate(windows):
        arriving.append(
            pltpu.make_async_copy(short_ref.at[window, :], terms.at[n], term_sem.at[n])
        )
        arriving[-1].start()
    for chain, factor in enumerate(factors):
        top = chain * depth
        right[top : top + depth, 0:width] = factor[...]
        right[top : top + half, width:] = factor[half:, :]
        right[top + half : top + depth, width:] = -factor[0:half, :]
    leaving = []
    for n, window in enumerate(windows):
        left = jnp.concatenate([parts[n * chains + chain][...] for chain in range(chains)], axis=1)
        total = jnp.dot(left, right[...], preferred_element_type=jnp.float32)
        arriving[n].wait()
        made[n] = (total + terms[n]).astype(made.dtype).reshape(made.shape[1:])
        leaving.append(pltpu.make_async_copy(made.at[n], out_ref.at[window], out_sem.at[n]))
        leaving[-1].start()
    for copy in leaving:
        copy.wait()


def own_sum(order, blocks, factors, short, earlier):
    rows, depth = blocks[0][0].shape
    width = factors[0].shape[1]
    row_count, columns = short.shape
    chains = len(factors)
    count = len(blocks)
    aliased = earlier is not None
    flat = [v for group in [*blocks, factors] for v in group]
    return pl.pallas_call(
        functools.partial(own_kernel, blocks=count, chains=chains, aliased=aliased),
        out_shape=pltpu.HBM((row_count, 2, width), jnp.bfloat16),
        in_specs=[pl.BlockSpec(memory_space=pltpu.SMEM)]
        + [pl.BlockSpec(memory_space=pltpu.VMEM)] * len(flat)
        + [pl.BlockSpec(memory_space=pltpu.HBM)] * (1 + aliased),
        out_specs=pl.BlockSpec(memory_space=pltpu.HBM),
        scratch_shapes=[
            pltpu.VMEM((chains * depth, 2 * width), jnp.bfloat16),
            pltpu.VMEM((count, rows, columns), jnp.float32),
            pltpu.VMEM((count, rows, 2, width), jnp.bfloat16),
            pltpu.SemaphoreType.DMA((count,)),
            pltpu.SemaphoreType.DMA((count,)),
        ],
        input_output_aliases={len(flat) + 2: 0} if aliased else {},
        compiler_params=pltpu.CompilerParams(vmem_limit_bytes=VMEM_BYTES),
        cost_estimate=SMALL_COST,
        name="own_sum",
    )(order, *flat, in_hbm(short), *([earlier] if aliased else []))


def final_kernel(order_ref, *refs, pieces, blocks, aliased):
    short_ref = refs[pieces]
    out_ref, terms, made, term_sem, out_sem = refs[pieces + 1 + aliased :]
    steps, rows = terms.shape[:2]
    windows = [pl.ds(pl.multiple_of(order_ref[n] * rows, rows), rows) for n in range(steps)]
    arriving = []
    for n, window in enumerate(windows):
        arriving.append(
            pltpu.make_async_copy(short_ref.at[window, :], terms.at[n], term_sem.at[n])
        )
        arriving[-1].start()
    leaving = []
    for n, window in enumerate(windows):
        arriving[n].wait()
        top = n % blocks * rows
        total = refs[n // blocks][top : top + rows, :].astype(jnp.float32) + terms[n]
        made[n] = total.astype(made.dtype).reshape(made.shape[1:])
        leaving.append(pltpu.make_async_copy(made.at[n], out_ref.at[window], out_sem.at[n]))
        leaving[-1].start()
    for copy in leaving:
        copy.wait()


def final_sum(order, pieces, short, earlier, rows):
    columns = pieces[0].shape[1]
    row_count = short.shape[0]
    count = len(pieces)
    blocks = pieces[0].shape[0] // rows
    steps = count * blocks
    return pl.pallas_call(
        functools.partial(final_kernel, pieces=count, blocks=blocks, aliased=True),
        out_shape=pltpu.HBM((row_count, 2, columns // 2), jnp.bfloat16),
        in_specs=[pl.BlockSpec(memory_space=pltpu.SMEM)]
        + [pl.BlockSpec(memory_space=pltpu.VMEM)] * count
        + [pl.BlockSpec(memory_space=pltpu.HBM)] * 2,
        out_specs=pl.BlockSpec(memory_space=pltpu.HBM),
        scratch_shapes=[
            pltpu.VMEM((steps, rows, columns), jnp.float32),
            pltpu.VMEM((steps, rows, 2, columns // 2), jnp.bfloat16),
            pltpu.SemaphoreType.DMA((steps,)),
            pltpu.SemaphoreType.DMA((steps,)),
        ],
        input_output_aliases={count + 2: 0},
        compiler_params=pltpu.CompilerParams(vmem_limit_bytes=VMEM_BYTES),
        cost_estimate=SMALL_COST,
        name="final_sum",
    )(order, *pieces, in_hbm(short), earlier)


def slot_table(image_dist, image_phase, images):
    chosen = images[None, :] == jnp.arange(image_dist.shape[0], dtype=jnp.int32)[:, None]
    distance = jnp.sum(jnp.where(chosen, image_dist[:, None], 0.0), axis=0)
    phase = jnp.sum(jnp.where(chosen, image_phase[:, None], 0.0), axis=0)
    return jnp.stack([distance, jnp.cos(phase), jnp.sin(phase)])


def slot_block(slots, items):
    digits = jnp.concatenate([slots // 128, slots % 128], axis=0).astype(items.dtype)
    fill = [(0, full - used) for full, used in zip(items.shape[1:], digits.shape)]
    return jnp.pad(digits, fill)[None]


def read_slots(packed, slots):
    count, share = slots.shape
    digits = packed[-1, 0 : 2 * count, 0:share].astype(jnp.int32)
    return digits[0:count] * 128 + digits[count:]


def after(value, *earlier):
    return lax.optimization_barrier((value, *earlier))[0] if earlier else value


def body(
    pair_ft,
    aux_ft,
    coul_weight,
    aux_basis,
    aux_decay,
    image_dist,
    image_phase,
    item_pair,
    item_image,
    item_sub,
    item_count,
):
    group_count = lax.axis_size("grp")
    member_count = lax.axis_size("dev")
    group = lax.axis_index("grp")
    member = lax.axis_index("dev")
    local_rows, _, local_g = pair_ft.shape
    subs = local_rows // item_pair.shape[2]
    rows = aux_ft.shape[0]
    row_count = rows * member_count // group_count
    half = jnp.reshape(group, (1,)).astype(jnp.int32)

    chips = member_count // CORES
    breadth = max(n for n in range(1, chips + 1) if chips % n == 0 and n * n <= chips)
    length = chips // breadth

    aux_flat = aux_ft.reshape(rows, 2 * local_g)
    pairs = after(pair_ft, aux_flat).astype(jnp.float32)
    weighted = (pairs * coul_weight[None, None, :]).astype(jnp.bfloat16)
    turned = weighted.reshape(local_rows, 2 * local_g).T
    item_rows = jnp.swapaxes(item_pair, 1, 2)
    live = (jnp.arange(item_image.shape[0], dtype=jnp.int32) < item_count[0]).astype(jnp.int32)
    slots = jnp.stack([item_image, item_sub, live])

    if group_count != 2 or length % 2:
        everything = lax.all_gather(aux_flat, "dev", axis=0, tiled=True)
        mine = lax.all_to_all(everything, "grp", split_axis=0, concat_axis=1, tiled=True)
        factor = lax.all_gather(turned, "grp", axis=0, tiled=True)
        parts = factor.reshape(group_count, 2, local_g, local_rows)
        other = jnp.stack([parts[:, 1], -parts[:, 0]], axis=1).reshape(factor.shape)
        long_part = jnp.concatenate(
            [
                jnp.dot(mine, factor, preferred_element_type=jnp.float32),
                jnp.dot(mine, other, preferred_element_type=jnp.float32),
            ],
            axis=1,
        )
        items = lax.all_gather(item_rows, "grp", axis=0, tiled=True)
        images, sub_ids, live = lax.all_gather(slots, "grp", axis=1, tiled=True)
        table = slot_table(image_dist, image_phase, images)
        short = short_range(
            half, live, sub_ids, table, aux_basis, aux_decay, [items], row_count, subs
        )
        return (long_part + short).astype(jnp.bfloat16).reshape(row_count, 2, local_rows)

    home = length // 2
    place = member // (breadth * CORES)
    across = member // CORES % breadth
    core = member % CORES

    def send(value, route):
        def index(g, z, y, c):
            return g * member_count + (z * breadth + y) * CORES + c

        pairs = []
        for g in range(group_count):
            for z in range(length):
                for y in range(breadth):
                    for c in range(CORES):
                        pairs.append((index(g, z, y, c), index(*route(g, z, y, c))))
        return lax.ppermute(value, AXES, pairs)

    def to_plane(value):
        return send(value, lambda g, z, y, c: (1 - g, z, y, c))

    ring = [*range(0, length, 2), *reversed(range(1, length, 2))]
    turn = {z: n for n, z in enumerate(ring)}

    def along(value, step):
        return send(value, lambda g, z, y, c: (g, ring[(turn[z] + step) % length], y, c))

    def over_y(value, s):
        return send(value, lambda g, z, y, c: (g, z, (y + s) % breadth, c))

    def over_core(value, t):
        return send(value, lambda g, z, y, c: (g, z, y, (c + t) % CORES))

    def hops_of(g, z):
        hops = [(turn[z] - turn[j]) % length for j in range(g * home, (g + 1) * home)]
        return sorted(hops, key=lambda k: (min(k, length - k), k))

    def here(number):
        return sum(
            jnp.where((group == g) & (place == z), number(g, z), 0)
            for g in range(group_count)
            for z in range(length)
        )

    def pick(other, n, *earlier):
        wanted = here(lambda g, z: hops_of(g ^ other, z)[n])
        possible = sorted({hops_of(g, z)[n] for g in range(group_count) for z in range(length)})
        blocks = lax.optimization_barrier((*(held[k] for k in possible), *earlier))
        value = blocks[len(possible) - 1]
        for k, block in reversed(list(zip(possible[:-1], blocks))):
            value = jnp.where(wanted == k, block, value)
        return value

    def numbers_of(n, s):
        slab = here(lambda g, z: ring[(turn[z] - hops_of(g, z)[n]) % length] - g * home)
        return [
            (slab * breadth + (across - s) % breadth) * CORES + (core - t) % CORES
            for t in range(CORES)
        ]

    def with_cores(value):
        return [value] + [over_core(value, t) for t in range(1, CORES)]

    held = {0: aux_flat, 1: along(aux_flat, 1), length - 1: along(aux_flat, -1)}
    packed = jnp.concatenate([item_rows, slot_block(slots, item_rows)], axis=0)
    turned_x = to_plane(turned)
    factors = [[turned, turned_x]] + [[over_y(turned, s)] for s in range(1, breadth)]
    items_x = to_plane(packed)
    mine = {}
    theirs = []
    crossed = []
    away = []
    arriving = []

    def blocks_of(i, *earlier):
        return list(zip(mine[i], [after(crossed[i][0], *earlier), *crossed[i][1:]]))

    def multiply(i):
        earlier = arriving[i - 1] if i else []
        away.append(long_range(blocks_of(i, *earlier), factors[1:]) if breadth > 1 else [])
        arriving.append([over_y(v, s) for s, v in enumerate(away[i], 1)])

    def shorts(*earlier):
        slots_x = read_slots(after(items_x, *earlier), slots)
        seen, sub_ids, live = jnp.concatenate([slots, slots_x], axis=1)
        table = slot_table(image_dist, image_phase, seen)
        all_items = [packed, items_x]
        return short_range(
            half, live, sub_ids, table, aux_basis, aux_decay, all_items, row_count, subs
        )

    def foreign(n, *earlier):
        theirs.append(pick(True, n, *earlier))
        return to_plane(theirs[n])

    moved = foreign(0)
    begun = [turned_x, items_x, *(pair[0] for pair in factors[1:])]
    for k in range(2, length // 2 + 1):
        held[k] = along(after(held[k - 1], held[1], held[length - 1]), 1)
    for k in range(2, (length + 1) // 2):
        held[length - k] = along(after(held[length - k + 1], held[1], held[length - 1]), -1)
    for s in range(1, breadth):
        factors[s].append(over_y(after(turned_x, theirs[0], *begun), s))
    short = shorts(theirs[0], *begun)

    for n in range(home):
        if n:
            moved = foreign(n, theirs[n - 1], *(away[n - 2] if n > 1 else [short]))
        mine[n] = with_cores(pick(False, n, theirs[n], *begun))
        if n:
            multiply(n - 1)
        crossed.append(with_cores(after(moved, *away[n - 1] if n else [short])))
    last = home - 1
    multiply(last)

    def order_of(n, places):
        return jnp.stack([v for s in places for v in numbers_of(n, s)]).astype(jnp.int32)

    out = None
    for n in range(home):
        blocks = blocks_of(n, *away[last])
        out = own_sum(order_of(n, [0]), blocks, factors[0], short, out)
    for n in range(home):
        if breadth > 1:
            out = final_sum(order_of(n, range(1, breadth)), arriving[n], short, out, rows)
    return out


def solution(mesh):
    return jax.shard_map(
        body,
        mesh=mesh,
        in_specs=(
            P("dev", None, "grp"),
            P("dev", None, "grp"),
            P("grp"),
            P(),
            P(),
            P(),
            P(),
            P(("grp", "dev"), None, None),
            P(("grp", "dev")),
            P(("grp", "dev")),
            P(("grp", "dev")),
        ),
        out_specs=P("grp", None, "dev"),
        check_vma=False,
    )
```

```python
import functools

import jax
import jax.numpy as jnp
from jax import lax
from jax.experimental import pallas as pl
from jax.experimental.pallas import tpu as pltpu
from jax.sharding import PartitionSpec as P

AXES = ("grp", "dev")
CORES = 2
SMALL_COST = pl.CostEstimate(flops=1, bytes_accessed=1, transcendentals=0)
GROUP_ITEMS = 4
SHORT_VMEM_BYTES = 20 * 1024 * 1024
VMEM_BYTES = 10 * 1024 * 1024


def in_hbm(value):
    return pltpu.with_memory_space_constraint(value, pltpu.HBM)


def short_kernel(
    half_ref, live_ref, sub_ref, meta_ref, basis_ref, decay_ref, *refs, share, subs, depth, width
):
    items, scratch = refs[:-10], refs[-10:]
    out_ref, basis, left, acc, made, dists, group_sub, cursor, basis_sem, out_sem = scratch
    slots = share * len(items)
    row_count = out_ref.shape[0]
    mine = pl.ds(pl.multiple_of(half_ref[0] * row_count, row_count), row_count)
    basis_copy = pltpu.make_async_copy(basis_ref.at[:, mine], basis, basis_sem)
    basis_copy.start()
    left[...] = jnp.zeros_like(left)
    acc[...] = jnp.zeros_like(acc)

    for s in range(subs):
        cursor[s] = 0

    def count(i, carry):
        cursor[sub_ref[i]] = cursor[sub_ref[i]] + live_ref[i]
        return carry

    lax.fori_loop(0, slots, count, 0)
    first = jnp.int32(0)
    for s in range(subs):
        groups = (cursor[s] + GROUP_ITEMS - 1) // GROUP_ITEMS

        def mark(i, carry, s=s):
            group_sub[i] = s
            return carry

        lax.fori_loop(first, first + groups, mark, 0)
        cursor[s] = first * GROUP_ITEMS
        first = first + groups

    def clear(i, carry):
        dists[i] = 0.0
        return carry

    lax.fori_loop(0, first * GROUP_ITEMS, clear, 0)

    for n, items_ref in enumerate(items):

        def place(k, carry, first=n * share, items_ref=items_ref):
            i = first + k

            @pl.when(live_ref[i] > 0)
            def _():
                s = sub_ref[i]
                at = cursor[s]
                cursor[s] = at + 1
                dists[at] = meta_ref[0, i]
                turned = items_ref[k].astype(jnp.float32)
                lanes = pl.ds(pl.multiple_of((at % GROUP_ITEMS) * depth, depth), depth)
                group = at // GROUP_ITEMS
                left[group, 0:width, lanes] = (turned * meta_ref[1, i]).astype(left.dtype)
                left[group, width:, lanes] = (turned * meta_ref[2, i]).astype(left.dtype)

            return carry

        lax.fori_loop(0, share, place, 0)

    tile = min(row_count, made.shape[1])
    decay = decay_ref[:, mine]
    basis_copy.wait()

    def one_group(group, carry):
        s = group_sub[group]
        damping = [
            jnp.exp(decay * -dists[group * GROUP_ITEMS + k]).astype(basis.dtype)
            for k in range(GROUP_ITEMS)
        ]
        for t in range(0, row_count, tile):
            right = jnp.concatenate(
                [
                    basis[:, t : t + tile] * damping[k][:, t : t + tile]
                    for k in range(GROUP_ITEMS)
                ],
                axis=0,
            )
            acc[s, :, t : t + tile] += jnp.dot(
                left[group], right, preferred_element_type=jnp.float32
            )
        return carry

    lax.fori_loop(0, first, one_group, 0)
    copies = []
    for n, t in enumerate(range(0, row_count, tile)):
        for s in range(subs):
            for c in range(2):
                column = (c * subs + s) * width
                made[n, :, column : column + width] = acc[
                    s, c * width : (c + 1) * width, t : t + tile
                ].T
        copies.append(pltpu.make_async_copy(made.at[n], out_ref.at[pl.ds(t, tile), :], out_sem.at[n]))
        copies[-1].start()
    for copy in copies:
        copy.wait()


def short_range(half, live, sub_ids, meta, aux_basis, aux_decay, items, row_count, subs):
    _, width, depth = items[0].shape
    slots = live.shape[0]
    share = slots // len(items)
    groups = slots // GROUP_ITEMS + subs
    tile = min(row_count, 512)
    kernel = functools.partial(short_kernel, share=share, subs=subs, depth=depth, width=width)
    return pl.pallas_call(
        kernel,
        out_shape=pltpu.HBM((row_count, 2 * subs * width), jnp.float32),
        in_specs=[pl.BlockSpec(memory_space=pltpu.SMEM)] * 4
        + [pl.BlockSpec(memory_space=pltpu.HBM)]
        + [pl.BlockSpec(memory_space=pltpu.VMEM)] * (1 + len(items)),
        out_specs=pl.BlockSpec(memory_space=pltpu.HBM),
        scratch_shapes=[
            pltpu.VMEM((depth, row_count), jnp.bfloat16),
            pltpu.VMEM((groups, 2 * width, GROUP_ITEMS * depth), jnp.bfloat16),
            pltpu.VMEM((subs, 2 * width, row_count), jnp.float32),
            pltpu.VMEM((row_count // tile, tile, 2 * subs * width), jnp.float32),
            pltpu.SMEM((groups * GROUP_ITEMS,), jnp.float32),
            pltpu.SMEM((groups,), jnp.int32),
            pltpu.SMEM((subs,), jnp.int32),
            pltpu.SemaphoreType.DMA,
            pltpu.SemaphoreType.DMA((row_count // tile,)),
        ],
        compiler_params=pltpu.CompilerParams(vmem_limit_bytes=SHORT_VMEM_BYTES),
        cost_estimate=pl.CostEstimate(
            flops=4 * row_count * slots * depth * width, bytes_accessed=1, transcendentals=0
        ),
        name="short_range",
    )(half, live, sub_ids, meta, in_hbm(aux_basis), aux_decay.reshape(1, -1), *items)


def long_kernel(*refs, blocks, chains, pieces, window):
    parts = refs[: blocks * chains]
    factors = refs[blocks * chains : (blocks + pieces) * chains]
    outs, scratch = refs[(blocks + pieces) * chains :][:pieces], refs[-pieces - 2 :]
    right, made, out_sem = scratch[0], scratch[1:-1], scratch[-1]
    depth, width = factors[0].shape
    half = depth // 2
    count = window[-1]
    copies = []
    for piece in reversed(range(pieces)):
        for chain in range(chains):
            factor = factors[piece * chains + chain]
            top = chain * depth
            right[top : top + depth, 0:width] = factor[...]
            right[top : top + half, width:] = factor[half:, :]
            right[top + half : top + depth, width:] = -factor[0:half, :]
        for block in range(blocks):
            left = jnp.concatenate(
                [
                    parts[block * chains + chain][pl.ds(window[chain], count), :]
                    for chain in range(chains)
                ],
                axis=1,
            )
            total = jnp.dot(left, right[...], preferred_element_type=jnp.float32)
            made[piece][block] = total.astype(outs[piece].dtype)
            target = outs[piece].at[pl.ds(block * count, count), :]
            copies.append(
                pltpu.make_async_copy(made[piece].at[block], target, out_sem.at[piece, block])
            )
            copies[-1].start()
    for copy in copies:
        copy.wait()


def long_range(blocks, factors, window):
    depth, width = factors[0][0].shape
    chains = len(factors[0])
    pieces = len(factors)
    count = window[-1]
    shape = (len(blocks) * count, 2 * width)
    dtypes = [jnp.bfloat16 if piece else jnp.float32 for piece in range(pieces)]
    flat = [v for group in [*blocks, *factors] for v in group]
    return pl.pallas_call(
        functools.partial(
            long_kernel, blocks=len(blocks), chains=chains, pieces=pieces, window=window
        ),
        out_shape=[pltpu.HBM(shape, dtype) for dtype in dtypes],
        in_specs=[pl.BlockSpec(memory_space=pltpu.VMEM)] * len(flat),
        out_specs=[pl.BlockSpec(memory_space=pltpu.HBM)] * pieces,
        scratch_shapes=[pltpu.VMEM((chains * depth, 2 * width), jnp.bfloat16)]
        + [pltpu.VMEM((len(blocks), count, 2 * width), dtype) for dtype in dtypes]
        + [pltpu.SemaphoreType.DMA((pieces, len(blocks)))],
        compiler_params=pltpu.CompilerParams(vmem_limit_bytes=VMEM_BYTES),
        cost_estimate=SMALL_COST,
        name="long_range",
    )(*flat)


def final_kernel(order_ref, *refs, pieces, blocks, rows, aliased, stay):
    short_ref = refs[pieces]
    out_ref, *scratch = refs[pieces + 1 + aliased :]
    parts, (terms, made, part_sem, term_sem, out_sem) = scratch[:-5], scratch[-5:]
    parts = [parts.pop(0) if held else ref for held, ref in zip(stay, refs)]
    steps = pieces * blocks
    windows = [pl.ds(pl.multiple_of(order_ref[n] * rows, rows), rows) for n in range(2 * steps)]
    windows, sources = windows[:steps], windows[steps:]
    arriving = []
    for n, source in enumerate(sources):
        arriving.append(
            pltpu.make_async_copy(short_ref.at[source, :], terms.at[n], term_sem.at[n])
        )
        arriving[-1].start()
        piece = n // blocks
        if n % blocks == 0 and stay[piece]:
            part = pltpu.make_async_copy(refs[piece], parts[piece], part_sem.at[piece])
            part.start()
            arriving[-1] = (part, arriving[-1])
        else:
            arriving[-1] = (arriving[-1],)
    leaving = []
    for n, window in enumerate(windows):
        for copy in arriving[n]:
            copy.wait()
        top = n % blocks * rows
        total = parts[n // blocks][top : top + rows, :].astype(jnp.float32) + terms[n]
        made[n] = total.astype(made.dtype).reshape(made.shape[1:])
        leaving.append(pltpu.make_async_copy(made.at[n], out_ref.at[window], out_sem.at[n]))
        leaving[-1].start()
    for copy in leaving:
        copy.wait()


def final_sum(order, pieces, short, earlier, rows, row_count):
    columns = pieces[0].shape[1]
    count = len(pieces)
    blocks = pieces[0].shape[0] // rows
    steps = count * blocks
    aliased = earlier is not None
    stay = [piece.dtype == jnp.float32 for piece in pieces]
    return pl.pallas_call(
        functools.partial(
            final_kernel, pieces=count, blocks=blocks, rows=rows, aliased=aliased, stay=stay
        ),
        out_shape=pltpu.HBM((row_count, 2, columns // 2), jnp.bfloat16),
        in_specs=[pl.BlockSpec(memory_space=pltpu.SMEM)]
        + [pl.BlockSpec(memory_space=pltpu.HBM if held else pltpu.VMEM) for held in stay]
        + [pl.BlockSpec(memory_space=pltpu.HBM)] * (1 + aliased),
        out_specs=pl.BlockSpec(memory_space=pltpu.HBM),
        scratch_shapes=[pltpu.VMEM(piece.shape, piece.dtype) for piece, held in zip(pieces, stay) if held]
        + [
            pltpu.VMEM((steps, rows, columns), jnp.float32),
            pltpu.VMEM((steps, rows, 2, columns // 2), jnp.bfloat16),
            pltpu.SemaphoreType.DMA((count,)),
            pltpu.SemaphoreType.DMA((steps,)),
            pltpu.SemaphoreType.DMA((steps,)),
        ],
        input_output_aliases={count + 2: 0} if aliased else {},
        compiler_params=pltpu.CompilerParams(vmem_limit_bytes=VMEM_BYTES),
        cost_estimate=SMALL_COST,
        name="final_sum",
    )(
        order,
        *(in_hbm(piece) if held else piece for piece, held in zip(pieces, stay)),
        in_hbm(short),
        *([earlier] if aliased else []),
    )


def slot_table(image_dist, image_phase, images):
    chosen = images[None, :] == jnp.arange(image_dist.shape[0], dtype=jnp.int32)[:, None]
    distance = jnp.sum(jnp.where(chosen, image_dist[:, None], 0.0), axis=0)
    phase = jnp.sum(jnp.where(chosen, image_phase[:, None], 0.0), axis=0)
    return jnp.stack([distance, jnp.cos(phase), jnp.sin(phase)])


def slot_block(slots, items):
    digits = jnp.concatenate([slots // 128, slots % 128], axis=0).astype(items.dtype)
    fill = [(0, full - used) for full, used in zip(items.shape[1:], digits.shape)]
    return jnp.pad(digits, fill)[None]


def read_slots(packed, slots):
    count, share = slots.shape
    digits = packed[-1, 0 : 2 * count, 0:share].astype(jnp.int32)
    return digits[0:count] * 128 + digits[count:]


def after(value, *earlier):
    return lax.optimization_barrier((value, *earlier))[0] if earlier else value


def body(
    pair_ft,
    aux_ft,
    coul_weight,
    aux_basis,
    aux_decay,
    image_dist,
    image_phase,
    item_pair,
    item_image,
    item_sub,
    item_count,
):
    group_count = lax.axis_size("grp")
    member_count = lax.axis_size("dev")
    group = lax.axis_index("grp")
    member = lax.axis_index("dev")
    local_rows, _, local_g = pair_ft.shape
    subs = local_rows // item_pair.shape[2]
    rows = aux_ft.shape[0]
    row_count = rows * member_count // group_count
    half = jnp.reshape(group, (1,)).astype(jnp.int32)

    chips = member_count // CORES
    breadth = max(n for n in range(1, chips + 1) if chips % n == 0 and n * n <= chips)
    length = chips // breadth

    aux_flat = aux_ft.reshape(rows, 2 * local_g)
    pairs = after(pair_ft, aux_flat).astype(jnp.float32)
    weighted = (pairs * coul_weight[None, None, :]).astype(jnp.bfloat16)
    turned = weighted.reshape(local_rows, 2 * local_g).T
    item_rows = jnp.swapaxes(item_pair, 1, 2)
    live = (jnp.arange(item_image.shape[0], dtype=jnp.int32) < item_count[0]).astype(jnp.int32)
    slots = jnp.stack([item_image, item_sub, live])

    if group_count != 2 or length % 2:
        everything = lax.all_gather(aux_flat, "dev", axis=0, tiled=True)
        mine = lax.all_to_all(everything, "grp", split_axis=0, concat_axis=1, tiled=True)
        factor = lax.all_gather(turned, "grp", axis=0, tiled=True)
        parts = factor.reshape(group_count, 2, local_g, local_rows)
        other = jnp.stack([parts[:, 1], -parts[:, 0]], axis=1).reshape(factor.shape)
        long_part = jnp.concatenate(
            [
                jnp.dot(mine, factor, preferred_element_type=jnp.float32),
                jnp.dot(mine, other, preferred_element_type=jnp.float32),
            ],
            axis=1,
        )
        items = lax.all_gather(item_rows, "grp", axis=0, tiled=True)
        images, sub_ids, live = lax.all_gather(slots, "grp", axis=1, tiled=True)
        table = slot_table(image_dist, image_phase, images)
        short = short_range(
            half, live, sub_ids, table, aux_basis, aux_decay, [items], row_count, subs
        )
        return (long_part + short).astype(jnp.bfloat16).reshape(row_count, 2, local_rows)

    home = length // 2
    place = member // (breadth * CORES)
    across = member // CORES % breadth
    core = member % CORES

    def send(value, route):
        def index(g, z, y, c):
            return g * member_count + (z * breadth + y) * CORES + c

        pairs = []
        for g in range(group_count):
            for z in range(length):
                for y in range(breadth):
                    for c in range(CORES):
                        pairs.append((index(g, z, y, c), index(*route(g, z, y, c))))
        return lax.ppermute(value, AXES, pairs)

    def to_plane(value):
        return send(value, lambda g, z, y, c: (1 - g, z, y, c))

    ring = [*range(0, length, 2), *reversed(range(1, length, 2))]
    turn = {z: n for n, z in enumerate(ring)}

    def along(value, step):
        return send(value, lambda g, z, y, c: (g, ring[(turn[z] + step) % length], y, c))

    def over_y(value, s):
        return send(value, lambda g, z, y, c: (g, z, (y + s) % breadth, c))

    def over_core(value, t):
        return send(value, lambda g, z, y, c: (g, z, y, (c + t) % CORES))

    def hops_of(g, z):
        hops = [(turn[z] - turn[j]) % length for j in range(g * home, (g + 1) * home)]
        return sorted(hops, key=lambda k: (min(k, length - k), k))

    def here(number):
        return sum(
            jnp.where((group == g) & (place == z), number(g, z), 0)
            for g in range(group_count)
            for z in range(length)
        )

    def pick(other, n, window, *earlier):
        wanted = here(lambda g, z: hops_of(g ^ other, z)[n])
        possible = sorted({hops_of(g, z)[n] for g in range(group_count) for z in range(length)})
        blocks = lax.optimization_barrier((*(held[k] for k in possible), *earlier))
        value = blocks[len(possible) - 1][window]
        for k, block in reversed(list(zip(possible[:-1], blocks))):
            value = jnp.where(wanted == k, block[window], value)
        return value

    slab_rows = rows * breadth * CORES

    def slab_of(n):
        return here(lambda g, z: ring[(turn[z] - hops_of(g, z)[n]) % length] - g * home)

    def numbers_of(s):
        return [(across - s) % breadth * CORES + (core - t) % CORES for t in range(CORES)]

    def with_cores(value):
        return [value] + [over_core(value, t) for t in range(1, CORES)]

    held = {0: aux_flat, 1: along(aux_flat, 1), length - 1: along(aux_flat, -1)}
    packed = jnp.concatenate([item_rows, slot_block(slots, item_rows)], axis=0)
    turned_x = to_plane(turned)
    factors = [[turned, turned_x]] + [[over_y(turned, s)] for s in range(1, breadth)]
    items_x = to_plane(packed)
    units = [(n, 0, rows) for n in range(home)]
    mine = {}
    theirs = []
    crossed = []
    away = []
    arriving = []
    own = []

    def multiply(i, *earlier):
        n, first, count = units[i]
        blocks = list(zip(mine[n], [after(crossed[i][0], *earlier), *crossed[i][1:]]))
        made = long_range(blocks, factors, (first, 0, count))
        own.append(made[0])
        away.append(made[1:])
        arriving.append([over_y(v, s) for s, v in enumerate(made[1:], 1)])

    def foreign(i, *earlier):
        n, first, count = units[i]
        theirs.append(pick(True, n, slice(first, first + count), *earlier))
        return to_plane(theirs[i])

    moved = foreign(0)
    begun = [turned_x, items_x, *(pair[0] for pair in factors[1:])]
    for k in range(2, length // 2 + 1):
        held[k] = along(after(held[k - 1], held[1], held[length - 1]), 1)
    for k in range(2, (length + 1) // 2):
        held[length - k] = along(after(held[length - k + 1], held[1], held[length - 1]), -1)
    for s in range(1, breadth):
        factors[s].append(over_y(after(turned_x, theirs[0], *begun), s))

    def short_of(n, *earlier):
        slots_x = read_slots(after(items_x, *earlier), slots)
        seen, sub_ids, live = jnp.concatenate([slots, slots_x], axis=1)
        table = slot_table(image_dist, image_phase, seen)
        which = jnp.reshape(group * home + slab_of(n), (1,)).astype(jnp.int32)
        all_items = [packed, items_x]
        return short_range(
            which, live, sub_ids, table, aux_basis, aux_decay, all_items, slab_rows, subs
        )

    shorts = [short_of(0, theirs[0], *begun)]
    for i, (n, _, _) in enumerate(units):
        if i:
            moved = foreign(i, theirs[i - 1], *(away[i - 2] if i > 1 else shorts))
        if i:
            multiply(i - 1)
        earlier = away[i - 1] if i else begun
        mine[n] = with_cores(pick(False, n, slice(None), theirs[i], *earlier))
        crossed.append(with_cores(after(moved, *[mine[n][0], *away[i - 1]] if i else shorts)))
        if i:
            shorts.append(short_of(i, *away[i - 1]))
    last = len(units) - 1

    multiply(last)
    out = None
    for n in range(home):
        entries = [(own[n], 0)] + [(v, s) for s, v in enumerate(arriving[n], 1)]
        for chosen in [entries] if n < last else [entries[:1], entries[1:]]:
            if chosen:
                inside = jnp.stack([v for _, s in chosen for v in numbers_of(s)])
                order = jnp.concatenate([inside + slab_of(n) * breadth * CORES, inside])
                pieces = [piece for piece, _ in chosen]
                order = order.astype(jnp.int32)
                out = final_sum(order, pieces, shorts[n], out, rows, row_count)
    return out


def solution(mesh):
    return jax.shard_map(
        body,
        mesh=mesh,
        in_specs=(
            P("dev", None, "grp"),
            P("dev", None, "grp"),
            P("grp"),
            P(),
            P(),
            P(),
            P(),
            P(("grp", "dev"), None, None),
            P(("grp", "dev")),
            P(("grp", "dev")),
            P(("grp", "dev")),
        ),
        out_specs=P("grp", None, "dev"),
        check_vma=False,
    )
```

```python
import functools

import jax
import jax.numpy as jnp
from jax import lax
from jax.experimental import pallas as pl
from jax.experimental.pallas import tpu as pltpu
from jax.sharding import PartitionSpec as P

AXES = ("grp", "dev")
CORES = 2
SMALL_COST = pl.CostEstimate(flops=1, bytes_accessed=1, transcendentals=0)
GROUP_ITEMS = 4
SHORT_VMEM_BYTES = 20 * 1024 * 1024
VMEM_BYTES = 10 * 1024 * 1024


def in_hbm(value):
    return pltpu.with_memory_space_constraint(value, pltpu.HBM)


def short_kernel(
    half_ref, live_ref, sub_ref, meta_ref, basis_ref, decay_ref, *refs, share, subs, depth, width
):
    items, scratch = refs[:-10], refs[-10:]
    out_ref, basis, left, acc, made, dists, group_sub, cursor, basis_sem, out_sem = scratch
    slots = share * len(items)
    row_count = out_ref.shape[0]
    mine = pl.ds(pl.multiple_of(half_ref[0] * row_count, row_count), row_count)
    basis_copy = pltpu.make_async_copy(basis_ref.at[:, mine], basis, basis_sem)
    basis_copy.start()
    left[...] = jnp.zeros_like(left)
    acc[...] = jnp.zeros_like(acc)

    for s in range(subs):
        cursor[s] = 0

    def count(i, carry):
        cursor[sub_ref[i]] = cursor[sub_ref[i]] + live_ref[i]
        return carry

    lax.fori_loop(0, slots, count, 0)
    first = jnp.int32(0)
    for s in range(subs):
        groups = (cursor[s] + GROUP_ITEMS - 1) // GROUP_ITEMS

        def mark(i, carry, s=s):
            group_sub[i] = s
            return carry

        lax.fori_loop(first, first + groups, mark, 0)
        cursor[s] = first * GROUP_ITEMS
        first = first + groups

    def clear(i, carry):
        dists[i] = 0.0
        return carry

    lax.fori_loop(0, first * GROUP_ITEMS, clear, 0)

    for n, items_ref in enumerate(items):

        def place(k, carry, first=n * share, items_ref=items_ref):
            i = first + k

            @pl.when(live_ref[i] > 0)
            def _():
                s = sub_ref[i]
                at = cursor[s]
                cursor[s] = at + 1
                dists[at] = meta_ref[0, i]
                turned = items_ref[k].astype(jnp.float32)
                lanes = pl.ds(pl.multiple_of((at % GROUP_ITEMS) * depth, depth), depth)
                group = at // GROUP_ITEMS
                left[group, 0:width, lanes] = (turned * meta_ref[1, i]).astype(left.dtype)
                left[group, width:, lanes] = (turned * meta_ref[2, i]).astype(left.dtype)

            return carry

        lax.fori_loop(0, share, place, 0)

    tile = min(row_count, made.shape[1])
    decay = decay_ref[:, mine]
    basis_copy.wait()

    def one_group(group, carry):
        s = group_sub[group]
        damping = [
            jnp.exp(decay * -dists[group * GROUP_ITEMS + k]).astype(basis.dtype)
            for k in range(GROUP_ITEMS)
        ]
        for t in range(0, row_count, tile):
            right = jnp.concatenate(
                [
                    basis[:, t : t + tile] * damping[k][:, t : t + tile]
                    for k in range(GROUP_ITEMS)
                ],
                axis=0,
            )
            acc[s, :, t : t + tile] += jnp.dot(
                left[group], right, preferred_element_type=jnp.float32
            )
        return carry

    lax.fori_loop(0, first, one_group, 0)
    copies = []
    for n, t in enumerate(range(0, row_count, tile)):
        for s in range(subs):
            for c in range(2):
                column = (c * subs + s) * width
                made[n, :, column : column + width] = acc[
                    s, c * width : (c + 1) * width, t : t + tile
                ].T
        copies.append(pltpu.make_async_copy(made.at[n], out_ref.at[pl.ds(t, tile), :], out_sem.at[n]))
        copies[-1].start()
    for copy in copies:
        copy.wait()


def short_range(half, live, sub_ids, meta, aux_basis, aux_decay, items, row_count, subs):
    _, width, depth = items[0].shape
    slots = live.shape[0]
    share = slots // len(items)
    groups = slots // GROUP_ITEMS + subs
    tile = min(row_count, 512)
    kernel = functools.partial(short_kernel, share=share, subs=subs, depth=depth, width=width)
    return pl.pallas_call(
        kernel,
        out_shape=pltpu.HBM((row_count, 2 * subs * width), jnp.float32),
        in_specs=[pl.BlockSpec(memory_space=pltpu.SMEM)] * 4
        + [pl.BlockSpec(memory_space=pltpu.HBM)]
        + [pl.BlockSpec(memory_space=pltpu.VMEM)] * (1 + len(items)),
        out_specs=pl.BlockSpec(memory_space=pltpu.HBM),
        scratch_shapes=[
            pltpu.VMEM((depth, row_count), jnp.bfloat16),
            pltpu.VMEM((groups, 2 * width, GROUP_ITEMS * depth), jnp.bfloat16),
            pltpu.VMEM((subs, 2 * width, row_count), jnp.float32),
            pltpu.VMEM((row_count // tile, tile, 2 * subs * width), jnp.float32),
            pltpu.SMEM((groups * GROUP_ITEMS,), jnp.float32),
            pltpu.SMEM((groups,), jnp.int32),
            pltpu.SMEM((subs,), jnp.int32),
            pltpu.SemaphoreType.DMA,
            pltpu.SemaphoreType.DMA((row_count // tile,)),
        ],
        compiler_params=pltpu.CompilerParams(vmem_limit_bytes=SHORT_VMEM_BYTES),
        cost_estimate=pl.CostEstimate(
            flops=4 * row_count * slots * depth * width, bytes_accessed=1, transcendentals=0
        ),
        name="short_range",
    )(half, live, sub_ids, meta, in_hbm(aux_basis), aux_decay.reshape(1, -1), *items)


def long_kernel(*refs, blocks, chains, pieces, width):
    parts = refs[: blocks * chains]
    factors = refs[blocks * chains : (blocks + pieces) * chains]
    outs, scratch = refs[(blocks + pieces) * chains :][:pieces], refs[-pieces - 2 :]
    right, made, out_sem = scratch[0], scratch[1:-1], scratch[-1]
    depth = factors[0].shape[0]
    half = depth // 2
    count = parts[0].shape[0]
    copies = []
    for piece in reversed(range(pieces)):
        for chain in range(chains):
            factor = factors[piece * chains + chain]
            top = chain * depth
            if factor.shape[1] > width:
                right[top : top + depth, :] = factor[...]
                continue
            right[top : top + depth, 0:width] = factor[...]
            right[top : top + half, width:] = factor[half:, :]
            right[top + half : top + depth, width:] = -factor[0:half, :]
        for block in range(blocks):
            left = jnp.concatenate(
                [parts[block * chains + chain][...] for chain in range(chains)], axis=1
            )
            total = jnp.dot(left, right[...], preferred_element_type=jnp.float32)
            made[piece][block] = total.astype(outs[piece].dtype)
            target = outs[piece].at[pl.ds(block * count, count), :]
            copies.append(
                pltpu.make_async_copy(made[piece].at[block], target, out_sem.at[piece, block])
            )
            copies[-1].start()
    for copy in copies:
        copy.wait()


def long_range(blocks, factors, width):
    depth = factors[0][0].shape[0]
    chains = len(factors[0])
    pieces = len(factors)
    count = blocks[0][0].shape[0]
    shape = (len(blocks) * count, 2 * width)
    dtypes = [jnp.bfloat16] * pieces
    flat = [v for group in [*blocks, *factors] for v in group]
    return pl.pallas_call(
        functools.partial(
            long_kernel, blocks=len(blocks), chains=chains, pieces=pieces, width=width
        ),
        out_shape=[pltpu.HBM(shape, dtype) for dtype in dtypes],
        in_specs=[pl.BlockSpec(memory_space=pltpu.VMEM)] * len(flat),
        out_specs=[pl.BlockSpec(memory_space=pltpu.HBM)] * pieces,
        scratch_shapes=[pltpu.VMEM((chains * depth, 2 * width), jnp.bfloat16)]
        + [pltpu.VMEM((len(blocks), count, 2 * width), dtype) for dtype in dtypes]
        + [pltpu.SemaphoreType.DMA((pieces, len(blocks)))],
        compiler_params=pltpu.CompilerParams(vmem_limit_bytes=VMEM_BYTES),
        cost_estimate=SMALL_COST,
        name="long_range",
    )(*flat)


def own_kernel(order_ref, *refs, blocks, chains, aliased):
    parts = refs[: blocks * chains]
    factors = refs[blocks * chains : (blocks + 1) * chains]
    short_ref = refs[(blocks + 1) * chains]
    out_ref, right, terms, made, term_sem, out_sem = refs[(blocks + 1) * chains + 1 + aliased :]
    rows = terms.shape[1]
    depth, width = factors[0].shape
    half = depth // 2
    windows = [pl.ds(pl.multiple_of(order_ref[n] * rows, rows), rows) for n in range(blocks)]
    arriving = []
    for n, window in enumerate(windows):
        arriving.append(
            pltpu.make_async_copy(short_ref.at[window, :], terms.at[n], term_sem.at[n])
        )
        arriving[-1].start()
    for chain, factor in enumerate(factors):
        top = chain * depth
        right[top : top + depth, 0:width] = factor[...]
        right[top : top + half, width:] = factor[half:, :]
        right[top + half : top + depth, width:] = -factor[0:half, :]
    leaving = []
    for n, window in enumerate(windows):
        left = jnp.concatenate([parts[n * chains + chain][...] for chain in range(chains)], axis=1)
        total = jnp.dot(left, right[...], preferred_element_type=jnp.float32)
        arriving[n].wait()
        made[n] = (total + terms[n]).astype(made.dtype).reshape(made.shape[1:])
        leaving.append(pltpu.make_async_copy(made.at[n], out_ref.at[window], out_sem.at[n]))
        leaving[-1].start()
    for copy in leaving:
        copy.wait()


def own_sum(order, blocks, factors, short, earlier):
    rows, depth = blocks[0][0].shape
    width = factors[0].shape[1]
    row_count, columns = short.shape
    chains = len(factors)
    count = len(blocks)
    aliased = earlier is not None
    flat = [v for group in [*blocks, factors] for v in group]
    return pl.pallas_call(
        functools.partial(own_kernel, blocks=count, chains=chains, aliased=aliased),
        out_shape=pltpu.HBM((row_count, 2, width), jnp.bfloat16),
        in_specs=[pl.BlockSpec(memory_space=pltpu.SMEM)]
        + [pl.BlockSpec(memory_space=pltpu.VMEM)] * len(flat)
        + [pl.BlockSpec(memory_space=pltpu.HBM)] * (1 + aliased),
        out_specs=pl.BlockSpec(memory_space=pltpu.HBM),
        scratch_shapes=[
            pltpu.VMEM((chains * depth, 2 * width), jnp.bfloat16),
            pltpu.VMEM((count, rows, columns), jnp.float32),
            pltpu.VMEM((count, rows, 2, width), jnp.bfloat16),
            pltpu.SemaphoreType.DMA((count,)),
            pltpu.SemaphoreType.DMA((count,)),
        ],
        input_output_aliases={len(flat) + 2: 0} if aliased else {},
        compiler_params=pltpu.CompilerParams(vmem_limit_bytes=VMEM_BYTES),
        cost_estimate=SMALL_COST,
        name="own_sum",
    )(order, *flat, in_hbm(short), *([earlier] if aliased else []))


def final_kernel(order_ref, *refs, pieces, blocks, aliased):
    short_ref = refs[pieces]
    out_ref, terms, made, term_sem, out_sem = refs[pieces + 1 + aliased :]
    steps, rows = terms.shape[:2]
    windows = [pl.ds(pl.multiple_of(order_ref[n] * rows, rows), rows) for n in range(steps)]
    arriving = []
    for n, window in enumerate(windows):
        arriving.append(
            pltpu.make_async_copy(short_ref.at[window, :], terms.at[n], term_sem.at[n])
        )
        arriving[-1].start()
    leaving = []
    for n, window in enumerate(windows):
        arriving[n].wait()
        top = n % blocks * rows
        total = refs[n // blocks][top : top + rows, :].astype(jnp.float32) + terms[n]
        made[n] = total.astype(made.dtype).reshape(made.shape[1:])
        leaving.append(pltpu.make_async_copy(made.at[n], out_ref.at[window], out_sem.at[n]))
        leaving[-1].start()
    for copy in leaving:
        copy.wait()


def final_sum(order, pieces, short, earlier, rows):
    columns = pieces[0].shape[1]
    row_count = short.shape[0]
    count = len(pieces)
    blocks = pieces[0].shape[0] // rows
    steps = count * blocks
    return pl.pallas_call(
        functools.partial(final_kernel, pieces=count, blocks=blocks, aliased=True),
        out_shape=pltpu.HBM((row_count, 2, columns // 2), jnp.bfloat16),
        in_specs=[pl.BlockSpec(memory_space=pltpu.SMEM)]
        + [pl.BlockSpec(memory_space=pltpu.VMEM)] * count
        + [pl.BlockSpec(memory_space=pltpu.HBM)] * 2,
        out_specs=pl.BlockSpec(memory_space=pltpu.HBM),
        scratch_shapes=[
            pltpu.VMEM((steps, rows, columns), jnp.float32),
            pltpu.VMEM((steps, rows, 2, columns // 2), jnp.bfloat16),
            pltpu.SemaphoreType.DMA((steps,)),
            pltpu.SemaphoreType.DMA((steps,)),
        ],
        input_output_aliases={count + 2: 0},
        compiler_params=pltpu.CompilerParams(vmem_limit_bytes=VMEM_BYTES),
        cost_estimate=SMALL_COST,
        name="final_sum",
    )(order, *pieces, in_hbm(short), earlier)


def slot_table(image_dist, image_phase, images):
    chosen = images[None, :] == jnp.arange(image_dist.shape[0], dtype=jnp.int32)[:, None]
    distance = jnp.sum(jnp.where(chosen, image_dist[:, None], 0.0), axis=0)
    phase = jnp.sum(jnp.where(chosen, image_phase[:, None], 0.0), axis=0)
    return jnp.stack([distance, jnp.cos(phase), jnp.sin(phase)])


def both_parts(factor):
    half = factor.shape[0] // 2
    return jnp.concatenate(
        [factor, jnp.concatenate([factor[half:], -factor[:half]], axis=0)], axis=1
    )


def slot_block(slots, items):
    digits = jnp.concatenate([slots // 128, slots % 128], axis=0).astype(items.dtype)
    fill = [(0, full - used) for full, used in zip(items.shape[1:], digits.shape)]
    return jnp.pad(digits, fill)[None]


def read_slots(packed, slots):
    count, share = slots.shape
    digits = packed[-1, 0 : 2 * count, 0:share].astype(jnp.int32)
    return digits[0:count] * 128 + digits[count:]


def after(value, *earlier):
    return lax.optimization_barrier((value, *earlier))[0] if earlier else value


def body(
    pair_ft,
    aux_ft,
    coul_weight,
    aux_basis,
    aux_decay,
    image_dist,
    image_phase,
    item_pair,
    item_image,
    item_sub,
    item_count,
):
    group_count = lax.axis_size("grp")
    member_count = lax.axis_size("dev")
    group = lax.axis_index("grp")
    member = lax.axis_index("dev")
    local_rows, _, local_g = pair_ft.shape
    subs = local_rows // item_pair.shape[2]
    rows = aux_ft.shape[0]
    row_count = rows * member_count // group_count
    half = jnp.reshape(group, (1,)).astype(jnp.int32)

    chips = member_count // CORES
    breadth = max(n for n in range(1, chips + 1) if chips % n == 0 and n * n <= chips)
    length = chips // breadth

    aux_flat = aux_ft.reshape(rows, 2 * local_g)
    pairs = after(pair_ft, aux_flat).astype(jnp.float32)
    weighted = (pairs * coul_weight[None, None, :]).astype(jnp.bfloat16)
    turned = weighted.reshape(local_rows, 2 * local_g).T
    item_rows = jnp.swapaxes(item_pair, 1, 2)
    live = (jnp.arange(item_image.shape[0], dtype=jnp.int32) < item_count[0]).astype(jnp.int32)
    slots = jnp.stack([item_image, item_sub, live])

    if group_count != 2 or length % 2:
        everything = lax.all_gather(aux_flat, "dev", axis=0, tiled=True)
        mine = lax.all_to_all(everything, "grp", split_axis=0, concat_axis=1, tiled=True)
        factor = lax.all_gather(turned, "grp", axis=0, tiled=True)
        parts = factor.reshape(group_count, 2, local_g, local_rows)
        other = jnp.stack([parts[:, 1], -parts[:, 0]], axis=1).reshape(factor.shape)
        long_part = jnp.concatenate(
            [
                jnp.dot(mine, factor, preferred_element_type=jnp.float32),
                jnp.dot(mine, other, preferred_element_type=jnp.float32),
            ],
            axis=1,
        )
        items = lax.all_gather(item_rows, "grp", axis=0, tiled=True)
        images, sub_ids, live = lax.all_gather(slots, "grp", axis=1, tiled=True)
        table = slot_table(image_dist, image_phase, images)
        short = short_range(
            half, live, sub_ids, table, aux_basis, aux_decay, [items], row_count, subs
        )
        return (long_part + short).astype(jnp.bfloat16).reshape(row_count, 2, local_rows)

    home = length // 2
    place = member // (breadth * CORES)
    across = member // CORES % breadth
    core = member % CORES

    def send(value, route):
        def index(g, z, y, c):
            return g * member_count + (z * breadth + y) * CORES + c

        pairs = []
        for g in range(group_count):
            for z in range(length):
                for y in range(breadth):
                    for c in range(CORES):
                        pairs.append((index(g, z, y, c), index(*route(g, z, y, c))))
        return lax.ppermute(value, AXES, pairs)

    def to_plane(value):
        return send(value, lambda g, z, y, c: (1 - g, z, y, c))

    ring = [*range(0, length, 2), *reversed(range(1, length, 2))]
    turn = {z: n for n, z in enumerate(ring)}

    def along(value, step):
        return send(value, lambda g, z, y, c: (g, ring[(turn[z] + step) % length], y, c))

    def over_y(value, s):
        return send(value, lambda g, z, y, c: (g, z, (y + s) % breadth, c))

    def over_core(value, t):
        return send(value, lambda g, z, y, c: (g, z, y, (c + t) % CORES))

    def hops_of(g, z):
        hops = [(turn[z] - turn[j]) % length for j in range(g * home, (g + 1) * home)]
        return sorted(hops, key=lambda k: (min(k, length - k), k))

    def here(number):
        return sum(
            jnp.where((group == g) & (place == z), number(g, z), 0)
            for g in range(group_count)
            for z in range(length)
        )

    def pick(other, n, *earlier):
        wanted = here(lambda g, z: hops_of(g ^ other, z)[n])
        possible = sorted({hops_of(g, z)[n] for g in range(group_count) for z in range(length)})
        blocks = lax.optimization_barrier((*(held[k] for k in possible), *earlier))
        value = blocks[len(possible) - 1]
        for k, block in reversed(list(zip(possible[:-1], blocks))):
            value = jnp.where(wanted == k, block, value)
        return value

    def slab_of(n):
        return here(lambda g, z: ring[(turn[z] - hops_of(g, z)[n]) % length] - g * home)

    def number_of(n, s, t):
        return (slab_of(n) * breadth + (across - s) % breadth) * CORES + (core - t) % CORES

    def with_cores(value):
        return [value] + [over_core(value, t) for t in range(1, CORES)]

    held = {0: aux_flat, 1: along(aux_flat, 1), length - 1: along(aux_flat, -1)}
    packed = jnp.concatenate([item_rows, slot_block(slots, item_rows)], axis=0)
    turned_x = to_plane(turned)
    factors = [[turned, turned_x]] + [[over_y(turned, s)] for s in range(1, breadth)]
    items_x = to_plane(packed)
    mine = []
    theirs = []
    crossed = []
    away = []
    arriving = []

    def foreign(n, *earlier):
        theirs.append(pick(True, n, *earlier))
        return to_plane(theirs[n])

    def multiply(n, t, away_factors):
        made = []
        if breadth > 1:
            made = long_range([(mine[n][t], crossed[n][t])], away_factors, local_rows)
        away[n].extend(made)
        arriving[n].append([over_y(v, s) for s, v in enumerate(made, 1)])

    moved = foreign(0)
    begun = [turned_x, items_x, *(pair[0] for pair in factors[1:])]
    for k in range(2, length // 2 + 1):
        held[k] = along(after(held[k - 1], held[1], held[length - 1]), 1)
    for k in range(2, (length + 1) // 2):
        held[length - k] = along(after(held[length - k + 1], held[1], held[length - 1]), -1)
    for s in range(1, breadth):
        factors[s].append(over_y(after(turned_x, theirs[0], *begun), s))
    slots_x = read_slots(after(items_x, theirs[0], *begun), slots)
    seen, sub_ids, live = jnp.concatenate([slots, slots_x], axis=1)
    table = slot_table(image_dist, image_phase, seen)
    short = short_range(
        half, live, sub_ids, table, aux_basis, aux_decay, [packed, items_x], row_count, subs
    )

    out = None
    for n in range(home):
        if n:
            moved = foreign(n, theirs[n - 1], *(away[n - 2] if n > 1 else [short]))
        away.append([])
        arriving.append([])
        mine.append(with_cores(pick(False, n, theirs[n], *(away[n - 1] if n else begun))))
        away_factors = factors[1:]
        if n:
            away_factors = [[both_parts(after(v, *away[0])) for v in pair] for pair in factors[1:]]
        crossed.append(with_cores(moved if n else after(moved, short)))
        for t in range(CORES):
            multiply(n, t, away_factors)
        blocks = [
            (after(mine[n][0], *away[n]), crossed[n][0]),
            *zip(mine[n][1:], crossed[n][1:]),
        ]
        order = jnp.stack([number_of(n, 0, t) for t in range(CORES)]).astype(jnp.int32)
        out = own_sum(order, blocks, factors[0], short, out)
    calls = []
    for n in range(home):
        calls += [
            [(v, number_of(n, s, t)) for s, v in enumerate(arriving[n][t], 1)] for t in range(CORES)
        ]
        if n < home - 1:
            calls[-CORES:] = [sum(calls[-CORES:], [])]
    for entries in calls:
        if entries:
            order = jnp.stack([number for _, number in entries]).astype(jnp.int32)
            out = final_sum(order, [piece for piece, _ in entries], short, out, rows)
    return out


def solution(mesh):
    return jax.shard_map(
        body,
        mesh=mesh,
        in_specs=(
            P("dev", None, "grp"),
            P("dev", None, "grp"),
            P("grp"),
            P(),
            P(),
            P(),
            P(),
            P(("grp", "dev"), None, None),
            P(("grp", "dev")),
            P(("grp", "dev")),
            P(("grp", "dev")),
        ),
        out_specs=P("grp", None, "dev"),
        check_vma=False,
    )
```

```python
import functools

import jax
import jax.numpy as jnp
from jax import lax
from jax.experimental import pallas as pl
from jax.experimental.pallas import tpu as pltpu
from jax.sharding import PartitionSpec as P

AXES = ("grp", "dev")
CORES = 2
SMALL_COST = pl.CostEstimate(flops=1, bytes_accessed=1, transcendentals=0)
GROUP_ITEMS = 4
SHORT_VMEM_BYTES = 24 * 1024 * 1024
VMEM_BYTES = 10 * 1024 * 1024


def in_hbm(value):
    return pltpu.with_memory_space_constraint(value, pltpu.HBM)


def short_kernel(
    half_ref, live_ref, sub_ref, meta_ref, basis_ref, decay_ref, *refs, share, subs, depth, width, adds
):
    if adds:
        *refs, before, before_sem = refs
    items, scratch = refs[: -10 - adds], refs[-10:]
    out_ref, basis, left, acc, made, dists, group_sub, cursor, basis_sem, out_sem = scratch
    slots = share * len(items)
    row_count = out_ref.shape[0]
    tile = made.shape[1]
    tiles = list(enumerate(range(0, row_count, tile)))
    before_copies = []
    for n, t in tiles if adds else []:
        source = refs[-11].at[pl.ds(t, tile), :]
        before_copies.append(pltpu.make_async_copy(source, before.at[n], before_sem.at[n]))
        before_copies[-1].start()
    mine = pl.ds(pl.multiple_of(half_ref[0] * row_count, row_count), row_count)
    basis_copy = pltpu.make_async_copy(basis_ref.at[:, mine], basis, basis_sem)
    basis_copy.start()
    left[...] = jnp.zeros_like(left)
    acc[...] = jnp.zeros_like(acc)

    for s in range(subs):
        cursor[s] = 0

    def count(i, carry):
        cursor[sub_ref[i]] = cursor[sub_ref[i]] + live_ref[i]
        return carry

    lax.fori_loop(0, slots, count, 0)
    first = jnp.int32(0)
    for s in range(subs):
        groups = (cursor[s] + GROUP_ITEMS - 1) // GROUP_ITEMS

        def mark(i, carry, s=s):
            group_sub[i] = s
            return carry

        lax.fori_loop(first, first + groups, mark, 0)
        cursor[s] = first * GROUP_ITEMS
        first = first + groups

    def clear(i, carry):
        dists[i] = 0.0
        return carry

    lax.fori_loop(0, first * GROUP_ITEMS, clear, 0)

    for n, items_ref in enumerate(items):

        def place(k, carry, first=n * share, items_ref=items_ref):
            i = first + k

            @pl.when(live_ref[i] > 0)
            def _():
                s = sub_ref[i]
                at = cursor[s]
                cursor[s] = at + 1
                dists[at] = meta_ref[0, i]
                turned = items_ref[k].astype(jnp.float32)
                lanes = pl.ds(pl.multiple_of((at % GROUP_ITEMS) * depth, depth), depth)
                group = at // GROUP_ITEMS
                left[group, 0:width, lanes] = (turned * meta_ref[1, i]).astype(left.dtype)
                left[group, width:, lanes] = (turned * meta_ref[2, i]).astype(left.dtype)

            return carry

        lax.fori_loop(0, share, place, 0)

    decay = decay_ref[:, mine]
    basis_copy.wait()

    def one_group(group, carry):
        s = group_sub[group]
        damping = [
            jnp.exp(decay * -dists[group * GROUP_ITEMS + k]).astype(basis.dtype)
            for k in range(GROUP_ITEMS)
        ]
        for t in range(0, row_count, tile):
            right = jnp.concatenate(
                [
                    basis[:, t : t + tile] * damping[k][:, t : t + tile]
                    for k in range(GROUP_ITEMS)
                ],
                axis=0,
            )
            acc[s, :, t : t + tile] += jnp.dot(
                left[group], right, preferred_element_type=jnp.float32
            )
        return carry

    lax.fori_loop(0, first, one_group, 0)
    copies = []
    for n, t in tiles:
        if adds:
            before_copies[n].wait()
        for s in range(subs):
            for c in range(2):
                column = (c * subs + s) * width
                part = acc[s, c * width : (c + 1) * width, t : t + tile].T
                if adds:
                    part = part + before[n, :, column : column + width]
                made[n, :, column : column + width] = part
        copies.append(pltpu.make_async_copy(made.at[n], out_ref.at[pl.ds(t, tile), :], out_sem.at[n]))
        copies[-1].start()
    for copy in copies:
        copy.wait()


def short_range(half, live, sub_ids, meta, aux_basis, aux_decay, items, row_count, subs, earlier=None):
    adds = earlier is not None
    _, width, depth = items[0].shape
    slots = live.shape[0]
    share = slots // len(items)
    groups = slots // GROUP_ITEMS + subs
    tile = min(row_count, 512)
    kernel = functools.partial(
        short_kernel, share=share, subs=subs, depth=depth, width=width, adds=adds
    )
    return pl.pallas_call(
        kernel,
        out_shape=pltpu.HBM((row_count, 2 * subs * width), jnp.float32),
        in_specs=[pl.BlockSpec(memory_space=pltpu.SMEM)] * 4
        + [pl.BlockSpec(memory_space=pltpu.HBM)]
        + [pl.BlockSpec(memory_space=pltpu.VMEM)] * (1 + len(items))
        + [pl.BlockSpec(memory_space=pltpu.HBM)] * adds,
        out_specs=pl.BlockSpec(memory_space=pltpu.HBM),
        scratch_shapes=[
            pltpu.VMEM((depth, row_count), jnp.bfloat16),
            pltpu.VMEM((groups, 2 * width, GROUP_ITEMS * depth), jnp.bfloat16),
            pltpu.VMEM((subs, 2 * width, row_count), jnp.float32),
            pltpu.VMEM((row_count // tile, tile, 2 * subs * width), jnp.float32),
            pltpu.SMEM((groups * GROUP_ITEMS,), jnp.float32),
            pltpu.SMEM((groups,), jnp.int32),
            pltpu.SMEM((subs,), jnp.int32),
            pltpu.SemaphoreType.DMA,
            pltpu.SemaphoreType.DMA((row_count // tile,)),
        ]
        + [
            pltpu.VMEM((row_count // tile, tile, 2 * subs * width), jnp.float32),
            pltpu.SemaphoreType.DMA((row_count // tile,)),
        ][: 2 * adds],
        compiler_params=pltpu.CompilerParams(vmem_limit_bytes=SHORT_VMEM_BYTES),
        cost_estimate=pl.CostEstimate(
            flops=4 * row_count * slots * depth * width, bytes_accessed=1, transcendentals=0
        ),
        name="short_range",
    )(
        half,
        live,
        sub_ids,
        meta,
        in_hbm(aux_basis),
        aux_decay.reshape(1, -1),
        *items,
        *([in_hbm(earlier)] if adds else []),
    )


def long_kernel(*refs, blocks, chains, pieces, width):
    parts = refs[: blocks * chains]
    factors = refs[blocks * chains : (blocks + pieces) * chains]
    outs, scratch = refs[(blocks + pieces) * chains :][:pieces], refs[-pieces - 2 :]
    right, made, out_sem = scratch[0], scratch[1:-1], scratch[-1]
    depth = factors[0].shape[0]
    half = depth // 2
    count = parts[0].shape[0]
    copies = []
    for piece in reversed(range(pieces)):
        for chain in range(chains):
            factor = factors[piece * chains + chain]
            top = chain * depth
            if factor.shape[1] > width:
                right[top : top + depth, :] = factor[...]
                continue
            right[top : top + depth, 0:width] = factor[...]
            right[top : top + half, width:] = factor[half:, :]
            right[top + half : top + depth, width:] = -factor[0:half, :]
        for block in range(blocks):
            left = jnp.concatenate(
                [parts[block * chains + chain][...] for chain in range(chains)], axis=1
            )
            total = jnp.dot(left, right[...], preferred_element_type=jnp.float32)
            made[piece][block] = total.astype(outs[piece].dtype)
            target = outs[piece].at[pl.ds(block * count, count), :]
            copies.append(
                pltpu.make_async_copy(made[piece].at[block], target, out_sem.at[piece, block])
            )
            copies[-1].start()
    for copy in copies:
        copy.wait()


def long_range(blocks, factors, width):
    depth = factors[0][0].shape[0]
    chains = len(factors[0])
    pieces = len(factors)
    count = blocks[0][0].shape[0]
    shape = (len(blocks) * count, 2 * width)
    dtypes = [jnp.bfloat16] * pieces
    flat = [v for group in [*blocks, *factors] for v in group]
    return pl.pallas_call(
        functools.partial(
            long_kernel, blocks=len(blocks), chains=chains, pieces=pieces, width=width
        ),
        out_shape=[pltpu.HBM(shape, dtype) for dtype in dtypes],
        in_specs=[pl.BlockSpec(memory_space=pltpu.VMEM)] * len(flat),
        out_specs=[pl.BlockSpec(memory_space=pltpu.HBM)] * pieces,
        scratch_shapes=[pltpu.VMEM((chains * depth, 2 * width), jnp.bfloat16)]
        + [pltpu.VMEM((len(blocks), count, 2 * width), dtype) for dtype in dtypes]
        + [pltpu.SemaphoreType.DMA((pieces, len(blocks)))],
        compiler_params=pltpu.CompilerParams(vmem_limit_bytes=VMEM_BYTES),
        cost_estimate=SMALL_COST,
        name="long_range",
    )(*flat)


def own_kernel(order_ref, *refs, blocks, chains, aliased):
    parts = refs[: blocks * chains]
    factors = refs[blocks * chains : (blocks + 1) * chains]
    short_ref = refs[(blocks + 1) * chains]
    out_ref, right, terms, made, term_sem, out_sem = refs[(blocks + 1) * chains + 1 + aliased :]
    rows = terms.shape[1]
    depth, width = factors[0].shape
    half = depth // 2
    windows = [pl.ds(pl.multiple_of(order_ref[n] * rows, rows), rows) for n in range(blocks)]
    arriving = []
    for n, window in enumerate(windows):
        arriving.append(
            pltpu.make_async_copy(short_ref.at[window, :], terms.at[n], term_sem.at[n])
        )
        arriving[-1].start()
    for chain, factor in enumerate(factors):
        top = chain * depth
        right[top : top + depth, 0:width] = factor[...]
        right[top : top + half, width:] = factor[half:, :]
        right[top + half : top + depth, width:] = -factor[0:half, :]
    leaving = []
    for n, window in enumerate(windows):
        left = jnp.concatenate([parts[n * chains + chain][...] for chain in range(chains)], axis=1)
        total = jnp.dot(left, right[...], preferred_element_type=jnp.float32)
        arriving[n].wait()
        made[n] = (total + terms[n]).astype(made.dtype).reshape(made.shape[1:])
        leaving.append(pltpu.make_async_copy(made.at[n], out_ref.at[window], out_sem.at[n]))
        leaving[-1].start()
    for copy in leaving:
        copy.wait()


def own_sum(order, blocks, factors, short, earlier):
    rows, depth = blocks[0][0].shape
    width = factors[0].shape[1]
    row_count, columns = short.shape
    chains = len(factors)
    count = len(blocks)
    aliased = earlier is not None
    flat = [v for group in [*blocks, factors] for v in group]
    return pl.pallas_call(
        functools.partial(own_kernel, blocks=count, chains=chains, aliased=aliased),
        out_shape=pltpu.HBM((row_count, 2, width), jnp.bfloat16),
        in_specs=[pl.BlockSpec(memory_space=pltpu.SMEM)]
        + [pl.BlockSpec(memory_space=pltpu.VMEM)] * len(flat)
        + [pl.BlockSpec(memory_space=pltpu.HBM)] * (1 + aliased),
        out_specs=pl.BlockSpec(memory_space=pltpu.HBM),
        scratch_shapes=[
            pltpu.VMEM((chains * depth, 2 * width), jnp.bfloat16),
            pltpu.VMEM((count, rows, columns), jnp.float32),
            pltpu.VMEM((count, rows, 2, width), jnp.bfloat16),
            pltpu.SemaphoreType.DMA((count,)),
            pltpu.SemaphoreType.DMA((count,)),
        ],
        input_output_aliases={len(flat) + 2: 0} if aliased else {},
        compiler_params=pltpu.CompilerParams(vmem_limit_bytes=VMEM_BYTES),
        cost_estimate=SMALL_COST,
        name="own_sum",
    )(order, *flat, in_hbm(short), *([earlier] if aliased else []))


def final_kernel(order_ref, *refs, pieces, blocks, aliased):
    short_ref = refs[pieces]
    out_ref, terms, made, term_sem, out_sem = refs[pieces + 1 + aliased :]
    steps, rows = terms.shape[:2]
    windows = [pl.ds(pl.multiple_of(order_ref[n] * rows, rows), rows) for n in range(steps)]
    arriving = []
    for n, window in enumerate(windows):
        arriving.append(
            pltpu.make_async_copy(short_ref.at[window, :], terms.at[n], term_sem.at[n])
        )
        arriving[-1].start()
    leaving = []
    for n, window in enumerate(windows):
        arriving[n].wait()
        top = n % blocks * rows
        total = refs[n // blocks][top : top + rows, :].astype(jnp.float32) + terms[n]
        made[n] = total.astype(made.dtype).reshape(made.shape[1:])
        leaving.append(pltpu.make_async_copy(made.at[n], out_ref.at[window], out_sem.at[n]))
        leaving[-1].start()
    for copy in leaving:
        copy.wait()


def final_sum(order, pieces, short, earlier, rows):
    columns = pieces[0].shape[1]
    row_count = short.shape[0]
    count = len(pieces)
    blocks = pieces[0].shape[0] // rows
    steps = count * blocks
    return pl.pallas_call(
        functools.partial(final_kernel, pieces=count, blocks=blocks, aliased=True),
        out_shape=pltpu.HBM((row_count, 2, columns // 2), jnp.bfloat16),
        in_specs=[pl.BlockSpec(memory_space=pltpu.SMEM)]
        + [pl.BlockSpec(memory_space=pltpu.VMEM)] * count
        + [pl.BlockSpec(memory_space=pltpu.HBM)] * 2,
        out_specs=pl.BlockSpec(memory_space=pltpu.HBM),
        scratch_shapes=[
            pltpu.VMEM((steps, rows, columns), jnp.float32),
            pltpu.VMEM((steps, rows, 2, columns // 2), jnp.bfloat16),
            pltpu.SemaphoreType.DMA((steps,)),
            pltpu.SemaphoreType.DMA((steps,)),
        ],
        input_output_aliases={count + 2: 0},
        compiler_params=pltpu.CompilerParams(vmem_limit_bytes=VMEM_BYTES),
        cost_estimate=SMALL_COST,
        name="final_sum",
    )(order, *pieces, in_hbm(short), earlier)


def slot_table(image_dist, image_phase, images):
    chosen = images[None, :] == jnp.arange(image_dist.shape[0], dtype=jnp.int32)[:, None]
    distance = jnp.sum(jnp.where(chosen, image_dist[:, None], 0.0), axis=0)
    phase = jnp.sum(jnp.where(chosen, image_phase[:, None], 0.0), axis=0)
    return jnp.stack([distance, jnp.cos(phase), jnp.sin(phase)])


def both_parts(factor):
    half = factor.shape[0] // 2
    return jnp.concatenate(
        [factor, jnp.concatenate([factor[half:], -factor[:half]], axis=0)], axis=1
    )


def slot_block(slots, items):
    digits = jnp.concatenate([slots // 128, slots % 128], axis=0).astype(items.dtype)
    fill = [(0, full - used) for full, used in zip(items.shape[1:], digits.shape)]
    return jnp.pad(digits, fill)[None]


def read_slots(packed, slots):
    count, share = slots.shape
    digits = packed[-1, 0 : 2 * count, 0:share].astype(jnp.int32)
    return digits[0:count] * 128 + digits[count:]


def after(value, *earlier):
    return lax.optimization_barrier((value, *earlier))[0] if earlier else value


def body(
    pair_ft,
    aux_ft,
    coul_weight,
    aux_basis,
    aux_decay,
    image_dist,
    image_phase,
    item_pair,
    item_image,
    item_sub,
    item_count,
):
    group_count = lax.axis_size("grp")
    member_count = lax.axis_size("dev")
    group = lax.axis_index("grp")
    member = lax.axis_index("dev")
    local_rows, _, local_g = pair_ft.shape
    subs = local_rows // item_pair.shape[2]
    rows = aux_ft.shape[0]
    row_count = rows * member_count // group_count
    half = jnp.reshape(group, (1,)).astype(jnp.int32)

    chips = member_count // CORES
    breadth = max(n for n in range(1, chips + 1) if chips % n == 0 and n * n <= chips)
    length = chips // breadth

    aux_flat = aux_ft.reshape(rows, 2 * local_g)
    pairs = pair_ft.astype(jnp.float32)
    weighted = (pairs * coul_weight[None, None, :]).astype(jnp.bfloat16)
    turned = weighted.reshape(local_rows, 2 * local_g).T
    item_rows = jnp.swapaxes(item_pair, 1, 2)
    live = (jnp.arange(item_image.shape[0], dtype=jnp.int32) < item_count[0]).astype(jnp.int32)
    slots = jnp.stack([item_image, item_sub, live])

    if group_count != 2 or length % 2:
        everything = lax.all_gather(aux_flat, "dev", axis=0, tiled=True)
        mine = lax.all_to_all(everything, "grp", split_axis=0, concat_axis=1, tiled=True)
        factor = lax.all_gather(turned, "grp", axis=0, tiled=True)
        parts = factor.reshape(group_count, 2, local_g, local_rows)
        other = jnp.stack([parts[:, 1], -parts[:, 0]], axis=1).reshape(factor.shape)
        long_part = jnp.concatenate(
            [
                jnp.dot(mine, factor, preferred_element_type=jnp.float32),
                jnp.dot(mine, other, preferred_element_type=jnp.float32),
            ],
            axis=1,
        )
        items = lax.all_gather(item_rows, "grp", axis=0, tiled=True)
        images, sub_ids, live = lax.all_gather(slots, "grp", axis=1, tiled=True)
        table = slot_table(image_dist, image_phase, images)
        short = short_range(
            half, live, sub_ids, table, aux_basis, aux_decay, [items], row_count, subs
        )
        return (long_part + short).astype(jnp.bfloat16).reshape(row_count, 2, local_rows)

    home = length // 2
    place = member // (breadth * CORES)
    across = member // CORES % breadth
    core = member % CORES

    def send(value, route):
        def index(g, z, y, c):
            return g * member_count + (z * breadth + y) * CORES + c

        pairs = []
        for g in range(group_count):
            for z in range(length):
                for y in range(breadth):
                    for c in range(CORES):
                        pairs.append((index(g, z, y, c), index(*route(g, z, y, c))))
        return lax.ppermute(value, AXES, pairs)

    def to_plane(value):
        return send(value, lambda g, z, y, c: (1 - g, z, y, c))

    ring = [*range(0, length, 2), *reversed(range(1, length, 2))]
    turn = {z: n for n, z in enumerate(ring)}

    def along(value, step):
        return send(value, lambda g, z, y, c: (g, ring[(turn[z] + step) % length], y, c))

    def over_y(value, s):
        return send(value, lambda g, z, y, c: (g, z, (y + s) % breadth, c))

    def over_core(value, t):
        return send(value, lambda g, z, y, c: (g, z, y, (c + t) % CORES))

    def hops_of(g, z):
        hops = [(turn[z] - turn[j]) % length for j in range(g * home, (g + 1) * home)]
        return sorted(hops, key=lambda k: (min(k, length - k), k))

    def here(number):
        return sum(
            jnp.where((group == g) & (place == z), number(g, z), 0)
            for g in range(group_count)
            for z in range(length)
        )

    def pick(other, n, *earlier):
        wanted = here(lambda g, z: hops_of(g ^ other, z)[n])
        possible = sorted({hops_of(g, z)[n] for g in range(group_count) for z in range(length)})
        blocks = lax.optimization_barrier((*(held[k] for k in possible), *earlier))
        value = blocks[len(possible) - 1]
        for k, block in reversed(list(zip(possible[:-1], blocks))):
            value = jnp.where(wanted == k, block, value)
        return value

    def slab_of(n):
        return here(lambda g, z: ring[(turn[z] - hops_of(g, z)[n]) % length] - g * home)

    def number_of(n, s, t):
        return (slab_of(n) * breadth + (across - s) % breadth) * CORES + (core - t) % CORES

    def with_cores(value):
        return [value] + [over_core(value, t) for t in range(1, CORES)]

    held = {0: aux_flat, 1: along(aux_flat, 1), length - 1: along(aux_flat, -1)}
    packed = jnp.concatenate([item_rows, slot_block(slots, item_rows)], axis=0)
    turned_x = to_plane(turned)
    factors = [[turned, turned_x]] + [[over_y(turned, s)] for s in range(1, breadth)]
    items_x = to_plane(packed)
    mine = []
    theirs = []
    crossed = []
    away = []
    arriving = []

    def foreign(n, *earlier):
        theirs.append(pick(True, n, *earlier))
        return to_plane(theirs[n])

    def multiply(n, t, away_factors):
        made = []
        if breadth > 1:
            made = long_range([(mine[n][t], crossed[n][t])], away_factors, local_rows)
        away[n].extend(made)
        arriving[n].append([over_y(v, s) for s, v in enumerate(made, 1)])

    def short_part(slots, items, earlier=None):
        images, sub_ids, live = slots
        table = slot_table(image_dist, image_phase, images)
        return short_range(
            half, live, sub_ids, table, aux_basis, aux_decay, [items], row_count, subs, earlier
        )

    short = short_part(slots, after(packed, *(pair[0] for pair in factors[1:])))

    moved = foreign(0, short)
    begun = [turned_x, items_x, *(pair[0] for pair in factors[1:])]
    for k in range(2, length // 2 + 1):
        held[k] = along(after(held[k - 1], held[1], held[length - 1], short), 1)
    for k in range(2, (length + 1) // 2):
        held[length - k] = along(after(held[length - k + 1], held[1], held[length - 1], short), -1)
    for s in range(1, breadth):
        factors[s].append(over_y(after(turned_x, theirs[0], *begun), s))

    short = short_part(read_slots(after(items_x, theirs[0], *begun), slots), items_x, short)

    out = None
    for n in range(home):
        if n:
            moved = foreign(n, theirs[n - 1], *(away[n - 2] if n > 1 else [short]))
        away.append([])
        arriving.append([])
        mine.append(with_cores(pick(False, n, theirs[n], *([*away[n - 1], out] if n else begun))))
        away_factors = factors[1:]
        if n:
            away_factors = [[both_parts(after(v, *away[0])) for v in pair] for pair in factors[1:]]
        crossed.append(with_cores(moved if n else after(moved, short)))
        for t in range(CORES):
            multiply(n, t, away_factors)
        blocks = [
            (after(mine[n][0], *away[n]), crossed[n][0]),
            *zip(mine[n][1:], crossed[n][1:]),
        ]
        order = jnp.stack([number_of(n, 0, t) for t in range(CORES)]).astype(jnp.int32)
        out = own_sum(order, blocks, factors[0], short, out)
    calls = []
    for n in range(home):
        calls += [
            [(v, number_of(n, s, t)) for s, v in enumerate(arriving[n][t], 1)] for t in range(CORES)
        ]
        if n < home - 1:
            calls[-CORES:] = [sum(calls[-CORES:], [])]
    for entries in calls:
        if entries:
            order = jnp.stack([number for _, number in entries]).astype(jnp.int32)
            out = final_sum(order, [piece for piece, _ in entries], short, out, rows)
    return out


def solution(mesh):
    return jax.shard_map(
        body,
        mesh=mesh,
        in_specs=(
            P("dev", None, "grp"),
            P("dev", None, "grp"),
            P("grp"),
            P(),
            P(),
            P(),
            P(),
            P(("grp", "dev"), None, None),
            P(("grp", "dev")),
            P(("grp", "dev")),
            P(("grp", "dev")),
        ),
        out_specs=P("grp", None, "dev"),
        check_vma=False,
    )
```

```python
import functools

import jax
import jax.numpy as jnp
from jax import lax
from jax.experimental import pallas as pl
from jax.experimental.pallas import tpu as pltpu
from jax.sharding import PartitionSpec as P

AXES = ("grp", "dev")
CORES = 2
SMALL_COST = pl.CostEstimate(flops=1, bytes_accessed=1, transcendentals=0)
GROUP_ITEMS = 4
SHORT_VMEM_BYTES = 20 * 1024 * 1024
VMEM_BYTES = 10 * 1024 * 1024


def in_hbm(value):
    return pltpu.with_memory_space_constraint(value, pltpu.HBM)


def short_kernel(
    half_ref, live_ref, sub_ref, meta_ref, basis_ref, decay_ref, *refs, share, subs, depth, width, adds, finishes
):
    items, scratch = refs[: -10 - adds], refs[-10:]
    out_ref, basis, left, acc, made, dists, group_sub, cursor, basis_sem, out_sem = scratch
    slots = share * len(items)
    row_count = acc.shape[2]
    tile = made.shape[1]
    if adds:
        acc_copy = pltpu.make_async_copy(refs[-11], acc, out_sem.at[0])
        acc_copy.start()
    else:
        acc[...] = jnp.zeros_like(acc)
    mine = pl.ds(pl.multiple_of(half_ref[0] * row_count, row_count), row_count)
    basis_copy = pltpu.make_async_copy(basis_ref.at[:, mine], basis, basis_sem)
    basis_copy.start()
    left[...] = jnp.zeros_like(left)

    for s in range(subs):
        cursor[s] = 0

    def count(i, carry):
        cursor[sub_ref[i]] = cursor[sub_ref[i]] + live_ref[i]
        return carry

    lax.fori_loop(0, slots, count, 0)
    first = jnp.int32(0)
    for s in range(subs):
        groups = (cursor[s] + GROUP_ITEMS - 1) // GROUP_ITEMS

        def mark(i, carry, s=s):
            group_sub[i] = s
            return carry

        lax.fori_loop(first, first + groups, mark, 0)
        cursor[s] = first * GROUP_ITEMS
        first = first + groups

    def clear(i, carry):
        dists[i] = 0.0
        return carry

    lax.fori_loop(0, first * GROUP_ITEMS, clear, 0)

    for n, items_ref in enumerate(items):

        def place(k, carry, first=n * share, items_ref=items_ref):
            i = first + k

            @pl.when(live_ref[i] > 0)
            def _():
                s = sub_ref[i]
                at = cursor[s]
                cursor[s] = at + 1
                dists[at] = meta_ref[0, i]
                turned = items_ref[k].astype(jnp.float32)
                lanes = pl.ds(pl.multiple_of((at % GROUP_ITEMS) * depth, depth), depth)
                group = at // GROUP_ITEMS
                left[group, 0:width, lanes] = (turned * meta_ref[1, i]).astype(left.dtype)
                left[group, width:, lanes] = (turned * meta_ref[2, i]).astype(left.dtype)

            return carry

        lax.fori_loop(0, share, place, 0)

    decay = decay_ref[:, mine]
    basis_copy.wait()
    if adds:
        acc_copy.wait()

    def one_group(group, carry):
        s = group_sub[group]
        damping = [
            jnp.exp(decay * -dists[group * GROUP_ITEMS + k]).astype(basis.dtype)
            for k in range(GROUP_ITEMS)
        ]
        for t in range(0, row_count, tile):
            right = jnp.concatenate(
                [
                    basis[:, t : t + tile] * damping[k][:, t : t + tile]
                    for k in range(GROUP_ITEMS)
                ],
                axis=0,
            )
            acc[s, :, t : t + tile] += jnp.dot(
                left[group], right, preferred_element_type=jnp.float32
            )
        return carry

    lax.fori_loop(0, first, one_group, 0)
    if not finishes:
        acc_copy = pltpu.make_async_copy(acc, out_ref, out_sem.at[0])
        acc_copy.start()
        acc_copy.wait()
        return
    copies = []
    for n, t in enumerate(range(0, row_count, tile)):
        for s in range(subs):
            for c in range(2):
                column = (c * subs + s) * width
                made[n, :, column : column + width] = acc[
                    s, c * width : (c + 1) * width, t : t + tile
                ].T
        copies.append(pltpu.make_async_copy(made.at[n], out_ref.at[pl.ds(t, tile), :], out_sem.at[n]))
        copies[-1].start()
    for copy in copies:
        copy.wait()


def short_range(half, live, sub_ids, meta, aux_basis, aux_decay, items, row_count, subs, earlier=None, finishes=True):
    adds = earlier is not None
    _, width, depth = items[0].shape
    slots = live.shape[0]
    share = slots // len(items)
    groups = slots // GROUP_ITEMS + subs
    tile = min(row_count, 512)
    kernel = functools.partial(
        short_kernel, share=share, subs=subs, depth=depth, width=width, adds=adds, finishes=finishes
    )
    return pl.pallas_call(
        kernel,
        out_shape=pltpu.HBM(
            (row_count, 2 * subs * width) if finishes else (subs, 2 * width, row_count), jnp.float32
        ),
        in_specs=[pl.BlockSpec(memory_space=pltpu.SMEM)] * 4
        + [pl.BlockSpec(memory_space=pltpu.HBM)]
        + [pl.BlockSpec(memory_space=pltpu.VMEM)] * (1 + len(items))
        + [pl.BlockSpec(memory_space=pltpu.HBM)] * adds,
        out_specs=pl.BlockSpec(memory_space=pltpu.HBM),
        scratch_shapes=[
            pltpu.VMEM((depth, row_count), jnp.bfloat16),
            pltpu.VMEM((groups, 2 * width, GROUP_ITEMS * depth), jnp.bfloat16),
            pltpu.VMEM((subs, 2 * width, row_count), jnp.float32),
            pltpu.VMEM((row_count // tile, tile, 2 * subs * width), jnp.float32),
            pltpu.SMEM((groups * GROUP_ITEMS,), jnp.float32),
            pltpu.SMEM((groups,), jnp.int32),
            pltpu.SMEM((subs,), jnp.int32),
            pltpu.SemaphoreType.DMA,
            pltpu.SemaphoreType.DMA((row_count // tile,)),
        ],
        compiler_params=pltpu.CompilerParams(vmem_limit_bytes=SHORT_VMEM_BYTES),
        cost_estimate=pl.CostEstimate(
            flops=4 * row_count * slots * depth * width, bytes_accessed=1, transcendentals=0
        ),
        name="short_range",
    )(
        half,
        live,
        sub_ids,
        meta,
        in_hbm(aux_basis),
        aux_decay.reshape(1, -1),
        *items,
        *([in_hbm(earlier)] if adds else []),
    )


def long_kernel(*refs, blocks, chains, pieces, width):
    parts = refs[: blocks * chains]
    factors = refs[blocks * chains : (blocks + pieces) * chains]
    outs, scratch = refs[(blocks + pieces) * chains :][:pieces], refs[-pieces - 2 :]
    right, made, out_sem = scratch[0], scratch[1:-1], scratch[-1]
    depth = factors[0].shape[0]
    half = depth // 2
    count = parts[0].shape[0]
    copies = []
    for piece in reversed(range(pieces)):
        for chain in range(chains):
            factor = factors[piece * chains + chain]
            top = chain * depth
            if factor.shape[1] > width:
                right[top : top + depth, :] = factor[...]
                continue
            right[top : top + depth, 0:width] = factor[...]
            right[top : top + half, width:] = factor[half:, :]
            right[top + half : top + depth, width:] = -factor[0:half, :]
        for block in range(blocks):
            left = jnp.concatenate(
                [parts[block * chains + chain][...] for chain in range(chains)], axis=1
            )
            total = jnp.dot(left, right[...], preferred_element_type=jnp.float32)
            made[piece][block] = total.astype(outs[piece].dtype)
            target = outs[piece].at[pl.ds(block * count, count), :]
            copies.append(
                pltpu.make_async_copy(made[piece].at[block], target, out_sem.at[piece, block])
            )
            copies[-1].start()
    for copy in copies:
        copy.wait()


def long_range(blocks, factors, width):
    depth = factors[0][0].shape[0]
    chains = len(factors[0])
    pieces = len(factors)
    count = blocks[0][0].shape[0]
    shape = (len(blocks) * count, 2 * width)
    dtypes = [jnp.bfloat16] * pieces
    flat = [v for group in [*blocks, *factors] for v in group]
    return pl.pallas_call(
        functools.partial(
            long_kernel, blocks=len(blocks), chains=chains, pieces=pieces, width=width
        ),
        out_shape=[pltpu.HBM(shape, dtype) for dtype in dtypes],
        in_specs=[pl.BlockSpec(memory_space=pltpu.VMEM)] * len(flat),
        out_specs=[pl.BlockSpec(memory_space=pltpu.HBM)] * pieces,
        scratch_shapes=[pltpu.VMEM((chains * depth, 2 * width), jnp.bfloat16)]
        + [pltpu.VMEM((len(blocks), count, 2 * width), dtype) for dtype in dtypes]
        + [pltpu.SemaphoreType.DMA((pieces, len(blocks)))],
        compiler_params=pltpu.CompilerParams(vmem_limit_bytes=VMEM_BYTES),
        cost_estimate=SMALL_COST,
        name="long_range",
    )(*flat)


def own_kernel(order_ref, *refs, blocks, chains, aliased):
    parts = refs[: blocks * chains]
    factors = refs[blocks * chains : (blocks + 1) * chains]
    short_ref = refs[(blocks + 1) * chains]
    out_ref, right, terms, made, term_sem, out_sem = refs[(blocks + 1) * chains + 1 + aliased :]
    rows = terms.shape[1]
    depth, width = factors[0].shape
    half = depth // 2
    windows = [pl.ds(pl.multiple_of(order_ref[n] * rows, rows), rows) for n in range(blocks)]
    arriving = []
    for n, window in enumerate(windows):
        arriving.append(
            pltpu.make_async_copy(short_ref.at[window, :], terms.at[n], term_sem.at[n])
        )
        arriving[-1].start()
    for chain, factor in enumerate(factors):
        top = chain * depth
        right[top : top + depth, 0:width] = factor[...]
        right[top : top + half, width:] = factor[half:, :]
        right[top + half : top + depth, width:] = -factor[0:half, :]
    leaving = []
    for n, window in enumerate(windows):
        left = jnp.concatenate([parts[n * chains + chain][...] for chain in range(chains)], axis=1)
        total = jnp.dot(left, right[...], preferred_element_type=jnp.float32)
        arriving[n].wait()
        made[n] = (total + terms[n]).astype(made.dtype).reshape(made.shape[1:])
        leaving.append(pltpu.make_async_copy(made.at[n], out_ref.at[window], out_sem.at[n]))
        leaving[-1].start()
    for copy in leaving:
        copy.wait()


def own_sum(order, blocks, factors, short, earlier):
    rows, depth = blocks[0][0].shape
    width = factors[0].shape[1]
    row_count, columns = short.shape
    chains = len(factors)
    count = len(blocks)
    aliased = earlier is not None
    flat = [v for group in [*blocks, factors] for v in group]
    return pl.pallas_call(
        functools.partial(own_kernel, blocks=count, chains=chains, aliased=aliased),
        out_shape=pltpu.HBM((row_count, 2, width), jnp.bfloat16),
        in_specs=[pl.BlockSpec(memory_space=pltpu.SMEM)]
        + [pl.BlockSpec(memory_space=pltpu.VMEM)] * len(flat)
        + [pl.BlockSpec(memory_space=pltpu.HBM)] * (1 + aliased),
        out_specs=pl.BlockSpec(memory_space=pltpu.HBM),
        scratch_shapes=[
            pltpu.VMEM((chains * depth, 2 * width), jnp.bfloat16),
            pltpu.VMEM((count, rows, columns), jnp.float32),
            pltpu.VMEM((count, rows, 2, width), jnp.bfloat16),
            pltpu.SemaphoreType.DMA((count,)),
            pltpu.SemaphoreType.DMA((count,)),
        ],
        input_output_aliases={len(flat) + 2: 0} if aliased else {},
        compiler_params=pltpu.CompilerParams(vmem_limit_bytes=VMEM_BYTES),
        cost_estimate=SMALL_COST,
        name="own_sum",
    )(order, *flat, in_hbm(short), *([earlier] if aliased else []))


def final_kernel(order_ref, *refs, pieces, blocks, aliased):
    short_ref = refs[pieces]
    out_ref, terms, made, term_sem, out_sem = refs[pieces + 1 + aliased :]
    steps, rows = terms.shape[:2]
    windows = [pl.ds(pl.multiple_of(order_ref[n] * rows, rows), rows) for n in range(steps)]
    arriving = []
    for n, window in enumerate(windows):
        arriving.append(
            pltpu.make_async_copy(short_ref.at[window, :], terms.at[n], term_sem.at[n])
        )
        arriving[-1].start()
    leaving = []
    for n, window in enumerate(windows):
        arriving[n].wait()
        top = n % blocks * rows
        total = refs[n // blocks][top : top + rows, :].astype(jnp.float32) + terms[n]
        made[n] = total.astype(made.dtype).reshape(made.shape[1:])
        leaving.append(pltpu.make_async_copy(made.at[n], out_ref.at[window], out_sem.at[n]))
        leaving[-1].start()
    for copy in leaving:
        copy.wait()


def final_sum(order, pieces, short, earlier, rows):
    columns = pieces[0].shape[1]
    row_count = short.shape[0]
    count = len(pieces)
    blocks = pieces[0].shape[0] // rows
    steps = count * blocks
    return pl.pallas_call(
        functools.partial(final_kernel, pieces=count, blocks=blocks, aliased=True),
        out_shape=pltpu.HBM((row_count, 2, columns // 2), jnp.bfloat16),
        in_specs=[pl.BlockSpec(memory_space=pltpu.SMEM)]
        + [pl.BlockSpec(memory_space=pltpu.VMEM)] * count
        + [pl.BlockSpec(memory_space=pltpu.HBM)] * 2,
        out_specs=pl.BlockSpec(memory_space=pltpu.HBM),
        scratch_shapes=[
            pltpu.VMEM((steps, rows, columns), jnp.float32),
            pltpu.VMEM((steps, rows, 2, columns // 2), jnp.bfloat16),
            pltpu.SemaphoreType.DMA((steps,)),
            pltpu.SemaphoreType.DMA((steps,)),
        ],
        input_output_aliases={count + 2: 0},
        compiler_params=pltpu.CompilerParams(vmem_limit_bytes=VMEM_BYTES),
        cost_estimate=SMALL_COST,
        name="final_sum",
    )(order, *pieces, in_hbm(short), earlier)


def slot_table(image_dist, image_phase, images):
    chosen = images[None, :] == jnp.arange(image_dist.shape[0], dtype=jnp.int32)[:, None]
    distance = jnp.sum(jnp.where(chosen, image_dist[:, None], 0.0), axis=0)
    phase = jnp.sum(jnp.where(chosen, image_phase[:, None], 0.0), axis=0)
    return jnp.stack([distance, jnp.cos(phase), jnp.sin(phase)])


def both_parts(factor):
    half = factor.shape[0] // 2
    return jnp.concatenate(
        [factor, jnp.concatenate([factor[half:], -factor[:half]], axis=0)], axis=1
    )


def slot_block(slots, items):
    digits = jnp.concatenate([slots // 128, slots % 128], axis=0).astype(items.dtype)
    fill = [(0, full - used) for full, used in zip(items.shape[1:], digits.shape)]
    return jnp.pad(digits, fill)[None]


def read_slots(packed, slots):
    count, share = slots.shape
    digits = packed[-1, 0 : 2 * count, 0:share].astype(jnp.int32)
    return digits[0:count] * 128 + digits[count:]


def after(value, *earlier):
    return lax.optimization_barrier((value, *earlier))[0] if earlier else value


def body(
    pair_ft,
    aux_ft,
    coul_weight,
    aux_basis,
    aux_decay,
    image_dist,
    image_phase,
    item_pair,
    item_image,
    item_sub,
    item_count,
):
    group_count = lax.axis_size("grp")
    member_count = lax.axis_size("dev")
    group = lax.axis_index("grp")
    member = lax.axis_index("dev")
    local_rows, _, local_g = pair_ft.shape
    subs = local_rows // item_pair.shape[2]
    rows = aux_ft.shape[0]
    row_count = rows * member_count // group_count
    half = jnp.reshape(group, (1,)).astype(jnp.int32)

    chips = member_count // CORES
    breadth = max(n for n in range(1, chips + 1) if chips % n == 0 and n * n <= chips)
    length = chips // breadth

    aux_flat = aux_ft.reshape(rows, 2 * local_g)
    pairs = pair_ft.astype(jnp.float32)
    weighted = (pairs * coul_weight[None, None, :]).astype(jnp.bfloat16)
    turned = weighted.reshape(local_rows, 2 * local_g).T
    item_rows = jnp.swapaxes(item_pair, 1, 2)
    live = (jnp.arange(item_image.shape[0], dtype=jnp.int32) < item_count[0]).astype(jnp.int32)
    slots = jnp.stack([item_image, item_sub, live])

    if group_count != 2 or length % 2:
        everything = lax.all_gather(aux_flat, "dev", axis=0, tiled=True)
        mine = lax.all_to_all(everything, "grp", split_axis=0, concat_axis=1, tiled=True)
        factor = lax.all_gather(turned, "grp", axis=0, tiled=True)
        parts = factor.reshape(group_count, 2, local_g, local_rows)
        other = jnp.stack([parts[:, 1], -parts[:, 0]], axis=1).reshape(factor.shape)
        long_part = jnp.concatenate(
            [
                jnp.dot(mine, factor, preferred_element_type=jnp.float32),
                jnp.dot(mine, other, preferred_element_type=jnp.float32),
            ],
            axis=1,
        )
        items = lax.all_gather(item_rows, "grp", axis=0, tiled=True)
        images, sub_ids, live = lax.all_gather(slots, "grp", axis=1, tiled=True)
        table = slot_table(image_dist, image_phase, images)
        short = short_range(
            half, live, sub_ids, table, aux_basis, aux_decay, [items], row_count, subs
        )
        return (long_part + short).astype(jnp.bfloat16).reshape(row_count, 2, local_rows)

    home = length // 2
    place = member // (breadth * CORES)
    across = member // CORES % breadth
    core = member % CORES

    def send(value, route):
        def index(g, z, y, c):
            return g * member_count + (z * breadth + y) * CORES + c

        pairs = []
        for g in range(group_count):
            for z in range(length):
                for y in range(breadth):
                    for c in range(CORES):
                        pairs.append((index(g, z, y, c), index(*route(g, z, y, c))))
        return lax.ppermute(value, AXES, pairs)

    def to_plane(value):
        return send(value, lambda g, z, y, c: (1 - g, z, y, c))

    ring = [*range(0, length, 2), *reversed(range(1, length, 2))]
    turn = {z: n for n, z in enumerate(ring)}

    def along(value, step):
        return send(value, lambda g, z, y, c: (g, ring[(turn[z] + step) % length], y, c))

    def over_y(value, s):
        return send(value, lambda g, z, y, c: (g, z, (y + s) % breadth, c))

    def over_core(value, t):
        return send(value, lambda g, z, y, c: (g, z, y, (c + t) % CORES))

    def hops_of(g, z):
        hops = [(turn[z] - turn[j]) % length for j in range(g * home, (g + 1) * home)]
        return sorted(hops, key=lambda k: (min(k, length - k), k))

    def here(number):
        return sum(
            jnp.where((group == g) & (place == z), number(g, z), 0)
            for g in range(group_count)
            for z in range(length)
        )

    def pick(other, n, *earlier):
        wanted = here(lambda g, z: hops_of(g ^ other, z)[n])
        possible = sorted({hops_of(g, z)[n] for g in range(group_count) for z in range(length)})
        blocks = lax.optimization_barrier((*(held[k] for k in possible), *earlier))
        value = blocks[len(possible) - 1]
        for k, block in reversed(list(zip(possible[:-1], blocks))):
            value = jnp.where(wanted == k, block, value)
        return value

    def slab_of(n):
        return here(lambda g, z: ring[(turn[z] - hops_of(g, z)[n]) % length] - g * home)

    def number_of(n, s, t):
        return (slab_of(n) * breadth + (across - s) % breadth) * CORES + (core - t) % CORES

    def with_cores(value):
        return [value] + [over_core(value, t) for t in range(1, CORES)]

    held = {0: aux_flat, 1: along(aux_flat, 1), length - 1: along(aux_flat, -1)}
    packed = jnp.concatenate([item_rows, slot_block(slots, item_rows)], axis=0)
    turned_x = to_plane(turned)
    factors = [[turned, turned_x]] + [[over_y(turned, s)] for s in range(1, breadth)]
    items_x = to_plane(packed)
    mine = []
    theirs = []
    crossed = []
    away = []
    arriving = []

    def foreign(n, *earlier):
        theirs.append(pick(True, n, *earlier))
        return to_plane(theirs[n])

    def multiply(n, t, away_factors):
        made = []
        if breadth > 1:
            made = long_range([(mine[n][t], crossed[n][t])], away_factors, local_rows)
        away[n].extend(made)
        arriving[n].append([over_y(v, s) for s, v in enumerate(made, 1)])

    def short_part(slots, items, *how):
        images, sub_ids, live = slots
        table = slot_table(image_dist, image_phase, images)
        return short_range(
            half, live, sub_ids, table, aux_basis, aux_decay, [items], row_count, subs, *how
        )

    short = short_part(slots, packed, None, False)

    moved = foreign(0, short)
    begun = [turned_x, items_x, *(pair[0] for pair in factors[1:])]
    for k in range(2, length // 2 + 1):
        held[k] = along(after(held[k - 1], held[1], held[length - 1], short), 1)
    for k in range(2, (length + 1) // 2):
        held[length - k] = along(after(held[length - k + 1], held[1], held[length - 1], short), -1)
    for s in range(1, breadth):
        factors[s].append(over_y(after(turned_x, theirs[0], *begun), s))

    short = short_part(read_slots(after(items_x, theirs[0], *begun), slots), items_x, short)

    out = None
    for n in range(home):
        if n:
            moved = foreign(n, theirs[n - 1], *(away[n - 2] if n > 1 else [short]))
        away.append([])
        arriving.append([])
        mine.append(with_cores(pick(False, n, theirs[n], *([*away[n - 1], out] if n else begun))))
        away_factors = factors[1:]
        if n:
            away_factors = [[both_parts(after(v, *away[0])) for v in pair] for pair in factors[1:]]
        crossed.append(with_cores(moved if n else after(moved, short)))
        for t in range(CORES):
            multiply(n, t, away_factors)
        blocks = [
            (after(mine[n][0], *away[n]), crossed[n][0]),
            *zip(mine[n][1:], crossed[n][1:]),
        ]
        order = jnp.stack([number_of(n, 0, t) for t in range(CORES)]).astype(jnp.int32)
        out = own_sum(order, blocks, factors[0], short, out)
    calls = []
    for n in range(home):
        calls += [
            [(v, number_of(n, s, t)) for s, v in enumerate(arriving[n][t], 1)] for t in range(CORES)
        ]
        if n < home - 1:
            calls[-CORES:] = [sum(calls[-CORES:], [])]
    for entries in calls:
        if entries:
            order = jnp.stack([number for _, number in entries]).astype(jnp.int32)
            out = final_sum(order, [piece for piece, _ in entries], short, out, rows)
    return out


def solution(mesh):
    return jax.shard_map(
        body,
        mesh=mesh,
        in_specs=(
            P("dev", None, "grp"),
            P("dev", None, "grp"),
            P("grp"),
            P(),
            P(),
            P(),
            P(),
            P(("grp", "dev"), None, None),
            P(("grp", "dev")),
            P(("grp", "dev")),
            P(("grp", "dev")),
        ),
        out_specs=P("grp", None, "dev"),
        check_vma=False,
    )
```

```python
import functools

import jax
import jax.numpy as jnp
from jax import lax
from jax.experimental import pallas as pl
from jax.experimental.pallas import tpu as pltpu
from jax.sharding import PartitionSpec as P

AXES = ("grp", "dev")
CORES = 2
SMALL_COST = pl.CostEstimate(flops=1, bytes_accessed=1, transcendentals=0)
GROUP_ITEMS = 4
SHORT_VMEM_BYTES = 20 * 1024 * 1024
VMEM_BYTES = 10 * 1024 * 1024


def in_hbm(value):
    return pltpu.with_memory_space_constraint(value, pltpu.HBM)


def short_kernel(
    half_ref, live_ref, sub_ref, meta_ref, basis_ref, decay_ref, *refs, share, subs, depth, width, adds, finishes
):
    items, scratch = refs[: -10 - adds], refs[-10:]
    out_ref, basis, left, acc, made, dists, group_sub, cursor, basis_sem, out_sem = scratch
    slots = share * len(items)
    row_count = acc.shape[2]
    tile = made.shape[1]
    if adds:
        acc_copy = pltpu.make_async_copy(refs[-11], acc, out_sem.at[0])
        acc_copy.start()
    else:
        acc[...] = jnp.zeros_like(acc)
    mine = pl.ds(pl.multiple_of(half_ref[0] * row_count, row_count), row_count)
    basis_copy = pltpu.make_async_copy(basis_ref.at[:, mine], basis, basis_sem)
    basis_copy.start()
    left[...] = jnp.zeros_like(left)

    for s in range(subs):
        cursor[s] = 0

    def count(i, carry):
        cursor[sub_ref[i]] = cursor[sub_ref[i]] + live_ref[i]
        return carry

    lax.fori_loop(0, slots, count, 0)
    first = jnp.int32(0)
    for s in range(subs):
        groups = (cursor[s] + GROUP_ITEMS - 1) // GROUP_ITEMS

        def mark(i, carry, s=s):
            group_sub[i] = s
            return carry

        lax.fori_loop(first, first + groups, mark, 0)
        cursor[s] = first * GROUP_ITEMS
        first = first + groups

    def clear(i, carry):
        dists[i] = 0.0
        return carry

    lax.fori_loop(0, first * GROUP_ITEMS, clear, 0)

    for n, items_ref in enumerate(items):

        def place(k, carry, first=n * share, items_ref=items_ref):
            i = first + k

            @pl.when(live_ref[i] > 0)
            def _():
                s = sub_ref[i]
                at = cursor[s]
                cursor[s] = at + 1
                dists[at] = meta_ref[0, i]
                turned = items_ref[k].astype(jnp.float32)
                lanes = pl.ds(pl.multiple_of((at % GROUP_ITEMS) * depth, depth), depth)
                group = at // GROUP_ITEMS
                left[group, 0:width, lanes] = (turned * meta_ref[1, i]).astype(left.dtype)
                left[group, width:, lanes] = (turned * meta_ref[2, i]).astype(left.dtype)

            return carry

        lax.fori_loop(0, share, place, 0)

    decay = decay_ref[:, mine]
    basis_copy.wait()
    if adds:
        acc_copy.wait()

    def one_group(group, carry):
        s = group_sub[group]
        damping = [
            jnp.exp(decay * -dists[group * GROUP_ITEMS + k]).astype(basis.dtype)
            for k in range(GROUP_ITEMS)
        ]
        for t in range(0, row_count, tile):
            right = jnp.concatenate(
                [
                    basis[:, t : t + tile] * damping[k][:, t : t + tile]
                    for k in range(GROUP_ITEMS)
                ],
                axis=0,
            )
            acc[s, :, t : t + tile] += jnp.dot(
                left[group], right, preferred_element_type=jnp.float32
            )
        return carry

    lax.fori_loop(0, first, one_group, 0)
    if not finishes:
        acc_copy = pltpu.make_async_copy(acc, out_ref, out_sem.at[0])
        acc_copy.start()
        acc_copy.wait()
        return
    copies = []
    for n, t in enumerate(range(0, row_count, tile)):
        for s in range(subs):
            for c in range(2):
                column = (c * subs + s) * width
                made[n, :, column : column + width] = acc[
                    s, c * width : (c + 1) * width, t : t + tile
                ].T
        copies.append(pltpu.make_async_copy(made.at[n], out_ref.at[pl.ds(t, tile), :], out_sem.at[n]))
        copies[-1].start()
    for copy in copies:
        copy.wait()


def short_range(half, live, sub_ids, meta, aux_basis, aux_decay, items, row_count, subs, earlier=None, finishes=True):
    adds = earlier is not None
    _, width, depth = items[0].shape
    slots = live.shape[0]
    share = slots // len(items)
    groups = slots // GROUP_ITEMS + subs
    tile = min(row_count, 512)
    kernel = functools.partial(
        short_kernel, share=share, subs=subs, depth=depth, width=width, adds=adds, finishes=finishes
    )
    return pl.pallas_call(
        kernel,
        out_shape=pltpu.HBM(
            (row_count, 2 * subs * width) if finishes else (subs, 2 * width, row_count), jnp.float32
        ),
        in_specs=[pl.BlockSpec(memory_space=pltpu.SMEM)] * 4
        + [pl.BlockSpec(memory_space=pltpu.HBM)]
        + [pl.BlockSpec(memory_space=pltpu.VMEM)] * (1 + len(items))
        + [pl.BlockSpec(memory_space=pltpu.HBM)] * adds,
        out_specs=pl.BlockSpec(memory_space=pltpu.HBM),
        scratch_shapes=[
            pltpu.VMEM((depth, row_count), jnp.bfloat16),
            pltpu.VMEM((groups, 2 * width, GROUP_ITEMS * depth), jnp.bfloat16),
            pltpu.VMEM((subs, 2 * width, row_count), jnp.float32),
            pltpu.VMEM((row_count // tile, tile, 2 * subs * width), jnp.float32),
            pltpu.SMEM((groups * GROUP_ITEMS,), jnp.float32),
            pltpu.SMEM((groups,), jnp.int32),
            pltpu.SMEM((subs,), jnp.int32),
            pltpu.SemaphoreType.DMA,
            pltpu.SemaphoreType.DMA((row_count // tile,)),
        ],
        compiler_params=pltpu.CompilerParams(vmem_limit_bytes=SHORT_VMEM_BYTES),
        cost_estimate=pl.CostEstimate(
            flops=4 * row_count * slots * depth * width, bytes_accessed=1, transcendentals=0
        ),
        name="short_range",
    )(
        half,
        live,
        sub_ids,
        meta,
        in_hbm(aux_basis),
        aux_decay.reshape(1, -1),
        *items,
        *([in_hbm(earlier)] if adds else []),
    )


def long_kernel(*refs, blocks, chains, pieces, width):
    parts = refs[: blocks * chains]
    factors = refs[blocks * chains : (blocks + pieces) * chains]
    outs, scratch = refs[(blocks + pieces) * chains :][:pieces], refs[-pieces - 2 :]
    right, made, out_sem = scratch[0], scratch[1:-1], scratch[-1]
    depth = factors[0].shape[0]
    half = depth // 2
    count = parts[0].shape[0]
    copies = []
    for piece in reversed(range(pieces)):
        for chain in range(chains):
            factor = factors[piece * chains + chain]
            top = chain * depth
            if factor.shape[1] > width:
                right[top : top + depth, :] = factor[...]
                continue
            right[top : top + depth, 0:width] = factor[...]
            right[top : top + half, width:] = factor[half:, :]
            right[top + half : top + depth, width:] = -factor[0:half, :]
        for block in range(blocks):
            left = jnp.concatenate(
                [parts[block * chains + chain][...] for chain in range(chains)], axis=1
            )
            total = jnp.dot(left, right[...], preferred_element_type=jnp.float32)
            made[piece][block] = total.astype(outs[piece].dtype)
            target = outs[piece].at[pl.ds(block * count, count), :]
            copies.append(
                pltpu.make_async_copy(made[piece].at[block], target, out_sem.at[piece, block])
            )
            copies[-1].start()
    for copy in copies:
        copy.wait()


def long_range(blocks, factors, width):
    depth = factors[0][0].shape[0]
    chains = len(factors[0])
    pieces = len(factors)
    count = blocks[0][0].shape[0]
    shape = (len(blocks) * count, 2 * width)
    dtypes = [jnp.bfloat16] * pieces
    flat = [v for group in [*blocks, *factors] for v in group]
    return pl.pallas_call(
        functools.partial(
            long_kernel, blocks=len(blocks), chains=chains, pieces=pieces, width=width
        ),
        out_shape=[pltpu.HBM(shape, dtype) for dtype in dtypes],
        in_specs=[pl.BlockSpec(memory_space=pltpu.VMEM)] * len(flat),
        out_specs=[pl.BlockSpec(memory_space=pltpu.HBM)] * pieces,
        scratch_shapes=[pltpu.VMEM((chains * depth, 2 * width), jnp.bfloat16)]
        + [pltpu.VMEM((len(blocks), count, 2 * width), dtype) for dtype in dtypes]
        + [pltpu.SemaphoreType.DMA((pieces, len(blocks)))],
        compiler_params=pltpu.CompilerParams(vmem_limit_bytes=VMEM_BYTES),
        cost_estimate=SMALL_COST,
        name="long_range",
    )(*flat)


def own_kernel(order_ref, *refs, blocks, chains, pieces, aliased):
    parts = refs[: blocks * chains]
    factors = refs[blocks * chains : (blocks + 1) * chains]
    arrived = refs[(blocks + 1) * chains :][:pieces]
    short_ref = refs[(blocks + 1) * chains + pieces]
    out_ref, right, terms, made, term_sem, out_sem = refs[(blocks + 1) * chains + pieces + 1 + aliased :]
    rows = terms.shape[1]
    depth, width = factors[0].shape
    half = depth // 2
    windows = [pl.ds(pl.multiple_of(order_ref[n] * rows, rows), rows) for n in range(blocks + pieces)]
    arriving = []
    for n, window in enumerate(windows):
        arriving.append(
            pltpu.make_async_copy(short_ref.at[window, :], terms.at[n], term_sem.at[n])
        )
        arriving[-1].start()
    for chain, factor in enumerate(factors):
        top = chain * depth
        right[top : top + depth, 0:width] = factor[...]
        right[top : top + half, width:] = factor[half:, :]
        right[top + half : top + depth, width:] = -factor[0:half, :]
    leaving = []
    for n, window in enumerate(windows):
        if n < blocks:
            left = [parts[n * chains + chain][...] for chain in range(chains)]
            left = jnp.concatenate(left, axis=1)
            total = jnp.dot(left, right[...], preferred_element_type=jnp.float32)
        else:
            total = arrived[n - blocks][...].astype(jnp.float32)
        arriving[n].wait()
        made[n] = (total + terms[n]).astype(made.dtype).reshape(made.shape[1:])
        leaving.append(pltpu.make_async_copy(made.at[n], out_ref.at[window], out_sem.at[n]))
        leaving[-1].start()
    for copy in leaving:
        copy.wait()


def own_sum(order, blocks, factors, pieces, short, earlier):
    rows, depth = blocks[0][0].shape
    width = factors[0].shape[1]
    row_count, columns = short.shape
    chains = len(factors)
    count = len(blocks) + len(pieces)
    aliased = earlier is not None
    flat = [v for group in [*blocks, factors, pieces] for v in group]
    return pl.pallas_call(
        functools.partial(
            own_kernel, blocks=len(blocks), chains=chains, pieces=len(pieces), aliased=aliased
        ),
        out_shape=pltpu.HBM((row_count, 2, width), jnp.bfloat16),
        in_specs=[pl.BlockSpec(memory_space=pltpu.SMEM)]
        + [pl.BlockSpec(memory_space=pltpu.VMEM)] * len(flat)
        + [pl.BlockSpec(memory_space=pltpu.HBM)] * (1 + aliased),
        out_specs=pl.BlockSpec(memory_space=pltpu.HBM),
        scratch_shapes=[
            pltpu.VMEM((chains * depth, 2 * width), jnp.bfloat16),
            pltpu.VMEM((count, rows, columns), jnp.float32),
            pltpu.VMEM((count, rows, 2, width), jnp.bfloat16),
            pltpu.SemaphoreType.DMA((count,)),
            pltpu.SemaphoreType.DMA((count,)),
        ],
        input_output_aliases={len(flat) + 2: 0} if aliased else {},
        compiler_params=pltpu.CompilerParams(vmem_limit_bytes=VMEM_BYTES),
        cost_estimate=SMALL_COST,
        name="own_sum",
    )(order, *flat, in_hbm(short), *([earlier] if aliased else []))


def final_kernel(order_ref, *refs, pieces, blocks, aliased):
    short_ref = refs[pieces]
    out_ref, terms, made, term_sem, out_sem = refs[pieces + 1 + aliased :]
    steps, rows = terms.shape[:2]
    windows = [pl.ds(pl.multiple_of(order_ref[n] * rows, rows), rows) for n in range(steps)]
    arriving = []
    for n, window in enumerate(windows):
        arriving.append(
            pltpu.make_async_copy(short_ref.at[window, :], terms.at[n], term_sem.at[n])
        )
        arriving[-1].start()
    leaving = []
    for n, window in enumerate(windows):
        arriving[n].wait()
        top = n % blocks * rows
        total = refs[n // blocks][top : top + rows, :].astype(jnp.float32) + terms[n]
        made[n] = total.astype(made.dtype).reshape(made.shape[1:])
        leaving.append(pltpu.make_async_copy(made.at[n], out_ref.at[window], out_sem.at[n]))
        leaving[-1].start()
    for copy in leaving:
        copy.wait()


def final_sum(order, pieces, short, earlier, rows):
    columns = pieces[0].shape[1]
    row_count = short.shape[0]
    count = len(pieces)
    blocks = pieces[0].shape[0] // rows
    steps = count * blocks
    return pl.pallas_call(
        functools.partial(final_kernel, pieces=count, blocks=blocks, aliased=True),
        out_shape=pltpu.HBM((row_count, 2, columns // 2), jnp.bfloat16),
        in_specs=[pl.BlockSpec(memory_space=pltpu.SMEM)]
        + [pl.BlockSpec(memory_space=pltpu.VMEM)] * count
        + [pl.BlockSpec(memory_space=pltpu.HBM)] * 2,
        out_specs=pl.BlockSpec(memory_space=pltpu.HBM),
        scratch_shapes=[
            pltpu.VMEM((steps, rows, columns), jnp.float32),
            pltpu.VMEM((steps, rows, 2, columns // 2), jnp.bfloat16),
            pltpu.SemaphoreType.DMA((steps,)),
            pltpu.SemaphoreType.DMA((steps,)),
        ],
        input_output_aliases={count + 2: 0},
        compiler_params=pltpu.CompilerParams(vmem_limit_bytes=VMEM_BYTES),
        cost_estimate=SMALL_COST,
        name="final_sum",
    )(order, *pieces, in_hbm(short), earlier)


def slot_table(image_dist, image_phase, images):
    chosen = images[None, :] == jnp.arange(image_dist.shape[0], dtype=jnp.int32)[:, None]
    distance = jnp.sum(jnp.where(chosen, image_dist[:, None], 0.0), axis=0)
    phase = jnp.sum(jnp.where(chosen, image_phase[:, None], 0.0), axis=0)
    return jnp.stack([distance, jnp.cos(phase), jnp.sin(phase)])


def both_parts(factor):
    half = factor.shape[0] // 2
    return jnp.concatenate(
        [factor, jnp.concatenate([factor[half:], -factor[:half]], axis=0)], axis=1
    )


def slot_block(slots, items):
    digits = jnp.concatenate([slots // 128, slots % 128], axis=0).astype(items.dtype)
    fill = [(0, full - used) for full, used in zip(items.shape[1:], digits.shape)]
    return jnp.pad(digits, fill)[None]


def read_slots(packed, slots):
    count, share = slots.shape
    digits = packed[-1, 0 : 2 * count, 0:share].astype(jnp.int32)
    return digits[0:count] * 128 + digits[count:]


def after(value, *earlier):
    return lax.optimization_barrier((value, *earlier))[0] if earlier else value


def body(
    pair_ft,
    aux_ft,
    coul_weight,
    aux_basis,
    aux_decay,
    image_dist,
    image_phase,
    item_pair,
    item_image,
    item_sub,
    item_count,
):
    group_count = lax.axis_size("grp")
    member_count = lax.axis_size("dev")
    group = lax.axis_index("grp")
    member = lax.axis_index("dev")
    local_rows, _, local_g = pair_ft.shape
    subs = local_rows // item_pair.shape[2]
    rows = aux_ft.shape[0]
    row_count = rows * member_count // group_count
    half = jnp.reshape(group, (1,)).astype(jnp.int32)

    chips = member_count // CORES
    breadth = max(n for n in range(1, chips + 1) if chips % n == 0 and n * n <= chips)
    length = chips // breadth

    aux_flat = aux_ft.reshape(rows, 2 * local_g)
    pairs = pair_ft.astype(jnp.float32)
    weighted = (pairs * coul_weight[None, None, :]).astype(jnp.bfloat16)
    turned = weighted.reshape(local_rows, 2 * local_g).T
    item_rows = jnp.swapaxes(item_pair, 1, 2)
    live = (jnp.arange(item_image.shape[0], dtype=jnp.int32) < item_count[0]).astype(jnp.int32)
    slots = jnp.stack([item_image, item_sub, live])

    if group_count != 2 or length % 2:
        everything = lax.all_gather(aux_flat, "dev", axis=0, tiled=True)
        mine = lax.all_to_all(everything, "grp", split_axis=0, concat_axis=1, tiled=True)
        factor = lax.all_gather(turned, "grp", axis=0, tiled=True)
        parts = factor.reshape(group_count, 2, local_g, local_rows)
        other = jnp.stack([parts[:, 1], -parts[:, 0]], axis=1).reshape(factor.shape)
        long_part = jnp.concatenate(
            [
                jnp.dot(mine, factor, preferred_element_type=jnp.float32),
                jnp.dot(mine, other, preferred_element_type=jnp.float32),
            ],
            axis=1,
        )
        items = lax.all_gather(item_rows, "grp", axis=0, tiled=True)
        images, sub_ids, live = lax.all_gather(slots, "grp", axis=1, tiled=True)
        table = slot_table(image_dist, image_phase, images)
        short = short_range(
            half, live, sub_ids, table, aux_basis, aux_decay, [items], row_count, subs
        )
        return (long_part + short).astype(jnp.bfloat16).reshape(row_count, 2, local_rows)

    home = length // 2
    place = member // (breadth * CORES)
    across = member // CORES % breadth
    core = member % CORES

    def send(value, route):
        def index(g, z, y, c):
            return g * member_count + (z * breadth + y) * CORES + c

        pairs = []
        for g in range(group_count):
            for z in range(length):
                for y in range(breadth):
                    for c in range(CORES):
                        pairs.append((index(g, z, y, c), index(*route(g, z, y, c))))
        return lax.ppermute(value, AXES, pairs)

    def to_plane(value):
        return send(value, lambda g, z, y, c: (1 - g, z, y, c))

    ring = [*range(0, length, 2), *reversed(range(1, length, 2))]
    turn = {z: n for n, z in enumerate(ring)}

    def along(value, step):
        return send(value, lambda g, z, y, c: (g, ring[(turn[z] + step) % length], y, c))

    def over_y(value, s):
        return send(value, lambda g, z, y, c: (g, z, (y + s) % breadth, c))

    def over_core(value, t):
        return send(value, lambda g, z, y, c: (g, z, y, (c + t) % CORES))

    def hops_of(g, z):
        hops = [(turn[z] - turn[j]) % length for j in range(g * home, (g + 1) * home)]
        return sorted(hops, key=lambda k: (min(k, length - k), k))

    def here(number):
        return sum(
            jnp.where((group == g) & (place == z), number(g, z), 0)
            for g in range(group_count)
            for z in range(length)
        )

    def pick(other, n, *earlier):
        wanted = here(lambda g, z: hops_of(g ^ other, z)[n])
        possible = sorted({hops_of(g, z)[n] for g in range(group_count) for z in range(length)})
        blocks = lax.optimization_barrier((*(held[k] for k in possible), *earlier))
        value = blocks[len(possible) - 1]
        for k, block in reversed(list(zip(possible[:-1], blocks))):
            value = jnp.where(wanted == k, block, value)
        return value

    def slab_of(n):
        return here(lambda g, z: ring[(turn[z] - hops_of(g, z)[n]) % length] - g * home)

    def number_of(n, s, t):
        return (slab_of(n) * breadth + (across - s) % breadth) * CORES + (core - t) % CORES

    def with_cores(value):
        return [value] + [over_core(value, t) for t in range(1, CORES)]

    held = {0: aux_flat, 1: along(aux_flat, 1), length - 1: along(aux_flat, -1)}
    packed = jnp.concatenate([item_rows, slot_block(slots, item_rows)], axis=0)
    turned_x = to_plane(turned)
    factors = [[turned, turned_x]] + [[over_y(turned, s)] for s in range(1, breadth)]
    items_x = to_plane(packed)
    mine = []
    theirs = []
    crossed = []
    away = []
    arriving = []

    def foreign(n, *earlier):
        theirs.append(pick(True, n, *earlier))
        return to_plane(theirs[n])

    def multiply(n, t, away_factors):
        made = []
        if breadth > 1:
            made = long_range([(mine[n][t], crossed[n][t])], away_factors, local_rows)
        away[n].extend(made)
        arriving[n].append([over_y(v, s) for s, v in enumerate(made, 1)])

    def short_part(slots, items, *how):
        images, sub_ids, live = slots
        table = slot_table(image_dist, image_phase, images)
        return short_range(
            half, live, sub_ids, table, aux_basis, aux_decay, [items], row_count, subs, *how
        )

    short = short_part(slots, packed, None, False)

    moved = foreign(0, short)
    begun = [turned_x, *(pair[0] for pair in factors[1:])]
    for k in range(2, length // 2 + 1):
        held[k] = along(after(held[k - 1], held[1], held[length - 1], short), 1)
    for k in range(2, (length + 1) // 2):
        held[length - k] = along(after(held[length - k + 1], held[1], held[length - 1], short), -1)
    for s in range(1, breadth):
        factors[s].append(over_y(after(turned_x, theirs[0], *begun), s))

    short = short_part(read_slots(after(items_x, theirs[0], *begun), slots), items_x, short)

    def arrived_of(n):
        return [
            [(v, number_of(n, s, t)) for s, v in enumerate(arriving[n][t], 1)] for t in range(CORES)
        ]

    out = None
    for n in range(home):
        if n:
            moved = foreign(n, theirs[n - 1], *(away[n - 2] if n > 1 else [short]))
        away.append([])
        arriving.append([])
        mine.append(with_cores(pick(False, n, theirs[n], *([*away[n - 1], out] if n else begun))))
        away_factors = factors[1:]
        if n:
            away_factors = [[both_parts(after(v, *away[0])) for v in pair] for pair in factors[1:]]
        crossed.append(with_cores(moved if n else after(moved, short)))
        for t in range(CORES):
            multiply(n, t, away_factors)
        blocks = [
            (after(mine[n][0], *away[n]), crossed[n][0]),
            *zip(mine[n][1:], crossed[n][1:]),
        ]
        numbers = [number_of(n, 0, t) for t in range(CORES)]
        pieces = []
        if n:
            come = [(v, number) for entries in arrived_of(n - 1) for v, number in entries]
            pieces = [v for v, _ in come]
            numbers += [number for _, number in come]
        out = own_sum(jnp.stack(numbers).astype(jnp.int32), blocks, factors[0], pieces, short, out)
    entries = sum(arrived_of(home - 1), [])
    if entries:
        order = jnp.stack([number for _, number in entries]).astype(jnp.int32)
        out = final_sum(order, [piece for piece, _ in entries], short, out, rows)
    return out


def solution(mesh):
    return jax.shard_map(
        body,
        mesh=mesh,
        in_specs=(
            P("dev", None, "grp"),
            P("dev", None, "grp"),
            P("grp"),
            P(),
            P(),
            P(),
            P(),
            P(("grp", "dev"), None, None),
            P(("grp", "dev")),
            P(("grp", "dev")),
            P(("grp", "dev")),
        ),
        out_specs=P("grp", None, "dev"),
        check_vma=False,
    )
```

```python
import functools

import jax
import jax.numpy as jnp
from jax import lax
from jax.experimental import pallas as pl
from jax.experimental.pallas import tpu as pltpu
from jax.sharding import PartitionSpec as P

AXES = ("grp", "dev")
CORES = 2
SMALL_COST = pl.CostEstimate(flops=1, bytes_accessed=1, transcendentals=0)
GROUP_ITEMS = 4
SHORT_VMEM_BYTES = 20 * 1024 * 1024
VMEM_BYTES = 10 * 1024 * 1024


def in_hbm(value):
    return pltpu.with_memory_space_constraint(value, pltpu.HBM)


def short_kernel(
    half_ref, live_ref, sub_ref, meta_ref, basis_ref, decay_ref, *refs, share, subs, depth, width, adds, finishes
):
    items, scratch = refs[: -10 - adds], refs[-10:]
    out_ref, basis, left, acc, made, dists, group_sub, cursor, basis_sem, out_sem = scratch
    slots = share * len(items)
    row_count = acc.shape[2]
    tile = made.shape[1]
    if adds:
        acc_copy = pltpu.make_async_copy(refs[-11], acc, out_sem.at[0])
        acc_copy.start()
    else:
        acc[...] = jnp.zeros_like(acc)
    mine = pl.ds(pl.multiple_of(half_ref[0] * row_count, row_count), row_count)
    basis_copy = pltpu.make_async_copy(basis_ref.at[:, mine], basis, basis_sem)
    basis_copy.start()
    left[...] = jnp.zeros_like(left)

    for s in range(subs):
        cursor[s] = 0

    def count(i, carry):
        cursor[sub_ref[i]] = cursor[sub_ref[i]] + live_ref[i]
        return carry

    lax.fori_loop(0, slots, count, 0)
    first = jnp.int32(0)
    for s in range(subs):
        groups = (cursor[s] + GROUP_ITEMS - 1) // GROUP_ITEMS

        def mark(i, carry, s=s):
            group_sub[i] = s
            return carry

        lax.fori_loop(first, first + groups, mark, 0)
        cursor[s] = first * GROUP_ITEMS
        first = first + groups

    def clear(i, carry):
        dists[i] = 0.0
        return carry

    lax.fori_loop(0, first * GROUP_ITEMS, clear, 0)

    for n, items_ref in enumerate(items):

        def place(k, carry, first=n * share, items_ref=items_ref):
            i = first + k

            @pl.when(live_ref[i] > 0)
            def _():
                s = sub_ref[i]
                at = cursor[s]
                cursor[s] = at + 1
                dists[at] = meta_ref[0, i]
                turned = items_ref[k].astype(jnp.float32)
                lanes = pl.ds(pl.multiple_of((at % GROUP_ITEMS) * depth, depth), depth)
                group = at // GROUP_ITEMS
                left[group, 0:width, lanes] = (turned * meta_ref[1, i]).astype(left.dtype)
                left[group, width:, lanes] = (turned * meta_ref[2, i]).astype(left.dtype)

            return carry

        lax.fori_loop(0, share, place, 0)

    decay = decay_ref[:, mine]
    basis_copy.wait()
    if adds:
        acc_copy.wait()

    def one_group(group, carry):
        s = group_sub[group]
        damping = [
            jnp.exp(decay * -dists[group * GROUP_ITEMS + k]).astype(basis.dtype)
            for k in range(GROUP_ITEMS)
        ]
        for t in range(0, row_count, tile):
            right = jnp.concatenate(
                [
                    basis[:, t : t + tile] * damping[k][:, t : t + tile]
                    for k in range(GROUP_ITEMS)
                ],
                axis=0,
            )
            acc[s, :, t : t + tile] += jnp.dot(
                left[group], right, preferred_element_type=jnp.float32
            )
        return carry

    lax.fori_loop(0, first, one_group, 0)
    if not finishes:
        acc_copy = pltpu.make_async_copy(acc, out_ref, out_sem.at[0])
        acc_copy.start()
        acc_copy.wait()
        return
    copies = []
    for n, t in enumerate(range(0, row_count, tile)):
        for s in range(subs):
            for c in range(2):
                column = (c * subs + s) * width
                made[n, :, column : column + width] = acc[
                    s, c * width : (c + 1) * width, t : t + tile
                ].T
        copies.append(pltpu.make_async_copy(made.at[n], out_ref.at[pl.ds(t, tile), :], out_sem.at[n]))
        copies[-1].start()
    for copy in copies:
        copy.wait()


def short_range(half, live, sub_ids, meta, aux_basis, aux_decay, items, row_count, subs, earlier=None, finishes=True):
    adds = earlier is not None
    _, width, depth = items[0].shape
    slots = live.shape[0]
    share = slots // len(items)
    groups = slots // GROUP_ITEMS + subs
    tile = min(row_count, 512)
    kernel = functools.partial(
        short_kernel, share=share, subs=subs, depth=depth, width=width, adds=adds, finishes=finishes
    )
    return pl.pallas_call(
        kernel,
        out_shape=pltpu.HBM(
            (row_count, 2 * subs * width) if finishes else (subs, 2 * width, row_count), jnp.float32
        ),
        in_specs=[pl.BlockSpec(memory_space=pltpu.SMEM)] * 4
        + [pl.BlockSpec(memory_space=pltpu.HBM)]
        + [pl.BlockSpec(memory_space=pltpu.VMEM)] * (1 + len(items))
        + [pl.BlockSpec(memory_space=pltpu.HBM)] * adds,
        out_specs=pl.BlockSpec(memory_space=pltpu.HBM),
        scratch_shapes=[
            pltpu.VMEM((depth, row_count), jnp.bfloat16),
            pltpu.VMEM((groups, 2 * width, GROUP_ITEMS * depth), jnp.bfloat16),
            pltpu.VMEM((subs, 2 * width, row_count), jnp.float32),
            pltpu.VMEM((row_count // tile, tile, 2 * subs * width), jnp.float32),
            pltpu.SMEM((groups * GROUP_ITEMS,), jnp.float32),
            pltpu.SMEM((groups,), jnp.int32),
            pltpu.SMEM((subs,), jnp.int32),
            pltpu.SemaphoreType.DMA,
            pltpu.SemaphoreType.DMA((row_count // tile,)),
        ],
        compiler_params=pltpu.CompilerParams(vmem_limit_bytes=SHORT_VMEM_BYTES),
        cost_estimate=pl.CostEstimate(
            flops=4 * row_count * slots * depth * width, bytes_accessed=1, transcendentals=0
        ),
        name="short_range",
    )(
        half,
        live,
        sub_ids,
        meta,
        in_hbm(aux_basis),
        aux_decay.reshape(1, -1),
        *items,
        *([in_hbm(earlier)] if adds else []),
    )


def long_kernel(*refs, blocks, chains, pieces, width):
    parts = refs[: blocks * chains]
    factors = refs[blocks * chains : (blocks + pieces) * chains]
    outs, scratch = refs[(blocks + pieces) * chains :][:pieces], refs[-pieces - 2 :]
    right, made, out_sem = scratch[0], scratch[1:-1], scratch[-1]
    depth = factors[0].shape[0]
    half = depth // 2
    count = parts[0].shape[0]
    copies = []
    for piece in reversed(range(pieces)):
        for chain in range(chains):
            factor = factors[piece * chains + chain]
            top = chain * depth
            if factor.shape[1] > width:
                right[top : top + depth, :] = factor[...]
                continue
            right[top : top + depth, 0:width] = factor[...]
            right[top : top + half, width:] = factor[half:, :]
            right[top + half : top + depth, width:] = -factor[0:half, :]
        for block in range(blocks):
            left = jnp.concatenate(
                [parts[block * chains + chain][...] for chain in range(chains)], axis=1
            )
            total = jnp.dot(left, right[...], preferred_element_type=jnp.float32)
            made[piece][block] = total.astype(outs[piece].dtype)
            target = outs[piece].at[pl.ds(block * count, count), :]
            copies.append(
                pltpu.make_async_copy(made[piece].at[block], target, out_sem.at[piece, block])
            )
            copies[-1].start()
    for copy in copies:
        copy.wait()


def long_range(blocks, factors, width):
    depth = factors[0][0].shape[0]
    chains = len(factors[0])
    pieces = len(factors)
    count = blocks[0][0].shape[0]
    shape = (len(blocks) * count, 2 * width)
    dtypes = [jnp.bfloat16] * pieces
    flat = [v for group in [*blocks, *factors] for v in group]
    return pl.pallas_call(
        functools.partial(
            long_kernel, blocks=len(blocks), chains=chains, pieces=pieces, width=width
        ),
        out_shape=[pltpu.HBM(shape, dtype) for dtype in dtypes],
        in_specs=[pl.BlockSpec(memory_space=pltpu.VMEM)] * len(flat),
        out_specs=[pl.BlockSpec(memory_space=pltpu.HBM)] * pieces,
        scratch_shapes=[pltpu.VMEM((chains * depth, 2 * width), jnp.bfloat16)]
        + [pltpu.VMEM((len(blocks), count, 2 * width), dtype) for dtype in dtypes]
        + [pltpu.SemaphoreType.DMA((pieces, len(blocks)))],
        compiler_params=pltpu.CompilerParams(vmem_limit_bytes=VMEM_BYTES),
        cost_estimate=SMALL_COST,
        name="long_range",
    )(*flat)


def own_kernel(order_ref, *refs, blocks, chains, pieces, aliased):
    parts = refs[: blocks * chains]
    factors = refs[blocks * chains : (blocks + 1) * chains]
    arrived = refs[(blocks + 1) * chains :][:pieces]
    short_ref = refs[(blocks + 1) * chains + pieces]
    out_ref, right, terms, made, term_sem, out_sem = refs[(blocks + 1) * chains + pieces + 1 + aliased :]
    rows = terms.shape[1]
    depth, width = factors[0].shape
    half = depth // 2
    windows = [pl.ds(pl.multiple_of(order_ref[n] * rows, rows), rows) for n in range(blocks + pieces)]
    arriving = []
    for n, window in enumerate(windows):
        arriving.append(
            pltpu.make_async_copy(short_ref.at[window, :], terms.at[n], term_sem.at[n])
        )
        arriving[-1].start()
    for chain, factor in enumerate(factors):
        top = chain * depth
        right[top : top + depth, 0:width] = factor[...]
        right[top : top + half, width:] = factor[half:, :]
        right[top + half : top + depth, width:] = -factor[0:half, :]
    leaving = []
    for n, window in enumerate(windows):
        if n < blocks:
            left = [parts[n * chains + chain][...] for chain in range(chains)]
            left = jnp.concatenate(left, axis=1)
            total = jnp.dot(left, right[...], preferred_element_type=jnp.float32)
        else:
            total = arrived[n - blocks][...].astype(jnp.float32)
        arriving[n].wait()
        made[n] = (total + terms[n]).astype(made.dtype).reshape(made.shape[1:])
        leaving.append(pltpu.make_async_copy(made.at[n], out_ref.at[window], out_sem.at[n]))
        leaving[-1].start()
    for copy in leaving:
        copy.wait()


def own_sum(order, blocks, factors, pieces, short, earlier):
    rows, depth = blocks[0][0].shape
    width = factors[0].shape[1]
    row_count, columns = short.shape
    chains = len(factors)
    count = len(blocks) + len(pieces)
    aliased = earlier is not None
    flat = [v for group in [*blocks, factors, pieces] for v in group]
    return pl.pallas_call(
        functools.partial(
            own_kernel, blocks=len(blocks), chains=chains, pieces=len(pieces), aliased=aliased
        ),
        out_shape=pltpu.HBM((row_count, 2, width), jnp.bfloat16),
        in_specs=[pl.BlockSpec(memory_space=pltpu.SMEM)]
        + [pl.BlockSpec(memory_space=pltpu.VMEM)] * len(flat)
        + [pl.BlockSpec(memory_space=pltpu.HBM)] * (1 + aliased),
        out_specs=pl.BlockSpec(memory_space=pltpu.HBM),
        scratch_shapes=[
            pltpu.VMEM((chains * depth, 2 * width), jnp.bfloat16),
            pltpu.VMEM((count, rows, columns), jnp.float32),
            pltpu.VMEM((count, rows, 2, width), jnp.bfloat16),
            pltpu.SemaphoreType.DMA((count,)),
            pltpu.SemaphoreType.DMA((count,)),
        ],
        input_output_aliases={len(flat) + 2: 0} if aliased else {},
        compiler_params=pltpu.CompilerParams(vmem_limit_bytes=VMEM_BYTES),
        cost_estimate=SMALL_COST,
        name="own_sum",
    )(order, *flat, in_hbm(short), *([earlier] if aliased else []))


def final_kernel(order_ref, *refs, pieces, blocks, aliased):
    short_ref = refs[pieces]
    out_ref, terms, made, term_sem, out_sem = refs[pieces + 1 + aliased :]
    steps, rows = terms.shape[:2]
    windows = [pl.ds(pl.multiple_of(order_ref[n] * rows, rows), rows) for n in range(steps)]
    arriving = []
    for n, window in enumerate(windows):
        arriving.append(
            pltpu.make_async_copy(short_ref.at[window, :], terms.at[n], term_sem.at[n])
        )
        arriving[-1].start()
    leaving = []
    for n, window in enumerate(windows):
        arriving[n].wait()
        top = n % blocks * rows
        total = refs[n // blocks][top : top + rows, :].astype(jnp.float32) + terms[n]
        made[n] = total.astype(made.dtype).reshape(made.shape[1:])
        leaving.append(pltpu.make_async_copy(made.at[n], out_ref.at[window], out_sem.at[n]))
        leaving[-1].start()
    for copy in leaving:
        copy.wait()


def final_sum(order, pieces, short, earlier, rows):
    columns = pieces[0].shape[1]
    row_count = short.shape[0]
    count = len(pieces)
    blocks = pieces[0].shape[0] // rows
    steps = count * blocks
    return pl.pallas_call(
        functools.partial(final_kernel, pieces=count, blocks=blocks, aliased=True),
        out_shape=pltpu.HBM((row_count, 2, columns // 2), jnp.bfloat16),
        in_specs=[pl.BlockSpec(memory_space=pltpu.SMEM)]
        + [pl.BlockSpec(memory_space=pltpu.VMEM)] * count
        + [pl.BlockSpec(memory_space=pltpu.HBM)] * 2,
        out_specs=pl.BlockSpec(memory_space=pltpu.HBM),
        scratch_shapes=[
            pltpu.VMEM((steps, rows, columns), jnp.float32),
            pltpu.VMEM((steps, rows, 2, columns // 2), jnp.bfloat16),
            pltpu.SemaphoreType.DMA((steps,)),
            pltpu.SemaphoreType.DMA((steps,)),
        ],
        input_output_aliases={count + 2: 0},
        compiler_params=pltpu.CompilerParams(vmem_limit_bytes=VMEM_BYTES),
        cost_estimate=SMALL_COST,
        name="final_sum",
    )(order, *pieces, in_hbm(short), earlier)


def slot_table(image_dist, image_phase, images):
    chosen = images[None, :] == jnp.arange(image_dist.shape[0], dtype=jnp.int32)[:, None]
    distance = jnp.sum(jnp.where(chosen, image_dist[:, None], 0.0), axis=0)
    phase = jnp.sum(jnp.where(chosen, image_phase[:, None], 0.0), axis=0)
    return jnp.stack([distance, jnp.cos(phase), jnp.sin(phase)])


def both_parts(factor):
    half = factor.shape[0] // 2
    return jnp.concatenate(
        [factor, jnp.concatenate([factor[half:], -factor[:half]], axis=0)], axis=1
    )


def slot_block(slots, items):
    digits = jnp.concatenate([slots // 128, slots % 128], axis=0).astype(items.dtype)
    fill = [(0, full - used) for full, used in zip(items.shape[1:], digits.shape)]
    return jnp.pad(digits, fill)[None]


def read_slots(packed, slots):
    count, share = slots.shape
    digits = packed[-1, 0 : 2 * count, 0:share].astype(jnp.int32)
    return digits[0:count] * 128 + digits[count:]


def after(value, *earlier):
    return lax.optimization_barrier((value, *earlier))[0] if earlier else value


def body(
    pair_ft,
    aux_ft,
    coul_weight,
    aux_basis,
    aux_decay,
    image_dist,
    image_phase,
    item_pair,
    item_image,
    item_sub,
    item_count,
):
    group_count = lax.axis_size("grp")
    member_count = lax.axis_size("dev")
    group = lax.axis_index("grp")
    member = lax.axis_index("dev")
    local_rows, _, local_g = pair_ft.shape
    subs = local_rows // item_pair.shape[2]
    rows = aux_ft.shape[0]
    row_count = rows * member_count // group_count
    half = jnp.reshape(group, (1,)).astype(jnp.int32)

    chips = member_count // CORES
    breadth = max(n for n in range(1, chips + 1) if chips % n == 0 and n * n <= chips)
    length = chips // breadth

    aux_flat = aux_ft.reshape(rows, 2 * local_g)
    pairs = pair_ft.astype(jnp.float32)
    weighted = (pairs * coul_weight[None, None, :]).astype(jnp.bfloat16)
    turned = weighted.reshape(local_rows, 2 * local_g).T
    item_rows = jnp.swapaxes(item_pair, 1, 2)
    live = (jnp.arange(item_image.shape[0], dtype=jnp.int32) < item_count[0]).astype(jnp.int32)
    slots = jnp.stack([item_image, item_sub, live])

    if group_count != 2 or length % 2:
        everything = lax.all_gather(aux_flat, "dev", axis=0, tiled=True)
        mine = lax.all_to_all(everything, "grp", split_axis=0, concat_axis=1, tiled=True)
        factor = lax.all_gather(turned, "grp", axis=0, tiled=True)
        parts = factor.reshape(group_count, 2, local_g, local_rows)
        other = jnp.stack([parts[:, 1], -parts[:, 0]], axis=1).reshape(factor.shape)
        long_part = jnp.concatenate(
            [
                jnp.dot(mine, factor, preferred_element_type=jnp.float32),
                jnp.dot(mine, other, preferred_element_type=jnp.float32),
            ],
            axis=1,
        )
        items = lax.all_gather(item_rows, "grp", axis=0, tiled=True)
        images, sub_ids, live = lax.all_gather(slots, "grp", axis=1, tiled=True)
        table = slot_table(image_dist, image_phase, images)
        short = short_range(
            half, live, sub_ids, table, aux_basis, aux_decay, [items], row_count, subs
        )
        return (long_part + short).astype(jnp.bfloat16).reshape(row_count, 2, local_rows)

    home = length // 2
    place = member // (breadth * CORES)
    across = member // CORES % breadth
    core = member % CORES

    def send(value, route):
        def index(g, z, y, c):
            return g * member_count + (z * breadth + y) * CORES + c

        pairs = []
        for g in range(group_count):
            for z in range(length):
                for y in range(breadth):
                    for c in range(CORES):
                        pairs.append((index(g, z, y, c), index(*route(g, z, y, c))))
        return lax.ppermute(value, AXES, pairs)

    def to_plane(value):
        return send(value, lambda g, z, y, c: (1 - g, z, y, c))

    ring = [*range(0, length, 2), *reversed(range(1, length, 2))]
    turn = {z: n for n, z in enumerate(ring)}

    def along(value, step):
        return send(value, lambda g, z, y, c: (g, ring[(turn[z] + step) % length], y, c))

    def over_y(value, s):
        return send(value, lambda g, z, y, c: (g, z, (y + s) % breadth, c))

    def over_core(value, t):
        return send(value, lambda g, z, y, c: (g, z, y, (c + t) % CORES))

    def hops_of(g, z):
        hops = [(turn[z] - turn[j]) % length for j in range(g * home, (g + 1) * home)]
        return sorted(hops, key=lambda k: (min(k, length - k), k))

    def here(number):
        return sum(
            jnp.where((group == g) & (place == z), number(g, z), 0)
            for g in range(group_count)
            for z in range(length)
        )

    def pick(other, n, *earlier):
        wanted = here(lambda g, z: hops_of(g ^ other, z)[n])
        possible = sorted({hops_of(g, z)[n] for g in range(group_count) for z in range(length)})
        blocks = lax.optimization_barrier((*(held[k] for k in possible), *earlier))
        value = blocks[len(possible) - 1]
        for k, block in reversed(list(zip(possible[:-1], blocks))):
            value = jnp.where(wanted == k, block, value)
        return value

    def slab_of(n):
        return here(lambda g, z: ring[(turn[z] - hops_of(g, z)[n]) % length] - g * home)

    def number_of(n, s, t):
        return (slab_of(n) * breadth + (across - s) % breadth) * CORES + (core - t) % CORES

    def with_cores(value):
        return [value] + [over_core(value, t) for t in range(1, CORES)]

    held = {0: aux_flat, 1: along(aux_flat, 1), length - 1: along(aux_flat, -1)}
    packed = jnp.concatenate([item_rows, slot_block(slots, item_rows)], axis=0)
    turned_x = to_plane(turned)
    factors = [[turned, turned_x]] + [[over_y(turned, s)] for s in range(1, breadth)]
    items_x = to_plane(packed)
    mine = []
    theirs = []
    crossed = []
    away = []
    arriving = []

    def foreign(n, *earlier):
        theirs.append(pick(True, n, *earlier))
        return to_plane(theirs[n])

    def multiply(n, t, away_factors):
        made = []
        if breadth > 1:
            made = long_range([(mine[n][t], crossed[n][t])], away_factors, local_rows)
        away[n].extend(made)
        arriving[n].append([over_y(v, s) for s, v in enumerate(made, 1)])

    def short_part(slots, items, *how):
        images, sub_ids, live = slots
        table = slot_table(image_dist, image_phase, images)
        return short_range(
            half, live, sub_ids, table, aux_basis, aux_decay, [items], row_count, subs, *how
        )

    short = short_part(slots, packed, None, False)

    moved = foreign(0, short)
    begun = [turned_x, *(pair[0] for pair in factors[1:])]
    for k in range(2, length // 2 + 1):
        held[k] = along(after(held[k - 1], held[1], held[length - 1], short), 1)
    for k in range(2, (length + 1) // 2):
        held[length - k] = along(after(held[length - k + 1], held[1], held[length - 1], short), -1)
    for s in range(1, breadth):
        factors[s].append(over_y(after(turned_x, theirs[0], *begun), s))

    short = short_part(read_slots(after(items_x, theirs[0], *begun), slots), items_x, short)

    def arrived_of(n):
        return [
            [(v, number_of(n, s, t)) for s, v in enumerate(arriving[n][t], 1)] for t in range(CORES)
        ]

    out = None
    for n in range(home):
        if n:
            moved = foreign(n, theirs[n - 1], *(away[n - 2] if n > 1 else [short]))
        away.append([])
        arriving.append([])
        mine.append(with_cores(pick(False, n, theirs[n], *([*away[n - 1], out] if n else begun))))
        away_factors = factors[1:]
        if n:
            away_factors = [[both_parts(after(v, *away[0])) for v in pair] for pair in factors[1:]]
        crossed.append(with_cores(moved if n else after(moved, short)))
        for t in range(CORES):
            multiply(n, t, away_factors)
        blocks = [
            (after(mine[n][0], *away[n]), crossed[n][0]),
            *zip(mine[n][1:], crossed[n][1:]),
        ]
        numbers = [number_of(n, 0, t) for t in range(CORES)]
        pieces = []
        if n:
            come = [(v, number) for entries in arrived_of(n - 1) for v, number in entries]
            pieces = [v for v, _ in come]
            numbers += [number for _, number in come]
        out = own_sum(jnp.stack(numbers).astype(jnp.int32), blocks, factors[0], pieces, short, out)
    for entries in arrived_of(home - 1):
        if entries:
            order = jnp.stack([number for _, number in entries]).astype(jnp.int32)
            out = final_sum(order, [piece for piece, _ in entries], short, out, rows)
    return out


def solution(mesh):
    return jax.shard_map(
        body,
        mesh=mesh,
        in_specs=(
            P("dev", None, "grp"),
            P("dev", None, "grp"),
            P("grp"),
            P(),
            P(),
            P(),
            P(),
            P(("grp", "dev"), None, None),
            P(("grp", "dev")),
            P(("grp", "dev")),
            P(("grp", "dev")),
        ),
        out_specs=P("grp", None, "dev"),
        check_vma=False,
    )
```

```python
import functools

import jax
import jax.numpy as jnp
from jax import lax
from jax.experimental import pallas as pl
from jax.experimental.pallas import tpu as pltpu
from jax.sharding import PartitionSpec as P

AXES = ("grp", "dev")
CORES = 2
SMALL_COST = pl.CostEstimate(flops=1, bytes_accessed=1, transcendentals=0)
GROUP_ITEMS = 4
SHORT_VMEM_BYTES = 20 * 1024 * 1024
VMEM_BYTES = 10 * 1024 * 1024


def in_hbm(value):
    return pltpu.with_memory_space_constraint(value, pltpu.HBM)


def short_kernel(
    half_ref, live_ref, sub_ref, meta_ref, basis_ref, decay_ref, *refs, share, subs, depth, width, adds, finishes
):
    items, scratch = refs[: -10 - adds], refs[-10:]
    out_ref, basis, left, acc, made, dists, group_sub, cursor, basis_sem, out_sem = scratch
    slots = share * len(items)
    row_count = acc.shape[2]
    tile = made.shape[1]
    if adds:
        acc_copy = pltpu.make_async_copy(refs[-11], acc, out_sem.at[0])
        acc_copy.start()
    else:
        acc[...] = jnp.zeros_like(acc)
    mine = pl.ds(pl.multiple_of(half_ref[0] * row_count, row_count), row_count)
    basis_copy = pltpu.make_async_copy(basis_ref.at[:, mine], basis, basis_sem)
    basis_copy.start()
    left[...] = jnp.zeros_like(left)

    for s in range(subs):
        cursor[s] = 0

    def count(i, carry):
        cursor[sub_ref[i]] = cursor[sub_ref[i]] + live_ref[i]
        return carry

    lax.fori_loop(0, slots, count, 0)
    first = jnp.int32(0)
    for s in range(subs):
        groups = (cursor[s] + GROUP_ITEMS - 1) // GROUP_ITEMS

        def mark(i, carry, s=s):
            group_sub[i] = s
            return carry

        lax.fori_loop(first, first + groups, mark, 0)
        cursor[s] = first * GROUP_ITEMS
        first = first + groups

    def clear(i, carry):
        dists[i] = 0.0
        return carry

    lax.fori_loop(0, first * GROUP_ITEMS, clear, 0)

    for n, items_ref in enumerate(items):

        def place(k, carry, first=n * share, items_ref=items_ref):
            i = first + k

            @pl.when(live_ref[i] > 0)
            def _():
                s = sub_ref[i]
                at = cursor[s]
                cursor[s] = at + 1
                dists[at] = meta_ref[0, i]
                turned = items_ref[k].astype(jnp.float32)
                lanes = pl.ds(pl.multiple_of((at % GROUP_ITEMS) * depth, depth), depth)
                group = at // GROUP_ITEMS
                left[group, 0:width, lanes] = (turned * meta_ref[1, i]).astype(left.dtype)
                left[group, width:, lanes] = (turned * meta_ref[2, i]).astype(left.dtype)

            return carry

        lax.fori_loop(0, share, place, 0)

    decay = decay_ref[:, mine]
    basis_copy.wait()
    if adds:
        acc_copy.wait()

    def one_group(group, carry):
        s = group_sub[group]
        damping = [
            jnp.exp(decay * -dists[group * GROUP_ITEMS + k]).astype(basis.dtype)
            for k in range(GROUP_ITEMS)
        ]
        for t in range(0, row_count, tile):
            right = jnp.concatenate(
                [
                    basis[:, t : t + tile] * damping[k][:, t : t + tile]
                    for k in range(GROUP_ITEMS)
                ],
                axis=0,
            )
            acc[s, :, t : t + tile] += jnp.dot(
                left[group], right, preferred_element_type=jnp.float32
            )
        return carry

    lax.fori_loop(0, first, one_group, 0)
    if not finishes:
        acc_copy = pltpu.make_async_copy(acc, out_ref, out_sem.at[0])
        acc_copy.start()
        acc_copy.wait()
        return
    copies = []
    for n, t in enumerate(range(0, row_count, tile)):
        for s in range(subs):
            for c in range(2):
                column = (c * subs + s) * width
                made[n, :, column : column + width] = acc[
                    s, c * width : (c + 1) * width, t : t + tile
                ].T
        copies.append(pltpu.make_async_copy(made.at[n], out_ref.at[pl.ds(t, tile), :], out_sem.at[n]))
        copies[-1].start()
    for copy in copies:
        copy.wait()


def short_range(half, live, sub_ids, meta, aux_basis, aux_decay, items, row_count, subs, earlier=None, finishes=True):
    adds = earlier is not None
    _, width, depth = items[0].shape
    slots = live.shape[0]
    share = slots // len(items)
    groups = slots // GROUP_ITEMS + subs
    tile = min(row_count, 512)
    kernel = functools.partial(
        short_kernel, share=share, subs=subs, depth=depth, width=width, adds=adds, finishes=finishes
    )
    return pl.pallas_call(
        kernel,
        out_shape=pltpu.HBM(
            (row_count, 2 * subs * width) if finishes else (subs, 2 * width, row_count), jnp.float32
        ),
        in_specs=[pl.BlockSpec(memory_space=pltpu.SMEM)] * 4
        + [pl.BlockSpec(memory_space=pltpu.HBM)]
        + [pl.BlockSpec(memory_space=pltpu.VMEM)] * (1 + len(items))
        + [pl.BlockSpec(memory_space=pltpu.HBM)] * adds,
        out_specs=pl.BlockSpec(memory_space=pltpu.HBM),
        scratch_shapes=[
            pltpu.VMEM((depth, row_count), jnp.bfloat16),
            pltpu.VMEM((groups, 2 * width, GROUP_ITEMS * depth), jnp.bfloat16),
            pltpu.VMEM((subs, 2 * width, row_count), jnp.float32),
            pltpu.VMEM((row_count // tile, tile, 2 * subs * width), jnp.float32),
            pltpu.SMEM((groups * GROUP_ITEMS,), jnp.float32),
            pltpu.SMEM((groups,), jnp.int32),
            pltpu.SMEM((subs,), jnp.int32),
            pltpu.SemaphoreType.DMA,
            pltpu.SemaphoreType.DMA((row_count // tile,)),
        ],
        compiler_params=pltpu.CompilerParams(vmem_limit_bytes=SHORT_VMEM_BYTES),
        cost_estimate=pl.CostEstimate(
            flops=4 * row_count * slots * depth * width, bytes_accessed=1, transcendentals=0
        ),
        name="short_range",
    )(
        half,
        live,
        sub_ids,
        meta,
        in_hbm(aux_basis),
        aux_decay.reshape(1, -1),
        *items,
        *([in_hbm(earlier)] if adds else []),
    )


def long_kernel(*refs, blocks, chains, pieces, width):
    parts = refs[: blocks * chains]
    factors = refs[blocks * chains : (blocks + pieces) * chains]
    outs, scratch = refs[(blocks + pieces) * chains :][:pieces], refs[-pieces - 2 :]
    right, made, out_sem = scratch[0], scratch[1:-1], scratch[-1]
    depth = factors[0].shape[0]
    half = depth // 2
    count = parts[0].shape[0]
    copies = []
    for piece in reversed(range(pieces)):
        for chain in range(chains):
            factor = factors[piece * chains + chain]
            top = chain * depth
            if factor.shape[1] > width:
                right[top : top + depth, :] = factor[...]
                continue
            right[top : top + depth, 0:width] = factor[...]
            right[top : top + half, width:] = factor[half:, :]
            right[top + half : top + depth, width:] = -factor[0:half, :]
        for block in range(blocks):
            left = jnp.concatenate(
                [parts[block * chains + chain][...] for chain in range(chains)], axis=1
            )
            total = jnp.dot(left, right[...], preferred_element_type=jnp.float32)
            made[piece][block] = total.astype(outs[piece].dtype)
            target = outs[piece].at[pl.ds(block * count, count), :]
            copies.append(
                pltpu.make_async_copy(made[piece].at[block], target, out_sem.at[piece, block])
            )
            copies[-1].start()
    for copy in copies:
        copy.wait()


def long_range(blocks, factors, width):
    depth = factors[0][0].shape[0]
    chains = len(factors[0])
    pieces = len(factors)
    count = blocks[0][0].shape[0]
    shape = (len(blocks) * count, 2 * width)
    dtypes = [jnp.bfloat16] * pieces
    flat = [v for group in [*blocks, *factors] for v in group]
    return pl.pallas_call(
        functools.partial(
            long_kernel, blocks=len(blocks), chains=chains, pieces=pieces, width=width
        ),
        out_shape=[pltpu.HBM(shape, dtype) for dtype in dtypes],
        in_specs=[pl.BlockSpec(memory_space=pltpu.VMEM)] * len(flat),
        out_specs=[pl.BlockSpec(memory_space=pltpu.HBM)] * pieces,
        scratch_shapes=[pltpu.VMEM((chains * depth, 2 * width), jnp.bfloat16)]
        + [pltpu.VMEM((len(blocks), count, 2 * width), dtype) for dtype in dtypes]
        + [pltpu.SemaphoreType.DMA((pieces, len(blocks)))],
        compiler_params=pltpu.CompilerParams(vmem_limit_bytes=VMEM_BYTES),
        cost_estimate=SMALL_COST,
        name="long_range",
    )(*flat)


def own_kernel(order_ref, *refs, blocks, chains, pieces, aliased):
    parts = refs[: blocks * chains]
    factors = refs[blocks * chains : (blocks + 1) * chains]
    arrived = refs[(blocks + 1) * chains :][:pieces]
    short_ref = refs[(blocks + 1) * chains + pieces]
    out_ref, right, terms, made, term_sem, out_sem = refs[(blocks + 1) * chains + pieces + 1 + aliased :]
    rows = terms.shape[1]
    depth, width = factors[0].shape
    half = depth // 2
    windows = [pl.ds(pl.multiple_of(order_ref[n] * rows, rows), rows) for n in range(blocks + pieces)]
    arriving = []
    for n, window in enumerate(windows):
        arriving.append(
            pltpu.make_async_copy(short_ref.at[window, :], terms.at[n], term_sem.at[n])
        )
        arriving[-1].start()
    for chain, factor in enumerate(factors):
        top = chain * depth
        right[top : top + depth, 0:width] = factor[...]
        right[top : top + half, width:] = factor[half:, :]
        right[top + half : top + depth, width:] = -factor[0:half, :]
    leaving = []
    for n, window in enumerate(windows):
        if n < blocks:
            left = [parts[n * chains + chain][...] for chain in range(chains)]
            left = jnp.concatenate(left, axis=1)
            total = jnp.dot(left, right[...], preferred_element_type=jnp.float32)
        else:
            total = arrived[n - blocks][...].astype(jnp.float32)
        arriving[n].wait()
        made[n] = (total + terms[n]).astype(made.dtype).reshape(made.shape[1:])
        leaving.append(pltpu.make_async_copy(made.at[n], out_ref.at[window], out_sem.at[n]))
        leaving[-1].start()
    for copy in leaving:
        copy.wait()


def own_sum(order, blocks, factors, pieces, short, earlier):
    rows, depth = blocks[0][0].shape
    width = factors[0].shape[1]
    row_count, columns = short.shape
    chains = len(factors)
    count = len(blocks) + len(pieces)
    aliased = earlier is not None
    flat = [v for group in [*blocks, factors, pieces] for v in group]
    return pl.pallas_call(
        functools.partial(
            own_kernel, blocks=len(blocks), chains=chains, pieces=len(pieces), aliased=aliased
        ),
        out_shape=pltpu.HBM((row_count, 2, width), jnp.bfloat16),
        in_specs=[pl.BlockSpec(memory_space=pltpu.SMEM)]
        + [pl.BlockSpec(memory_space=pltpu.VMEM)] * len(flat)
        + [pl.BlockSpec(memory_space=pltpu.HBM)] * (1 + aliased),
        out_specs=pl.BlockSpec(memory_space=pltpu.HBM),
        scratch_shapes=[
            pltpu.VMEM((chains * depth, 2 * width), jnp.bfloat16),
            pltpu.VMEM((count, rows, columns), jnp.float32),
            pltpu.VMEM((count, rows, 2, width), jnp.bfloat16),
            pltpu.SemaphoreType.DMA((count,)),
            pltpu.SemaphoreType.DMA((count,)),
        ],
        input_output_aliases={len(flat) + 2: 0} if aliased else {},
        compiler_params=pltpu.CompilerParams(vmem_limit_bytes=VMEM_BYTES),
        cost_estimate=SMALL_COST,
        name="own_sum",
    )(order, *flat, in_hbm(short), *([earlier] if aliased else []))


def final_kernel(order_ref, *refs, pieces, blocks, aliased):
    short_ref = refs[pieces]
    out_ref, terms, made, term_sem, out_sem = refs[pieces + 1 + aliased :]
    steps, rows = terms.shape[:2]
    windows = [pl.ds(pl.multiple_of(order_ref[n] * rows, rows), rows) for n in range(steps)]
    arriving = []
    for n, window in enumerate(windows):
        arriving.append(
            pltpu.make_async_copy(short_ref.at[window, :], terms.at[n], term_sem.at[n])
        )
        arriving[-1].start()
    leaving = []
    for n, window in enumerate(windows):
        arriving[n].wait()
        top = n % blocks * rows
        total = refs[n // blocks][top : top + rows, :].astype(jnp.float32) + terms[n]
        made[n] = total.astype(made.dtype).reshape(made.shape[1:])
        leaving.append(pltpu.make_async_copy(made.at[n], out_ref.at[window], out_sem.at[n]))
        leaving[-1].start()
    for copy in leaving:
        copy.wait()


def final_sum(order, pieces, short, earlier, rows):
    columns = pieces[0].shape[1]
    row_count = short.shape[0]
    count = len(pieces)
    blocks = pieces[0].shape[0] // rows
    steps = count * blocks
    return pl.pallas_call(
        functools.partial(final_kernel, pieces=count, blocks=blocks, aliased=True),
        out_shape=pltpu.HBM((row_count, 2, columns // 2), jnp.bfloat16),
        in_specs=[pl.BlockSpec(memory_space=pltpu.SMEM)]
        + [pl.BlockSpec(memory_space=pltpu.VMEM)] * count
        + [pl.BlockSpec(memory_space=pltpu.HBM)] * 2,
        out_specs=pl.BlockSpec(memory_space=pltpu.HBM),
        scratch_shapes=[
            pltpu.VMEM((steps, rows, columns), jnp.float32),
            pltpu.VMEM((steps, rows, 2, columns // 2), jnp.bfloat16),
            pltpu.SemaphoreType.DMA((steps,)),
            pltpu.SemaphoreType.DMA((steps,)),
        ],
        input_output_aliases={count + 2: 0},
        compiler_params=pltpu.CompilerParams(vmem_limit_bytes=VMEM_BYTES),
        cost_estimate=SMALL_COST,
        name="final_sum",
    )(order, *pieces, in_hbm(short), earlier)


def slot_table(image_dist, image_phase, images):
    chosen = images[None, :] == jnp.arange(image_dist.shape[0], dtype=jnp.int32)[:, None]
    distance = jnp.sum(jnp.where(chosen, image_dist[:, None], 0.0), axis=0)
    phase = jnp.sum(jnp.where(chosen, image_phase[:, None], 0.0), axis=0)
    return jnp.stack([distance, jnp.cos(phase), jnp.sin(phase)])


def both_parts(factor):
    half = factor.shape[0] // 2
    return jnp.concatenate(
        [factor, jnp.concatenate([factor[half:], -factor[:half]], axis=0)], axis=1
    )


def slot_block(slots, items):
    digits = jnp.concatenate([slots // 128, slots % 128], axis=0).astype(items.dtype)
    fill = [(0, full - used) for full, used in zip(items.shape[1:], digits.shape)]
    return jnp.pad(digits, fill)[None]


def read_slots(packed, slots):
    count, share = slots.shape
    digits = packed[-1, 0 : 2 * count, 0:share].astype(jnp.int32)
    return digits[0:count] * 128 + digits[count:]


def after(value, *earlier):
    return lax.optimization_barrier((value, *earlier))[0] if earlier else value


def body(
    pair_ft,
    aux_ft,
    coul_weight,
    aux_basis,
    aux_decay,
    image_dist,
    image_phase,
    item_pair,
    item_image,
    item_sub,
    item_count,
):
    group_count = lax.axis_size("grp")
    member_count = lax.axis_size("dev")
    group = lax.axis_index("grp")
    member = lax.axis_index("dev")
    local_rows, _, local_g = pair_ft.shape
    subs = local_rows // item_pair.shape[2]
    rows = aux_ft.shape[0]
    row_count = rows * member_count // group_count
    half = jnp.reshape(group, (1,)).astype(jnp.int32)

    chips = member_count // CORES
    breadth = max(n for n in range(1, chips + 1) if chips % n == 0 and n * n <= chips)
    length = chips // breadth

    aux_flat = aux_ft.reshape(rows, 2 * local_g)
    pairs = pair_ft.astype(jnp.float32)
    weighted = (pairs * coul_weight[None, None, :]).astype(jnp.bfloat16)
    turned = weighted.reshape(local_rows, 2 * local_g).T
    item_rows = jnp.swapaxes(item_pair, 1, 2)
    live = (jnp.arange(item_image.shape[0], dtype=jnp.int32) < item_count[0]).astype(jnp.int32)
    slots = jnp.stack([item_image, item_sub, live])

    if group_count != 2 or length % 2:
        everything = lax.all_gather(aux_flat, "dev", axis=0, tiled=True)
        mine = lax.all_to_all(everything, "grp", split_axis=0, concat_axis=1, tiled=True)
        factor = lax.all_gather(turned, "grp", axis=0, tiled=True)
        parts = factor.reshape(group_count, 2, local_g, local_rows)
        other = jnp.stack([parts[:, 1], -parts[:, 0]], axis=1).reshape(factor.shape)
        long_part = jnp.concatenate(
            [
                jnp.dot(mine, factor, preferred_element_type=jnp.float32),
                jnp.dot(mine, other, preferred_element_type=jnp.float32),
            ],
            axis=1,
        )
        items = lax.all_gather(item_rows, "grp", axis=0, tiled=True)
        images, sub_ids, live = lax.all_gather(slots, "grp", axis=1, tiled=True)
        table = slot_table(image_dist, image_phase, images)
        short = short_range(
            half, live, sub_ids, table, aux_basis, aux_decay, [items], row_count, subs
        )
        return (long_part + short).astype(jnp.bfloat16).reshape(row_count, 2, local_rows)

    home = length // 2
    place = member // (breadth * CORES)
    across = member // CORES % breadth
    core = member % CORES

    def send(value, route):
        def index(g, z, y, c):
            return g * member_count + (z * breadth + y) * CORES + c

        pairs = []
        for g in range(group_count):
            for z in range(length):
                for y in range(breadth):
                    for c in range(CORES):
                        pairs.append((index(g, z, y, c), index(*route(g, z, y, c))))
        return lax.ppermute(value, AXES, pairs)

    def to_plane(value):
        return send(value, lambda g, z, y, c: (1 - g, z, y, c))

    ring = [*range(0, length, 2), *reversed(range(1, length, 2))]
    turn = {z: n for n, z in enumerate(ring)}

    def along(value, step):
        return send(value, lambda g, z, y, c: (g, ring[(turn[z] + step) % length], y, c))

    def over_y(value, s):
        return send(value, lambda g, z, y, c: (g, z, (y + s) % breadth, c))

    def over_core(value, t):
        return send(value, lambda g, z, y, c: (g, z, y, (c + t) % CORES))

    def hops_of(g, z):
        hops = [(turn[z] - turn[j]) % length for j in range(g * home, (g + 1) * home)]
        return sorted(hops, key=lambda k: (min(k, length - k), k))

    def here(number):
        return sum(
            jnp.where((group == g) & (place == z), number(g, z), 0)
            for g in range(group_count)
            for z in range(length)
        )

    def pick(other, n, *earlier):
        wanted = here(lambda g, z: hops_of(g ^ other, z)[n])
        possible = sorted({hops_of(g, z)[n] for g in range(group_count) for z in range(length)})
        blocks = lax.optimization_barrier((*(held[k] for k in possible), *earlier))
        value = blocks[len(possible) - 1]
        for k, block in reversed(list(zip(possible[:-1], blocks))):
            value = jnp.where(wanted == k, block, value)
        return value

    def slab_of(n):
        return here(lambda g, z: ring[(turn[z] - hops_of(g, z)[n]) % length] - g * home)

    def number_of(n, s, t):
        return (slab_of(n) * breadth + (across - s) % breadth) * CORES + (core - t) % CORES

    def with_cores(value):
        return [value] + [over_core(value, t) for t in range(1, CORES)]

    held = {0: aux_flat, 1: along(aux_flat, 1), length - 1: along(aux_flat, -1)}
    packed = jnp.concatenate([item_rows, slot_block(slots, item_rows)], axis=0)
    turned_x = to_plane(turned)
    factors = [[turned, turned_x]] + [[over_y(turned, s)] for s in range(1, breadth)]
    items_x = to_plane(packed)
    mine = []
    theirs = []
    crossed = []
    away = []
    arriving = []

    def foreign(n, *earlier):
        theirs.append(pick(True, n, *earlier))
        return to_plane(theirs[n])

    def multiply(n, t, away_factors):
        made = []
        if breadth > 1:
            made = long_range([(mine[n][t], crossed[n][t])], away_factors, local_rows)
        away[n].extend(made)
        arriving[n].append([over_y(v, s) for s, v in enumerate(made, 1)])

    def short_part(slots, items, *how):
        images, sub_ids, live = slots
        table = slot_table(image_dist, image_phase, images)
        return short_range(
            half, live, sub_ids, table, aux_basis, aux_decay, [items], row_count, subs, *how
        )

    short = short_part(slots, packed, None, False)

    moved = foreign(0, short)
    begun = [turned_x, *(pair[0] for pair in factors[1:])]
    for k in range(2, length // 2 + 1):
        held[k] = along(after(held[k - 1], held[1], held[length - 1], short), 1)
    for k in range(2, (length + 1) // 2):
        held[length - k] = along(after(held[length - k + 1], held[1], held[length - 1], short), -1)
    for s in range(1, breadth):
        factors[s].append(over_y(after(turned_x, theirs[0], *begun), s))

    short = short_part(read_slots(after(items_x, theirs[0], *begun), slots), items_x, short)

    def arrived_of(n):
        return [
            [(v, number_of(n, s, t)) for s, v in enumerate(arriving[n][t], 1)] for t in range(CORES)
        ]

    out = None
    for n in range(home):
        if n:
            moved = foreign(n, theirs[n - 1], *(away[n - 2] if n > 1 else [short]))
        away.append([])
        arriving.append([])
        mine.append(with_cores(pick(False, n, theirs[n], *([*away[n - 1], out] if n else begun))))
        away_factors = factors[1:]
        if n:
            away_factors = [[both_parts(after(v, *away[0])) for v in pair] for pair in factors[1:]]
        crossed.append(with_cores(moved if n else after(moved, short, held[length // 2])))
        for t in range(CORES):
            multiply(n, t, away_factors)
        blocks = [
            (after(mine[n][0], *away[n]), crossed[n][0]),
            *zip(mine[n][1:], crossed[n][1:]),
        ]
        numbers = [number_of(n, 0, t) for t in range(CORES)]
        pieces = []
        if n:
            come = [(v, number) for entries in arrived_of(n - 1) for v, number in entries]
            pieces = [v for v, _ in come]
            numbers += [number for _, number in come]
        out = own_sum(jnp.stack(numbers).astype(jnp.int32), blocks, factors[0], pieces, short, out)
    for entries in arrived_of(home - 1):
        if entries:
            order = jnp.stack([number for _, number in entries]).astype(jnp.int32)
            out = final_sum(order, [piece for piece, _ in entries], short, out, rows)
    return out


def solution(mesh):
    return jax.shard_map(
        body,
        mesh=mesh,
        in_specs=(
            P("dev", None, "grp"),
            P("dev", None, "grp"),
            P("grp"),
            P(),
            P(),
            P(),
            P(),
            P(("grp", "dev"), None, None),
            P(("grp", "dev")),
            P(("grp", "dev")),
            P(("grp", "dev")),
        ),
        out_specs=P("grp", None, "dev"),
        check_vma=False,
    )
```

```python
import functools

import jax
import jax.numpy as jnp
from jax import lax
from jax.experimental import pallas as pl
from jax.experimental.pallas import tpu as pltpu
from jax.sharding import PartitionSpec as P

AXES = ("grp", "dev")
CORES = 2
SMALL_COST = pl.CostEstimate(flops=1, bytes_accessed=1, transcendentals=0)
GROUP_ITEMS = 4
SHORT_VMEM_BYTES = 20 * 1024 * 1024
VMEM_BYTES = 10 * 1024 * 1024


def in_hbm(value):
    return pltpu.with_memory_space_constraint(value, pltpu.HBM)


def short_kernel(
    half_ref, live_ref, sub_ref, meta_ref, basis_ref, decay_ref, *refs, share, subs, depth, width, adds, finishes
):
    items, scratch = refs[: -10 - adds], refs[-10:]
    out_ref, basis, left, acc, made, dists, group_sub, cursor, basis_sem, out_sem = scratch
    slots = share * len(items)
    row_count = acc.shape[2]
    tile = made.shape[1]
    if adds:
        acc_copy = pltpu.make_async_copy(refs[-11], acc, out_sem.at[0])
        acc_copy.start()
    else:
        acc[...] = jnp.zeros_like(acc)
    mine = pl.ds(pl.multiple_of(half_ref[0] * row_count, row_count), row_count)
    basis_copy = pltpu.make_async_copy(basis_ref.at[:, mine], basis, basis_sem)
    basis_copy.start()
    left[...] = jnp.zeros_like(left)

    for s in range(subs):
        cursor[s] = 0

    def count(i, carry):
        cursor[sub_ref[i]] = cursor[sub_ref[i]] + live_ref[i]
        return carry

    lax.fori_loop(0, slots, count, 0)
    first = jnp.int32(0)
    for s in range(subs):
        groups = (cursor[s] + GROUP_ITEMS - 1) // GROUP_ITEMS

        def mark(i, carry, s=s):
            group_sub[i] = s
            return carry

        lax.fori_loop(first, first + groups, mark, 0)
        cursor[s] = first * GROUP_ITEMS
        first = first + groups

    def clear(i, carry):
        dists[i] = 0.0
        return carry

    lax.fori_loop(0, first * GROUP_ITEMS, clear, 0)

    for n, items_ref in enumerate(items):

        def place(k, carry, first=n * share, items_ref=items_ref):
            i = first + k

            @pl.when(live_ref[i] > 0)
            def _():
                s = sub_ref[i]
                at = cursor[s]
                cursor[s] = at + 1
                dists[at] = meta_ref[0, i]
                turned = items_ref[k].astype(jnp.float32)
                lanes = pl.ds(pl.multiple_of((at % GROUP_ITEMS) * depth, depth), depth)
                group = at // GROUP_ITEMS
                left[group, 0:width, lanes] = (turned * meta_ref[1, i]).astype(left.dtype)
                left[group, width:, lanes] = (turned * meta_ref[2, i]).astype(left.dtype)

            return carry

        lax.fori_loop(0, share, place, 0)

    decay = decay_ref[:, mine]
    basis_copy.wait()
    if adds:
        acc_copy.wait()

    def one_group(group, carry):
        s = group_sub[group]
        damping = [
            jnp.exp(decay * -dists[group * GROUP_ITEMS + k]).astype(basis.dtype)
            for k in range(GROUP_ITEMS)
        ]
        for t in range(0, row_count, tile):
            right = jnp.concatenate(
                [
                    basis[:, t : t + tile] * damping[k][:, t : t + tile]
                    for k in range(GROUP_ITEMS)
                ],
                axis=0,
            )
            acc[s, :, t : t + tile] += jnp.dot(
                left[group], right, preferred_element_type=jnp.float32
            )
        return carry

    lax.fori_loop(0, first, one_group, 0)
    if not finishes:
        acc_copy = pltpu.make_async_copy(acc, out_ref, out_sem.at[0])
        acc_copy.start()
        acc_copy.wait()
        return
    copies = []
    for n, t in enumerate(range(0, row_count, tile)):
        for s in range(subs):
            for c in range(2):
                column = (c * subs + s) * width
                made[n, :, column : column + width] = acc[
                    s, c * width : (c + 1) * width, t : t + tile
                ].T
        copies.append(pltpu.make_async_copy(made.at[n], out_ref.at[pl.ds(t, tile), :], out_sem.at[n]))
        copies[-1].start()
    for copy in copies:
        copy.wait()


def short_range(half, live, sub_ids, meta, aux_basis, aux_decay, items, row_count, subs, earlier=None, finishes=True):
    adds = earlier is not None
    _, width, depth = items[0].shape
    slots = live.shape[0]
    share = slots // len(items)
    groups = slots // GROUP_ITEMS + subs
    tile = min(row_count, 512)
    kernel = functools.partial(
        short_kernel, share=share, subs=subs, depth=depth, width=width, adds=adds, finishes=finishes
    )
    return pl.pallas_call(
        kernel,
        out_shape=pltpu.HBM(
            (row_count, 2 * subs * width) if finishes else (subs, 2 * width, row_count), jnp.float32
        ),
        in_specs=[pl.BlockSpec(memory_space=pltpu.SMEM)] * 4
        + [pl.BlockSpec(memory_space=pltpu.HBM)]
        + [pl.BlockSpec(memory_space=pltpu.VMEM)] * (1 + len(items))
        + [pl.BlockSpec(memory_space=pltpu.HBM)] * adds,
        out_specs=pl.BlockSpec(memory_space=pltpu.HBM),
        scratch_shapes=[
            pltpu.VMEM((depth, row_count), jnp.bfloat16),
            pltpu.VMEM((groups, 2 * width, GROUP_ITEMS * depth), jnp.bfloat16),
            pltpu.VMEM((subs, 2 * width, row_count), jnp.float32),
            pltpu.VMEM((row_count // tile, tile, 2 * subs * width), jnp.float32),
            pltpu.SMEM((groups * GROUP_ITEMS,), jnp.float32),
            pltpu.SMEM((groups,), jnp.int32),
            pltpu.SMEM((subs,), jnp.int32),
            pltpu.SemaphoreType.DMA,
            pltpu.SemaphoreType.DMA((row_count // tile,)),
        ],
        compiler_params=pltpu.CompilerParams(vmem_limit_bytes=SHORT_VMEM_BYTES),
        cost_estimate=pl.CostEstimate(
            flops=4 * row_count * slots * depth * width, bytes_accessed=1, transcendentals=0
        ),
        name="short_range",
    )(
        half,
        live,
        sub_ids,
        meta,
        in_hbm(aux_basis),
        aux_decay.reshape(1, -1),
        *items,
        *([in_hbm(earlier)] if adds else []),
    )


def long_kernel(*refs, blocks, chains, pieces, width):
    parts = refs[: blocks * chains]
    factors = refs[blocks * chains : (blocks + pieces) * chains]
    outs, scratch = refs[(blocks + pieces) * chains :][:pieces], refs[-pieces - 2 :]
    right, made, out_sem = scratch[0], scratch[1:-1], scratch[-1]
    depth = factors[0].shape[0]
    half = depth // 2
    count = parts[0].shape[0]
    copies = []
    for piece in reversed(range(pieces)):
        for chain in range(chains):
            factor = factors[piece * chains + chain]
            top = chain * depth
            if factor.shape[1] > width:
                right[top : top + depth, :] = factor[...]
                continue
            right[top : top + depth, 0:width] = factor[...]
            right[top : top + half, width:] = factor[half:, :]
            right[top + half : top + depth, width:] = -factor[0:half, :]
        for block in range(blocks):
            left = jnp.concatenate(
                [parts[block * chains + chain][...] for chain in range(chains)], axis=1
            )
            total = jnp.dot(left, right[...], preferred_element_type=jnp.float32)
            made[piece][block] = total.astype(outs[piece].dtype)
            target = outs[piece].at[pl.ds(block * count, count), :]
            copies.append(
                pltpu.make_async_copy(made[piece].at[block], target, out_sem.at[piece, block])
            )
            copies[-1].start()
    for copy in copies:
        copy.wait()


def long_range(blocks, factors, width):
    depth = factors[0][0].shape[0]
    chains = len(factors[0])
    pieces = len(factors)
    count = blocks[0][0].shape[0]
    shape = (len(blocks) * count, 2 * width)
    dtypes = [jnp.bfloat16] * pieces
    flat = [v for group in [*blocks, *factors] for v in group]
    return pl.pallas_call(
        functools.partial(
            long_kernel, blocks=len(blocks), chains=chains, pieces=pieces, width=width
        ),
        out_shape=[pltpu.HBM(shape, dtype) for dtype in dtypes],
        in_specs=[pl.BlockSpec(memory_space=pltpu.VMEM)] * len(flat),
        out_specs=[pl.BlockSpec(memory_space=pltpu.HBM)] * pieces,
        scratch_shapes=[pltpu.VMEM((chains * depth, 2 * width), jnp.bfloat16)]
        + [pltpu.VMEM((len(blocks), count, 2 * width), dtype) for dtype in dtypes]
        + [pltpu.SemaphoreType.DMA((pieces, len(blocks)))],
        compiler_params=pltpu.CompilerParams(vmem_limit_bytes=VMEM_BYTES),
        cost_estimate=SMALL_COST,
        name="long_range",
    )(*flat)


def own_kernel(order_ref, *refs, blocks, chains, pieces, aliased):
    parts = refs[: blocks * chains]
    factors = refs[blocks * chains : (blocks + 1) * chains]
    arrived = refs[(blocks + 1) * chains :][:pieces]
    short_ref = refs[(blocks + 1) * chains + pieces]
    out_ref, right, terms, made, right_sem, term_sem, out_sem = refs[
        (blocks + 1) * chains + pieces + 1 + aliased :
    ]
    rows = terms.shape[1]
    depth, width = factors[0].shape
    half = depth // 2
    right_copies = []
    for chain, factor in enumerate(factors):
        target = right.at[pl.ds(chain * depth, depth), pl.ds(0, width)]
        right_copies.append(pltpu.make_async_copy(factor, target, right_sem.at[chain]))
        right_copies[-1].start()
    windows = [pl.ds(pl.multiple_of(order_ref[n] * rows, rows), rows) for n in range(blocks + pieces)]
    arriving = []
    for n, window in enumerate(windows):
        arriving.append(
            pltpu.make_async_copy(short_ref.at[window, :], terms.at[n], term_sem.at[n])
        )
        arriving[-1].start()
    for chain, copy in enumerate(right_copies):
        copy.wait()
        top = chain * depth
        right[top : top + half, width:] = right[top + half : top + depth, 0:width]
        right[top + half : top + depth, width:] = -right[top : top + half, 0:width]
    leaving = []
    for n, window in enumerate(windows):
        if n < blocks:
            left = [parts[n * chains + chain][...] for chain in range(chains)]
            left = jnp.concatenate(left, axis=1)
            total = jnp.dot(left, right[...], preferred_element_type=jnp.float32)
        else:
            total = arrived[n - blocks][...].astype(jnp.float32)
        arriving[n].wait()
        made[n] = (total + terms[n]).astype(made.dtype).reshape(made.shape[1:])
        leaving.append(pltpu.make_async_copy(made.at[n], out_ref.at[window], out_sem.at[n]))
        leaving[-1].start()
    for copy in leaving:
        copy.wait()


def own_sum(order, blocks, factors, pieces, short, earlier):
    rows, depth = blocks[0][0].shape
    width = factors[0].shape[1]
    row_count, columns = short.shape
    chains = len(factors)
    count = len(blocks) + len(pieces)
    aliased = earlier is not None
    flat = [v for group in blocks for v in group] + [in_hbm(v) for v in factors] + pieces
    return pl.pallas_call(
        functools.partial(
            own_kernel, blocks=len(blocks), chains=chains, pieces=len(pieces), aliased=aliased
        ),
        out_shape=pltpu.HBM((row_count, 2, width), jnp.bfloat16),
        in_specs=[pl.BlockSpec(memory_space=pltpu.SMEM)]
        + [pl.BlockSpec(memory_space=pltpu.VMEM)] * (chains * len(blocks))
        + [pl.BlockSpec(memory_space=pltpu.HBM)] * chains
        + [pl.BlockSpec(memory_space=pltpu.VMEM)] * len(pieces)
        + [pl.BlockSpec(memory_space=pltpu.HBM)] * (1 + aliased),
        out_specs=pl.BlockSpec(memory_space=pltpu.HBM),
        scratch_shapes=[
            pltpu.VMEM((chains * depth, 2 * width), jnp.bfloat16),
            pltpu.VMEM((count, rows, columns), jnp.float32),
            pltpu.VMEM((count, rows, 2, width), jnp.bfloat16),
            pltpu.SemaphoreType.DMA((chains,)),
            pltpu.SemaphoreType.DMA((count,)),
            pltpu.SemaphoreType.DMA((count,)),
        ],
        input_output_aliases={len(flat) + 2: 0} if aliased else {},
        compiler_params=pltpu.CompilerParams(vmem_limit_bytes=VMEM_BYTES),
        cost_estimate=SMALL_COST,
        name="own_sum",
    )(order, *flat, in_hbm(short), *([earlier] if aliased else []))


def final_kernel(order_ref, *refs, pieces, blocks, aliased):
    short_ref = refs[pieces]
    out_ref, terms, made, term_sem, out_sem = refs[pieces + 1 + aliased :]
    steps, rows = terms.shape[:2]
    windows = [pl.ds(pl.multiple_of(order_ref[n] * rows, rows), rows) for n in range(steps)]
    arriving = []
    for n, window in enumerate(windows):
        arriving.append(
            pltpu.make_async_copy(short_ref.at[window, :], terms.at[n], term_sem.at[n])
        )
        arriving[-1].start()
    leaving = []
    for n, window in enumerate(windows):
        arriving[n].wait()
        top = n % blocks * rows
        total = refs[n // blocks][top : top + rows, :].astype(jnp.float32) + terms[n]
        made[n] = total.astype(made.dtype).reshape(made.shape[1:])
        leaving.append(pltpu.make_async_copy(made.at[n], out_ref.at[window], out_sem.at[n]))
        leaving[-1].start()
    for copy in leaving:
        copy.wait()


def final_sum(order, pieces, short, earlier, rows):
    columns = pieces[0].shape[1]
    row_count = short.shape[0]
    count = len(pieces)
    blocks = pieces[0].shape[0] // rows
    steps = count * blocks
    return pl.pallas_call(
        functools.partial(final_kernel, pieces=count, blocks=blocks, aliased=True),
        out_shape=pltpu.HBM((row_count, 2, columns // 2), jnp.bfloat16),
        in_specs=[pl.BlockSpec(memory_space=pltpu.SMEM)]
        + [pl.BlockSpec(memory_space=pltpu.VMEM)] * count
        + [pl.BlockSpec(memory_space=pltpu.HBM)] * 2,
        out_specs=pl.BlockSpec(memory_space=pltpu.HBM),
        scratch_shapes=[
            pltpu.VMEM((steps, rows, columns), jnp.float32),
            pltpu.VMEM((steps, rows, 2, columns // 2), jnp.bfloat16),
            pltpu.SemaphoreType.DMA((steps,)),
            pltpu.SemaphoreType.DMA((steps,)),
        ],
        input_output_aliases={count + 2: 0},
        compiler_params=pltpu.CompilerParams(vmem_limit_bytes=VMEM_BYTES),
        cost_estimate=SMALL_COST,
        name="final_sum",
    )(order, *pieces, in_hbm(short), earlier)


def slot_table(image_dist, image_phase, images):
    chosen = images[None, :] == jnp.arange(image_dist.shape[0], dtype=jnp.int32)[:, None]
    distance = jnp.sum(jnp.where(chosen, image_dist[:, None], 0.0), axis=0)
    phase = jnp.sum(jnp.where(chosen, image_phase[:, None], 0.0), axis=0)
    return jnp.stack([distance, jnp.cos(phase), jnp.sin(phase)])


def both_parts(factor):
    half = factor.shape[0] // 2
    return jnp.concatenate(
        [factor, jnp.concatenate([factor[half:], -factor[:half]], axis=0)], axis=1
    )


def slot_block(slots, items):
    digits = jnp.concatenate([slots // 128, slots % 128], axis=0).astype(items.dtype)
    fill = [(0, full - used) for full, used in zip(items.shape[1:], digits.shape)]
    return jnp.pad(digits, fill)[None]


def read_slots(packed, slots):
    count, share = slots.shape
    digits = packed[-1, 0 : 2 * count, 0:share].astype(jnp.int32)
    return digits[0:count] * 128 + digits[count:]


def after(value, *earlier):
    return lax.optimization_barrier((value, *earlier))[0] if earlier else value


def body(
    pair_ft,
    aux_ft,
    coul_weight,
    aux_basis,
    aux_decay,
    image_dist,
    image_phase,
    item_pair,
    item_image,
    item_sub,
    item_count,
):
    group_count = lax.axis_size("grp")
    member_count = lax.axis_size("dev")
    group = lax.axis_index("grp")
    member = lax.axis_index("dev")
    local_rows, _, local_g = pair_ft.shape
    subs = local_rows // item_pair.shape[2]
    rows = aux_ft.shape[0]
    row_count = rows * member_count // group_count
    half = jnp.reshape(group, (1,)).astype(jnp.int32)

    chips = member_count // CORES
    breadth = max(n for n in range(1, chips + 1) if chips % n == 0 and n * n <= chips)
    length = chips // breadth

    aux_flat = aux_ft.reshape(rows, 2 * local_g)
    pairs = pair_ft.astype(jnp.float32)
    weighted = (pairs * coul_weight[None, None, :]).astype(jnp.bfloat16)
    turned = weighted.reshape(local_rows, 2 * local_g).T
    item_rows = jnp.swapaxes(item_pair, 1, 2)
    live = (jnp.arange(item_image.shape[0], dtype=jnp.int32) < item_count[0]).astype(jnp.int32)
    slots = jnp.stack([item_image, item_sub, live])

    if group_count != 2 or length % 2:
        everything = lax.all_gather(aux_flat, "dev", axis=0, tiled=True)
        mine = lax.all_to_all(everything, "grp", split_axis=0, concat_axis=1, tiled=True)
        factor = lax.all_gather(turned, "grp", axis=0, tiled=True)
        parts = factor.reshape(group_count, 2, local_g, local_rows)
        other = jnp.stack([parts[:, 1], -parts[:, 0]], axis=1).reshape(factor.shape)
        long_part = jnp.concatenate(
            [
                jnp.dot(mine, factor, preferred_element_type=jnp.float32),
                jnp.dot(mine, other, preferred_element_type=jnp.float32),
            ],
            axis=1,
        )
        items = lax.all_gather(item_rows, "grp", axis=0, tiled=True)
        images, sub_ids, live = lax.all_gather(slots, "grp", axis=1, tiled=True)
        table = slot_table(image_dist, image_phase, images)
        short = short_range(
            half, live, sub_ids, table, aux_basis, aux_decay, [items], row_count, subs
        )
        return (long_part + short).astype(jnp.bfloat16).reshape(row_count, 2, local_rows)

    home = length // 2
    place = member // (breadth * CORES)
    across = member // CORES % breadth
    core = member % CORES

    def send(value, route):
        def index(g, z, y, c):
            return g * member_count + (z * breadth + y) * CORES + c

        pairs = []
        for g in range(group_count):
            for z in range(length):
                for y in range(breadth):
                    for c in range(CORES):
                        pairs.append((index(g, z, y, c), index(*route(g, z, y, c))))
        return lax.ppermute(value, AXES, pairs)

    def to_plane(value):
        return send(value, lambda g, z, y, c: (1 - g, z, y, c))

    ring = [*range(0, length, 2), *reversed(range(1, length, 2))]
    turn = {z: n for n, z in enumerate(ring)}

    def along(value, step):
        return send(value, lambda g, z, y, c: (g, ring[(turn[z] + step) % length], y, c))

    def over_y(value, s):
        return send(value, lambda g, z, y, c: (g, z, (y + s) % breadth, c))

    def over_core(value, t):
        return send(value, lambda g, z, y, c: (g, z, y, (c + t) % CORES))

    def hops_of(g, z):
        hops = [(turn[z] - turn[j]) % length for j in range(g * home, (g + 1) * home)]
        return sorted(hops, key=lambda k: (min(k, length - k), k))

    def here(number):
        return sum(
            jnp.where((group == g) & (place == z), number(g, z), 0)
            for g in range(group_count)
            for z in range(length)
        )

    def pick(other, n, *earlier):
        wanted = here(lambda g, z: hops_of(g ^ other, z)[n])
        possible = sorted({hops_of(g, z)[n] for g in range(group_count) for z in range(length)})
        blocks = lax.optimization_barrier((*(held[k] for k in possible), *earlier))
        value = blocks[len(possible) - 1]
        for k, block in reversed(list(zip(possible[:-1], blocks))):
            value = jnp.where(wanted == k, block, value)
        return value

    def slab_of(n):
        return here(lambda g, z: ring[(turn[z] - hops_of(g, z)[n]) % length] - g * home)

    def number_of(n, s, t):
        return (slab_of(n) * breadth + (across - s) % breadth) * CORES + (core - t) % CORES

    def with_cores(value):
        return [value] + [over_core(value, t) for t in range(1, CORES)]

    held = {0: aux_flat, 1: along(aux_flat, 1), length - 1: along(aux_flat, -1)}
    packed = jnp.concatenate([item_rows, slot_block(slots, item_rows)], axis=0)
    turned_x = to_plane(turned)
    factors = [[turned, turned_x]] + [[over_y(turned, s)] for s in range(1, breadth)]
    items_x = to_plane(packed)
    mine = []
    theirs = []
    crossed = []
    away = []
    arriving = []

    def foreign(n, *earlier):
        theirs.append(pick(True, n, *earlier))
        return to_plane(theirs[n])

    def multiply(n, t, away_factors):
        made = []
        if breadth > 1:
            made = long_range([(mine[n][t], crossed[n][t])], away_factors, local_rows)
        away[n].extend(made)
        arriving[n].append([over_y(v, s) for s, v in enumerate(made, 1)])

    def short_part(slots, items, *how):
        images, sub_ids, live = slots
        table = slot_table(image_dist, image_phase, images)
        return short_range(
            half, live, sub_ids, table, aux_basis, aux_decay, [items], row_count, subs, *how
        )

    short = short_part(slots, packed, None, False)

    moved = foreign(0, short)
    begun = [turned_x, *(pair[0] for pair in factors[1:])]
    for k in range(2, length // 2 + 1):
        held[k] = along(after(held[k - 1], held[1], held[length - 1], short), 1)
    for k in range(2, (length + 1) // 2):
        held[length - k] = along(after(held[length - k + 1], held[1], held[length - 1], short), -1)
    for s in range(1, breadth):
        factors[s].append(over_y(after(turned_x, theirs[0], *begun), s))

    short = short_part(read_slots(after(items_x, theirs[0], *begun), slots), items_x, short)

    def arrived_of(n):
        return [
            [(v, number_of(n, s, t)) for s, v in enumerate(arriving[n][t], 1)] for t in range(CORES)
        ]

    out = None
    for n in range(home):
        if n:
            moved = foreign(n, theirs[n - 1], *(away[n - 2] if n > 1 else [short]))
        away.append([])
        arriving.append([])
        mine.append(with_cores(pick(False, n, theirs[n], *([*away[n - 1], out] if n else begun))))
        away_factors = factors[1:]
        if n:
            away_factors = [[both_parts(after(v, *away[0])) for v in pair] for pair in factors[1:]]
        crossed.append(with_cores(moved if n else after(moved, short, held[length // 2])))
        for t in range(CORES):
            multiply(n, t, away_factors)
        blocks = [
            (after(mine[n][0], *away[n]), crossed[n][0]),
            *zip(mine[n][1:], crossed[n][1:]),
        ]
        numbers = [number_of(n, 0, t) for t in range(CORES)]
        pieces = []
        if n:
            come = [(v, number) for entries in arrived_of(n - 1) for v, number in entries]
            pieces = [v for v, _ in come]
            numbers += [number for _, number in come]
        out = own_sum(jnp.stack(numbers).astype(jnp.int32), blocks, factors[0], pieces, short, out)
    for entries in arrived_of(home - 1):
        if entries:
            order = jnp.stack([number for _, number in entries]).astype(jnp.int32)
            out = final_sum(order, [piece for piece, _ in entries], short, out, rows)
    return out


def solution(mesh):
    return jax.shard_map(
        body,
        mesh=mesh,
        in_specs=(
            P("dev", None, "grp"),
            P("dev", None, "grp"),
            P("grp"),
            P(),
            P(),
            P(),
            P(),
            P(("grp", "dev"), None, None),
            P(("grp", "dev")),
            P(("grp", "dev")),
            P(("grp", "dev")),
        ),
        out_specs=P("grp", None, "dev"),
        check_vma=False,
    )
```

```python
import functools

import jax
import jax.numpy as jnp
from jax import lax
from jax.experimental import pallas as pl
from jax.experimental.pallas import tpu as pltpu
from jax.sharding import PartitionSpec as P

AXES = ("grp", "dev")
CORES = 2
SMALL_COST = pl.CostEstimate(flops=1, bytes_accessed=1, transcendentals=0)
GROUP_ITEMS = 4
SHORT_VMEM_BYTES = 15 * 1024 * 1024
VMEM_BYTES = 10 * 1024 * 1024


def in_hbm(value):
    return pltpu.with_memory_space_constraint(value, pltpu.HBM)


def short_kernel(
    half_ref, live_ref, sub_ref, meta_ref, basis_ref, decay_ref, *refs, share, subs, depth, width, adds, finishes, tile
):
    items, scratch = refs[: -10 - adds], refs[-10:]
    out_ref, basis, left, acc, made, dists, group_sub, cursor, basis_sem, out_sem = scratch
    slots = share * len(items)
    row_count = acc.shape[2]
    if adds:
        acc_copy = pltpu.make_async_copy(refs[-11], acc, out_sem.at[0])
        acc_copy.start()
    else:
        acc[...] = jnp.zeros_like(acc)
    mine = pl.ds(pl.multiple_of(half_ref[0] * row_count, row_count), row_count)
    basis_copy = pltpu.make_async_copy(basis_ref.at[:, mine], basis, basis_sem)
    basis_copy.start()
    left[...] = jnp.zeros_like(left)

    for s in range(subs):
        cursor[s] = 0

    def count(i, carry):
        cursor[sub_ref[i]] = cursor[sub_ref[i]] + live_ref[i]
        return carry

    lax.fori_loop(0, slots, count, 0)
    first = jnp.int32(0)
    for s in range(subs):
        groups = (cursor[s] + GROUP_ITEMS - 1) // GROUP_ITEMS

        def mark(i, carry, s=s):
            group_sub[i] = s
            return carry

        lax.fori_loop(first, first + groups, mark, 0)
        cursor[s] = first * GROUP_ITEMS
        first = first + groups

    def clear(i, carry):
        dists[i] = 0.0
        return carry

    lax.fori_loop(0, first * GROUP_ITEMS, clear, 0)

    for n, items_ref in enumerate(items):

        def place(k, carry, first=n * share, items_ref=items_ref):
            i = first + k

            @pl.when(live_ref[i] > 0)
            def _():
                s = sub_ref[i]
                at = cursor[s]
                cursor[s] = at + 1
                dists[at] = meta_ref[0, i]
                turned = items_ref[k].astype(jnp.float32)
                lanes = pl.ds(pl.multiple_of((at % GROUP_ITEMS) * depth, depth), depth)
                group = at // GROUP_ITEMS
                left[group, 0:width, lanes] = (turned * meta_ref[1, i]).astype(left.dtype)
                left[group, width:, lanes] = (turned * meta_ref[2, i]).astype(left.dtype)

            return carry

        lax.fori_loop(0, share, place, 0)

    decay = decay_ref[:, mine]
    basis_copy.wait()
    if adds:
        acc_copy.wait()

    def one_group(group, carry):
        s = group_sub[group]
        damping = [
            jnp.exp(decay * -dists[group * GROUP_ITEMS + k]).astype(basis.dtype)
            for k in range(GROUP_ITEMS)
        ]
        for t in range(0, row_count, tile):
            right = jnp.concatenate(
                [
                    basis[:, t : t + tile] * damping[k][:, t : t + tile]
                    for k in range(GROUP_ITEMS)
                ],
                axis=0,
            )
            acc[s, :, t : t + tile] += jnp.dot(
                left[group], right, preferred_element_type=jnp.float32
            )
        return carry

    lax.fori_loop(0, first, one_group, 0)
    if not finishes:
        acc_copy = pltpu.make_async_copy(acc, out_ref, out_sem.at[0])
        acc_copy.start()
        acc_copy.wait()
        return
    copies = []
    for n, t in enumerate(range(0, row_count, tile)):
        for s in range(subs):
            for c in range(2):
                column = (c * subs + s) * width
                made[n, :, column : column + width] = acc[
                    s, c * width : (c + 1) * width, t : t + tile
                ].T
        copies.append(pltpu.make_async_copy(made.at[n], out_ref.at[pl.ds(t, tile), :], out_sem.at[n]))
        copies[-1].start()
    for copy in copies:
        copy.wait()


def short_range(half, live, sub_ids, meta, aux_basis, aux_decay, items, row_count, subs, earlier=None, finishes=True):
    adds = earlier is not None
    _, width, depth = items[0].shape
    slots = live.shape[0]
    share = slots // len(items)
    groups = slots // GROUP_ITEMS + subs
    tile = min(row_count, 512)
    kernel = functools.partial(
        short_kernel, share=share, subs=subs, depth=depth, width=width, adds=adds, finishes=finishes, tile=tile
    )
    return pl.pallas_call(
        kernel,
        out_shape=pltpu.HBM(
            (row_count, 2 * subs * width) if finishes else (subs, 2 * width, row_count), jnp.float32
        ),
        in_specs=[pl.BlockSpec(memory_space=pltpu.SMEM)] * 4
        + [pl.BlockSpec(memory_space=pltpu.HBM)]
        + [pl.BlockSpec(memory_space=pltpu.VMEM)] * (1 + len(items))
        + [pl.BlockSpec(memory_space=pltpu.HBM)] * adds,
        out_specs=pl.BlockSpec(memory_space=pltpu.HBM),
        scratch_shapes=[
            pltpu.VMEM((depth, row_count), jnp.bfloat16),
            pltpu.VMEM((groups, 2 * width, GROUP_ITEMS * depth), jnp.bfloat16),
            pltpu.VMEM((subs, 2 * width, row_count), jnp.float32),
            pltpu.VMEM((row_count // tile, tile if finishes else 8, 2 * subs * width), jnp.float32),
            pltpu.SMEM((groups * GROUP_ITEMS,), jnp.float32),
            pltpu.SMEM((groups,), jnp.int32),
            pltpu.SMEM((subs,), jnp.int32),
            pltpu.SemaphoreType.DMA,
            pltpu.SemaphoreType.DMA((row_count // tile,)),
        ],
        compiler_params=pltpu.CompilerParams(vmem_limit_bytes=SHORT_VMEM_BYTES if finishes else VMEM_BYTES),
        cost_estimate=pl.CostEstimate(
            flops=4 * row_count * slots * depth * width, bytes_accessed=1, transcendentals=0
        ),
        name="short_range",
    )(
        half,
        live,
        sub_ids,
        meta,
        in_hbm(aux_basis),
        aux_decay.reshape(1, -1),
        *items,
        *([in_hbm(earlier)] if adds else []),
    )


def long_kernel(*refs, blocks, chains, pieces, width):
    parts = refs[: blocks * chains]
    factors = refs[blocks * chains : (blocks + pieces) * chains]
    outs, scratch = refs[(blocks + pieces) * chains :][:pieces], refs[-pieces - 2 :]
    right, made, out_sem = scratch[0], scratch[1:-1], scratch[-1]
    depth = factors[0].shape[0]
    half = depth // 2
    count = parts[0].shape[0]
    copies = []
    for piece in reversed(range(pieces)):
        for chain in range(chains):
            factor = factors[piece * chains + chain]
            top = chain * depth
            if factor.shape[1] > width:
                right[top : top + depth, :] = factor[...]
                continue
            right[top : top + depth, 0:width] = factor[...]
            right[top : top + half, width:] = factor[half:, :]
            right[top + half : top + depth, width:] = -factor[0:half, :]
        for block in range(blocks):
            left = jnp.concatenate(
                [parts[block * chains + chain][...] for chain in range(chains)], axis=1
            )
            total = jnp.dot(left, right[...], preferred_element_type=jnp.float32)
            made[piece][block] = total.astype(outs[piece].dtype)
            target = outs[piece].at[pl.ds(block * count, count), :]
            copies.append(
                pltpu.make_async_copy(made[piece].at[block], target, out_sem.at[piece, block])
            )
            copies[-1].start()
    for copy in copies:
        copy.wait()


def long_range(blocks, factors, width):
    depth = factors[0][0].shape[0]
    chains = len(factors[0])
    pieces = len(factors)
    count = blocks[0][0].shape[0]
    shape = (len(blocks) * count, 2 * width)
    dtypes = [jnp.bfloat16] * pieces
    flat = [v for group in [*blocks, *factors] for v in group]
    return pl.pallas_call(
        functools.partial(
            long_kernel, blocks=len(blocks), chains=chains, pieces=pieces, width=width
        ),
        out_shape=[pltpu.HBM(shape, dtype) for dtype in dtypes],
        in_specs=[pl.BlockSpec(memory_space=pltpu.VMEM)] * len(flat),
        out_specs=[pl.BlockSpec(memory_space=pltpu.HBM)] * pieces,
        scratch_shapes=[pltpu.VMEM((chains * depth, 2 * width), jnp.bfloat16)]
        + [pltpu.VMEM((len(blocks), count, 2 * width), dtype) for dtype in dtypes]
        + [pltpu.SemaphoreType.DMA((pieces, len(blocks)))],
        compiler_params=pltpu.CompilerParams(vmem_limit_bytes=VMEM_BYTES),
        cost_estimate=SMALL_COST,
        name="long_range",
    )(*flat)


def own_kernel(order_ref, *refs, blocks, chains, pieces, aliased):
    parts = refs[: blocks * chains]
    factors = refs[blocks * chains : (blocks + 1) * chains]
    arrived = refs[(blocks + 1) * chains :][:pieces]
    short_ref = refs[(blocks + 1) * chains + pieces]
    out_ref, right, terms, made, right_sem, term_sem, out_sem = refs[
        (blocks + 1) * chains + pieces + 1 + aliased :
    ]
    rows = terms.shape[1]
    depth, width = factors[0].shape
    half = depth // 2
    right_copies = []
    for chain, factor in enumerate(factors):
        target = right.at[pl.ds(chain * depth, depth), pl.ds(0, width)]
        right_copies.append(pltpu.make_async_copy(factor, target, right_sem.at[chain]))
        right_copies[-1].start()
    windows = [pl.ds(pl.multiple_of(order_ref[n] * rows, rows), rows) for n in range(blocks + pieces)]
    arriving = []
    for n, window in enumerate(windows):
        arriving.append(
            pltpu.make_async_copy(short_ref.at[window, :], terms.at[n], term_sem.at[n])
        )
        arriving[-1].start()
    for chain, copy in enumerate(right_copies):
        copy.wait()
        top = chain * depth
        right[top : top + half, width:] = right[top + half : top + depth, 0:width]
        right[top + half : top + depth, width:] = -right[top : top + half, 0:width]
    leaving = []
    for n, window in enumerate(windows):
        if n < blocks:
            left = [parts[n * chains + chain][...] for chain in range(chains)]
            left = jnp.concatenate(left, axis=1)
            total = jnp.dot(left, right[...], preferred_element_type=jnp.float32)
        else:
            total = arrived[n - blocks][...].astype(jnp.float32)
        arriving[n].wait()
        made[n] = (total + terms[n]).astype(made.dtype).reshape(made.shape[1:])
        leaving.append(pltpu.make_async_copy(made.at[n], out_ref.at[window], out_sem.at[n]))
        leaving[-1].start()
    for copy in leaving:
        copy.wait()


def own_sum(order, blocks, factors, pieces, short, earlier):
    rows, depth = blocks[0][0].shape
    width = factors[0].shape[1]
    row_count, columns = short.shape
    chains = len(factors)
    count = len(blocks) + len(pieces)
    aliased = earlier is not None
    flat = [v for group in blocks for v in group] + [in_hbm(v) for v in factors] + pieces
    return pl.pallas_call(
        functools.partial(
            own_kernel, blocks=len(blocks), chains=chains, pieces=len(pieces), aliased=aliased
        ),
        out_shape=pltpu.HBM((row_count, 2, width), jnp.bfloat16),
        in_specs=[pl.BlockSpec(memory_space=pltpu.SMEM)]
        + [pl.BlockSpec(memory_space=pltpu.VMEM)] * (chains * len(blocks))
        + [pl.BlockSpec(memory_space=pltpu.HBM)] * chains
        + [pl.BlockSpec(memory_space=pltpu.VMEM)] * len(pieces)
        + [pl.BlockSpec(memory_space=pltpu.HBM)] * (1 + aliased),
        out_specs=pl.BlockSpec(memory_space=pltpu.HBM),
        scratch_shapes=[
            pltpu.VMEM((chains * depth, 2 * width), jnp.bfloat16),
            pltpu.VMEM((count, rows, columns), jnp.float32),
            pltpu.VMEM((count, rows, 2, width), jnp.bfloat16),
            pltpu.SemaphoreType.DMA((chains,)),
            pltpu.SemaphoreType.DMA((count,)),
            pltpu.SemaphoreType.DMA((count,)),
        ],
        input_output_aliases={len(flat) + 2: 0} if aliased else {},
        compiler_params=pltpu.CompilerParams(vmem_limit_bytes=VMEM_BYTES),
        cost_estimate=SMALL_COST,
        name="own_sum",
    )(order, *flat, in_hbm(short), *([earlier] if aliased else []))


def final_kernel(order_ref, *refs, pieces, blocks, aliased):
    short_ref = refs[pieces]
    out_ref, terms, made, term_sem, out_sem = refs[pieces + 1 + aliased :]
    steps, rows = terms.shape[:2]
    windows = [pl.ds(pl.multiple_of(order_ref[n] * rows, rows), rows) for n in range(steps)]
    arriving = []
    for n, window in enumerate(windows):
        arriving.append(
            pltpu.make_async_copy(short_ref.at[window, :], terms.at[n], term_sem.at[n])
        )
        arriving[-1].start()
    leaving = []
    for n, window in enumerate(windows):
        arriving[n].wait()
        top = n % blocks * rows
        total = refs[n // blocks][top : top + rows, :].astype(jnp.float32) + terms[n]
        made[n] = total.astype(made.dtype).reshape(made.shape[1:])
        leaving.append(pltpu.make_async_copy(made.at[n], out_ref.at[window], out_sem.at[n]))
        leaving[-1].start()
    for copy in leaving:
        copy.wait()


def final_sum(order, pieces, short, earlier, rows):
    columns = pieces[0].shape[1]
    row_count = short.shape[0]
    count = len(pieces)
    blocks = pieces[0].shape[0] // rows
    steps = count * blocks
    return pl.pallas_call(
        functools.partial(final_kernel, pieces=count, blocks=blocks, aliased=True),
        out_shape=pltpu.HBM((row_count, 2, columns // 2), jnp.bfloat16),
        in_specs=[pl.BlockSpec(memory_space=pltpu.SMEM)]
        + [pl.BlockSpec(memory_space=pltpu.VMEM)] * count
        + [pl.BlockSpec(memory_space=pltpu.HBM)] * 2,
        out_specs=pl.BlockSpec(memory_space=pltpu.HBM),
        scratch_shapes=[
            pltpu.VMEM((steps, rows, columns), jnp.float32),
            pltpu.VMEM((steps, rows, 2, columns // 2), jnp.bfloat16),
            pltpu.SemaphoreType.DMA((steps,)),
            pltpu.SemaphoreType.DMA((steps,)),
        ],
        input_output_aliases={count + 2: 0},
        compiler_params=pltpu.CompilerParams(vmem_limit_bytes=VMEM_BYTES),
        cost_estimate=SMALL_COST,
        name="final_sum",
    )(order, *pieces, in_hbm(short), earlier)


def slot_table(image_dist, image_phase, images):
    chosen = images[None, :] == jnp.arange(image_dist.shape[0], dtype=jnp.int32)[:, None]
    distance = jnp.sum(jnp.where(chosen, image_dist[:, None], 0.0), axis=0)
    phase = jnp.sum(jnp.where(chosen, image_phase[:, None], 0.0), axis=0)
    return jnp.stack([distance, jnp.cos(phase), jnp.sin(phase)])


def both_parts(factor):
    half = factor.shape[0] // 2
    return jnp.concatenate(
        [factor, jnp.concatenate([factor[half:], -factor[:half]], axis=0)], axis=1
    )


def slot_block(slots, items):
    digits = jnp.concatenate([slots // 128, slots % 128], axis=0).astype(items.dtype)
    fill = [(0, full - used) for full, used in zip(items.shape[1:], digits.shape)]
    return jnp.pad(digits, fill)[None]


def read_slots(packed, slots):
    count, share = slots.shape
    digits = packed[-1, 0 : 2 * count, 0:share].astype(jnp.int32)
    return digits[0:count] * 128 + digits[count:]


def after(value, *earlier):
    return lax.optimization_barrier((value, *earlier))[0] if earlier else value


def body(
    pair_ft,
    aux_ft,
    coul_weight,
    aux_basis,
    aux_decay,
    image_dist,
    image_phase,
    item_pair,
    item_image,
    item_sub,
    item_count,
):
    group_count = lax.axis_size("grp")
    member_count = lax.axis_size("dev")
    group = lax.axis_index("grp")
    member = lax.axis_index("dev")
    local_rows, _, local_g = pair_ft.shape
    subs = local_rows // item_pair.shape[2]
    rows = aux_ft.shape[0]
    row_count = rows * member_count // group_count
    half = jnp.reshape(group, (1,)).astype(jnp.int32)

    chips = member_count // CORES
    breadth = max(n for n in range(1, chips + 1) if chips % n == 0 and n * n <= chips)
    length = chips // breadth

    aux_flat = aux_ft.reshape(rows, 2 * local_g)
    pairs = pair_ft.astype(jnp.float32)
    weighted = (pairs * coul_weight[None, None, :]).astype(jnp.bfloat16)
    turned = weighted.reshape(local_rows, 2 * local_g).T
    item_rows = jnp.swapaxes(item_pair, 1, 2)
    live = (jnp.arange(item_image.shape[0], dtype=jnp.int32) < item_count[0]).astype(jnp.int32)
    slots = jnp.stack([item_image, item_sub, live])

    if group_count != 2 or length % 2:
        everything = lax.all_gather(aux_flat, "dev", axis=0, tiled=True)
        mine = lax.all_to_all(everything, "grp", split_axis=0, concat_axis=1, tiled=True)
        factor = lax.all_gather(turned, "grp", axis=0, tiled=True)
        parts = factor.reshape(group_count, 2, local_g, local_rows)
        other = jnp.stack([parts[:, 1], -parts[:, 0]], axis=1).reshape(factor.shape)
        long_part = jnp.concatenate(
            [
                jnp.dot(mine, factor, preferred_element_type=jnp.float32),
                jnp.dot(mine, other, preferred_element_type=jnp.float32),
            ],
            axis=1,
        )
        items = lax.all_gather(item_rows, "grp", axis=0, tiled=True)
        images, sub_ids, live = lax.all_gather(slots, "grp", axis=1, tiled=True)
        table = slot_table(image_dist, image_phase, images)
        short = short_range(
            half, live, sub_ids, table, aux_basis, aux_decay, [items], row_count, subs
        )
        return (long_part + short).astype(jnp.bfloat16).reshape(row_count, 2, local_rows)

    home = length // 2
    place = member // (breadth * CORES)
    across = member // CORES % breadth
    core = member % CORES

    def send(value, route):
        def index(g, z, y, c):
            return g * member_count + (z * breadth + y) * CORES + c

        pairs = []
        for g in range(group_count):
            for z in range(length):
                for y in range(breadth):
                    for c in range(CORES):
                        pairs.append((index(g, z, y, c), index(*route(g, z, y, c))))
        return lax.ppermute(value, AXES, pairs)

    def to_plane(value):
        return send(value, lambda g, z, y, c: (1 - g, z, y, c))

    ring = [*range(0, length, 2), *reversed(range(1, length, 2))]
    turn = {z: n for n, z in enumerate(ring)}

    def along(value, step):
        return send(value, lambda g, z, y, c: (g, ring[(turn[z] + step) % length], y, c))

    def over_y(value, s):
        return send(value, lambda g, z, y, c: (g, z, (y + s) % breadth, c))

    def over_core(value, t):
        return send(value, lambda g, z, y, c: (g, z, y, (c + t) % CORES))

    def hops_of(g, z):
        hops = [(turn[z] - turn[j]) % length for j in range(g * home, (g + 1) * home)]
        return sorted(hops, key=lambda k: (min(k, length - k), k))

    def here(number):
        return sum(
            jnp.where((group == g) & (place == z), number(g, z), 0)
            for g in range(group_count)
            for z in range(length)
        )

    def pick(other, n, *earlier):
        wanted = here(lambda g, z: hops_of(g ^ other, z)[n])
        possible = sorted({hops_of(g, z)[n] for g in range(group_count) for z in range(length)})
        blocks = lax.optimization_barrier((*(held[k] for k in possible), *earlier))
        value = blocks[len(possible) - 1]
        for k, block in reversed(list(zip(possible[:-1], blocks))):
            value = jnp.where(wanted == k, block, value)
        return value

    def slab_of(n):
        return here(lambda g, z: ring[(turn[z] - hops_of(g, z)[n]) % length] - g * home)

    def number_of(n, s, t):
        return (slab_of(n) * breadth + (across - s) % breadth) * CORES + (core - t) % CORES

    def with_cores(value):
        return [value] + [over_core(value, t) for t in range(1, CORES)]

    held = {0: aux_flat, 1: along(aux_flat, 1), length - 1: along(aux_flat, -1)}
    packed = jnp.concatenate([item_rows, slot_block(slots, item_rows)], axis=0)
    turned_x = to_plane(turned)
    factors = [[turned, turned_x]] + [[over_y(turned, s)] for s in range(1, breadth)]
    items_x = to_plane(packed)
    mine = []
    theirs = []
    crossed = []
    away = []
    arriving = []

    def foreign(n, *earlier):
        theirs.append(pick(True, n, *earlier))
        return to_plane(theirs[n])

    def multiply(n, t, away_factors):
        made = []
        if breadth > 1:
            made = long_range([(mine[n][t], crossed[n][t])], away_factors, local_rows)
        away[n].extend(made)
        arriving[n].append([over_y(v, s) for s, v in enumerate(made, 1)])

    def short_part(slots, items, *how):
        images, sub_ids, live = slots
        table = slot_table(image_dist, image_phase, images)
        return short_range(
            half, live, sub_ids, table, aux_basis, aux_decay, [items], row_count, subs, *how
        )

    short = short_part(slots, packed, None, False)

    moved = foreign(0, short)
    begun = [turned_x, *(pair[0] for pair in factors[1:])]
    for k in range(2, length // 2 + 1):
        held[k] = along(after(held[k - 1], held[1], held[length - 1], short), 1)
    for k in range(2, (length + 1) // 2):
        held[length - k] = along(after(held[length - k + 1], held[1], held[length - 1], short), -1)
    for s in range(1, breadth):
        factors[s].append(over_y(after(turned_x, theirs[0], *begun), s))

    short = short_part(read_slots(after(items_x, theirs[0], *begun), slots), items_x, short)

    def arrived_of(n):
        return [
            [(v, number_of(n, s, t)) for s, v in enumerate(arriving[n][t], 1)] for t in range(CORES)
        ]

    out = None
    for n in range(home):
        if n:
            moved = foreign(n, theirs[n - 1], *(away[n - 2] if n > 1 else [short]))
        away.append([])
        arriving.append([])
        mine.append(with_cores(pick(False, n, theirs[n], *([*away[n - 1], out] if n else begun))))
        away_factors = factors[1:]
        if n:
            away_factors = [[both_parts(after(v, *away[0])) for v in pair] for pair in factors[1:]]
        crossed.append(with_cores(moved if n else after(moved, short, held[length // 2])))
        for t in range(CORES):
            multiply(n, t, away_factors)
        blocks = [
            (after(mine[n][0], *away[n]), crossed[n][0]),
            *zip(mine[n][1:], crossed[n][1:]),
        ]
        numbers = [number_of(n, 0, t) for t in range(CORES)]
        pieces = []
        if n:
            come = [(v, number) for entries in arrived_of(n - 1) for v, number in entries]
            pieces = [v for v, _ in come]
            numbers += [number for _, number in come]
        out = own_sum(jnp.stack(numbers).astype(jnp.int32), blocks, factors[0], pieces, short, out)
    for entries in arrived_of(home - 1):
        if entries:
            order = jnp.stack([number for _, number in entries]).astype(jnp.int32)
            out = final_sum(order, [piece for piece, _ in entries], short, out, rows)
    return out


def solution(mesh):
    return jax.shard_map(
        body,
        mesh=mesh,
        in_specs=(
            P("dev", None, "grp"),
            P("dev", None, "grp"),
            P("grp"),
            P(),
            P(),
            P(),
            P(),
            P(("grp", "dev"), None, None),
            P(("grp", "dev")),
            P(("grp", "dev")),
            P(("grp", "dev")),
        ),
        out_specs=P("grp", None, "dev"),
        check_vma=False,
    )
```

```python
import functools

import jax
import jax.numpy as jnp
from jax import lax
from jax.experimental import pallas as pl
from jax.experimental.pallas import tpu as pltpu
from jax.sharding import PartitionSpec as P

AXES = ("grp", "dev")
CORES = 2
SMALL_COST = pl.CostEstimate(flops=1, bytes_accessed=1, transcendentals=0)
GROUP_ITEMS = 8
SHORT_VMEM_BYTES = 20 * 1024 * 1024
VMEM_BYTES = 10 * 1024 * 1024


def in_hbm(value):
    return pltpu.with_memory_space_constraint(value, pltpu.HBM)


def short_kernel(
    half_ref, live_ref, sub_ref, meta_ref, basis_ref, decay_ref, *refs, share, subs, depth, width, adds, finishes
):
    items, scratch = refs[: -10 - adds], refs[-10:]
    out_ref, basis, left, acc, made, dists, group_sub, cursor, basis_sem, out_sem = scratch
    slots = share * len(items)
    row_count = acc.shape[2]
    tile = made.shape[1]
    if adds:
        acc_copy = pltpu.make_async_copy(refs[-11], acc, out_sem.at[0])
        acc_copy.start()
    else:
        acc[...] = jnp.zeros_like(acc)
    mine = pl.ds(pl.multiple_of(half_ref[0] * row_count, row_count), row_count)
    basis_copy = pltpu.make_async_copy(basis_ref.at[:, mine], basis, basis_sem)
    basis_copy.start()
    left[...] = jnp.zeros_like(left)

    for s in range(subs):
        cursor[s] = 0

    def count(i, carry):
        cursor[sub_ref[i]] = cursor[sub_ref[i]] + live_ref[i]
        return carry

    lax.fori_loop(0, slots, count, 0)
    first = jnp.int32(0)
    for s in range(subs):
        groups = (cursor[s] + GROUP_ITEMS - 1) // GROUP_ITEMS

        def mark(i, carry, s=s):
            group_sub[i] = s
            return carry

        lax.fori_loop(first, first + groups, mark, 0)
        cursor[s] = first * GROUP_ITEMS
        first = first + groups

    def clear(i, carry):
        dists[i] = 0.0
        return carry

    lax.fori_loop(0, first * GROUP_ITEMS, clear, 0)

    for n, items_ref in enumerate(items):

        def place(k, carry, first=n * share, items_ref=items_ref):
            i = first + k

            @pl.when(live_ref[i] > 0)
            def _():
                s = sub_ref[i]
                at = cursor[s]
                cursor[s] = at + 1
                dists[at] = meta_ref[0, i]
                turned = items_ref[k].astype(jnp.float32)
                lanes = pl.ds(pl.multiple_of((at % GROUP_ITEMS) * depth, depth), depth)
                group = at // GROUP_ITEMS
                left[group, 0:width, lanes] = (turned * meta_ref[1, i]).astype(left.dtype)
                left[group, width:, lanes] = (turned * meta_ref[2, i]).astype(left.dtype)

            return carry

        lax.fori_loop(0, share, place, 0)

    decay = decay_ref[:, mine]
    basis_copy.wait()
    if adds:
        acc_copy.wait()

    def one_group(group, carry):
        s = group_sub[group]
        damping = [
            jnp.exp(decay * -dists[group * GROUP_ITEMS + k]).astype(basis.dtype)
            for k in range(GROUP_ITEMS)
        ]
        for t in range(0, row_count, tile):
            right = jnp.concatenate(
                [
                    basis[:, t : t + tile] * damping[k][:, t : t + tile]
                    for k in range(GROUP_ITEMS)
                ],
                axis=0,
            )
            acc[s, :, t : t + tile] += jnp.dot(
                left[group], right, preferred_element_type=jnp.float32
            )
        return carry

    lax.fori_loop(0, first, one_group, 0)
    if not finishes:
        acc_copy = pltpu.make_async_copy(acc, out_ref, out_sem.at[0])
        acc_copy.start()
        acc_copy.wait()
        return
    copies = []
    for n, t in enumerate(range(0, row_count, tile)):
        for s in range(subs):
            for c in range(2):
                column = (c * subs + s) * width
                made[n, :, column : column + width] = acc[
                    s, c * width : (c + 1) * width, t : t + tile
                ].T
        copies.append(pltpu.make_async_copy(made.at[n], out_ref.at[pl.ds(t, tile), :], out_sem.at[n]))
        copies[-1].start()
    for copy in copies:
        copy.wait()


def short_range(half, live, sub_ids, meta, aux_basis, aux_decay, items, row_count, subs, earlier=None, finishes=True):
    adds = earlier is not None
    _, width, depth = items[0].shape
    slots = live.shape[0]
    share = slots // len(items)
    groups = slots // GROUP_ITEMS + subs
    tile = min(row_count, 512)
    kernel = functools.partial(
        short_kernel, share=share, subs=subs, depth=depth, width=width, adds=adds, finishes=finishes
    )
    return pl.pallas_call(
        kernel,
        out_shape=pltpu.HBM(
            (row_count, 2 * subs * width) if finishes else (subs, 2 * width, row_count), jnp.float32
        ),
        in_specs=[pl.BlockSpec(memory_space=pltpu.SMEM)] * 4
        + [pl.BlockSpec(memory_space=pltpu.HBM)]
        + [pl.BlockSpec(memory_space=pltpu.VMEM)] * (1 + len(items))
        + [pl.BlockSpec(memory_space=pltpu.HBM)] * adds,
        out_specs=pl.BlockSpec(memory_space=pltpu.HBM),
        scratch_shapes=[
            pltpu.VMEM((depth, row_count), jnp.bfloat16),
            pltpu.VMEM((groups, 2 * width, GROUP_ITEMS * depth), jnp.bfloat16),
            pltpu.VMEM((subs, 2 * width, row_count), jnp.float32),
            pltpu.VMEM((row_count // tile, tile, 2 * subs * width), jnp.float32),
            pltpu.SMEM((groups * GROUP_ITEMS,), jnp.float32),
            pltpu.SMEM((groups,), jnp.int32),
            pltpu.SMEM((subs,), jnp.int32),
            pltpu.SemaphoreType.DMA,
            pltpu.SemaphoreType.DMA((row_count // tile,)),
        ],
        compiler_params=pltpu.CompilerParams(vmem_limit_bytes=SHORT_VMEM_BYTES),
        cost_estimate=pl.CostEstimate(
            flops=4 * row_count * slots * depth * width, bytes_accessed=1, transcendentals=0
        ),
        name="short_range",
    )(
        half,
        live,
        sub_ids,
        meta,
        in_hbm(aux_basis),
        aux_decay.reshape(1, -1),
        *items,
        *([in_hbm(earlier)] if adds else []),
    )


def long_kernel(*refs, blocks, chains, pieces, width):
    parts = refs[: blocks * chains]
    factors = refs[blocks * chains : (blocks + pieces) * chains]
    outs, scratch = refs[(blocks + pieces) * chains :][:pieces], refs[-pieces - 2 :]
    right, made, out_sem = scratch[0], scratch[1:-1], scratch[-1]
    depth = factors[0].shape[0]
    half = depth // 2
    count = parts[0].shape[0]
    copies = []
    for piece in reversed(range(pieces)):
        for chain in range(chains):
            factor = factors[piece * chains + chain]
            top = chain * depth
            if factor.shape[1] > width:
                right[top : top + depth, :] = factor[...]
                continue
            right[top : top + depth, 0:width] = factor[...]
            right[top : top + half, width:] = factor[half:, :]
            right[top + half : top + depth, width:] = -factor[0:half, :]
        for block in range(blocks):
            left = jnp.concatenate(
                [parts[block * chains + chain][...] for chain in range(chains)], axis=1
            )
            total = jnp.dot(left, right[...], preferred_element_type=jnp.float32)
            made[piece][block] = total.astype(outs[piece].dtype)
            target = outs[piece].at[pl.ds(block * count, count), :]
            copies.append(
                pltpu.make_async_copy(made[piece].at[block], target, out_sem.at[piece, block])
            )
            copies[-1].start()
    for copy in copies:
        copy.wait()


def long_range(blocks, factors, width):
    depth = factors[0][0].shape[0]
    chains = len(factors[0])
    pieces = len(factors)
    count = blocks[0][0].shape[0]
    shape = (len(blocks) * count, 2 * width)
    dtypes = [jnp.bfloat16] * pieces
    flat = [v for group in [*blocks, *factors] for v in group]
    return pl.pallas_call(
        functools.partial(
            long_kernel, blocks=len(blocks), chains=chains, pieces=pieces, width=width
        ),
        out_shape=[pltpu.HBM(shape, dtype) for dtype in dtypes],
        in_specs=[pl.BlockSpec(memory_space=pltpu.VMEM)] * len(flat),
        out_specs=[pl.BlockSpec(memory_space=pltpu.HBM)] * pieces,
        scratch_shapes=[pltpu.VMEM((chains * depth, 2 * width), jnp.bfloat16)]
        + [pltpu.VMEM((len(blocks), count, 2 * width), dtype) for dtype in dtypes]
        + [pltpu.SemaphoreType.DMA((pieces, len(blocks)))],
        compiler_params=pltpu.CompilerParams(vmem_limit_bytes=VMEM_BYTES),
        cost_estimate=SMALL_COST,
        name="long_range",
    )(*flat)


def own_kernel(order_ref, *refs, blocks, chains, pieces, aliased):
    parts = refs[: blocks * chains]
    factors = refs[blocks * chains : (blocks + 1) * chains]
    arrived = refs[(blocks + 1) * chains :][:pieces]
    short_ref = refs[(blocks + 1) * chains + pieces]
    out_ref, right, terms, made, right_sem, term_sem, out_sem = refs[
        (blocks + 1) * chains + pieces + 1 + aliased :
    ]
    rows = terms.shape[1]
    depth, width = factors[0].shape
    half = depth // 2
    right_copies = []
    for chain, factor in enumerate(factors):
        target = right.at[pl.ds(chain * depth, depth), pl.ds(0, width)]
        right_copies.append(pltpu.make_async_copy(factor, target, right_sem.at[chain]))
        right_copies[-1].start()
    windows = [pl.ds(pl.multiple_of(order_ref[n] * rows, rows), rows) for n in range(blocks + pieces)]
    arriving = []
    for n, window in enumerate(windows):
        arriving.append(
            pltpu.make_async_copy(short_ref.at[window, :], terms.at[n], term_sem.at[n])
        )
        arriving[-1].start()
    for chain, copy in enumerate(right_copies):
        copy.wait()
        top = chain * depth
        right[top : top + half, width:] = right[top + half : top + depth, 0:width]
        right[top + half : top + depth, width:] = -right[top : top + half, 0:width]
    leaving = []
    for n, window in enumerate(windows):
        if n < blocks:
            left = [parts[n * chains + chain][...] for chain in range(chains)]
            left = jnp.concatenate(left, axis=1)
            total = jnp.dot(left, right[...], preferred_element_type=jnp.float32)
        else:
            total = arrived[n - blocks][...].astype(jnp.float32)
        arriving[n].wait()
        made[n] = (total + terms[n]).astype(made.dtype).reshape(made.shape[1:])
        leaving.append(pltpu.make_async_copy(made.at[n], out_ref.at[window], out_sem.at[n]))
        leaving[-1].start()
    for copy in leaving:
        copy.wait()


def own_sum(order, blocks, factors, pieces, short, earlier):
    rows, depth = blocks[0][0].shape
    width = factors[0].shape[1]
    row_count, columns = short.shape
    chains = len(factors)
    count = len(blocks) + len(pieces)
    aliased = earlier is not None
    flat = [v for group in blocks for v in group] + [in_hbm(v) for v in factors] + pieces
    return pl.pallas_call(
        functools.partial(
            own_kernel, blocks=len(blocks), chains=chains, pieces=len(pieces), aliased=aliased
        ),
        out_shape=pltpu.HBM((row_count, 2, width), jnp.bfloat16),
        in_specs=[pl.BlockSpec(memory_space=pltpu.SMEM)]
        + [pl.BlockSpec(memory_space=pltpu.VMEM)] * (chains * len(blocks))
        + [pl.BlockSpec(memory_space=pltpu.HBM)] * chains
        + [pl.BlockSpec(memory_space=pltpu.VMEM)] * len(pieces)
        + [pl.BlockSpec(memory_space=pltpu.HBM)] * (1 + aliased),
        out_specs=pl.BlockSpec(memory_space=pltpu.HBM),
        scratch_shapes=[
            pltpu.VMEM((chains * depth, 2 * width), jnp.bfloat16),
            pltpu.VMEM((count, rows, columns), jnp.float32),
            pltpu.VMEM((count, rows, 2, width), jnp.bfloat16),
            pltpu.SemaphoreType.DMA((chains,)),
            pltpu.SemaphoreType.DMA((count,)),
            pltpu.SemaphoreType.DMA((count,)),
        ],
        input_output_aliases={len(flat) + 2: 0} if aliased else {},
        compiler_params=pltpu.CompilerParams(vmem_limit_bytes=VMEM_BYTES),
        cost_estimate=SMALL_COST,
        name="own_sum",
    )(order, *flat, in_hbm(short), *([earlier] if aliased else []))


def final_kernel(order_ref, *refs, pieces, blocks, aliased):
    short_ref = refs[pieces]
    out_ref, terms, made, term_sem, out_sem = refs[pieces + 1 + aliased :]
    steps, rows = terms.shape[:2]
    windows = [pl.ds(pl.multiple_of(order_ref[n] * rows, rows), rows) for n in range(steps)]
    arriving = []
    for n, window in enumerate(windows):
        arriving.append(
            pltpu.make_async_copy(short_ref.at[window, :], terms.at[n], term_sem.at[n])
        )
        arriving[-1].start()
    leaving = []
    for n, window in enumerate(windows):
        arriving[n].wait()
        top = n % blocks * rows
        total = refs[n // blocks][top : top + rows, :].astype(jnp.float32) + terms[n]
        made[n] = total.astype(made.dtype).reshape(made.shape[1:])
        leaving.append(pltpu.make_async_copy(made.at[n], out_ref.at[window], out_sem.at[n]))
        leaving[-1].start()
    for copy in leaving:
        copy.wait()


def final_sum(order, pieces, short, earlier, rows):
    columns = pieces[0].shape[1]
    row_count = short.shape[0]
    count = len(pieces)
    blocks = pieces[0].shape[0] // rows
    steps = count * blocks
    return pl.pallas_call(
        functools.partial(final_kernel, pieces=count, blocks=blocks, aliased=True),
        out_shape=pltpu.HBM((row_count, 2, columns // 2), jnp.bfloat16),
        in_specs=[pl.BlockSpec(memory_space=pltpu.SMEM)]
        + [pl.BlockSpec(memory_space=pltpu.VMEM)] * count
        + [pl.BlockSpec(memory_space=pltpu.HBM)] * 2,
        out_specs=pl.BlockSpec(memory_space=pltpu.HBM),
        scratch_shapes=[
            pltpu.VMEM((steps, rows, columns), jnp.float32),
            pltpu.VMEM((steps, rows, 2, columns // 2), jnp.bfloat16),
            pltpu.SemaphoreType.DMA((steps,)),
            pltpu.SemaphoreType.DMA((steps,)),
        ],
        input_output_aliases={count + 2: 0},
        compiler_params=pltpu.CompilerParams(vmem_limit_bytes=VMEM_BYTES),
        cost_estimate=SMALL_COST,
        name="final_sum",
    )(order, *pieces, in_hbm(short), earlier)


def slot_table(image_dist, image_phase, images):
    chosen = images[None, :] == jnp.arange(image_dist.shape[0], dtype=jnp.int32)[:, None]
    distance = jnp.sum(jnp.where(chosen, image_dist[:, None], 0.0), axis=0)
    phase = jnp.sum(jnp.where(chosen, image_phase[:, None], 0.0), axis=0)
    return jnp.stack([distance, jnp.cos(phase), jnp.sin(phase)])


def both_parts(factor):
    half = factor.shape[0] // 2
    return jnp.concatenate(
        [factor, jnp.concatenate([factor[half:], -factor[:half]], axis=0)], axis=1
    )


def slot_block(slots, items):
    digits = jnp.concatenate([slots // 128, slots % 128], axis=0).astype(items.dtype)
    fill = [(0, full - used) for full, used in zip(items.shape[1:], digits.shape)]
    return jnp.pad(digits, fill)[None]


def read_slots(packed, slots):
    count, share = slots.shape
    digits = packed[-1, 0 : 2 * count, 0:share].astype(jnp.int32)
    return digits[0:count] * 128 + digits[count:]


def after(value, *earlier):
    return lax.optimization_barrier((value, *earlier))[0] if earlier else value


def body(
    pair_ft,
    aux_ft,
    coul_weight,
    aux_basis,
    aux_decay,
    image_dist,
    image_phase,
    item_pair,
    item_image,
    item_sub,
    item_count,
):
    group_count = lax.axis_size("grp")
    member_count = lax.axis_size("dev")
    group = lax.axis_index("grp")
    member = lax.axis_index("dev")
    local_rows, _, local_g = pair_ft.shape
    subs = local_rows // item_pair.shape[2]
    rows = aux_ft.shape[0]
    row_count = rows * member_count // group_count
    half = jnp.reshape(group, (1,)).astype(jnp.int32)

    chips = member_count // CORES
    breadth = max(n for n in range(1, chips + 1) if chips % n == 0 and n * n <= chips)
    length = chips // breadth

    aux_flat = aux_ft.reshape(rows, 2 * local_g)
    pairs = pair_ft.astype(jnp.float32)
    weighted = (pairs * coul_weight[None, None, :]).astype(jnp.bfloat16)
    turned = weighted.reshape(local_rows, 2 * local_g).T
    item_rows = jnp.swapaxes(item_pair, 1, 2)
    live = (jnp.arange(item_image.shape[0], dtype=jnp.int32) < item_count[0]).astype(jnp.int32)
    slots = jnp.stack([item_image, item_sub, live])

    if group_count != 2 or length % 2:
        everything = lax.all_gather(aux_flat, "dev", axis=0, tiled=True)
        mine = lax.all_to_all(everything, "grp", split_axis=0, concat_axis=1, tiled=True)
        factor = lax.all_gather(turned, "grp", axis=0, tiled=True)
        parts = factor.reshape(group_count, 2, local_g, local_rows)
        other = jnp.stack([parts[:, 1], -parts[:, 0]], axis=1).reshape(factor.shape)
        long_part = jnp.concatenate(
            [
                jnp.dot(mine, factor, preferred_element_type=jnp.float32),
                jnp.dot(mine, other, preferred_element_type=jnp.float32),
            ],
            axis=1,
        )
        items = lax.all_gather(item_rows, "grp", axis=0, tiled=True)
        images, sub_ids, live = lax.all_gather(slots, "grp", axis=1, tiled=True)
        table = slot_table(image_dist, image_phase, images)
        short = short_range(
            half, live, sub_ids, table, aux_basis, aux_decay, [items], row_count, subs
        )
        return (long_part + short).astype(jnp.bfloat16).reshape(row_count, 2, local_rows)

    home = length // 2
    place = member // (breadth * CORES)
    across = member // CORES % breadth
    core = member % CORES

    def send(value, route):
        def index(g, z, y, c):
            return g * member_count + (z * breadth + y) * CORES + c

        pairs = []
        for g in range(group_count):
            for z in range(length):
                for y in range(breadth):
                    for c in range(CORES):
                        pairs.append((index(g, z, y, c), index(*route(g, z, y, c))))
        return lax.ppermute(value, AXES, pairs)

    def to_plane(value):
        return send(value, lambda g, z, y, c: (1 - g, z, y, c))

    ring = [*range(0, length, 2), *reversed(range(1, length, 2))]
    turn = {z: n for n, z in enumerate(ring)}

    def along(value, step):
        return send(value, lambda g, z, y, c: (g, ring[(turn[z] + step) % length], y, c))

    def over_y(value, s):
        return send(value, lambda g, z, y, c: (g, z, (y + s) % breadth, c))

    def over_core(value, t):
        return send(value, lambda g, z, y, c: (g, z, y, (c + t) % CORES))

    def hops_of(g, z):
        hops = [(turn[z] - turn[j]) % length for j in range(g * home, (g + 1) * home)]
        return sorted(hops, key=lambda k: (min(k, length - k), k))

    def here(number):
        return sum(
            jnp.where((group == g) & (place == z), number(g, z), 0)
            for g in range(group_count)
            for z in range(length)
        )

    def pick(other, n, *earlier):
        wanted = here(lambda g, z: hops_of(g ^ other, z)[n])
        possible = sorted({hops_of(g, z)[n] for g in range(group_count) for z in range(length)})
        blocks = lax.optimization_barrier((*(held[k] for k in possible), *earlier))
        value = blocks[len(possible) - 1]
        for k, block in reversed(list(zip(possible[:-1], blocks))):
            value = jnp.where(wanted == k, block, value)
        return value

    def slab_of(n):
        return here(lambda g, z: ring[(turn[z] - hops_of(g, z)[n]) % length] - g * home)

    def number_of(n, s, t):
        return (slab_of(n) * breadth + (across - s) % breadth) * CORES + (core - t) % CORES

    def with_cores(value):
        return [value] + [over_core(value, t) for t in range(1, CORES)]

    held = {0: aux_flat, 1: along(aux_flat, 1), length - 1: along(aux_flat, -1)}
    packed = jnp.concatenate([item_rows, slot_block(slots, item_rows)], axis=0)
    turned_x = to_plane(turned)
    factors = [[turned, turned_x]] + [[over_y(turned, s)] for s in range(1, breadth)]
    items_x = to_plane(packed)
    mine = []
    theirs = []
    crossed = []
    away = []
    arriving = []

    def foreign(n, *earlier):
        theirs.append(pick(True, n, *earlier))
        return to_plane(theirs[n])

    def multiply(n, t, away_factors):
        made = []
        if breadth > 1:
            made = long_range([(mine[n][t], crossed[n][t])], away_factors, local_rows)
        away[n].extend(made)
        arriving[n].append([over_y(v, s) for s, v in enumerate(made, 1)])

    def short_part(slots, items, *how):
        images, sub_ids, live = slots
        table = slot_table(image_dist, image_phase, images)
        return short_range(
            half, live, sub_ids, table, aux_basis, aux_decay, [items], row_count, subs, *how
        )

    short = short_part(slots, packed, None, False)

    moved = foreign(0, short)
    begun = [turned_x, *(pair[0] for pair in factors[1:])]
    for k in range(2, length // 2 + 1):
        held[k] = along(after(held[k - 1], held[1], held[length - 1], short), 1)
    for k in range(2, (length + 1) // 2):
        held[length - k] = along(after(held[length - k + 1], held[1], held[length - 1], short), -1)
    for s in range(1, breadth):
        factors[s].append(over_y(after(turned_x, theirs[0], *begun), s))

    short = short_part(read_slots(after(items_x, theirs[0], *begun), slots), items_x, short)

    def arrived_of(n):
        return [
            [(v, number_of(n, s, t)) for s, v in enumerate(arriving[n][t], 1)] for t in range(CORES)
        ]

    out = None
    for n in range(home):
        if n:
            moved = foreign(n, theirs[n - 1], *(away[n - 2] if n > 1 else [short]))
        away.append([])
        arriving.append([])
        mine.append(with_cores(pick(False, n, theirs[n], *([*away[n - 1], out] if n else begun))))
        away_factors = factors[1:]
        if n:
            away_factors = [[both_parts(after(v, *away[0])) for v in pair] for pair in factors[1:]]
        crossed.append(with_cores(moved if n else after(moved, short, held[length // 2])))
        for t in range(CORES):
            multiply(n, t, away_factors)
        blocks = [
            (after(mine[n][0], *away[n]), crossed[n][0]),
            *zip(mine[n][1:], crossed[n][1:]),
        ]
        numbers = [number_of(n, 0, t) for t in range(CORES)]
        pieces = []
        if n:
            come = [(v, number) for entries in arrived_of(n - 1) for v, number in entries]
            pieces = [v for v, _ in come]
            numbers += [number for _, number in come]
        out = own_sum(jnp.stack(numbers).astype(jnp.int32), blocks, factors[0], pieces, short, out)
    for entries in arrived_of(home - 1):
        if entries:
            order = jnp.stack([number for _, number in entries]).astype(jnp.int32)
            out = final_sum(order, [piece for piece, _ in entries], short, out, rows)
    return out


def solution(mesh):
    return jax.shard_map(
        body,
        mesh=mesh,
        in_specs=(
            P("dev", None, "grp"),
            P("dev", None, "grp"),
            P("grp"),
            P(),
            P(),
            P(),
            P(),
            P(("grp", "dev"), None, None),
            P(("grp", "dev")),
            P(("grp", "dev")),
            P(("grp", "dev")),
        ),
        out_specs=P("grp", None, "dev"),
        check_vma=False,
    )
```

```python
import functools

import jax
import jax.numpy as jnp
from jax import lax
from jax.experimental import pallas as pl
from jax.experimental.pallas import tpu as pltpu
from jax.sharding import PartitionSpec as P

AXES = ("grp", "dev")
CORES = 2
SMALL_COST = pl.CostEstimate(flops=1, bytes_accessed=1, transcendentals=0)
GROUP_ITEMS = 4
SHORT_VMEM_BYTES = 15 * 1024 * 1024
VMEM_BYTES = 10 * 1024 * 1024
SMALL_VMEM_BYTES = 6 * 1024 * 1024


def in_hbm(value):
    return pltpu.with_memory_space_constraint(value, pltpu.HBM)


def short_kernel(
    half_ref, live_ref, sub_ref, meta_ref, basis_ref, decay_ref, *refs, share, subs, depth, width, adds, finishes, tile
):
    items, scratch = refs[: -10 - adds], refs[-10:]
    out_ref, basis, left, acc, made, dists, group_sub, cursor, basis_sem, out_sem = scratch
    slots = share * len(items)
    row_count = acc.shape[2]
    if adds:
        acc_copy = pltpu.make_async_copy(refs[-11], acc, out_sem.at[0])
        acc_copy.start()
    else:
        acc[...] = jnp.zeros_like(acc)
    mine = pl.ds(pl.multiple_of(half_ref[0] * row_count, row_count), row_count)
    basis_copy = pltpu.make_async_copy(basis_ref.at[:, mine], basis, basis_sem)
    basis_copy.start()
    left[...] = jnp.zeros_like(left)

    for s in range(subs):
        cursor[s] = 0

    def count(i, carry):
        cursor[sub_ref[i]] = cursor[sub_ref[i]] + live_ref[i]
        return carry

    lax.fori_loop(0, slots, count, 0)
    first = jnp.int32(0)
    for s in range(subs):
        groups = (cursor[s] + GROUP_ITEMS - 1) // GROUP_ITEMS

        def mark(i, carry, s=s):
            group_sub[i] = s
            return carry

        lax.fori_loop(first, first + groups, mark, 0)
        cursor[s] = first * GROUP_ITEMS
        first = first + groups

    def clear(i, carry):
        dists[i] = 0.0
        return carry

    lax.fori_loop(0, first * GROUP_ITEMS, clear, 0)

    for n, items_ref in enumerate(items):

        def place(k, carry, first=n * share, items_ref=items_ref):
            i = first + k

            @pl.when(live_ref[i] > 0)
            def _():
                s = sub_ref[i]
                at = cursor[s]
                cursor[s] = at + 1
                dists[at] = meta_ref[0, i]
                turned = items_ref[k].astype(jnp.float32)
                lanes = pl.ds(pl.multiple_of((at % GROUP_ITEMS) * depth, depth), depth)
                group = at // GROUP_ITEMS
                left[group, 0:width, lanes] = (turned * meta_ref[1, i]).astype(left.dtype)
                left[group, width:, lanes] = (turned * meta_ref[2, i]).astype(left.dtype)

            return carry

        lax.fori_loop(0, share, place, 0)

    decay = decay_ref[:, mine]
    basis_copy.wait()
    if adds:
        acc_copy.wait()

    def one_group(group, carry):
        s = group_sub[group]
        damping = [
            jnp.exp(decay * -dists[group * GROUP_ITEMS + k]).astype(basis.dtype)
            for k in range(GROUP_ITEMS)
        ]
        for t in range(0, row_count, tile):
            right = jnp.concatenate(
                [
                    basis[:, t : t + tile] * damping[k][:, t : t + tile]
                    for k in range(GROUP_ITEMS)
                ],
                axis=0,
            )
            acc[s, :, t : t + tile] += jnp.dot(
                left[group], right, preferred_element_type=jnp.float32
            )
        return carry

    lax.fori_loop(0, first, one_group, 0)
    if not finishes:
        acc_copy = pltpu.make_async_copy(acc, out_ref, out_sem.at[0])
        acc_copy.start()
        acc_copy.wait()
        return
    copies = []
    for n, t in enumerate(range(0, row_count, tile)):
        for s in range(subs):
            for c in range(2):
                column = (c * subs + s) * width
                made[n, :, column : column + width] = acc[
                    s, c * width : (c + 1) * width, t : t + tile
                ].T
        copies.append(pltpu.make_async_copy(made.at[n], out_ref.at[pl.ds(t, tile), :], out_sem.at[n]))
        copies[-1].start()
    for copy in copies:
        copy.wait()


def short_range(half, live, sub_ids, meta, aux_basis, aux_decay, items, row_count, subs, earlier=None, finishes=True):
    adds = earlier is not None
    _, width, depth = items[0].shape
    slots = live.shape[0]
    share = slots // len(items)
    groups = slots // GROUP_ITEMS + subs
    tile = min(row_count, 512)
    kernel = functools.partial(
        short_kernel, share=share, subs=subs, depth=depth, width=width, adds=adds, finishes=finishes, tile=tile
    )
    return pl.pallas_call(
        kernel,
        out_shape=pltpu.HBM(
            (row_count, 2 * subs * width) if finishes else (subs, 2 * width, row_count), jnp.float32
        ),
        in_specs=[pl.BlockSpec(memory_space=pltpu.SMEM)] * 4
        + [pl.BlockSpec(memory_space=pltpu.HBM)]
        + [pl.BlockSpec(memory_space=pltpu.VMEM)] * (1 + len(items))
        + [pl.BlockSpec(memory_space=pltpu.HBM)] * adds,
        out_specs=pl.BlockSpec(memory_space=pltpu.HBM),
        scratch_shapes=[
            pltpu.VMEM((depth, row_count), jnp.bfloat16),
            pltpu.VMEM((groups, 2 * width, GROUP_ITEMS * depth), jnp.bfloat16),
            pltpu.VMEM((subs, 2 * width, row_count), jnp.float32),
            pltpu.VMEM((row_count // tile, tile if finishes else 8, 2 * subs * width), jnp.float32),
            pltpu.SMEM((groups * GROUP_ITEMS,), jnp.float32),
            pltpu.SMEM((groups,), jnp.int32),
            pltpu.SMEM((subs,), jnp.int32),
            pltpu.SemaphoreType.DMA,
            pltpu.SemaphoreType.DMA((row_count // tile,)),
        ],
        compiler_params=pltpu.CompilerParams(vmem_limit_bytes=SHORT_VMEM_BYTES if finishes else VMEM_BYTES),
        cost_estimate=pl.CostEstimate(
            flops=4 * row_count * slots * depth * width, bytes_accessed=1, transcendentals=0
        ),
        name="short_range",
    )(
        half,
        live,
        sub_ids,
        meta,
        in_hbm(aux_basis),
        aux_decay.reshape(1, -1),
        *items,
        *([in_hbm(earlier)] if adds else []),
    )


def long_kernel(*refs, blocks, chains, pieces, width):
    parts = refs[: blocks * chains]
    factors = refs[blocks * chains : (blocks + pieces) * chains]
    outs, scratch = refs[(blocks + pieces) * chains :][:pieces], refs[-pieces - 2 :]
    right, made, out_sem = scratch[0], scratch[1:-1], scratch[-1]
    depth = factors[0].shape[0]
    half = depth // 2
    count = parts[0].shape[0]
    copies = []
    for piece in reversed(range(pieces)):
        for chain in range(chains):
            factor = factors[piece * chains + chain]
            top = chain * depth
            if factor.shape[1] > width:
                right[top : top + depth, :] = factor[...]
                continue
            right[top : top + depth, 0:width] = factor[...]
            right[top : top + half, width:] = factor[half:, :]
            right[top + half : top + depth, width:] = -factor[0:half, :]
        for block in range(blocks):
            left = jnp.concatenate(
                [parts[block * chains + chain][...] for chain in range(chains)], axis=1
            )
            total = jnp.dot(left, right[...], preferred_element_type=jnp.float32)
            made[piece][block] = total.astype(outs[piece].dtype)
            target = outs[piece].at[pl.ds(block * count, count), :]
            copies.append(
                pltpu.make_async_copy(made[piece].at[block], target, out_sem.at[piece, block])
            )
            copies[-1].start()
    for copy in copies:
        copy.wait()


def long_range(blocks, factors, width):
    depth = factors[0][0].shape[0]
    chains = len(factors[0])
    pieces = len(factors)
    count = blocks[0][0].shape[0]
    shape = (len(blocks) * count, 2 * width)
    dtypes = [jnp.bfloat16] * pieces
    flat = [v for group in [*blocks, *factors] for v in group]
    return pl.pallas_call(
        functools.partial(
            long_kernel, blocks=len(blocks), chains=chains, pieces=pieces, width=width
        ),
        out_shape=[pltpu.HBM(shape, dtype) for dtype in dtypes],
        in_specs=[pl.BlockSpec(memory_space=pltpu.VMEM)] * len(flat),
        out_specs=[pl.BlockSpec(memory_space=pltpu.HBM)] * pieces,
        scratch_shapes=[pltpu.VMEM((chains * depth, 2 * width), jnp.bfloat16)]
        + [pltpu.VMEM((len(blocks), count, 2 * width), dtype) for dtype in dtypes]
        + [pltpu.SemaphoreType.DMA((pieces, len(blocks)))],
        compiler_params=pltpu.CompilerParams(vmem_limit_bytes=SMALL_VMEM_BYTES),
        cost_estimate=SMALL_COST,
        name="long_range",
    )(*flat)


def own_kernel(order_ref, *refs, blocks, chains, pieces, aliased):
    parts = refs[: blocks * chains]
    factors = refs[blocks * chains : (blocks + 1) * chains]
    arrived = refs[(blocks + 1) * chains :][:pieces]
    short_ref = refs[(blocks + 1) * chains + pieces]
    out_ref, right, terms, made, right_sem, term_sem, out_sem = refs[
        (blocks + 1) * chains + pieces + 1 + aliased :
    ]
    rows = terms.shape[1]
    depth, width = factors[0].shape
    half = depth // 2
    right_copies = []
    for chain, factor in enumerate(factors):
        target = right.at[pl.ds(chain * depth, depth), pl.ds(0, width)]
        right_copies.append(pltpu.make_async_copy(factor, target, right_sem.at[chain]))
        right_copies[-1].start()
    windows = [pl.ds(pl.multiple_of(order_ref[n] * rows, rows), rows) for n in range(blocks + pieces)]
    arriving = []
    for n, window in enumerate(windows):
        arriving.append(
            pltpu.make_async_copy(short_ref.at[window, :], terms.at[n], term_sem.at[n])
        )
        arriving[-1].start()
    for chain, copy in enumerate(right_copies):
        copy.wait()
        top = chain * depth
        right[top : top + half, width:] = right[top + half : top + depth, 0:width]
        right[top + half : top + depth, width:] = -right[top : top + half, 0:width]
    leaving = []
    for n, window in enumerate(windows):
        if n < blocks:
            left = [parts[n * chains + chain][...] for chain in range(chains)]
            left = jnp.concatenate(left, axis=1)
            total = jnp.dot(left, right[...], preferred_element_type=jnp.float32)
        else:
            total = arrived[n - blocks][...].astype(jnp.float32)
        arriving[n].wait()
        made[n] = (total + terms[n]).astype(made.dtype).reshape(made.shape[1:])
        leaving.append(pltpu.make_async_copy(made.at[n], out_ref.at[window], out_sem.at[n]))
        leaving[-1].start()
    for copy in leaving:
        copy.wait()


def own_sum(order, blocks, factors, pieces, short, earlier):
    rows, depth = blocks[0][0].shape
    width = factors[0].shape[1]
    row_count, columns = short.shape
    chains = len(factors)
    count = len(blocks) + len(pieces)
    aliased = earlier is not None
    flat = [v for group in blocks for v in group] + [in_hbm(v) for v in factors] + pieces
    return pl.pallas_call(
        functools.partial(
            own_kernel, blocks=len(blocks), chains=chains, pieces=len(pieces), aliased=aliased
        ),
        out_shape=pltpu.HBM((row_count, 2, width), jnp.bfloat16),
        in_specs=[pl.BlockSpec(memory_space=pltpu.SMEM)]
        + [pl.BlockSpec(memory_space=pltpu.VMEM)] * (chains * len(blocks))
        + [pl.BlockSpec(memory_space=pltpu.HBM)] * chains
        + [pl.BlockSpec(memory_space=pltpu.VMEM)] * len(pieces)
        + [pl.BlockSpec(memory_space=pltpu.HBM)] * (1 + aliased),
        out_specs=pl.BlockSpec(memory_space=pltpu.HBM),
        scratch_shapes=[
            pltpu.VMEM((chains * depth, 2 * width), jnp.bfloat16),
            pltpu.VMEM((count, rows, columns), jnp.float32),
            pltpu.VMEM((count, rows, 2, width), jnp.bfloat16),
            pltpu.SemaphoreType.DMA((chains,)),
            pltpu.SemaphoreType.DMA((count,)),
            pltpu.SemaphoreType.DMA((count,)),
        ],
        input_output_aliases={len(flat) + 2: 0} if aliased else {},
        compiler_params=pltpu.CompilerParams(vmem_limit_bytes=VMEM_BYTES),
        cost_estimate=SMALL_COST,
        name="own_sum",
    )(order, *flat, in_hbm(short), *([earlier] if aliased else []))


def final_kernel(order_ref, *refs, pieces, blocks, aliased):
    short_ref = refs[pieces]
    out_ref, terms, made, term_sem, out_sem = refs[pieces + 1 + aliased :]
    steps, rows = terms.shape[:2]
    windows = [pl.ds(pl.multiple_of(order_ref[n] * rows, rows), rows) for n in range(steps)]
    arriving = []
    for n, window in enumerate(windows):
        arriving.append(
            pltpu.make_async_copy(short_ref.at[window, :], terms.at[n], term_sem.at[n])
        )
        arriving[-1].start()
    leaving = []
    for n, window in enumerate(windows):
        arriving[n].wait()
        top = n % blocks * rows
        total = refs[n // blocks][top : top + rows, :].astype(jnp.float32) + terms[n]
        made[n] = total.astype(made.dtype).reshape(made.shape[1:])
        leaving.append(pltpu.make_async_copy(made.at[n], out_ref.at[window], out_sem.at[n]))
        leaving[-1].start()
    for copy in leaving:
        copy.wait()


def final_sum(order, pieces, short, earlier, rows):
    columns = pieces[0].shape[1]
    row_count = short.shape[0]
    count = len(pieces)
    blocks = pieces[0].shape[0] // rows
    steps = count * blocks
    return pl.pallas_call(
        functools.partial(final_kernel, pieces=count, blocks=blocks, aliased=True),
        out_shape=pltpu.HBM((row_count, 2, columns // 2), jnp.bfloat16),
        in_specs=[pl.BlockSpec(memory_space=pltpu.SMEM)]
        + [pl.BlockSpec(memory_space=pltpu.VMEM)] * count
        + [pl.BlockSpec(memory_space=pltpu.HBM)] * 2,
        out_specs=pl.BlockSpec(memory_space=pltpu.HBM),
        scratch_shapes=[
            pltpu.VMEM((steps, rows, columns), jnp.float32),
            pltpu.VMEM((steps, rows, 2, columns // 2), jnp.bfloat16),
            pltpu.SemaphoreType.DMA((steps,)),
            pltpu.SemaphoreType.DMA((steps,)),
        ],
        input_output_aliases={count + 2: 0},
        compiler_params=pltpu.CompilerParams(vmem_limit_bytes=SMALL_VMEM_BYTES),
        cost_estimate=SMALL_COST,
        name="final_sum",
    )(order, *pieces, in_hbm(short), earlier)


def slot_table(image_dist, image_phase, images):
    chosen = images[None, :] == jnp.arange(image_dist.shape[0], dtype=jnp.int32)[:, None]
    distance = jnp.sum(jnp.where(chosen, image_dist[:, None], 0.0), axis=0)
    phase = jnp.sum(jnp.where(chosen, image_phase[:, None], 0.0), axis=0)
    return jnp.stack([distance, jnp.cos(phase), jnp.sin(phase)])


def both_parts(factor):
    half = factor.shape[0] // 2
    return jnp.concatenate(
        [factor, jnp.concatenate([factor[half:], -factor[:half]], axis=0)], axis=1
    )


def slot_block(slots, items):
    digits = jnp.concatenate([slots // 128, slots % 128], axis=0).astype(items.dtype)
    fill = [(0, full - used) for full, used in zip(items.shape[1:], digits.shape)]
    return jnp.pad(digits, fill)[None]


def read_slots(packed, slots):
    count, share = slots.shape
    digits = packed[-1, 0 : 2 * count, 0:share].astype(jnp.int32)
    return digits[0:count] * 128 + digits[count:]


def after(value, *earlier):
    return lax.optimization_barrier((value, *earlier))[0] if earlier else value


def body(
    pair_ft,
    aux_ft,
    coul_weight,
    aux_basis,
    aux_decay,
    image_dist,
    image_phase,
    item_pair,
    item_image,
    item_sub,
    item_count,
):
    group_count = lax.axis_size("grp")
    member_count = lax.axis_size("dev")
    group = lax.axis_index("grp")
    member = lax.axis_index("dev")
    local_rows, _, local_g = pair_ft.shape
    subs = local_rows // item_pair.shape[2]
    rows = aux_ft.shape[0]
    row_count = rows * member_count // group_count
    half = jnp.reshape(group, (1,)).astype(jnp.int32)

    chips = member_count // CORES
    breadth = max(n for n in range(1, chips + 1) if chips % n == 0 and n * n <= chips)
    length = chips // breadth

    aux_flat = aux_ft.reshape(rows, 2 * local_g)
    pairs = pair_ft.astype(jnp.float32)
    weighted = (pairs * coul_weight[None, None, :]).astype(jnp.bfloat16)
    turned = weighted.reshape(local_rows, 2 * local_g).T
    item_rows = jnp.swapaxes(item_pair, 1, 2)
    live = (jnp.arange(item_image.shape[0], dtype=jnp.int32) < item_count[0]).astype(jnp.int32)
    slots = jnp.stack([item_image, item_sub, live])

    if group_count != 2 or length % 2:
        everything = lax.all_gather(aux_flat, "dev", axis=0, tiled=True)
        mine = lax.all_to_all(everything, "grp", split_axis=0, concat_axis=1, tiled=True)
        factor = lax.all_gather(turned, "grp", axis=0, tiled=True)
        parts = factor.reshape(group_count, 2, local_g, local_rows)
        other = jnp.stack([parts[:, 1], -parts[:, 0]], axis=1).reshape(factor.shape)
        long_part = jnp.concatenate(
            [
                jnp.dot(mine, factor, preferred_element_type=jnp.float32),
                jnp.dot(mine, other, preferred_element_type=jnp.float32),
            ],
            axis=1,
        )
        items = lax.all_gather(item_rows, "grp", axis=0, tiled=True)
        images, sub_ids, live = lax.all_gather(slots, "grp", axis=1, tiled=True)
        table = slot_table(image_dist, image_phase, images)
        short = short_range(
            half, live, sub_ids, table, aux_basis, aux_decay, [items], row_count, subs
        )
        return (long_part + short).astype(jnp.bfloat16).reshape(row_count, 2, local_rows)

    home = length // 2
    place = member // (breadth * CORES)
    across = member // CORES % breadth
    core = member % CORES

    def send(value, route):
        def index(g, z, y, c):
            return g * member_count + (z * breadth + y) * CORES + c

        pairs = []
        for g in range(group_count):
            for z in range(length):
                for y in range(breadth):
                    for c in range(CORES):
                        pairs.append((index(g, z, y, c), index(*route(g, z, y, c))))
        return lax.ppermute(value, AXES, pairs)

    def to_plane(value):
        return send(value, lambda g, z, y, c: (1 - g, z, y, c))

    ring = [*range(0, length, 2), *reversed(range(1, length, 2))]
    turn = {z: n for n, z in enumerate(ring)}

    def along(value, step):
        return send(value, lambda g, z, y, c: (g, ring[(turn[z] + step) % length], y, c))

    def over_y(value, s):
        return send(value, lambda g, z, y, c: (g, z, (y + s) % breadth, c))

    def over_core(value, t):
        return send(value, lambda g, z, y, c: (g, z, y, (c + t) % CORES))

    def hops_of(g, z):
        hops = [(turn[z] - turn[j]) % length for j in range(g * home, (g + 1) * home)]
        return sorted(hops, key=lambda k: (min(k, length - k), k))

    def here(number):
        return sum(
            jnp.where((group == g) & (place == z), number(g, z), 0)
            for g in range(group_count)
            for z in range(length)
        )

    def pick(other, n, *earlier):
        wanted = here(lambda g, z: hops_of(g ^ other, z)[n])
        possible = sorted({hops_of(g, z)[n] for g in range(group_count) for z in range(length)})
        blocks = lax.optimization_barrier((*(held[k] for k in possible), *earlier))
        value = blocks[len(possible) - 1]
        for k, block in reversed(list(zip(possible[:-1], blocks))):
            value = jnp.where(wanted == k, block, value)
        return value

    def slab_of(n):
        return here(lambda g, z: ring[(turn[z] - hops_of(g, z)[n]) % length] - g * home)

    def number_of(n, s, t):
        return (slab_of(n) * breadth + (across - s) % breadth) * CORES + (core - t) % CORES

    def with_cores(value):
        return [value] + [over_core(value, t) for t in range(1, CORES)]

    held = {0: aux_flat, 1: along(aux_flat, 1), length - 1: along(aux_flat, -1)}
    packed = jnp.concatenate([item_rows, slot_block(slots, item_rows)], axis=0)
    turned_x = to_plane(turned)
    factors = [[turned, turned_x]] + [[over_y(turned, s)] for s in range(1, breadth)]
    items_x = to_plane(packed)
    mine = []
    theirs = []
    crossed = []
    away = []
    arriving = []

    def foreign(n, *earlier):
        theirs.append(pick(True, n, *earlier))
        return to_plane(theirs[n])

    def multiply(n, t, away_factors):
        made = []
        if breadth > 1:
            made = long_range([(mine[n][t], crossed[n][t])], away_factors, local_rows)
        away[n].extend(made)
        arriving[n].append([over_y(v, s) for s, v in enumerate(made, 1)])

    def short_part(slots, items, *how):
        images, sub_ids, live = slots
        table = slot_table(image_dist, image_phase, images)
        return short_range(
            half, live, sub_ids, table, aux_basis, aux_decay, [items], row_count, subs, *how
        )

    short = short_part(slots, packed, None, False)

    moved = foreign(0, short)
    begun = [turned_x, *(pair[0] for pair in factors[1:])]
    for k in range(2, length // 2 + 1):
        held[k] = along(after(held[k - 1], held[1], held[length - 1], short), 1)
    for k in range(2, (length + 1) // 2):
        held[length - k] = along(after(held[length - k + 1], held[1], held[length - 1], short), -1)
    for s in range(1, breadth):
        factors[s].append(over_y(after(turned_x, theirs[0], *begun), s))

    short = short_part(read_slots(after(items_x, theirs[0], *begun), slots), items_x, short)

    def arrived_of(n):
        return [
            [(v, number_of(n, s, t)) for s, v in enumerate(arriving[n][t], 1)] for t in range(CORES)
        ]

    out = None
    for n in range(home):
        if n:
            moved = foreign(n, theirs[n - 1], *(away[n - 2] if n > 1 else [short]))
        away.append([])
        arriving.append([])
        mine.append(with_cores(pick(False, n, theirs[n], *([*away[n - 1], out] if n else begun))))
        away_factors = factors[1:]
        if n:
            away_factors = [[both_parts(after(v, *away[0])) for v in pair] for pair in factors[1:]]
        crossed.append(with_cores(moved if n else after(moved, short, held[length // 2])))
        for t in range(CORES):
            multiply(n, t, away_factors)
        blocks = [
            (after(mine[n][0], *away[n]), crossed[n][0]),
            *zip(mine[n][1:], crossed[n][1:]),
        ]
        numbers = [number_of(n, 0, t) for t in range(CORES)]
        pieces = []
        if n:
            come = [(v, number) for entries in arrived_of(n - 1) for v, number in entries]
            pieces = [v for v, _ in come]
            numbers += [number for _, number in come]
        out = own_sum(jnp.stack(numbers).astype(jnp.int32), blocks, factors[0], pieces, short, out)
    for entries in arrived_of(home - 1):
        if entries:
            order = jnp.stack([number for _, number in entries]).astype(jnp.int32)
            out = final_sum(order, [piece for piece, _ in entries], short, out, rows)
    return out


def solution(mesh):
    return jax.shard_map(
        body,
        mesh=mesh,
        in_specs=(
            P("dev", None, "grp"),
            P("dev", None, "grp"),
            P("grp"),
            P(),
            P(),
            P(),
            P(),
            P(("grp", "dev"), None, None),
            P(("grp", "dev")),
            P(("grp", "dev")),
            P(("grp", "dev")),
        ),
        out_specs=P("grp", None, "dev"),
        check_vma=False,
    )
```

```python
import functools

import jax
import jax.numpy as jnp
from jax import lax
from jax.experimental import pallas as pl
from jax.experimental.pallas import tpu as pltpu
from jax.sharding import PartitionSpec as P

AXES = ("grp", "dev")
CORES = 2
SMALL_COST = pl.CostEstimate(flops=1, bytes_accessed=1, transcendentals=0)
GROUP_ITEMS = 4
SHORT_VMEM_BYTES = 20 * 1024 * 1024
VMEM_BYTES = 10 * 1024 * 1024


def in_hbm(value):
    return pltpu.with_memory_space_constraint(value, pltpu.HBM)


def short_kernel(
    half_ref, live_ref, sub_ref, meta_ref, basis_ref, decay_ref, *refs, share, subs, depth, width, adds, finishes
):
    items, scratch = refs[: -10 - adds], refs[-10:]
    out_ref, basis, left, acc, made, dists, group_sub, cursor, basis_sem, out_sem = scratch
    slots = share * len(items)
    row_count = acc.shape[2]
    tile = made.shape[1]
    if adds:
        acc_copy = pltpu.make_async_copy(refs[-11], acc, out_sem.at[0])
        acc_copy.start()
    else:
        acc[...] = jnp.zeros_like(acc)
    mine = pl.ds(pl.multiple_of(half_ref[0] * row_count, row_count), row_count)
    basis_copy = pltpu.make_async_copy(basis_ref.at[:, mine], basis, basis_sem)
    basis_copy.start()
    left[...] = jnp.zeros_like(left)

    for s in range(subs):
        cursor[s] = 0

    def count(i, carry):
        cursor[sub_ref[i]] = cursor[sub_ref[i]] + live_ref[i]
        return carry

    lax.fori_loop(0, slots, count, 0)
    first = jnp.int32(0)
    for s in range(subs):
        groups = (cursor[s] + GROUP_ITEMS - 1) // GROUP_ITEMS

        def mark(i, carry, s=s):
            group_sub[i] = s
            return carry

        lax.fori_loop(first, first + groups, mark, 0)
        cursor[s] = first * GROUP_ITEMS
        first = first + groups

    def clear(i, carry):
        dists[i] = 0.0
        return carry

    lax.fori_loop(0, first * GROUP_ITEMS, clear, 0)

    for n, items_ref in enumerate(items):

        def place(k, carry, first=n * share, items_ref=items_ref):
            i = first + k

            @pl.when(live_ref[i] > 0)
            def _():
                s = sub_ref[i]
                at = cursor[s]
                cursor[s] = at + 1
                dists[at] = meta_ref[0, i]
                turned = items_ref[k].astype(jnp.float32)
                lanes = pl.ds(pl.multiple_of((at % GROUP_ITEMS) * depth, depth), depth)
                group = at // GROUP_ITEMS
                left[group, 0:width, lanes] = (turned * meta_ref[1, i]).astype(left.dtype)
                left[group, width:, lanes] = (turned * meta_ref[2, i]).astype(left.dtype)

            return carry

        lax.fori_loop(0, share, place, 0)

    decay = decay_ref[:, mine]
    basis_copy.wait()
    if adds:
        acc_copy.wait()

    def one_group(group, carry):
        s = group_sub[group]
        damping = [
            jnp.exp(decay * -dists[group * GROUP_ITEMS + k]).astype(basis.dtype)
            for k in range(GROUP_ITEMS)
        ]
        for t in range(0, row_count, tile):
            right = jnp.concatenate(
                [
                    basis[:, t : t + tile] * damping[k][:, t : t + tile]
                    for k in range(GROUP_ITEMS)
                ],
                axis=0,
            )
            acc[s, :, t : t + tile] += jnp.dot(
                left[group], right, preferred_element_type=jnp.float32
            )
        return carry

    lax.fori_loop(0, first, one_group, 0)
    if not finishes:
        acc_copy = pltpu.make_async_copy(acc, out_ref, out_sem.at[0])
        acc_copy.start()
        acc_copy.wait()
        return
    copies = []
    for n, t in enumerate(range(0, row_count, tile)):
        for s in range(subs):
            for c in range(2):
                column = (c * subs + s) * width
                made[n, :, column : column + width] = acc[
                    s, c * width : (c + 1) * width, t : t + tile
                ].T
        copies.append(pltpu.make_async_copy(made.at[n], out_ref.at[pl.ds(t, tile), :], out_sem.at[n]))
        copies[-1].start()
    for copy in copies:
        copy.wait()


def short_range(half, live, sub_ids, meta, aux_basis, aux_decay, items, row_count, subs, earlier=None, finishes=True):
    adds = earlier is not None
    _, width, depth = items[0].shape
    slots = live.shape[0]
    share = slots // len(items)
    groups = slots // GROUP_ITEMS + subs
    tile = min(row_count, 512)
    kernel = functools.partial(
        short_kernel, share=share, subs=subs, depth=depth, width=width, adds=adds, finishes=finishes
    )
    return pl.pallas_call(
        kernel,
        out_shape=pltpu.HBM(
            (row_count, 2 * subs * width) if finishes else (subs, 2 * width, row_count), jnp.float32
        ),
        in_specs=[pl.BlockSpec(memory_space=pltpu.SMEM)] * 4
        + [pl.BlockSpec(memory_space=pltpu.HBM)]
        + [pl.BlockSpec(memory_space=pltpu.VMEM)] * (1 + len(items))
        + [pl.BlockSpec(memory_space=pltpu.HBM)] * adds,
        out_specs=pl.BlockSpec(memory_space=pltpu.HBM),
        scratch_shapes=[
            pltpu.VMEM((depth, row_count), jnp.bfloat16),
            pltpu.VMEM((groups, 2 * width, GROUP_ITEMS * depth), jnp.bfloat16),
            pltpu.VMEM((subs, 2 * width, row_count), jnp.float32),
            pltpu.VMEM((row_count // tile, tile, 2 * subs * width), jnp.float32),
            pltpu.SMEM((groups * GROUP_ITEMS,), jnp.float32),
            pltpu.SMEM((groups,), jnp.int32),
            pltpu.SMEM((subs,), jnp.int32),
            pltpu.SemaphoreType.DMA,
            pltpu.SemaphoreType.DMA((row_count // tile,)),
        ],
        compiler_params=pltpu.CompilerParams(vmem_limit_bytes=SHORT_VMEM_BYTES),
        cost_estimate=pl.CostEstimate(
            flops=4 * row_count * slots * depth * width, bytes_accessed=1, transcendentals=0
        ),
        name="short_range",
    )(
        half,
        live,
        sub_ids,
        meta,
        in_hbm(aux_basis),
        aux_decay.reshape(1, -1),
        *items,
        *([in_hbm(earlier)] if adds else []),
    )


def long_kernel(*refs, blocks, chains, pieces, width):
    parts = refs[: blocks * chains]
    factors = refs[blocks * chains : (blocks + pieces) * chains]
    outs, scratch = refs[(blocks + pieces) * chains :][:pieces], refs[-pieces - 2 :]
    right, made, out_sem = scratch[0], scratch[1:-1], scratch[-1]
    depth = factors[0].shape[0]
    half = depth // 2
    count = parts[0].shape[0]
    copies = []
    for piece in reversed(range(pieces)):
        for chain in range(chains):
            factor = factors[piece * chains + chain]
            top = chain * depth
            if factor.shape[1] > width:
                right[top : top + depth, :] = factor[...]
                continue
            right[top : top + depth, 0:width] = factor[...]
            right[top : top + half, width:] = factor[half:, :]
            right[top + half : top + depth, width:] = -factor[0:half, :]
        for block in range(blocks):
            left = jnp.concatenate(
                [parts[block * chains + chain][...] for chain in range(chains)], axis=1
            )
            total = jnp.dot(left, right[...], preferred_element_type=jnp.float32)
            made[piece][block] = total.astype(outs[piece].dtype)
            target = outs[piece].at[pl.ds(block * count, count), :]
            copies.append(
                pltpu.make_async_copy(made[piece].at[block], target, out_sem.at[piece, block])
            )
            copies[-1].start()
    for copy in copies:
        copy.wait()


def long_range(blocks, factors, width):
    depth = factors[0][0].shape[0]
    chains = len(factors[0])
    pieces = len(factors)
    count = blocks[0][0].shape[0]
    shape = (len(blocks) * count, 2 * width)
    dtypes = [jnp.bfloat16] * pieces
    flat = [v for group in [*blocks, *factors] for v in group]
    return pl.pallas_call(
        functools.partial(
            long_kernel, blocks=len(blocks), chains=chains, pieces=pieces, width=width
        ),
        out_shape=[pltpu.HBM(shape, dtype) for dtype in dtypes],
        in_specs=[pl.BlockSpec(memory_space=pltpu.VMEM)] * len(flat),
        out_specs=[pl.BlockSpec(memory_space=pltpu.HBM)] * pieces,
        scratch_shapes=[pltpu.VMEM((chains * depth, 2 * width), jnp.bfloat16)]
        + [pltpu.VMEM((len(blocks), count, 2 * width), dtype) for dtype in dtypes]
        + [pltpu.SemaphoreType.DMA((pieces, len(blocks)))],
        compiler_params=pltpu.CompilerParams(vmem_limit_bytes=VMEM_BYTES),
        cost_estimate=SMALL_COST,
        name="long_range",
    )(*flat)


def own_kernel(order_ref, *refs, blocks, chains, pieces, aliased):
    parts = refs[: blocks * chains]
    factors = refs[blocks * chains : (blocks + 1) * chains]
    arrived = refs[(blocks + 1) * chains :][:pieces]
    short_ref = refs[(blocks + 1) * chains + pieces]
    out_ref, right, terms, made, right_sem, term_sem, out_sem = refs[
        (blocks + 1) * chains + pieces + 1 + aliased :
    ]
    rows = terms.shape[1]
    depth, width = factors[0].shape
    half = depth // 2
    right_copies = []
    for chain, factor in enumerate(factors):
        target = right.at[pl.ds(chain * depth, depth), pl.ds(0, width)]
        right_copies.append(pltpu.make_async_copy(factor, target, right_sem.at[chain]))
        right_copies[-1].start()
    windows = [pl.ds(pl.multiple_of(order_ref[n] * rows, rows), rows) for n in range(blocks + pieces)]
    arriving = []
    for n, window in enumerate(windows):
        arriving.append(
            pltpu.make_async_copy(short_ref.at[window, :], terms.at[n], term_sem.at[n])
        )
        arriving[-1].start()
    for chain, copy in enumerate(right_copies):
        copy.wait()
        top = chain * depth
        right[top : top + half, width:] = right[top + half : top + depth, 0:width]
        right[top + half : top + depth, width:] = -right[top : top + half, 0:width]
    leaving = []
    for n, window in enumerate(windows):
        if n < blocks:
            left = [parts[n * chains + chain][...] for chain in range(chains)]
            left = jnp.concatenate(left, axis=1)
            total = jnp.dot(left, right[...], preferred_element_type=jnp.float32)
        else:
            total = arrived[n - blocks][...].astype(jnp.float32)
        arriving[n].wait()
        made[n] = (total + terms[n]).astype(made.dtype).reshape(made.shape[1:])
        leaving.append(pltpu.make_async_copy(made.at[n], out_ref.at[window], out_sem.at[n]))
        leaving[-1].start()
    for copy in leaving:
        copy.wait()


def own_sum(order, blocks, factors, pieces, short, earlier):
    rows, depth = blocks[0][0].shape
    width = factors[0].shape[1]
    row_count, columns = short.shape
    chains = len(factors)
    count = len(blocks) + len(pieces)
    aliased = earlier is not None
    flat = [v for group in blocks for v in group] + [in_hbm(v) for v in factors] + pieces
    return pl.pallas_call(
        functools.partial(
            own_kernel, blocks=len(blocks), chains=chains, pieces=len(pieces), aliased=aliased
        ),
        out_shape=pltpu.HBM((row_count, 2, width), jnp.bfloat16),
        in_specs=[pl.BlockSpec(memory_space=pltpu.SMEM)]
        + [pl.BlockSpec(memory_space=pltpu.VMEM)] * (chains * len(blocks))
        + [pl.BlockSpec(memory_space=pltpu.HBM)] * chains
        + [pl.BlockSpec(memory_space=pltpu.VMEM)] * len(pieces)
        + [pl.BlockSpec(memory_space=pltpu.HBM)] * (1 + aliased),
        out_specs=pl.BlockSpec(memory_space=pltpu.HBM),
        scratch_shapes=[
            pltpu.VMEM((chains * depth, 2 * width), jnp.bfloat16),
            pltpu.VMEM((count, rows, columns), jnp.float32),
            pltpu.VMEM((count, rows, 2, width), jnp.bfloat16),
            pltpu.SemaphoreType.DMA((chains,)),
            pltpu.SemaphoreType.DMA((count,)),
            pltpu.SemaphoreType.DMA((count,)),
        ],
        input_output_aliases={len(flat) + 2: 0} if aliased else {},
        compiler_params=pltpu.CompilerParams(vmem_limit_bytes=VMEM_BYTES),
        cost_estimate=SMALL_COST,
        name="own_sum",
    )(order, *flat, in_hbm(short), *([earlier] if aliased else []))


def final_kernel(order_ref, *refs, pieces, blocks, aliased):
    short_ref = refs[pieces]
    out_ref, terms, made, term_sem, out_sem = refs[pieces + 1 + aliased :]
    steps, rows = terms.shape[:2]
    windows = [pl.ds(pl.multiple_of(order_ref[n] * rows, rows), rows) for n in range(steps)]
    arriving = []
    for n, window in enumerate(windows):
        arriving.append(
            pltpu.make_async_copy(short_ref.at[window, :], terms.at[n], term_sem.at[n])
        )
        arriving[-1].start()
    leaving = []
    for n, window in enumerate(windows):
        arriving[n].wait()
        top = n % blocks * rows
        total = refs[n // blocks][top : top + rows, :].astype(jnp.float32) + terms[n]
        made[n] = total.astype(made.dtype).reshape(made.shape[1:])
        leaving.append(pltpu.make_async_copy(made.at[n], out_ref.at[window], out_sem.at[n]))
        leaving[-1].start()
    for copy in leaving:
        copy.wait()


def final_sum(order, pieces, short, earlier, rows):
    columns = pieces[0].shape[1]
    row_count = short.shape[0]
    count = len(pieces)
    blocks = pieces[0].shape[0] // rows
    steps = count * blocks
    return pl.pallas_call(
        functools.partial(final_kernel, pieces=count, blocks=blocks, aliased=True),
        out_shape=pltpu.HBM((row_count, 2, columns // 2), jnp.bfloat16),
        in_specs=[pl.BlockSpec(memory_space=pltpu.SMEM)]
        + [pl.BlockSpec(memory_space=pltpu.VMEM)] * count
        + [pl.BlockSpec(memory_space=pltpu.HBM)] * 2,
        out_specs=pl.BlockSpec(memory_space=pltpu.HBM),
        scratch_shapes=[
            pltpu.VMEM((steps, rows, columns), jnp.float32),
            pltpu.VMEM((steps, rows, 2, columns // 2), jnp.bfloat16),
            pltpu.SemaphoreType.DMA((steps,)),
            pltpu.SemaphoreType.DMA((steps,)),
        ],
        input_output_aliases={count + 2: 0},
        compiler_params=pltpu.CompilerParams(vmem_limit_bytes=VMEM_BYTES),
        cost_estimate=SMALL_COST,
        name="final_sum",
    )(order, *pieces, in_hbm(short), earlier)


def slot_table(image_dist, image_phase, images):
    chosen = images[None, :] == jnp.arange(image_dist.shape[0], dtype=jnp.int32)[:, None]
    distance = jnp.sum(jnp.where(chosen, image_dist[:, None], 0.0), axis=0)
    phase = jnp.sum(jnp.where(chosen, image_phase[:, None], 0.0), axis=0)
    return jnp.stack([distance, jnp.cos(phase), jnp.sin(phase)])


def both_parts(factor):
    half = factor.shape[0] // 2
    return jnp.concatenate(
        [factor, jnp.concatenate([factor[half:], -factor[:half]], axis=0)], axis=1
    )


def slot_block(slots, items):
    digits = jnp.concatenate([slots // 128, slots % 128], axis=0).astype(items.dtype)
    fill = [(0, full - used) for full, used in zip(items.shape[1:], digits.shape)]
    return jnp.pad(digits, fill)[None]


def read_slots(packed, slots):
    count, share = slots.shape
    digits = packed[-1, 0 : 2 * count, 0:share].astype(jnp.int32)
    return digits[0:count] * 128 + digits[count:]


def after(value, *earlier):
    return lax.optimization_barrier((value, *earlier))[0] if earlier else value


def body(
    pair_ft,
    aux_ft,
    coul_weight,
    aux_basis,
    aux_decay,
    image_dist,
    image_phase,
    item_pair,
    item_image,
    item_sub,
    item_count,
):
    group_count = lax.axis_size("grp")
    member_count = lax.axis_size("dev")
    group = lax.axis_index("grp")
    member = lax.axis_index("dev")
    local_rows, _, local_g = pair_ft.shape
    subs = local_rows // item_pair.shape[2]
    rows = aux_ft.shape[0]
    row_count = rows * member_count // group_count
    half = jnp.reshape(group, (1,)).astype(jnp.int32)

    chips = member_count // CORES
    breadth = max(n for n in range(1, chips + 1) if chips % n == 0 and n * n <= chips)
    length = chips // breadth

    aux_flat = aux_ft.reshape(rows, 2 * local_g)
    pairs = pair_ft.astype(jnp.float32)
    weighted = (pairs * coul_weight[None, None, :]).astype(jnp.bfloat16)
    turned = weighted.reshape(local_rows, 2 * local_g).T
    item_rows = jnp.swapaxes(item_pair, 1, 2)
    live = (jnp.arange(item_image.shape[0], dtype=jnp.int32) < item_count[0]).astype(jnp.int32)
    slots = jnp.stack([item_image, item_sub, live])

    if group_count != 2 or length % 2:
        everything = lax.all_gather(aux_flat, "dev", axis=0, tiled=True)
        mine = lax.all_to_all(everything, "grp", split_axis=0, concat_axis=1, tiled=True)
        factor = lax.all_gather(turned, "grp", axis=0, tiled=True)
        parts = factor.reshape(group_count, 2, local_g, local_rows)
        other = jnp.stack([parts[:, 1], -parts[:, 0]], axis=1).reshape(factor.shape)
        long_part = jnp.concatenate(
            [
                jnp.dot(mine, factor, preferred_element_type=jnp.float32),
                jnp.dot(mine, other, preferred_element_type=jnp.float32),
            ],
            axis=1,
        )
        items = lax.all_gather(item_rows, "grp", axis=0, tiled=True)
        images, sub_ids, live = lax.all_gather(slots, "grp", axis=1, tiled=True)
        table = slot_table(image_dist, image_phase, images)
        short = short_range(
            half, live, sub_ids, table, aux_basis, aux_decay, [items], row_count, subs
        )
        return (long_part + short).astype(jnp.bfloat16).reshape(row_count, 2, local_rows)

    home = length // 2
    place = member // (breadth * CORES)
    across = member // CORES % breadth
    core = member % CORES

    def send(value, route):
        def index(g, z, y, c):
            return g * member_count + (z * breadth + y) * CORES + c

        pairs = []
        for g in range(group_count):
            for z in range(length):
                for y in range(breadth):
                    for c in range(CORES):
                        pairs.append((index(g, z, y, c), index(*route(g, z, y, c))))
        return lax.ppermute(value, AXES, pairs)

    def to_plane(value):
        return send(value, lambda g, z, y, c: (1 - g, z, y, c))

    ring = [*range(0, length, 2), *reversed(range(1, length, 2))]
    turn = {z: n for n, z in enumerate(ring)}

    def along(value, step):
        return send(value, lambda g, z, y, c: (g, ring[(turn[z] + step) % length], y, c))

    def over_y(value, s):
        return send(value, lambda g, z, y, c: (g, z, (y + s) % breadth, c))

    def over_core(value, t):
        return send(value, lambda g, z, y, c: (g, z, y, (c + t) % CORES))

    def hops_of(g, z):
        hops = [(turn[z] - turn[j]) % length for j in range(g * home, (g + 1) * home)]
        return sorted(hops, key=lambda k: (min(k, length - k), k))

    def here(number):
        return sum(
            jnp.where((group == g) & (place == z), number(g, z), 0)
            for g in range(group_count)
            for z in range(length)
        )

    def pick(other, n, *earlier):
        wanted = here(lambda g, z: hops_of(g ^ other, z)[n])
        possible = sorted({hops_of(g, z)[n] for g in range(group_count) for z in range(length)})
        blocks = lax.optimization_barrier((*(held[k] for k in possible), *earlier))
        value = blocks[len(possible) - 1]
        for k, block in reversed(list(zip(possible[:-1], blocks))):
            value = jnp.where(wanted == k, block, value)
        return value

    def slab_of(n):
        return here(lambda g, z: ring[(turn[z] - hops_of(g, z)[n]) % length] - g * home)

    def number_of(n, s, t):
        return (slab_of(n) * breadth + (across - s) % breadth) * CORES + (core - t) % CORES

    def with_cores(value):
        return [value] + [over_core(value, t) for t in range(1, CORES)]

    held = {0: aux_flat, 1: along(aux_flat, 1), length - 1: along(aux_flat, -1)}
    packed = jnp.concatenate([item_rows, slot_block(slots, item_rows)], axis=0)
    turned_x = to_plane(turned)
    factors = [[turned, turned_x]] + [[over_y(turned, s)] for s in range(1, breadth)]
    items_x = to_plane(packed)
    mine = []
    theirs = []
    crossed = []
    away = []
    arriving = []

    def foreign(n, *earlier):
        theirs.append(pick(True, n, *earlier))
        return to_plane(theirs[n])

    def multiply(n, t, away_factors):
        made = []
        if breadth > 1:
            made = long_range([(mine[n][t], crossed[n][t])], away_factors, local_rows)
        away[n].extend(made)
        arriving[n].append([over_y(v, s) for s, v in enumerate(made, 1)])

    def short_part(slots, items, *how):
        images, sub_ids, live = slots
        table = slot_table(image_dist, image_phase, images)
        return short_range(
            half, live, sub_ids, table, aux_basis, aux_decay, [items], row_count, subs, *how
        )

    short = short_part(slots, packed, None, False)

    moved = foreign(0, short)
    begun = [turned_x, *(pair[0] for pair in factors[1:])]
    for k in range(2, length // 2 + 1):
        held[k] = along(after(held[k - 1], held[1], held[length - 1], short), 1)
    for k in range(2, (length + 1) // 2):
        held[length - k] = along(after(held[length - k + 1], held[1], held[length - 1], short), -1)
    for s in range(1, breadth):
        factors[s].append(over_y(after(turned_x, theirs[0], *begun), s))

    short = short_part(read_slots(after(items_x, theirs[0], *begun), slots), items_x, short)

    def arrived_of(n):
        return [
            [(v, number_of(n, s, t)) for s, v in enumerate(arriving[n][t], 1)] for t in range(CORES)
        ]

    out = None
    for n in range(home):
        if n:
            moved = foreign(n, theirs[n - 1], *(away[n - 2] if n > 1 else [short]))
        away.append([])
        arriving.append([])
        mine.append(with_cores(pick(False, n, theirs[n], *([*away[n - 1], out] if n else begun))))
        away_factors = factors[1:]
        if n:
            away_factors = [[both_parts(after(v, *away[0])) for v in pair] for pair in factors[1:]]
        crossed.append(with_cores(moved) if n else [after(moved, short, held[length // 2])])
        for t in range(CORES):
            if t == len(crossed[n]):
                crossed[n].append(over_core(after(crossed[n][0], *away[n]), t))
            multiply(n, t, away_factors)
        blocks = [
            (after(mine[n][0], *away[n]), crossed[n][0]),
            *zip(mine[n][1:], crossed[n][1:]),
        ]
        numbers = [number_of(n, 0, t) for t in range(CORES)]
        pieces = []
        if n:
            come = [(v, number) for entries in arrived_of(n - 1) for v, number in entries]
            pieces = [v for v, _ in come]
            numbers += [number for _, number in come]
        out = own_sum(jnp.stack(numbers).astype(jnp.int32), blocks, factors[0], pieces, short, out)
    for entries in arrived_of(home - 1):
        if entries:
            order = jnp.stack([number for _, number in entries]).astype(jnp.int32)
            out = final_sum(order, [piece for piece, _ in entries], short, out, rows)
    return out


def solution(mesh):
    return jax.shard_map(
        body,
        mesh=mesh,
        in_specs=(
            P("dev", None, "grp"),
            P("dev", None, "grp"),
            P("grp"),
            P(),
            P(),
            P(),
            P(),
            P(("grp", "dev"), None, None),
            P(("grp", "dev")),
            P(("grp", "dev")),
            P(("grp", "dev")),
        ),
        out_specs=P("grp", None, "dev"),
        check_vma=False,
    )
```
